32 devices in a mesh: dp: 8 (over z, y), head: 4 (over x, core).
Axes of the slice: x: 2, y: 2, z: 4, core: 2. Of those that a mesh axis runs over, the one named last changes fastest.
Arguments:
- block_input: bfloat16 [2, 4096, 768], P(None, ('dp', 'head')), may hold values from -6 to 6
- part_lengths: int32 [2, 8, 2], P(None, 'dp'), may hold values from 4 to 254, as said below
- query_weight: bfloat16 [2, 768, 768], replicated, may hold values from -0.21875 to 0.21875
- key_weight: bfloat16 [2, 768, 768], replicated, may hold values from -0.21875 to 0.21875
- value_weight: bfloat16 [2, 768, 768], replicated, may hold values from -0.21875 to 0.21875
- out_weight: bfloat16 [2, 768, 768], replicated, may hold values from -1.75 to 1.75
- down_shared: bfloat16 [768, 1024], replicated, may hold values from -0.21875 to 0.21875
- up_shared: bfloat16 [1024, 768], replicated, may hold values from -0.1875 to 0.1875
- scale_d: float32 [2, 2, 1024], replicated, may hold values from 0.3 to 3
- scale_b: float32 [2, 2, 768], replicated, may hold values from -3 to 3
- ln_gain: float32 [2, 2, 768], replicated, may hold values from 0.25 to 1.75
- ffn_in: bfloat16 [2, 768, 3072], P(None, 'dp'), may hold values from -0.21875 to 0.21875
- ffn_out: bfloat16 [2, 3072, 768], P(None, 'dp'), may hold values from -0.109375 to 0.109375
- out_grad: float32 [2, 4096, 768], P(None, ('dp', 'head')), may hold values from -6 to 6
Outputs:
- block_output: bfloat16 [2, 4096, 768], P(None, ('dp', 'head'))
- input_grad: float32 [2, 4096, 768], P(None, ('dp', 'head'))
- grad_d: float32 [2, 2, 1024], replicated
- grad_b: float32 [2, 2, 768], replicated
The draws below stay inside these ranges and needn't reach their ends.
Inputs may be any that keep to these rules, and one draw needn't show every extreme that they name: Each row holds the token counts of the two texts of a sequence, which with its four separators fill the first part_lengths[m, s, 0] + part_lengths[m, s, 1] + 4 positions; the rest is padding. Among the 2 sequences of each index of dp, one drawn from the seed has both counts equal to 254 and so fills all 512 positions.
All inputs are finite; a program needn't handle non-finite values.
Results may differ from the reference program's by a relative error of at most 0.029.
Values may be sent and summed in bfloat16 or wider, within the bound.
No kernel may reach another device: no remote copies, remote signals or barrier semaphores. Data moves between devices by JAX's collectives and lax.ppermute only.
A program may use at most 192 MiB of HBM per device.

```python
import math
import jax
import jax.numpy as jnp
from jax import lax

D = 768
HEADS = 12
HEAD_DIM = 64
FF = 3072
RANK = 1024
LEN = 512
LAYERS = 2
MBS = 2
SEQ_MB = 1
SEQS = 8
TOK = 4096


def draw_part_lengths(key, part):
    key = jax.random.fold_in(key, 7)
    first_key, second_key = jax.random.split(key)
    half_len = (LEN - 4) // 2
    drawn = jax.random.randint(first_key, (MBS, SEQS, 2), 4, half_len + 1, dtype=jnp.int32)
    group_count = SEQS // SEQ_MB
    chosen = jax.random.randint(second_key, (group_count,), 0, MBS * SEQ_MB, dtype=jnp.int32)
    micro_index = jnp.arange(MBS, dtype=jnp.int32)[:, None]
    seq_index = jnp.arange(SEQS, dtype=jnp.int32)[None, :]
    slot_index = micro_index * SEQ_MB + seq_index % SEQ_MB
    filled = slot_index == chosen[seq_index // SEQ_MB]
    return jnp.where(filled[:, :, None], half_len, drawn).astype(jnp.int32)


def block_levels(stream_key, shape, pieces, least, high):
    factor_of, own = 1.0, jax.random.fold_in(stream_key, 6)
    for position, shards_of in pieces:
        heights = jnp.exp(jax.random.uniform(jax.random.fold_in(own, position), (shards_of,), jnp.float32, least / len(pieces), high / len(pieces)))
        factor_of = factor_of * jnp.repeat(heights, shape[position] // shards_of).reshape([-1 if axis == position else 1 for axis in range(len(shape))])
    return factor_of


def bell_draw(rng, shape, width, most, shards=(), kind=jnp.bfloat16):
    entries = jax.random.normal(rng, shape, jnp.float32) * width
    if len(shards) > 0:
        entries = block_levels(rng, shape, shards, -0.22, 0.18) * entries
    return jnp.clip(entries, min=-most, max=most).astype(kind)


def setup_inputs(seed: int = 0) -> dict:
    arg_keys = jax.random.split(jax.random.key(seed), 15)
    block_input = bell_draw(arg_keys[0], (MBS, TOK, D), 1.0, 6.0, ((1, 32),))
    part_lengths = draw_part_lengths(jax.random.fold_in(arg_keys[14], 71), 0)
    query_weight = bell_draw(arg_keys[2], (LAYERS, D, D), D ** -0.5, 0.21875)
    key_weight = bell_draw(arg_keys[3], (LAYERS, D, D), D ** -0.5, 0.21875)
    value_weight = bell_draw(arg_keys[4], (LAYERS, D, D), D ** -0.5, 0.21875)
    out_weight = bell_draw(arg_keys[5], (LAYERS, D, D), (max(D // 64, 1)) ** -0.5, 1.75)
    down_shared = bell_draw(arg_keys[6], (D, RANK), D ** -0.5, 0.21875)
    up_shared = bell_draw(arg_keys[7], (RANK, D), RANK ** -0.5, 0.1875)
    scale_d = jnp.clip(jnp.exp(jax.random.uniform(arg_keys[8], (LAYERS, 2, RANK), jnp.float32, math.log(0.3), math.log(3.0))), 0.3, 3.0)
    scale_b = bell_draw(arg_keys[9], (LAYERS, 2, D), 0.5, 3.0, (), jnp.float32)
    ln_gain = jnp.clip(1.0 + 0.15 * jax.random.normal(arg_keys[10], (LAYERS, 2, D), jnp.float32), 0.25, 1.75)
    ffn_in = bell_draw(arg_keys[11], (LAYERS, D, FF), D ** -0.5, 0.21875, ((1, 8),))
    ffn_out = bell_draw(arg_keys[12], (LAYERS, FF, D), FF ** -0.5, 0.109375, ((1, 8),))
    out_grad = bell_draw(arg_keys[13], (MBS, TOK, D), 1.0, 6.0, ((1, 32),), jnp.float32)
    return dict(block_input=block_input, part_lengths=part_lengths, query_weight=query_weight, key_weight=key_weight, value_weight=value_weight, out_weight=out_weight, down_shared=down_shared, up_shared=up_shared, scale_d=scale_d, scale_b=scale_b, ln_gain=ln_gain, ffn_in=ffn_in, ffn_out=ffn_out, out_grad=out_grad)


@jax.custom_vjp
def low(v):
    return lax.optimization_barrier(v.astype(jnp.bfloat16)).astype(jnp.float32)

@jax.custom_vjp
def low_back(v):
    return v

def low_keep(v):
    return (low(v), None)

def low_pass(kept, grad):
    return (grad,)

def back_keep(v):
    return (v, None)

def back_low(kept, grad):
    return (low(grad),)
low.defvjp(low_keep, low_pass)
low_back.defvjp(back_keep, back_low)

def matmul_high(left, right):
    return jnp.dot(left, right, precision=lax.Precision.HIGHEST, preferred_element_type=jnp.float32)

def layer_norm(hidden, gain_row):
    centred = hidden - lax.optimization_barrier(jnp.mean(hidden, axis=-1, keepdims=True))
    variance = lax.optimization_barrier(jnp.mean(centred * centred, axis=-1, keepdims=True))
    return centred * lax.rsqrt(variance + 1e-05) * gain_row

def attend(queries, keys_in, values, valid_count):
    raw_scores = jnp.einsum('qhd,khd->hqk', queries, keys_in, precision=lax.Precision.HIGHEST)
    key_mask = jnp.arange(LEN, dtype=jnp.int32) < valid_count
    scores = low_back(jnp.where(key_mask[None, None, :], raw_scores * HEAD_DIM ** (-0.5), -1000000000.0))
    soft_weights = jax.nn.softmax(scores, axis=-1)
    return jnp.einsum('hqk,khd->qhd', low(soft_weights), values, precision=lax.Precision.HIGHEST)

def attend_item(block_item):
    return attend(block_item[0], block_item[1], block_item[2], block_item[3])

def one_layer(hidden, valid_counts, layer_index, frozen, vector_d, vector_b):
    query_weight, key_weight, value_weight, out_weight, down_shared, up_shared, ln_gain, ffn_in, ffn_out = frozen
    row_count = hidden.shape[0]
    seq_count = row_count // LEN
    shrunk = low(hidden)
    base_q = matmul_high(shrunk, query_weight[layer_index])
    base_k = matmul_high(shrunk, key_weight[layer_index])
    base_v = matmul_high(shrunk, value_weight[layer_index])
    vera_inner = low_back(matmul_high(shrunk, down_shared))
    proj_q = low(vector_d[layer_index, 0] * vera_inner)
    proj_v = low(vector_d[layer_index, 1] * vera_inner)
    lift_q = low_back(matmul_high(proj_q, up_shared))
    lift_v = low_back(matmul_high(proj_v, up_shared))
    queries = low_back(low(base_q + vector_b[layer_index, 0] * lift_q))
    keys_in = low_back(low(base_k))
    values = low_back(low(base_v + vector_b[layer_index, 1] * lift_v))
    shape_heads = (seq_count, LEN, HEADS, HEAD_DIM)
    context = lax.map(jax.checkpoint(attend_item), (queries.reshape(shape_heads), keys_in.reshape(shape_heads), values.reshape(shape_heads), valid_counts))
    context = low_back(low(context.reshape(row_count, D)))
    attn_out = low_back(matmul_high(context, out_weight[layer_index]))
    first_norm = layer_norm(hidden + attn_out, ln_gain[layer_index, 0])
    pre_act = low_back(matmul_high(low(first_norm), ffn_in[layer_index]))
    activation = low(jax.nn.gelu(pre_act, approximate=False))
    branch = low_back(matmul_high(activation, ffn_out[layer_index]))
    return layer_norm(first_norm + branch, ln_gain[layer_index, 1])

def reference(block_input, part_lengths, query_weight, key_weight, value_weight, out_weight, down_shared, up_shared, scale_d, scale_b, ln_gain, ffn_in, ffn_out, out_grad):
    frozen = tuple((tensor.astype(jnp.float32) for tensor in (query_weight, key_weight, value_weight, out_weight, down_shared, up_shared, ln_gain, ffn_in, ffn_out)))
    seq_group = 8
    block_count = MBS * SEQS // seq_group
    inputs = block_input.astype(jnp.float32).reshape(block_count, seq_group * LEN, D)
    cotangents = out_grad.astype(jnp.float32).reshape(block_count, seq_group * LEN, D)
    valid_all = (part_lengths[:, :, 0] + part_lengths[:, :, 1] + 4).astype(jnp.int32).reshape(block_count, seq_group)
    vector_d = scale_d.astype(jnp.float32)
    vector_b = scale_b.astype(jnp.float32)

    def step(carry, block_item):
        span_in, span_cot, span_valid = block_item

        def forward(hidden, given_d, given_b):
            for layer_index in range(LAYERS):
                hidden = one_layer(hidden, span_valid, layer_index, frozen, given_d, given_b)
            return hidden
        result, pullback = jax.vjp(forward, span_in, vector_d, vector_b)
        grad_in, grad_dvec, grad_bvec = pullback(span_cot)
        return ((carry[0] + grad_dvec, carry[1] + grad_bvec), (result.astype(jnp.bfloat16), grad_in))
    start = (jnp.zeros(scale_d.shape, jnp.float32), jnp.zeros(scale_b.shape, jnp.float32))
    totals, stacked = lax.scan(step, start, (inputs, cotangents, valid_all))
    block_output = stacked[0].reshape(MBS, TOK, D)
    input_grad = stacked[1].reshape(MBS, TOK, D)
    return (block_output, input_grad, totals[0], totals[1])
```

```python
import functools

import jax
import jax.numpy as jnp
from jax import lax
from jax.experimental import pallas as pl
from jax.experimental.pallas import tpu as pltpu
from jax.sharding import PartitionSpec as P

D = 768
HEADS = 12
HEAD_DIM = 64
FF = 3072
RANK = 1024
LEN = 512
LAYERS = 2
PAIRS = HEADS // 2
PAIR = 2 * HEAD_DIM
BLOCK = LEN // 4
ROWS = 2 * BLOCK
CB = D
NCB = FF // CB
SCALE = HEAD_DIM ** (-0.5)
BF = jnp.bfloat16
F32 = jnp.float32
MIB = 1 << 20

VM = pl.BlockSpec(memory_space=pltpu.VMEM)
ANY = pl.BlockSpec(memory_space=pl.ANY)
SM = pl.BlockSpec(memory_space=pltpu.SMEM)


def dot(left, right):
    return jnp.dot(left, right, preferred_element_type=F32)


def dot_nt(left, right):
    return lax.dot_general(left, right, (((1,), (1,)), ((), ())), preferred_element_type=F32)


def normed(t):
    centred = t - jnp.mean(t, axis=-1, keepdims=True)
    inverse = lax.rsqrt(jnp.mean(centred * centred, axis=-1, keepdims=True) + 1e-05)
    return centred * inverse, inverse


def norm_back(t, gain, cotangent):
    unit, inverse = normed(t)
    scaled = cotangent * gain
    mean_e = jnp.mean(scaled, axis=-1, keepdims=True)
    mean_en = jnp.mean(scaled * unit, axis=-1, keepdims=True)
    return inverse * (scaled - mean_e - unit * mean_en)


class Loads:
    def __init__(self, sems):
        self.sems, self.count = sems, 0

    def start(self, src, dst):
        copy = pltpu.make_async_copy(src, dst, self.sems.at[self.count])
        self.count += 1
        copy.start()
        return copy


def call(body, outs, ins, specs, out_specs, scratch, limit, cost):
    return pl.pallas_call(
        body,
        out_shape=outs,
        in_specs=specs,
        out_specs=out_specs,
        scratch_shapes=scratch,
        compiler_params=pltpu.CompilerParams(vmem_limit_bytes=limit * MIB),
        cost_estimate=pl.CostEstimate(flops=cost[0], bytes_accessed=cost[1], transcendentals=0),
    )(*ins)


def sds(shape, dtype):
    return jax.ShapeDtypeStruct(shape, dtype)


def kv_body(layer, x_ref, wk_ref, wv_ref, down_ref, up_ref, sd_ref, sb_ref,
            kv_ref, inner_ref, lift_ref, wk, wv, down, up, sems):
    loads = Loads(sems)
    c_down = loads.start(down_ref, down)
    c_up = loads.start(up_ref, up)
    c_v = loads.start(wv_ref.at[layer], wv)
    c_k = loads.start(wk_ref.at[layer], wk)
    xb = x_ref[...].astype(BF)
    c_down.wait()
    inner = dot(xb, down[...])
    inner_ref[...] = inner
    pv = (sd_ref[layer, 1:2, :] * inner).astype(BF)
    c_up.wait()
    lift = dot(pv, up[...])
    lift_ref[...] = lift
    c_v.wait()
    kv_ref[:, D:] = (dot(xb, wv[...]) + sb_ref[layer, 1:2, :] * lift).astype(BF)
    c_k.wait()
    kv_ref[:, :D] = dot(xb, wk[...]).astype(BF)


def kv_call(layer, x, wk, wv, down, up, sd, sb):
    return call(
        functools.partial(kv_body, layer),
        (sds((ROWS, 2 * D), BF), sds((ROWS, RANK), F32), sds((ROWS, D), F32)),
        (x, wk, wv, down, up, sd, sb),
        (VM, ANY, ANY, ANY, ANY, VM, VM), (VM, VM, VM),
        [pltpu.VMEM((D, D), BF), pltpu.VMEM((D, D), BF), pltpu.VMEM((D, RANK), BF),
         pltpu.VMEM((RANK, D), BF), pltpu.SemaphoreType.DMA((4,))],
        24, (2 * ROWS * D * (2 * D + 2 * RANK), 6_000_000),
    )


def q_body(layer, x_ref, inner_ref, wq_ref, up_ref, sd_ref, sb_ref,
           q_ref, qt_ref, lift_ref, wq, up, sems):
    loads = Loads(sems)
    c_up = loads.start(up_ref, up)
    c_q = loads.start(wq_ref.at[layer], wq)
    pq = (sd_ref[layer, 0:1, :] * inner_ref[...]).astype(BF)
    xb = x_ref[...].astype(BF)
    c_up.wait()
    lift = dot(pq, up[...])
    lift_ref[...] = lift
    c_q.wait()
    q = (dot(xb, wq[...]) + sb_ref[layer, 0:1, :] * lift).astype(BF)
    q_ref[...] = q
    qt_ref[...] = q.T


def q_call(layer, x, inner, wq, up, sd, sb):
    return call(
        functools.partial(q_body, layer),
        (sds((ROWS, D), BF), sds((D, ROWS), BF), sds((ROWS, D), F32)),
        (x, inner, wq, up, sd, sb),
        (VM, VM, ANY, ANY, VM, VM), (VM, VM, VM),
        [pltpu.VMEM((D, D), BF), pltpu.VMEM((RANK, D), BF), pltpu.SemaphoreType.DMA((2,))],
        20, (2 * ROWS * D * (D + RANK), 5_000_000),
    )


def split_heads(t):
    zero = jnp.zeros((HEAD_DIM, t.shape[1]), t.dtype)
    first = jnp.concatenate([t[:HEAD_DIM], zero], axis=0)
    second = jnp.concatenate([zero, t[HEAD_DIM:]], axis=0)
    return jnp.concatenate([first, second], axis=1)


def join_heads(t):
    n = t.shape[1] // 2
    return jnp.concatenate([t[:HEAD_DIM, :n], t[HEAD_DIM:, n:]], axis=0)


def stack_heads(t):
    lane = lax.broadcasted_iota(jnp.int32, (1, PAIR), 1)
    first = (lane < HEAD_DIM).astype(F32).astype(BF)
    second = (lane >= HEAD_DIM).astype(F32).astype(BF)
    return jnp.concatenate([t * first, t * second], axis=0)


def attend_body(layer, thr_ref, x_ref, qt_ref, kv_ref, far_ref, wo_ref, gain_ref,
                y_ref, h_ref, p_ref, wo, p_all, ctx, sems):
    loads = Loads(sems)
    c_o = loads.start(wo_ref.at[layer], wo)
    row = lax.broadcasted_iota(jnp.int32, (BLOCK, 2 * ROWS), 0)
    stores = []
    for pair in range(PAIRS):
        cols = slice(pair * PAIR, (pair + 1) * PAIR)
        vcols = slice(D + pair * PAIR, D + (pair + 1) * PAIR)
        keys = jnp.concatenate([kv_ref[:, cols], far_ref[:, cols]], axis=0)
        vals = jnp.concatenate([kv_ref[:, vcols], far_ref[:, vcols]], axis=0)
        raw = dot(keys, split_heads(qt_ref[cols, :])) * SCALE
        scores = jnp.concatenate(
            [jnp.where(row < thr_ref[b], raw[b * BLOCK:(b + 1) * BLOCK], -1000000000.0) for b in range(4)],
            axis=0,
        )
        peak = jnp.max(scores, axis=0, keepdims=True)
        grown = jnp.exp(scores - peak)
        total = jnp.sum(grown, axis=0, keepdims=True)
        p_all[pair] = (grown * (1.0 / total)).astype(BF)
        stores.append(loads.start(p_all.at[pair], p_ref.at[pair]))
        ctx_t = join_heads(dot(vals.T, p_all[pair]))
        ctx[:, cols] = ctx_t.T.astype(BF)
    c_o.wait()
    first_in = x_ref[...].astype(F32) + dot(ctx[...], wo[...])
    h_ref[...] = first_in
    y_ref[...] = normed(first_in)[0] * gain_ref[layer, 0:1, :]
    for copy in stores:
        copy.wait()


def attend_call(layer, thr, x, qt, kv, far, wo, gain):
    return call(
        functools.partial(attend_body, layer),
        (sds((ROWS, D), F32), sds((ROWS, D), F32), sds((PAIRS, LEN, 2 * ROWS), BF)),
        (thr, x, qt, kv, far, wo, gain),
        (SM, VM, VM, VM, VM, ANY, VM), (VM, VM, ANY),
        [pltpu.VMEM((D, D), BF), pltpu.VMEM((PAIRS, LEN, 2 * ROWS), BF),
         pltpu.VMEM((ROWS, D), BF), pltpu.SemaphoreType.DMA((1 + PAIRS,))],
        32, (4 * ROWS * LEN * D * 4, 10_000_000),
    )


def start_ffn(loads, plan, refs, w_in, w_out):
    needs = [[] for _ in range(NCB)]
    for cb in range(NCB):
        for kind in ("in", "out"):
            for ref, src, block, dst in plan[kind]:
                if block == cb:
                    source = refs[ref].at[src] if src is not None else refs[ref]
                    target = (w_in if kind == "in" else w_out).at[dst]
                    needs[cb].append(loads.start(source, target))
    return needs


def ffn_body(layer, plan, n_refs, y_ref, gain_ref, *rest):
    refs = rest[:n_refs]
    x_ref, h_ref, g_ref, w_in, w_out, sems = rest[n_refs:]
    needs = start_ffn(Loads(sems), plan, refs, w_in, w_out)
    y = y_ref[...]
    yb = y.astype(BF)
    total = y
    for cb in range(NCB):
        for copy in needs[cb]:
            copy.wait()
        cols = slice(cb * CB, (cb + 1) * CB)
        z = dot(yb, w_in[:, cols])
        cdf = 0.5 * (1.0 + lax.erf(z * (0.5 ** 0.5)))
        g_ref[:, cols] = (cdf + z * (jnp.exp(-0.5 * z * z) * 0.3989422804014327)).astype(BF)
        total = total + dot((z * cdf).astype(BF), w_out[cols, :])
    h_ref[...] = total
    x_ref[...] = normed(total)[0] * gain_ref[layer, 1:2, :]


def ffn_call(layer, plan, pieces, y, gain):
    count = sum(len(plan[kind]) for kind in plan)
    return call(
        functools.partial(ffn_body, layer, plan, len(pieces)),
        (sds((ROWS, D), F32), sds((ROWS, D), F32), sds((ROWS, FF), BF)),
        (y, gain, *pieces),
        (VM, VM) + (ANY,) * len(pieces), (VM, VM, VM),
        [pltpu.VMEM((D, FF), BF), pltpu.VMEM((FF, D), BF), pltpu.SemaphoreType.DMA((count,))],
        40, (4 * ROWS * D * FF, 13_000_000),
    )


def ffn_back_body(layer, plan, n_refs, c_ref, h2_ref, g_ref, h1_ref, gain_ref, wo_ref, *rest):
    refs = rest[:n_refs]
    dh_ref, dctx_ref, w_in, w_out, wo, sems = rest[n_refs:]
    loads = Loads(sems)
    needs = start_ffn(loads, plan, refs, w_in, w_out)
    c_o = loads.start(wo_ref.at[layer], wo)
    dh2 = norm_back(h2_ref[...], gain_ref[layer, 1:2, :], c_ref[...])
    dfb = dh2.astype(BF)
    total = dh2
    for cb in range(NCB):
        for copy in needs[cb]:
            copy.wait()
        cols = slice(cb * CB, (cb + 1) * CB)
        da = dot_nt(dfb, w_out[cols, :])
        dz = (g_ref[:, cols].astype(F32) * da).astype(BF)
        total = total + dot_nt(dz, w_in[:, cols])
    dh1 = norm_back(h1_ref[...], gain_ref[layer, 0:1, :], total)
    dh_ref[...] = dh1
    c_o.wait()
    dctx_ref[...] = dot_nt(dh1.astype(BF), wo[...]).astype(BF)


def ffn_back_call(layer, plan, pieces, c, h2, g, h1, gain, wo):
    count = sum(len(plan[kind]) for kind in plan) + 1
    return call(
        functools.partial(ffn_back_body, layer, plan, len(pieces)),
        (sds((ROWS, D), F32), sds((ROWS, D), BF)),
        (c, h2, g, h1, gain, wo, *pieces),
        (VM, VM, VM, VM, VM, ANY) + (ANY,) * len(pieces), (VM, VM),
        [pltpu.VMEM((D, FF), BF), pltpu.VMEM((FF, D), BF), pltpu.VMEM((D, D), BF),
         pltpu.SemaphoreType.DMA((count,))],
        40, (4 * ROWS * D * FF, 14_000_000),
    )


def attend_back_body(dctx_ref, q_ref, kv_ref, far_ref, p_ref, dq_ref, own_ref, send_ref, p_all, sems):
    loads = Loads(sems)
    copies = [loads.start(p_ref.at[pair], p_all.at[pair]) for pair in range(PAIRS)]
    for pair in range(PAIRS):
        cols = slice(pair * PAIR, (pair + 1) * PAIR)
        vcols = slice(D + pair * PAIR, D + (pair + 1) * PAIR)
        keys = jnp.concatenate([kv_ref[:, cols], far_ref[:, cols]], axis=0)
        vals = jnp.concatenate([kv_ref[:, vcols], far_ref[:, vcols]], axis=0)
        dctx = dctx_ref[:, cols]
        dp = dot(vals, split_heads(dctx.T))
        copies[pair].wait()
        pb = p_all[pair]
        pf = pb.astype(F32)
        weighted = pf * dp
        ds = (weighted - pf * jnp.sum(weighted, axis=0, keepdims=True)).astype(BF)
        dv = dot(pb, stack_heads(dctx))
        dk = dot(ds, stack_heads(q_ref[:, cols])) * SCALE
        own_ref[:, cols] = dk[:ROWS]
        own_ref[:, vcols] = dv[:ROWS]
        send_ref[:, cols] = dk[ROWS:].astype(BF)
        send_ref[:, vcols] = dv[ROWS:].astype(BF)
        dq_t = join_heads(dot(keys.T, ds)) * SCALE
        dq_ref[:, cols] = dq_t.T.astype(BF)


def attend_back_call(dctx, q, kv, far, p):
    return call(
        attend_back_body,
        (sds((ROWS, D), BF), sds((ROWS, 2 * D), F32), sds((ROWS, 2 * D), BF)),
        (dctx, q, kv, far, p),
        (VM, VM, VM, VM, ANY), (VM, VM, VM),
        [pltpu.VMEM((PAIRS, LEN, 2 * ROWS), BF), pltpu.SemaphoreType.DMA((PAIRS,))],
        32, (8 * ROWS * LEN * D * 2, 10_000_000),
    )


def dq_body(layer, dh_ref, dq_ref, lift_ref, inner_ref, wq_ref, up_ref, sd_ref, sb_ref,
            dx_ref, dub_ref, gd_ref, gb_ref, wq, up, sems):
    loads = Loads(sems)
    c_up = loads.start(up_ref, up)
    c_q = loads.start(wq_ref.at[layer], wq)
    dq = dq_ref[...]
    dqf = dq.astype(F32)
    gb_ref[...] = jnp.sum(dqf * lift_ref[...], axis=0, keepdims=True)
    c_up.wait()
    dpq = dot_nt((sb_ref[layer, 0:1, :] * dqf).astype(BF), up[...])
    gd_ref[...] = jnp.sum(dpq * inner_ref[...], axis=0, keepdims=True)
    dub_ref[...] = sd_ref[layer, 0:1, :] * dpq
    c_q.wait()
    dx_ref[...] = dh_ref[...] + dot_nt(dq, wq[...])


def dq_call(layer, dh, dq, lift, inner, wq, up, sd, sb):
    return call(
        functools.partial(dq_body, layer),
        (sds((ROWS, D), F32), sds((ROWS, RANK), F32), sds((1, RANK), F32), sds((1, D), F32)),
        (dh, dq, lift, inner, wq, up, sd, sb),
        (VM, VM, VM, VM, ANY, ANY, VM, VM), (VM, VM, VM, VM),
        [pltpu.VMEM((D, D), BF), pltpu.VMEM((RANK, D), BF), pltpu.SemaphoreType.DMA((2,))],
        20, (2 * ROWS * D * (D + RANK), 6_000_000),
    )


def dkv_body(layer, dx_ref, dub_ref, own_ref, got_ref, lift_ref, inner_ref, wk_ref, wv_ref, down_ref, up_ref,
             sd_ref, sb_ref, out_ref, gd_ref, gb_ref, wk, wv, down, up, sems):
    loads = Loads(sems)
    c_up = loads.start(up_ref, up)
    c_down = loads.start(down_ref, down)
    c_v = loads.start(wv_ref.at[layer], wv)
    c_k = loads.start(wk_ref.at[layer], wk)
    dv = (own_ref[:, D:] + got_ref[:, D:].astype(F32)).astype(BF)
    dk = (own_ref[:, :D] + got_ref[:, :D].astype(F32)).astype(BF)
    dvf = dv.astype(F32)
    gb_ref[...] = jnp.sum(dvf * lift_ref[...], axis=0, keepdims=True)
    c_up.wait()
    dpv = dot_nt((sb_ref[layer, 1:2, :] * dvf).astype(BF), up[...])
    gd_ref[...] = jnp.sum(dpv * inner_ref[...], axis=0, keepdims=True)
    dub = (dub_ref[...] + sd_ref[layer, 1:2, :] * dpv).astype(BF)
    c_down.wait()
    total = dx_ref[...] + dot_nt(dub, down[...])
    c_v.wait()
    total = total + dot_nt(dv, wv[...])
    c_k.wait()
    out_ref[...] = total + dot_nt(dk, wk[...])


def dkv_call(layer, dx, dub, own, got, lift, inner, wk, wv, down, up, sd, sb):
    return call(
        functools.partial(dkv_body, layer),
        (sds((ROWS, D), F32), sds((1, RANK), F32), sds((1, D), F32)),
        (dx, dub, own, got, lift, inner, wk, wv, down, up, sd, sb),
        (VM, VM, VM, VM, VM, VM, ANY, ANY, ANY, ANY, VM, VM), (VM, VM, VM),
        [pltpu.VMEM((D, D), BF), pltpu.VMEM((D, D), BF), pltpu.VMEM((D, RANK), BF),
         pltpu.VMEM((RANK, D), BF), pltpu.SemaphoreType.DMA((4,))],
        32, (2 * ROWS * D * (2 * D + 2 * RANK), 9_000_000),
    )


def gather_pieces(shard_in, shard_out):
    n = lax.axis_size("dp")
    heads = lax.axis_size("head")
    here = lax.axis_index("head")
    rows_in, rows_out = shard_in.shape[0], shard_out.shape[0]
    if rows_in % 16 or rows_out % 16 or heads != NCB or CB % rows_out:
        whole_in = lax.all_gather(shard_in, "dp", axis=0, tiled=True)
        whole_out = lax.all_gather(shard_out, "dp", axis=0, tiled=True)
        plan = {
            "in": [(0, None, 0, (slice(None), slice(None)))],
            "out": [(1, None, 0, (slice(None), slice(None)))],
        }
        return plan, (whole_in, whole_out)
    stacked = jnp.concatenate([shard_in[:, cb * CB:(cb + 1) * CB] for cb in range(NCB)] + [shard_out], axis=0)
    per = stacked.shape[0] // heads
    part = lax.dynamic_slice_in_dim(stacked, here * per, per, axis=0)
    whole = lax.all_gather(part, ("dp", "head"), axis=0, tiled=True)
    plan = {"in": [], "out": []}
    for d in range(n):
        base = d * stacked.shape[0]
        for cb in range(NCB):
            plan["in"].append((0, pl.ds(base + cb * rows_in, rows_in), cb,
                               (pl.ds(d * rows_in, rows_in), pl.ds(cb * CB, CB))))
        plan["out"].append((0, pl.ds(base + NCB * rows_in, rows_out), d * rows_out // CB,
                            (pl.ds(d * rows_out, rows_out), slice(None))))
    return plan, (whole,)


def local(block_input, part_lengths, query_weight, key_weight, value_weight, out_weight, down_shared, up_shared,
          scale_d, scale_b, ln_gain, ffn_in, ffn_out, out_grad):
    here = lax.axis_index("head")
    across = [(i, i ^ 2) for i in range(4)]
    beside = [(i, i ^ 1) for i in range(4)]
    mine = here // 2

    def swap(t, axis_perm):
        return lax.ppermute(t, "head", axis_perm)

    def pick(t, index):
        return lax.dynamic_index_in_dim(t, index, 0, keepdims=False)

    def regroup(t):
        return jnp.concatenate([pick(t, mine), swap(pick(t, 1 - mine), across)], axis=0)

    def ungroup(t, kept, dtype):
        got = swap(t[BLOCK:].astype(BF), across).astype(dtype)
        own = kept[:BLOCK].astype(dtype)
        first = mine == 0
        return jnp.stack([jnp.where(first, own, got), jnp.where(first, got, own)])

    x = regroup(block_input)
    valid = (part_lengths[:, 0, 0] + part_lengths[:, 0, 1] + 4).astype(jnp.int32)
    blocks = jnp.stack([here, here ^ 2, here ^ 1, here ^ 3]).astype(jnp.int32)
    thr = pick(valid, mine) - BLOCK * blocks
    pieces = [gather_pieces(ffn_in[layer], ffn_out[layer]) for layer in range(LAYERS)]
    cotangent = jnp.concatenate(
        [pick(out_grad, mine), swap(pick(out_grad, 1 - mine).astype(BF), across).astype(F32)], axis=0)
    stored = []
    for layer in range(LAYERS):
        kv, inner, lift_v = kv_call(layer, x, key_weight, value_weight, down_shared, up_shared, scale_d, scale_b)
        far = swap(kv, beside)
        q, qt, lift_q = q_call(layer, x, inner, query_weight, up_shared, scale_d, scale_b)
        y, h1, p = attend_call(layer, thr, x, qt, kv, far, out_weight, ln_gain)
        x, h2, g = ffn_call(layer, *pieces[layer], y, ln_gain)
        stored.append((kv, far, q, inner, lift_q, lift_v, h1, p, h2, g))
    block_output = ungroup(x, x, BF)
    grads_d, grads_b = [], []
    for layer in reversed(range(LAYERS)):
        kv, far, q, inner, lift_q, lift_v, h1, p, h2, g = stored[layer]
        dh, dctx = ffn_back_call(layer, *pieces[layer], cotangent, h2, g, h1, ln_gain, out_weight)
        dq, own, send = attend_back_call(dctx, q, kv, far, p)
        got = swap(send, beside)
        dx, dub, gd_q, gb_q = dq_call(layer, dh, dq, lift_q, inner, query_weight, up_shared, scale_d, scale_b)
        cotangent, gd_v, gb_v = dkv_call(
            layer, dx, dub, own, got, lift_v, inner, key_weight, value_weight, down_shared, up_shared,
            scale_d, scale_b)
        grads_d.append(jnp.concatenate([gd_q, gd_v], axis=0))
        grads_b.append(jnp.concatenate([gb_q, gb_v], axis=0))
    grad_d, grad_b = lax.psum((jnp.stack(grads_d[::-1]), jnp.stack(grads_b[::-1])), ("dp", "head"))
    input_grad = ungroup(cotangent, cotangent, F32)
    return block_output, input_grad, grad_d, grad_b


def solution(mesh):
    both = P(None, ("dp", "head"), None)
    in_specs = (both, P(None, "dp", None), P(), P(), P(), P(), P(), P(), P(), P(), P(),
                P(None, "dp", None), P(None, "dp", None), both)
    out_specs = (both, both, P(), P())
    return jax.shard_map(local, mesh=mesh, in_specs=in_specs, out_specs=out_specs, check_vma=False)
```

```python
import functools

import jax
import jax.numpy as jnp
from jax import lax
from jax.experimental import pallas as pl
from jax.experimental.pallas import tpu as pltpu
from jax.sharding import PartitionSpec as P

D = 768
HEADS = 12
HEAD_DIM = 64
FF = 3072
RANK = 1024
LEN = 512
LAYERS = 2
PAIRS = HEADS // 2
PAIR = 2 * HEAD_DIM
BLOCK = LEN // 4
ROWS = 2 * BLOCK
CB = D
NCB = FF // CB
SCALE = HEAD_DIM ** (-0.5)
BF = jnp.bfloat16
F32 = jnp.float32
MIB = 1 << 20

COLOURS = {"v": pltpu.VMEM, "h": pltpu.HBM}
SPACES = {
    "v": pl.BlockSpec(memory_space=pltpu.VMEM),
    "h": pl.BlockSpec(memory_space=pltpu.HBM),
    "s": pl.BlockSpec(memory_space=pltpu.SMEM),
    "a": pl.BlockSpec(memory_space=pl.ANY),
}


def dot(left, right):
    return jnp.dot(left, right, preferred_element_type=F32)


def dot_nt(left, right):
    return lax.dot_general(left, right, (((1,), (1,)), ((), ())), preferred_element_type=F32)


def normed(t):
    centred = t - jnp.mean(t, axis=-1, keepdims=True)
    inverse = lax.rsqrt(jnp.mean(centred * centred, axis=-1, keepdims=True) + 1e-05)
    return centred * inverse, inverse


def norm_back(t, gain, cotangent):
    unit, inverse = normed(t)
    scaled = cotangent * gain
    mean_e = jnp.mean(scaled, axis=-1, keepdims=True)
    mean_en = jnp.mean(scaled * unit, axis=-1, keepdims=True)
    return inverse * (scaled - mean_e - unit * mean_en)


class Copies:
    def __init__(self, sems, first=0):
        self.sems, self.count = sems, first

    def __call__(self, src, dst):
        copy = pltpu.make_async_copy(src, dst, self.sems.at[self.count])
        self.count += 1
        copy.start()
        return copy


class Sequence:
    def __init__(self):
        self.token = None

    def __call__(self, body, ins, outs, scratch=(), copies=0, name="keep", fetch=(), joins=(), through=(), limit=12,
                 cost=0.3, save=()):
        handed = list(through)
        if self.token is not None:
            handed.append(pltpu.with_memory_space_constraint(self.token, pltpu.HBM))
        parts = [part for join in joins for part in join]
        joined = [((len(join),) + join[0].shape, join[0].dtype) for join in joins]
        fetched = [(t.shape if part is None else t.shape[1:] if isinstance(part, int) else part[1], t.dtype)
                   for t, part in fetch]
        n_in, n_fetch, n_part, n_hand = len(ins), len(fetch), len(parts), len(handed)
        n_out, n_join, n_save = len(outs), len(joins), len(save)
        first = self.token is None

        def whole(*refs):
            refs = list(refs)
            in_refs, fetch_refs = refs[:n_in], refs[n_in:n_in + n_fetch]
            refs = refs[n_in + n_fetch:]
            part_refs = refs[:n_part]
            refs = refs[n_part + n_hand:]
            out_refs, fetch_outs = refs[:n_out], refs[n_out:n_out + n_fetch]
            refs = refs[n_out + n_fetch:]
            join_refs = refs[:n_join]
            save_refs = refs[n_join + n_hand + first:][:n_save]
            refs = refs[n_join + n_hand + first + n_save:]
            scratch_refs, sems = refs[:len(scratch)], refs[len(scratch)]
            copy = Copies(sems, copies)
            waits = []
            for join, target in zip(joins, join_refs, strict=True):
                for i, _ in enumerate(join):
                    waits.append(copy(part_refs.pop(0), target.at[in_refs[0][20 + i]]))
            for (_, part), source, target in zip(fetch, fetch_refs, fetch_outs, strict=True):
                if part is not None:
                    source = source.at[part if isinstance(part, int) else part[0](in_refs[0])]
                waits.append(copy(source, target))
            for place, target in zip(save, save_refs, strict=True):
                waits.append(copy(in_refs[place], target))
            if body is not None:
                body(*in_refs, *out_refs, *scratch_refs, sems)
            for wait in waits:
                wait.wait()

        shapes = [COLOURS[space](shape, dtype) for space, shape, dtype in outs]
        shapes += [pltpu.VMEM(shape, dtype) for shape, dtype in fetched + joined]
        shapes += [jax.ShapeDtypeStruct(t.shape, t.dtype) for t in through]
        shapes += [pltpu.HBM((8, 128), F32)]
        shapes += [pltpu.HBM(ins[place][1].shape, ins[place][1].dtype) for place in save]
        results = pl.pallas_call(
            whole,
            out_shape=tuple(shapes),
            in_specs=[SPACES[space] for space, _ in ins] + [SPACES["h"]] * n_fetch + [SPACES["a"]] * (n_part + n_hand),
            out_specs=tuple([SPACES[space] for space, _, _ in outs] + [SPACES["v"]] * (n_fetch + n_join)
                            + [SPACES["a"]] * (n_hand + first) + [SPACES["h"]] * n_save),
            scratch_shapes=[pltpu.VMEM(shape, dtype) for shape, dtype in scratch]
            + [pltpu.SemaphoreType.DMA((copies + n_fetch + n_part + n_save + 1,))],
            input_output_aliases={n_in + n_fetch + n_part + i: n_out + n_fetch + n_join + i for i in range(n_hand)},
            compiler_params=pltpu.CompilerParams(vmem_limit_bytes=limit * MIB),
            cost_estimate=pl.CostEstimate(
                flops=int(cost * 8e8), bytes_accessed=int(cost * 2.5e6), transcendentals=0),
            name=name,
        )(*[pltpu.with_memory_space_constraint(t, COLOURS[space]) if space in COLOURS else t for space, t in ins],
          *[pltpu.with_memory_space_constraint(t, pltpu.HBM) for t, _ in fetch],
          *parts, *handed)
        results = list(results)
        split = n_out + n_fetch + n_join + len(through)
        self.token = results[split]
        return results[:split] + results[split + 1:]


def kv_body(layer, x_ref, got_ref, wk, wv, down, up, sd_ref, sb_ref, kv, inner_out, lift_out, xb_ref, sems):
    if layer == 0:
        xb_ref[:BLOCK] = x_ref[...]
        xb_ref[BLOCK:] = got_ref[...]
    else:
        xb_ref[...] = x_ref[...].astype(BF)
    xb = xb_ref[...]
    inner = dot(xb, down[...])
    inner_out[...] = inner
    lift = dot((sd_ref[layer, 1:2, :] * inner).astype(BF), up[...])
    lift_out[...] = lift.astype(BF)
    kv[:, D:] = (dot(xb, wv[...]) + sb_ref[layer, 1:2, :] * lift).astype(BF)
    kv[:, :D] = dot(xb, wk[...]).astype(BF)


def kv_call(seq, layer, x, got, wk, wv, down, up, sd, sb, **extra):
    return seq(
        functools.partial(kv_body, layer),
        [("v", t) for t in (x, got, wk, wv, down, up, sd, sb)],
        [("v", (ROWS, 2 * D), BF), ("v", (ROWS, RANK), F32), ("v", (ROWS, D), BF), ("v", (ROWS, D), BF)],
        name="keys_values", cost=3.5, **extra)


def q_body(layer, x_ref, inner, wq, up, sd_ref, sb_ref, _, q_ref, qt_ref, lift_out, sems):
    lift = dot((sd_ref[layer, 0:1, :] * inner[...]).astype(BF), up[...])
    lift_out[...] = lift.astype(BF)
    q = (dot(x_ref[...], wq[...]) + sb_ref[layer, 0:1, :] * lift).astype(BF)
    q_ref[...] = q
    qt_ref[...] = q.T


def q_call(seq, layer, x, inner, wq, up, sd, sb, lift_v, **extra):
    return seq(
        functools.partial(q_body, layer),
        [("v", x), ("v", inner), ("v", wq), ("v", up), ("v", sd), ("v", sb), ("v", lift_v)],
        [("v", (ROWS, D), BF), ("v", (D, ROWS), BF), ("v", (ROWS, D), BF)],
        name="queries", cost=1.5, **extra)


def split_heads(t):
    zero = jnp.zeros((HEAD_DIM, t.shape[1]), t.dtype)
    first = jnp.concatenate([t[:HEAD_DIM], zero], axis=0)
    second = jnp.concatenate([zero, t[HEAD_DIM:]], axis=0)
    return jnp.concatenate([first, second], axis=1)


def join_heads(t):
    n = t.shape[1] // 2
    return jnp.concatenate([t[:HEAD_DIM, :n], t[HEAD_DIM:, n:]], axis=0)


def stack_heads(t):
    lane = lax.broadcasted_iota(jnp.int32, (1, PAIR), 1)
    first = (lane < HEAD_DIM).astype(F32).astype(BF)
    second = (lane >= HEAD_DIM).astype(F32).astype(BF)
    return jnp.concatenate([t * first, t * second], axis=0)


def both_halves(near, far, cols):
    return jnp.concatenate([near[:, cols], far[:, cols]], axis=0)


def attend_body(layer, ids, lengths, x_ref, qt_ref, kv, far, wo, gain_ref, y_ref, h_ref, p_out, ctx, *rest):
    copy = Copies(rest[-1])
    p_ref = rest[0] if layer == 0 else p_out
    stores = []
    row = lax.broadcasted_iota(jnp.int32, (BLOCK, 2 * ROWS), 0)
    live = lengths[ids[6], 0, 0] + lengths[ids[6], 0, 1] + 4
    limits = [live - BLOCK * ids[place] for place in (12, 14, 13, 15)]
    for pair in range(PAIRS):
        cols = slice(pair * PAIR, (pair + 1) * PAIR)
        vcols = slice(D + pair * PAIR, D + (pair + 1) * PAIR)
        raw = dot(both_halves(kv, far, cols), split_heads(qt_ref[cols, :])) * SCALE
        scores = jnp.concatenate(
            [jnp.where(row < limits[b], raw[b * BLOCK:(b + 1) * BLOCK], -1000000000.0) for b in range(4)],
            axis=0,
        )
        peak = jnp.max(scores, axis=0, keepdims=True)
        grown = jnp.exp(scores - peak)
        total = jnp.sum(grown, axis=0, keepdims=True)
        p_ref[pair] = (grown * (1.0 / total)).astype(BF)
        if layer == 0:
            stores.append(copy(p_ref.at[pair], p_out.at[pair]))
        ctx_t = join_heads(dot(both_halves(kv, far, vcols).T, p_ref[pair]))
        ctx[:, cols] = ctx_t.T.astype(BF)
    h = x_ref[...].astype(F32) + dot(ctx[...], wo[...])
    h_ref[...] = h
    y_ref[...] = normed(h)[0] * gain_ref[layer, 0:1, :]
    for store in stores:
        store.wait()


def attend_call(seq, layer, ids, lengths, x, qt, kv, far, wo, gain, **extra):
    return seq(
        functools.partial(attend_body, layer),
        [("s", ids), ("s", lengths), ("v", x), ("v", qt), ("v", kv), ("v", far), ("v", wo), ("v", gain)],
        [("v", (ROWS, D), F32), ("v", (ROWS, D), F32),
         ("h" if layer == 0 else "v", (PAIRS, LEN, 2 * ROWS), BF)],
        [((ROWS, D), BF)] + [((PAIRS, LEN, 2 * ROWS), BF)] * (layer == 0), PAIRS, "attention", cost=5, limit=20 if layer == 0 else 12,
        **extra)


def start_pieces(copy, plan, refs, ids, dst):
    return [copy(source, target) for source, target in plan(ids, refs, dst)]


def ffn_forward(copy, plans, refs, ids, y, w_in, w_out, a_ref, g_ref):
    waits = [start_pieces(copy, plans[0][slot], refs[0], ids, w_in.at[slot]) for slot in range(NCB)]
    waits_out = start_pieces(copy, plans[1], refs[1], ids, w_out)
    yb = y.astype(BF)
    for slot in range(NCB):
        for wait in waits[slot]:
            wait.wait()
        z = dot(yb, w_in[slot].reshape(D, CB))
        cdf = 0.5 * (1.0 + lax.erf(z * (0.5 ** 0.5)))
        g_ref[slot] = (cdf + z * (jnp.exp(-0.5 * z * z) * 0.3989422804014327)).astype(BF)
        a_ref[slot] = (z * cdf).astype(BF)
    for wait in waits_out:
        wait.wait()
    total = y
    for slot in range(NCB):
        total = total + dot(a_ref[slot], w_out[ids[12 + slot]].reshape(CB, D))
    return total


def ffn_backward(layer, ids, c, h2, g_ref, h1, gain_ref, wo, w_in, w_out, dh_ref, dctx_ref):
    dh2 = norm_back(h2, gain_ref[layer, 1:2, :], c)
    dfb = dh2.astype(BF)
    total = dh2
    for slot in range(NCB):
        da = dot_nt(dfb, w_out[ids[12 + slot]].reshape(CB, D))
        dz = (g_ref[slot].astype(F32) * da).astype(BF)
        total = total + dot_nt(dz, w_in[slot].reshape(D, CB))
    dh1 = norm_back(h1, gain_ref[layer, 0:1, :], total)
    dh_ref[...] = dh1
    dctx_ref[...] = dot_nt(dh1.astype(BF), wo[...]).astype(BF)


def ffn_body(layer, plans, counts, ids, y_ref, gain_ref, *rest):
    n_in, n_out = counts
    refs = (rest[:n_in], rest[n_in:n_in + n_out])
    x_ref, h_ref, g_ref, w_in, w_out, a_ref, sems = rest[n_in + n_out:]
    h_ref[...] = ffn_forward(Copies(sems), plans, refs, ids, y_ref[...], w_in, w_out, a_ref, g_ref)
    x_ref[...] = normed(h_ref[...])[0] * gain_ref[layer, 1:2, :]


FFN_SHAPE = (NCB, ROWS, CB)


def ffn_call(seq, layer, ids, plans, spaces, pieces, shapes, y, gain, **extra):
    return seq(
        functools.partial(ffn_body, layer, plans, (len(pieces[0]), len(pieces[1]))),
        [("s", ids), ("v", y), ("v", gain)] + [(space, t) for space, group in zip(spaces, pieces, strict=True) for t in group],
        [("v", (ROWS, D), F32), ("v", (ROWS, D), F32), ("v", FFN_SHAPE, BF)]
        + [("v", (NCB,) + shape, BF) for shape in shapes],
        [(FFN_SHAPE, BF)], 4 * NCB, "ffn", cost=7, limit=16, **extra)


def ffn_both_body(layer, plans, counts, ids, y_ref, h1, gain_ref, wo, got_ref, c_ref, *rest):
    n_in, n_out = counts
    refs = (rest[:n_in], rest[n_in:n_in + n_out])
    x_ref, send_ref, dh_ref, dctx_ref, w_in, w_out, a_ref, g_ref, c, sems = rest[n_in + n_out:]
    copy = Copies(sems)
    own = copy(c_ref.at[ids[6]], c.at[pl.ds(0, BLOCK)])
    h2 = ffn_forward(copy, plans, refs, ids, y_ref[...], w_in, w_out, a_ref, g_ref)
    dh_ref[...] = h2
    x = normed(h2)[0] * gain_ref[layer, 1:2, :]
    x_ref[...] = x[:BLOCK].astype(BF)
    send_ref[...] = x[BLOCK:].astype(BF)
    own.wait()
    c[BLOCK:] = got_ref[...].astype(F32)
    ffn_backward(layer, ids, c[...], dh_ref[...], g_ref, h1[...], gain_ref, wo, w_in, w_out, dh_ref, dctx_ref)


def ffn_both_call(seq, layer, ids, plans, spaces, pieces, shapes, y, h1, gain, wo, got, c, **extra):
    return seq(
        functools.partial(ffn_both_body, layer, plans, (len(pieces[0]), len(pieces[1]))),
        [("s", ids)] + [("v", t) for t in (y, h1, gain, wo, got)] + [("h", c)]
        + [(space, t) for space, group in zip(spaces, pieces, strict=True) for t in group],
        [("v", (BLOCK, D), BF), ("v", (BLOCK, D), BF), ("v", (ROWS, D), F32), ("v", (ROWS, D), BF)],
        [((NCB,) + shape, BF) for shape in shapes] + [(FFN_SHAPE, BF), (FFN_SHAPE, BF), ((ROWS, D), F32)],
        4 * NCB, "ffn_both", cost=10, limit=24, **extra)


def ffn_back_body(layer, ids, c_ref, h2, g, h1, gain_ref, wo, w_in, w_out, dh_ref, dctx_ref, sems):
    ffn_backward(layer, ids, c_ref[...], h2[...], g, h1[...], gain_ref, wo, w_in, w_out, dh_ref, dctx_ref)


def ffn_back_call(seq, layer, ids, c, h2, g, h1, gain, wo, w_in, w_out, **extra):
    return seq(
        functools.partial(ffn_back_body, layer),
        [("s", ids)] + [("v", t) for t in (c, h2, g, h1, gain, wo, w_in, w_out)],
        [("v", (ROWS, D), F32), ("v", (ROWS, D), BF)],
        name="ffn_back", cost=4.5, **extra)


def attend_back_body(dctx_ref, q, kv, far, p_ref, dq_ref, own_ref, send_ref, sems):
    for pair in range(PAIRS):
        cols = slice(pair * PAIR, (pair + 1) * PAIR)
        vcols = slice(D + pair * PAIR, D + (pair + 1) * PAIR)
        dctx = dctx_ref[:, cols]
        dp = dot(both_halves(kv, far, vcols), split_heads(dctx.T))
        pb = p_ref[pair]
        pf = pb.astype(F32)
        weighted = pf * dp
        ds = (weighted - pf * jnp.sum(weighted, axis=0, keepdims=True)).astype(BF)
        dv = dot(pb, stack_heads(dctx))
        dk = dot(ds, stack_heads(q[:, cols])) * SCALE
        own_ref[:, cols] = dk[:ROWS]
        own_ref[:, vcols] = dv[:ROWS]
        send_ref[:, cols] = dk[ROWS:].astype(BF)
        send_ref[:, vcols] = dv[ROWS:].astype(BF)
        dq_t = join_heads(dot(both_halves(kv, far, cols).T, ds)) * SCALE
        dq_ref[:, cols] = dq_t.T.astype(BF)


def attend_back_call(seq, dctx, q, kv, far, p, **extra):
    return seq(
        attend_back_body,
        [("v", dctx), ("v", q), ("v", kv), ("v", far), ("v", p)],
        [("v", (ROWS, D), BF), ("v", (ROWS, 2 * D), F32), ("v", (ROWS, 2 * D), BF)],
        name="attention_back", cost=5, **extra)


def dq_body(layer, dh_ref, dq_ref, lift, inner, wq, up, sd_ref, sb_ref, dx_ref, dub_ref, gd_ref, gb_ref, sems):
    dq = dq_ref[...]
    dqf = dq.astype(F32)
    gb_ref[...] = jnp.sum(dqf * lift[...].astype(F32), axis=0, keepdims=True)
    dpq = dot_nt((sb_ref[layer, 0:1, :] * dqf).astype(BF), up[...])
    gd_ref[...] = jnp.sum(dpq * inner[...], axis=0, keepdims=True)
    dub_ref[...] = sd_ref[layer, 0:1, :] * dpq
    dx_ref[...] = dh_ref[...] + dot_nt(dq, wq[...])


def dq_call(seq, layer, dh, dq, lift, inner, wq, up, sd, sb, **extra):
    return seq(
        functools.partial(dq_body, layer),
        [("v", dh), ("v", dq), ("v", lift), ("v", inner), ("v", wq), ("v", up), ("v", sd), ("v", sb)],
        [("v", (ROWS, D), F32), ("v", (ROWS, RANK), F32), ("v", (1, RANK), F32), ("v", (1, D), F32)],
        name="queries_back", cost=1, **extra)


def dv_body(layer, dub_ref, own_ref, got_ref, lift, inner, up, sd_ref, sb_ref, gdq_ref, gbq_ref, before_ref,
            dub_out, dk_ref, dv_ref, sums_ref, sems):
    sums_ref[...] = before_ref[...]
    sums_ref[4 * layer:4 * layer + 1, :] = gdq_ref[...]
    sums_ref[4 * layer + 2:4 * layer + 3, :D] = gbq_ref[...]
    dv = (own_ref[:, D:] + got_ref[:, D:].astype(F32)).astype(BF)
    dv_ref[...] = dv
    dk_ref[...] = (own_ref[:, :D] + got_ref[:, :D].astype(F32)).astype(BF)
    dvf = dv.astype(F32)
    sums_ref[4 * layer + 3:4 * layer + 4, :D] = jnp.sum(dvf * lift[...].astype(F32), axis=0, keepdims=True)
    dpv = dot_nt((sb_ref[layer, 1:2, :] * dvf).astype(BF), up[...])
    sums_ref[4 * layer + 1:4 * layer + 2, :] = jnp.sum(dpv * inner[...], axis=0, keepdims=True)
    dub_out[...] = (dub_ref[...] + sd_ref[layer, 1:2, :] * dpv).astype(BF)


def dv_call(seq, layer, dub, own, got, lift, inner, up, sd, sb, gd, gb, before, **extra):
    return seq(
        functools.partial(dv_body, layer),
        [("v", t) for t in (dub, own, got, lift, inner, up, sd, sb, gd, gb, before)],
        [("v", (ROWS, RANK), BF), ("v", (ROWS, D), BF), ("v", (ROWS, D), BF), ("v", (4 * LAYERS, RANK), F32)],
        name="values_back", cost=1, **extra)


def dx_body(layer, ids, dx_ref, dub_ref, dk_ref, dv_ref, wk, wv, down, *rest):
    total = dx_ref[...] + dot_nt(dub_ref[...], down[...])
    total = total + dot_nt(dv_ref[...], wv[...])
    total = total + dot_nt(dk_ref[...], wk[...])
    if layer == 0:
        send_ref, grad_ref, own, sems = rest
        own[...] = total[:BLOCK]
        store = Copies(sems)(own, grad_ref.at[ids[6]])
        send_ref[...] = total[BLOCK:].astype(BF)
        store.wait()
    else:
        rest[0][...] = total


def dx_call(seq, layer, ids, dx, dub, dk, dv, wk, wv, down, **extra):
    return seq(
        functools.partial(dx_body, layer),
        [("s", ids)] + [("v", t) for t in (dx, dub, dk, dv, wk, wv, down)],
        [("v", (BLOCK, D), BF), ("h", (2, BLOCK, D), F32)] if layer == 0 else [("v", (ROWS, D), F32)],
        [((BLOCK, D), F32)] * (layer == 0), 1, name="input_back", cost=1.5, **extra)


def place_body(ids, own_ref, got_ref, out_ref, sems):
    copy = Copies(sems)
    stores = [copy(own_ref, out_ref.at[ids[6]]), copy(got_ref, out_ref.at[1 - ids[6]])]
    for store in stores:
        store.wait()


def place_call(seq, ids, own, got, **extra):
    return seq(place_body, [("s", ids), ("v", own), ("v", got)], [("h", (2,) + own.shape, own.dtype)], [], 2, "place",
               cost=0.8, **extra)[0]


def fill_call(seq, ids, whole, got):
    def body(ids_ref, whole_ref, got_ref, out_ref, wide, sems):
        wide[...] = got_ref[...].astype(F32)
        Copies(sems)(wide, out_ref.at[1 - ids_ref[6]]).wait()

    return pl.pallas_call(
        body,
        out_shape=pltpu.HBM(whole.shape, F32),
        in_specs=[SPACES["s"], SPACES["h"], SPACES["v"]],
        out_specs=SPACES["h"],
        scratch_shapes=[pltpu.VMEM(got.shape, F32), pltpu.SemaphoreType.DMA((1,))],
        input_output_aliases={1: 0},
        compiler_params=pltpu.CompilerParams(vmem_limit_bytes=12 * MIB),
        name="fill",
    )(ids, pltpu.with_memory_space_constraint(whole, pltpu.HBM), got)


def add_call(seq, *terms, last=False, **extra):
    def body(*refs):
        total = refs[0][...]
        for ref in refs[1:len(terms)]:
            total = total + ref[...]
        if last:
            gd_out, gb_out, gd_ref, gb_ref, sems = refs[len(terms):]
            for layer in range(LAYERS):
                gd_ref[layer] = total[4 * layer:4 * layer + 2]
                gb_ref[layer] = total[4 * layer + 2:4 * layer + 4, :D]
            copy = Copies(sems)
            stores = [copy(gd_ref, gd_out), copy(gb_ref, gb_out)]
            for store in stores:
                store.wait()
        else:
            refs[len(terms)][...] = total

    shapes = [((LAYERS, 2, RANK), F32), ((LAYERS, 2, D), F32)] if last else []
    outs = [("h", *t) for t in shapes] if last else [("v", terms[0].shape, F32)]
    return seq(body, [("v", t) for t in terms], outs, shapes, len(shapes), "add", **extra)


def prepare_body(ids, x_ref, c_ref, in_ref, out_ref, xs, own, cs, in0, last, both, c_send, sems):
    copy = Copies(sems)
    here, mine = ids[4], ids[6]
    rows_in = in_ref.shape[1]
    quarter = out_ref.shape[1] // 4
    cols = pl.ds(pl.multiple_of(here * CB, CB), CB)
    waits = [
        copy(in_ref.at[1, :, cols], both.at[pl.ds(0, rows_in)]),
        copy(out_ref.at[1, pl.ds(pl.multiple_of(here * quarter, quarter), quarter)], both.at[pl.ds(rows_in, quarter)]),
        copy(c_ref.at[1 - mine], c_send),
        copy(x_ref.at[1 - mine], xs),
        copy(in_ref.at[0, :, cols], in0),
        copy(x_ref.at[mine], own),
    ]
    for wait in waits[:2]:
        wait.wait()
    store = copy(both, last)
    waits[2].wait()
    cs[...] = c_send[...].astype(BF)
    for wait in waits[3:]:
        wait.wait()
    store.wait()


def prepare_call(seq, ids, x, c, ffn_in, ffn_out, **extra):
    quarter = (ffn_out.shape[1] // 4, D)
    block = (ffn_in.shape[1], CB)
    both = (block[0] + quarter[0], D)
    rows = (BLOCK, D)
    return seq(
        prepare_body,
        [("s", ids), ("h", x), ("h", c), ("h", ffn_in), ("h", ffn_out)],
        [("v", rows, BF), ("v", rows, BF), ("v", rows, BF), ("v", block, BF), ("h", both, BF)],
        [(both, BF), (rows, F32)], 7, "prepare", cost=2, **extra)


def z_shift(step):
    return [(2 * z + y, 2 * ((z + step) % 4) + y) for z in range(4) for y in range(2)]


Y_SWAP = [(i, i ^ 1) for i in range(8)]
ACROSS = [(i, i ^ 2) for i in range(4)]
BESIDE = [(i, i ^ 1) for i in range(4)]


def swap(t, pairs):
    return lax.ppermute(t, "head", pairs)


def along_z(piece):
    return [lax.ppermute(piece, "dp", z_shift(step)) for step in (1, 2, 3)]


def across_y(line):
    return lax.ppermute(line, "dp", Y_SWAP)


def plan_in(ids, refs, dst, slot):
    return [(refs[2 * slot + part], dst.at[:, ids[16 + part]]) for part in range(2)]


def plan_out_halves(ids, refs, dst):
    return [(refs[4 * part + kind], dst.at[:, ids[16 + kind % 2], ids[18 + kind // 2], part])
            for part in range(2) for kind in range(4)]


def plan_in_gathered(ids, refs, dst, slot):
    return [(refs[0].at[:, :, ids[12 + slot], pl.ds(0, dst.shape[2])], dst)]


def plan_out_gathered(ids, refs, dst):
    rows = dst.shape[4]
    return [(refs[0].at[:, :, :, :, pl.ds(refs[0].shape[4] - rows, rows)], dst)]


def plan_plain(ids, refs, dst, slot=None):
    return [(refs[0], dst) if slot is None else (refs[0].at[ids[12 + slot]], dst)]


def plain_gather(shard_in, shard_out):
    whole_in = lax.all_gather(shard_in, "dp", axis=0, tiled=True)
    blocks = jnp.stack([whole_in[:, cb * CB:(cb + 1) * CB] for cb in range(NCB)])
    whole_out = lax.all_gather(shard_out, "dp", axis=0, tiled=True)
    return blocks, whole_out.reshape(NCB, CB, D)


def slots_of(plan):
    return [functools.partial(plan, slot=slot) for slot in range(NCB)]


BOTH_SWAP = [((2 * w + y) * 4 + h, (2 * w + 1 - y) * 4 + (h ^ 2)) for w in range(4) for y in range(2) for h in range(4)]


def local(block_input, part_lengths, query_weight, key_weight, value_weight, out_weight, down_shared, up_shared,
          scale_d, scale_b, ln_gain, ffn_in, ffn_out, out_grad):
    here = lax.axis_index("head")
    place = lax.axis_index("dp")
    mine = here // 2
    dp = lax.axis_size("dp")
    z, y = place // 2, place % 2
    core = here % 2
    ids = jnp.stack([z * 0] * 4 + [here, core, mine] + [z * 0] * 5 + [here ^ s for s in range(4)]
                    + [y, 1 - y, core, 1 - core] + [(z - i) % 4 for i in range(4)]).astype(jnp.int32)
    seq = Sequence()
    scales = (scale_d, scale_b)
    if dp == 8:
        rows_in, quarter = ffn_in.shape[1], ffn_out.shape[1] // 4

        def out_part(part):
            return (lambda ids_ref: (0, pl.ds(pl.multiple_of((2 * ids_ref[5] + part) * quarter, quarter), quarter)),
                    (quarter, D))

        def join(parts, **extra):
            return seq(None, [("s", ids)], [], name="join", joins=[parts], cost=1.2, **extra)

        xs, own, cs, in0, last = prepare_call(seq, ids, block_input, out_grad, ffn_in, ffn_out)
        got = swap(xs, ACROSS)
        gathered = lax.all_gather(last, ("dp", "head"), axis=0, tiled=True)
        in0_z = along_z(in0)
        wk, wv, down, up = seq(
            None, [], [], name="fetch", cost=2.5,
            fetch=[(key_weight, 0), (value_weight, 0), (down_shared, None), (up_shared, None)])
        kv, inner, lift_v, xb, wq = kv_call(seq, 0, own, got, wk, wv, down, up, *scales, fetch=[(query_weight, 0)])
        q, qt, lift_q, wo, inner0, lift_v0 = q_call(
            seq, 0, xb, inner, wq, up, *scales, lift_v, fetch=[(out_weight, 0)], save=[1, 6])
        out0a, in0_line, kv = join([in0] + in0_z, fetch=[(ffn_out, out_part(0))], through=[kv])
        far = swap(kv, BESIDE)
        in0_far, in0_y = swap(in0_line, ACROSS), across_y(in0_line)
        out0a_z = along_z(out0a)
        y, h1, p0, kv0, far0 = attend_call(
            seq, 0, ids, part_lengths, xb, qt, kv, far, wo, ln_gain, save=[4, 5])
        out0b, out0a_line, in0_y, in0_far, cs, q0, lift_q0, h10 = seq(
            None, [("s", ids), ("v", q), ("v", lift_q), ("v", h1)], [], name="join", joins=[[out0a] + out0a_z], cost=1.2,
            fetch=[(ffn_out, out_part(1))], through=[in0_y, in0_far, cs], save=[1, 2, 3])
        out0b_z = along_z(out0b)
        in0_y_far, out0a_y = swap(in0_y, ACROSS), across_y(out0a_line)
        out0b_line, in0_y_far, out0a_y = join([out0b] + out0b_z, through=[in0_y_far, out0a_y])
        out0b_y, c_got = across_y(out0b_line), swap(cs, ACROSS)
        pieces = [(piece, swap(piece, BESIDE)) for piece in (in0_line, in0_y, in0_far, in0_y_far)]
        pieces_in = [pieces[0][0], pieces[1][0], pieces[0][1], pieces[1][1],
                     pieces[2][0], pieces[3][0], pieces[2][1], pieces[3][1]]
        pieces_out = [out0a_line, out0a_y, swap(out0a_line, BESIDE), swap(out0a_y, BESIDE),
                      out0b_line, out0b_y, swap(out0b_line, BESIDE), swap(out0b_y, BESIDE)]
        shapes = ((4, 2, rows_in, CB), (2, 2, 2, quarter, D))
        [c_got] = seq(None, [("h", gathered)], [], through=[c_got])
        x, h20, g0, w_in0, w_out0, wk, wv, down, up = ffn_call(
            seq, 0, ids, (slots_of(plan_in), plan_out_halves), "aa", (pieces_in, pieces_out), shapes, y, ln_gain,
            fetch=[(key_weight, 1), (value_weight, 1), (down_shared, None), (up_shared, None)])
        stored0 = (kv0, far0, q0, inner0, lift_q0, lift_v0, h10, p0)
        kv, inner, lift_v, xb, wq = kv_call(
            seq, 1, x, got, wk, wv, down, up, *scales, fetch=[(query_weight, 1)])
        far = swap(kv, BESIDE)
        q, qt, lift_q, wo = q_call(seq, 1, xb, inner, wq, up, *scales, lift_v, fetch=[(out_weight, 1)])
        y, h1, p = attend_call(seq, 1, ids, part_lengths, x, qt, kv, far, wo, ln_gain)
        both = rows_in + quarter
        pieces = ([gathered.reshape(4, 2, NCB, both, D)], [gathered.reshape(4, 2, 2, 2, both, D)])
        plans, spaces = (slots_of(plan_in_gathered), plan_out_gathered), "hh"
    else:
        def pick(t, index):
            return lax.dynamic_index_in_dim(t, index, 0, keepdims=False)

        x, got = pick(block_input, mine), swap(pick(block_input, 1 - mine), ACROSS)
        c_got = swap(pick(out_grad, 1 - mine).astype(BF), ACROSS)
        plans, spaces, shapes = (slots_of(plan_plain), plan_plain), "hh", ((D, CB), (CB, D))
        for layer in range(LAYERS):
            pieces = [[t] for t in plain_gather(ffn_in[layer], ffn_out[layer])]
            wk, wv, down, up, wq, wo = seq(
                None, [], [], name="fetch",
                fetch=[(key_weight, layer), (value_weight, layer), (down_shared, None), (up_shared, None),
                       (query_weight, layer), (out_weight, layer)])
            kv, inner, lift_v, xb = kv_call(seq, layer, x, got, wk, wv, down, up, *scales)
            far = swap(kv, BESIDE)
            q, qt, lift_q = q_call(seq, layer, xb, inner, wq, up, *scales, lift_v)
            y, h1, p = attend_call(
                seq, layer, ids, part_lengths, xb if layer == 0 else x, qt, kv, far, wo, ln_gain)
            if layer == 0:
                x, h20, g0, w_in0, w_out0 = ffn_call(seq, 0, ids, plans, spaces, pieces, shapes, y, ln_gain)
                kv0, far0, q0, inner0, lift_q0, lift_v0, h10 = seq(
                    None, [("v", t) for t in (kv, far, q, inner, lift_q, lift_v, h1)], [], save=list(range(7)))
                stored0 = (kv0, far0, q0, inner0, lift_q0, lift_v0, h10, p)
    output, send, dh, dctx, wq, = ffn_both_call(
        seq, 1, ids, plans, spaces, pieces, shapes, y, h1, ln_gain, wo, c_got, out_grad, fetch=[(query_weight, 1)])
    other_output = swap(send, ACROSS)
    kv0, far0, q0, inner0, lift_q0, lift_v0, h10, p0 = stored0
    dq, own, send, wv, wk, wo, h1 = attend_back_call(
        seq, dctx, q, kv, far, p, fetch=[(value_weight, 1), (key_weight, 1), (out_weight, 0), (h10, None)])
    got = swap(send, BESIDE)
    dx, dub, gd_q, gb_q = dq_call(seq, 1, dh, dq, lift_q, inner, wq, up, *scales)
    dub, dk, dv, sums = dv_call(
        seq, 1, dub, own, got, lift_v, inner, up, *scales, gd_q, gb_q, jnp.zeros((4 * LAYERS, RANK), F32))
    [cotangent] = dx_call(seq, 1, ids, dx, dub, dk, dv, wk, wv, down)
    dh, dctx, q, kv, far, p = ffn_back_call(
        seq, 0, ids, cotangent, h20, g0, h1, ln_gain, wo, w_in0, w_out0,
        fetch=[(q0, None), (kv0, None), (far0, None), (p0, None)])
    dq, own, send, wq, wv, wk, inner, lift_q, lift_v = attend_back_call(
        seq, dctx, q, kv, far, p,
        fetch=[(query_weight, 0), (value_weight, 0), (key_weight, 0), (inner0, None), (lift_q0, None), (lift_v0, None)])
    got = swap(send, BESIDE)
    dx, dub, gd_q, gb_q = dq_call(seq, 0, dh, dq, lift_q, inner, wq, up, *scales)
    dub, dk, dv, sums = dv_call(seq, 0, dub, own, got, lift_v, inner, up, *scales, gd_q, gb_q, sums)
    if dp == 8:
        [sums] = add_call(seq, sums, swap(sums, BESIDE))
        parts = [swap(sums, ACROSS), across_y(sums), lax.ppermute(sums, ("dp", "head"), BOTH_SWAP)]
        last_rows, input_grad = dx_call(seq, 0, ids, dx, dub, dk, dv, wk, wv, down)
        sums, last_rows = add_call(seq, sums, *parts, through=[last_rows])
        got = swap(last_rows, ACROSS)
        block_output = place_call(seq, ids, output, other_output)
        grad_d, grad_b = add_call(seq, sums, *along_z(sums), last=True)
    else:
        last_rows, input_grad = dx_call(seq, 0, ids, dx, dub, dk, dv, wk, wv, down)
        got = swap(last_rows, ACROSS)
        block_output = place_call(seq, ids, output, other_output)
        grad_d, grad_b = add_call(seq, lax.psum(sums, ("dp", "head")), last=True)
    return block_output, fill_call(seq, ids, input_grad, got), grad_d, grad_b


def solution(mesh):
    both = P(None, ("dp", "head"), None)
    in_specs = (both, P(None, "dp", None), P(), P(), P(), P(), P(), P(), P(), P(), P(),
                P(None, "dp", None), P(None, "dp", None), both)
    out_specs = (both, both, P(), P())
    return jax.shard_map(local, mesh=mesh, in_specs=in_specs, out_specs=out_specs, check_vma=False)
```

```python
import functools

import jax
import jax.numpy as jnp
from jax import lax
from jax.experimental import pallas as pl
from jax.experimental.pallas import tpu as pltpu
from jax.sharding import PartitionSpec as P

D = 768
HEADS = 12
HEAD_DIM = 64
FF = 3072
RANK = 1024
LEN = 512
LAYERS = 2
PAIRS = HEADS // 2
PAIR = 2 * HEAD_DIM
BLOCK = LEN // 4
ROWS = 2 * BLOCK
CB = D
NCB = FF // CB
SCALE = HEAD_DIM ** (-0.5)
BF = jnp.bfloat16
F32 = jnp.float32
MIB = 1 << 20

COLOURS = {"v": pltpu.VMEM, "h": pltpu.HBM}
SPACES = {
    "v": pl.BlockSpec(memory_space=pltpu.VMEM),
    "h": pl.BlockSpec(memory_space=pltpu.HBM),
    "s": pl.BlockSpec(memory_space=pltpu.SMEM),
    "a": pl.BlockSpec(memory_space=pl.ANY),
}


HERE, CORE, MINE, Z, Y, OTHER_Y, Z_TWO, Z_NEAR, Z_BESIDE, OTHER_CORE = range(10)
SLOTS, BLOCKS = 10, 14


def dot(left, right):
    return jnp.dot(left, right, preferred_element_type=F32)


def dot_nt(left, right):
    return lax.dot_general(left, right, (((1,), (1,)), ((), ())), preferred_element_type=F32)


def normed(t):
    centred = t - jnp.mean(t, axis=-1, keepdims=True)
    inverse = lax.rsqrt(jnp.mean(centred * centred, axis=-1, keepdims=True) + 1e-05)
    return centred * inverse, inverse


def norm_back(t, gain, cotangent):
    unit, inverse = normed(t)
    scaled = cotangent * gain
    mean_e = jnp.mean(scaled, axis=-1, keepdims=True)
    mean_en = jnp.mean(scaled * unit, axis=-1, keepdims=True)
    return inverse * (scaled - mean_e - unit * mean_en)


class Copies:
    def __init__(self, sems, first=0):
        self.sems, self.count = sems, first

    def __call__(self, src, dst):
        copy = pltpu.make_async_copy(src, dst, self.sems.at[self.count])
        self.count += 1
        copy.start()
        return copy


class Sequence:
    def __init__(self):
        self.token = None

    def __call__(self, body, ins, outs, scratch=(), copies=0, name="keep", fetch=(), fill=(), fill_hbm=(), through=(), limit=12,
                 cost=0.3, save=()):
        handed = [pltpu.with_memory_space_constraint(t, pltpu.VMEM) for t in fill]
        handed += [pltpu.with_memory_space_constraint(t, pltpu.HBM) for t in fill_hbm]
        handed += list(through)
        if self.token is not None:
            handed.append(pltpu.with_memory_space_constraint(self.token, pltpu.HBM))
        fetched = [(t.shape if part is None else t.shape[1:] if isinstance(part, int) else part[1], t.dtype)
                   for t, part in fetch]
        n_in, n_fetch, n_hand, n_fill = len(ins), len(fetch), len(handed), len(fill) + len(fill_hbm)
        n_out, n_save = len(outs), len(save)
        first = self.token is None

        def whole(*refs):
            refs = list(refs)
            in_refs, fetch_refs = refs[:n_in], refs[n_in:n_in + n_fetch]
            refs = refs[n_in + n_fetch:]
            refs = refs[n_hand:]
            out_refs, fetch_outs = refs[:n_out], refs[n_out:n_out + n_fetch]
            refs = refs[n_out + n_fetch:]
            fill_refs = refs[:n_fill]
            save_refs = refs[n_hand + first:][:n_save]
            refs = refs[n_hand + first + n_save:]
            scratch_refs, sems = refs[:len(scratch)], refs[len(scratch)]
            copy = Copies(sems, copies)
            waits = []
            for (_, part), source, target in zip(fetch, fetch_refs, fetch_outs, strict=True):
                if part is not None:
                    source = source.at[part if isinstance(part, int) else part[0](in_refs[0])]
                waits.append(copy(source, target))
            for place, target in zip(save, save_refs, strict=True):
                waits.append(copy(in_refs[place], target))
            if body is not None:
                body(*in_refs, *fill_refs, *out_refs, *scratch_refs, sems)
            for wait in waits:
                wait.wait()

        shapes = [COLOURS[space](shape, dtype) for space, shape, dtype in outs]
        shapes += [pltpu.VMEM(shape, dtype) for shape, dtype in fetched]
        shapes += [pltpu.VMEM(t.shape, t.dtype) for t in fill] + [pltpu.HBM(t.shape, t.dtype) for t in fill_hbm]
        shapes += [jax.ShapeDtypeStruct(t.shape, t.dtype) for t in through]
        shapes += [pltpu.HBM((8, 128), F32)]
        shapes += [pltpu.HBM(ins[place][1].shape, ins[place][1].dtype) for place in save]
        results = pl.pallas_call(
            whole,
            out_shape=tuple(shapes),
            in_specs=[SPACES[space] for space, _ in ins] + [SPACES["h"]] * n_fetch + [SPACES["v"]] * len(fill)
            + [SPACES["h"]] * len(fill_hbm) + [SPACES["a"]] * (n_hand - n_fill),
            out_specs=tuple([SPACES[space] for space, _, _ in outs] + [SPACES["v"]] * (n_fetch + len(fill))
                            + [SPACES["h"]] * len(fill_hbm) + [SPACES["a"]] * (n_hand - n_fill + first) + [SPACES["h"]] * n_save),
            scratch_shapes=[pltpu.VMEM(shape, dtype) for shape, dtype in scratch]
            + [pltpu.SemaphoreType.DMA((copies + n_fetch + n_save + 1,))],
            input_output_aliases={n_in + n_fetch + i: n_out + n_fetch + i for i in range(n_hand)},
            compiler_params=pltpu.CompilerParams(vmem_limit_bytes=limit * MIB),
            cost_estimate=pl.CostEstimate(
                flops=int(cost * 8e8), bytes_accessed=int(cost * 2.5e6), transcendentals=0),
            name=name,
        )(*[pltpu.with_memory_space_constraint(t, COLOURS[space]) if space in COLOURS else t for space, t in ins],
          *[pltpu.with_memory_space_constraint(t, pltpu.HBM) for t, _ in fetch],
          *handed)
        results = list(results)
        split = n_out + n_fetch + n_fill + len(through)
        self.token = results[split]
        return results[:split] + results[split + 1:]


def kv_body(layer, x_ref, got_ref, wk, wv, down, up, sd_ref, sb_ref, kv, inner_out, lift_out, xb_ref, sems):
    if layer == 0:
        xb_ref[:BLOCK] = x_ref[...]
        xb_ref[BLOCK:] = got_ref[...]
    else:
        xb_ref[...] = x_ref[...].astype(BF)
    xb = xb_ref[...]
    inner = dot(xb, down[...])
    inner_out[...] = inner
    lift = dot((sd_ref[layer, 1:2, :] * inner).astype(BF), up[...])
    lift_out[...] = lift.astype(BF)
    kv[:, D:] = (dot(xb, wv[...]) + sb_ref[layer, 1:2, :] * lift).astype(BF)
    kv[:, :D] = dot(xb, wk[...]).astype(BF)


def kv_call(seq, layer, x, got, wk, wv, down, up, sd, sb, **extra):
    return seq(
        functools.partial(kv_body, layer),
        [("v", t) for t in (x, got, wk, wv, down, up, sd, sb)],
        [("v", (ROWS, 2 * D), BF), ("v", (ROWS, RANK), F32), ("v", (ROWS, D), BF), ("v", (ROWS, D), BF)],
        name="keys_values", cost=3.5, **extra)


def q_body(layer, x_ref, inner, wq, up, sd_ref, sb_ref, _, q_ref, qt_ref, lift_out, sems):
    lift = dot((sd_ref[layer, 0:1, :] * inner[...]).astype(BF), up[...])
    lift_out[...] = lift.astype(BF)
    q = (dot(x_ref[...], wq[...]) + sb_ref[layer, 0:1, :] * lift).astype(BF)
    q_ref[...] = q
    qt_ref[...] = q.T


def q_call(seq, layer, x, inner, wq, up, sd, sb, lift_v, **extra):
    return seq(
        functools.partial(q_body, layer),
        [("v", x), ("v", inner), ("v", wq), ("v", up), ("v", sd), ("v", sb), ("v", lift_v)],
        [("v", (ROWS, D), BF), ("v", (D, ROWS), BF), ("v", (ROWS, D), BF)],
        name="queries", cost=1.5, **extra)


def split_heads(t):
    zero = jnp.zeros((HEAD_DIM, t.shape[1]), t.dtype)
    first = jnp.concatenate([t[:HEAD_DIM], zero], axis=0)
    second = jnp.concatenate([zero, t[HEAD_DIM:]], axis=0)
    return jnp.concatenate([first, second], axis=1)


def join_heads(t):
    n = t.shape[1] // 2
    return jnp.concatenate([t[:HEAD_DIM, :n], t[HEAD_DIM:, n:]], axis=0)


def stack_heads(t):
    lane = lax.broadcasted_iota(jnp.int32, (1, PAIR), 1)
    first = (lane < HEAD_DIM).astype(F32).astype(BF)
    second = (lane >= HEAD_DIM).astype(F32).astype(BF)
    return jnp.concatenate([t * first, t * second], axis=0)


def both_halves(near, far, cols):
    return jnp.concatenate([near[:, cols], far[:, cols]], axis=0)


def attend_body(layer, ids, lengths, x_ref, qt_ref, kv, far, wo, gain_ref, y_ref, h_ref, p_out, ctx, *rest):
    copy = Copies(rest[-1])
    p_ref = rest[0] if layer == 0 else p_out
    stores = []
    row = lax.broadcasted_iota(jnp.int32, (BLOCK, 2 * ROWS), 0)
    live = lengths[ids[MINE], 0, 0] + lengths[ids[MINE], 0, 1] + 4
    limits = [live - BLOCK * ids[BLOCKS + b] for b in range(4)]
    for pair in range(PAIRS):
        cols = slice(pair * PAIR, (pair + 1) * PAIR)
        vcols = slice(D + pair * PAIR, D + (pair + 1) * PAIR)
        raw = dot(both_halves(kv, far, cols), split_heads(qt_ref[cols, :])) * SCALE
        scores = jnp.concatenate(
            [jnp.where(row < limits[b], raw[b * BLOCK:(b + 1) * BLOCK], -1000000000.0) for b in range(4)],
            axis=0,
        )
        peak = jnp.max(scores, axis=0, keepdims=True)
        grown = jnp.exp(scores - peak)
        total = jnp.sum(grown, axis=0, keepdims=True)
        p_ref[pair] = (grown * (1.0 / total)).astype(BF)
        if layer == 0:
            stores.append(copy(p_ref.at[pair], p_out.at[pair]))
        ctx_t = join_heads(dot(both_halves(kv, far, vcols).T, p_ref[pair]))
        ctx[:, cols] = ctx_t.T.astype(BF)
    h = x_ref[...].astype(F32) + dot(ctx[...], wo[...])
    h_ref[...] = h
    y_ref[...] = normed(h)[0] * gain_ref[layer, 0:1, :]
    for store in stores:
        store.wait()


def attend_call(seq, layer, ids, lengths, x, qt, kv, far, wo, gain, **extra):
    return seq(
        functools.partial(attend_body, layer),
        [("s", ids), ("s", lengths), ("v", x), ("v", qt), ("v", kv), ("v", far), ("v", wo), ("v", gain)],
        [("v", (ROWS, D), F32), ("v", (ROWS, D), F32),
         ("h" if layer == 0 else "v", (PAIRS, LEN, 2 * ROWS), BF)],
        [((ROWS, D), BF)] + [((PAIRS, LEN, 2 * ROWS), BF)] * (layer == 0), PAIRS, "attention", cost=5,
        limit=20 if layer == 0 else 12, **extra)


class Matrix:
    def __init__(self, own, own_arrays, rest, rest_arrays, shape):
        self.own, self.rest, self.shape = own, rest, (NCB,) + shape
        self.count = (len(own_arrays), len(rest_arrays))
        self.ins = [("h", t) for t in own_arrays] + [("v", t) for t in rest_arrays]

    def start(self, copy, ids, refs, dst):
        return [copy(source, target) for source, target in self.own(ids, refs[:self.count[0]], dst)]

    def move(self, ids, refs, dst):
        for source, target in self.rest(ids, refs[self.count[0]:], dst):
            target[...] = source[...]


def split_refs(matrices, refs):
    groups, start = [], 0
    for matrix in matrices:
        groups.append(refs[start:start + sum(matrix.count)])
        start += sum(matrix.count)
    return groups, refs[start:]


def ffn_hidden(yb, w_in, a_ref, g_ref):
    for slot in range(NCB):
        z = dot(yb, w_in[slot].reshape(D, CB))
        cdf = 0.5 * (1.0 + lax.erf(z * (0.5 ** 0.5)))
        g_ref[slot] = (cdf + z * (jnp.exp(-0.5 * z * z) * 0.3989422804014327)).astype(BF)
        a_ref[slot] = (z * cdf).astype(BF)


def ffn_result(ids, total, a_ref, w_out):
    for slot in range(NCB):
        total = total + dot(a_ref[slot], w_out[ids[SLOTS + slot]].reshape(CB, D))
    return total


def ffn_backward(layer, ids, c, h2, g_ref, h1, gain_ref, wo, w_in, w_out, dh_ref, dctx_ref):
    dh2 = norm_back(h2, gain_ref[layer, 1:2, :], c)
    dfb = dh2.astype(BF)
    total = dh2
    for slot in range(NCB):
        da = dot_nt(dfb, w_out[ids[SLOTS + slot]].reshape(CB, D))
        dz = (g_ref[slot].astype(F32) * da).astype(BF)
        total = total + dot_nt(dz, w_in[slot].reshape(D, CB))
    dh1 = norm_back(h1, gain_ref[layer, 0:1, :], total)
    dh_ref[...] = dh1
    dctx_ref[...] = dot_nt(dh1.astype(BF), wo[...]).astype(BF)


FFN_SHAPE = (NCB, ROWS, CB)


def ffn_body(layer, matrices, ids, y_ref, gain_ref, *rest):
    groups, rest = split_refs(matrices, rest)
    x_ref, h_ref, g_ref, *dsts = rest[:3 + len(matrices)]
    a_ref, sems = rest[3 + len(matrices):]
    copy = Copies(sems)
    waits = [matrix.start(copy, ids, refs, dst) for matrix, refs, dst in zip(matrices, groups, dsts, strict=True)]
    for i, (matrix, refs, dst) in enumerate(zip(matrices, groups, dsts, strict=True)):
        matrix.move(ids, refs, dst)
        for wait in waits[i]:
            wait.wait()
        if i == 0:
            ffn_hidden(y_ref[...].astype(BF), dst, a_ref, g_ref)
        elif i == 1:
            total = ffn_result(ids, y_ref[...], a_ref, dst)
            h_ref[...] = total
            x_ref[...] = normed(total)[0] * gain_ref[layer, 1:2, :]


def ffn_call(seq, layer, ids, matrices, y, gain, **extra):
    return seq(
        functools.partial(ffn_body, layer, matrices),
        [("s", ids), ("v", y), ("v", gain)] + [t for matrix in matrices for t in matrix.ins],
        [("v", (ROWS, D), F32), ("v", (ROWS, D), F32), ("v", FFN_SHAPE, BF)]
        + [("v", matrix.shape, BF) for matrix in matrices],
        [(FFN_SHAPE, BF)], 4 * NCB, "ffn", cost=7, limit=12, **extra)


def ffn_both_body(layer, matrix, ids, y_ref, h1, gain_ref, wo, got_ref, w_in, c_ref, *rest):
    [refs], rest = split_refs([matrix], rest)
    x_ref, send_ref, dh_ref, dctx_ref, w_out, a_ref, g_ref, c, sems = rest
    copy = Copies(sems)
    own = copy(c_ref.at[ids[MINE]], c.at[pl.ds(0, BLOCK)])
    waits = matrix.start(copy, ids, refs, w_out)
    ffn_hidden(y_ref[...].astype(BF), w_in, a_ref, g_ref)
    matrix.move(ids, refs, w_out)
    for wait in waits:
        wait.wait()
    h2 = ffn_result(ids, y_ref[...], a_ref, w_out)
    dh_ref[...] = h2
    x = normed(h2)[0] * gain_ref[layer, 1:2, :]
    x_ref[...] = x[:BLOCK].astype(BF)
    send_ref[...] = x[BLOCK:].astype(BF)
    own.wait()
    c[BLOCK:] = got_ref[...].astype(F32)
    ffn_backward(layer, ids, c[...], dh_ref[...], g_ref, h1[...], gain_ref, wo, w_in, w_out, dh_ref, dctx_ref)


def ffn_both_call(seq, layer, ids, w_in, matrix, y, h1, gain, wo, got, c, **extra):
    return seq(
        functools.partial(ffn_both_body, layer, matrix),
        [("s", ids)] + [("v", t) for t in (y, h1, gain, wo, got, w_in)] + [("h", c)] + matrix.ins,
        [("v", (BLOCK, D), BF), ("v", (BLOCK, D), BF), ("v", (ROWS, D), F32), ("v", (ROWS, D), BF)],
        [(matrix.shape, BF), (FFN_SHAPE, BF), (FFN_SHAPE, BF), ((ROWS, D), F32)], 1 + NCB, "ffn_both", cost=10, limit=16,
        **extra)


def ffn_back_body(layer, ids, c_ref, h2, g, h1, gain_ref, wo, w_in, w_out, dh_ref, dctx_ref, sems):
    ffn_backward(layer, ids, c_ref[...], h2[...], g, h1[...], gain_ref, wo, w_in, w_out, dh_ref, dctx_ref)


def ffn_back_call(seq, layer, ids, c, h2, g, h1, gain, wo, w_in, w_out, **extra):
    return seq(
        functools.partial(ffn_back_body, layer),
        [("s", ids)] + [("v", t) for t in (c, h2, g, h1, gain, wo, w_in, w_out)],
        [("v", (ROWS, D), F32), ("v", (ROWS, D), BF)],
        name="ffn_back", cost=4.5, **extra)


def attend_back_body(dctx_ref, q, kv, far, p_ref, dq_ref, own_ref, send_ref, sems):
    for pair in range(PAIRS):
        cols = slice(pair * PAIR, (pair + 1) * PAIR)
        vcols = slice(D + pair * PAIR, D + (pair + 1) * PAIR)
        dctx = dctx_ref[:, cols]
        dp = dot(both_halves(kv, far, vcols), split_heads(dctx.T))
        pb = p_ref[pair]
        pf = pb.astype(F32)
        weighted = pf * dp
        ds = (weighted - pf * jnp.sum(weighted, axis=0, keepdims=True)).astype(BF)
        dv = dot(pb, stack_heads(dctx))
        dk = dot(ds, stack_heads(q[:, cols])) * SCALE
        own_ref[:, cols] = dk[:ROWS]
        own_ref[:, vcols] = dv[:ROWS]
        send_ref[:, cols] = dk[ROWS:].astype(BF)
        send_ref[:, vcols] = dv[ROWS:].astype(BF)
        dq_t = join_heads(dot(both_halves(kv, far, cols).T, ds)) * SCALE
        dq_ref[:, cols] = dq_t.T.astype(BF)


def attend_back_call(seq, dctx, q, kv, far, p, **extra):
    return seq(
        attend_back_body,
        [("v", dctx), ("v", q), ("v", kv), ("v", far), ("v", p)],
        [("v", (ROWS, D), BF), ("v", (ROWS, 2 * D), F32), ("v", (ROWS, 2 * D), BF)],
        name="attention_back", cost=5, **extra)


def dq_body(layer, dh_ref, dq_ref, lift, inner, wq, up, sd_ref, sb_ref, dx_ref, dub_ref, gd_ref, gb_ref, sems):
    dq = dq_ref[...]
    dqf = dq.astype(F32)
    gb_ref[...] = jnp.sum(dqf * lift[...].astype(F32), axis=0, keepdims=True)
    dpq = dot_nt((sb_ref[layer, 0:1, :] * dqf).astype(BF), up[...])
    gd_ref[...] = jnp.sum(dpq * inner[...], axis=0, keepdims=True)
    dub_ref[...] = sd_ref[layer, 0:1, :] * dpq
    dx_ref[...] = dh_ref[...] + dot_nt(dq, wq[...])


def dq_call(seq, layer, dh, dq, lift, inner, wq, up, sd, sb, **extra):
    return seq(
        functools.partial(dq_body, layer),
        [("v", dh), ("v", dq), ("v", lift), ("v", inner), ("v", wq), ("v", up), ("v", sd), ("v", sb)],
        [("v", (ROWS, D), F32), ("v", (ROWS, RANK), F32), ("v", (1, RANK), F32), ("v", (1, D), F32)],
        name="queries_back", cost=1, **extra)


def dv_body(layer, dub_ref, own_ref, got_ref, lift, inner, up, sd_ref, sb_ref, gdq_ref, gbq_ref, before_ref,
            dub_out, dk_ref, dv_ref, sums_ref, sems):
    sums_ref[...] = before_ref[...]
    sums_ref[4 * layer:4 * layer + 1, :] = gdq_ref[...]
    sums_ref[4 * layer + 2:4 * layer + 3, :D] = gbq_ref[...]
    dv = (own_ref[:, D:] + got_ref[:, D:].astype(F32)).astype(BF)
    dv_ref[...] = dv
    dk_ref[...] = (own_ref[:, :D] + got_ref[:, :D].astype(F32)).astype(BF)
    dvf = dv.astype(F32)
    sums_ref[4 * layer + 3:4 * layer + 4, :D] = jnp.sum(dvf * lift[...].astype(F32), axis=0, keepdims=True)
    dpv = dot_nt((sb_ref[layer, 1:2, :] * dvf).astype(BF), up[...])
    sums_ref[4 * layer + 1:4 * layer + 2, :] = jnp.sum(dpv * inner[...], axis=0, keepdims=True)
    dub_out[...] = (dub_ref[...] + sd_ref[layer, 1:2, :] * dpv).astype(BF)


def dv_call(seq, layer, dub, own, got, lift, inner, up, sd, sb, gd, gb, before, **extra):
    return seq(
        functools.partial(dv_body, layer),
        [("v", t) for t in (dub, own, got, lift, inner, up, sd, sb, gd, gb, before)],
        [("v", (ROWS, RANK), BF), ("v", (ROWS, D), BF), ("v", (ROWS, D), BF), ("v", (4 * LAYERS, RANK), F32)],
        name="values_back", cost=1, **extra)


def dx_body(layer, ids, dx_ref, dub_ref, dk_ref, dv_ref, wk, wv, down, *rest):
    total = dx_ref[...] + dot_nt(dub_ref[...], down[...])
    total = total + dot_nt(dv_ref[...], wv[...])
    total = total + dot_nt(dk_ref[...], wk[...])
    if layer == 0:
        send_ref, grad_ref, own, sems = rest
        own[...] = total[:BLOCK]
        store = Copies(sems)(own, grad_ref.at[ids[MINE]])
        send_ref[...] = total[BLOCK:].astype(BF)
        store.wait()
    else:
        rest[0][...] = total


def dx_call(seq, layer, ids, dx, dub, dk, dv, wk, wv, down, **extra):
    return seq(
        functools.partial(dx_body, layer),
        [("s", ids)] + [("v", t) for t in (dx, dub, dk, dv, wk, wv, down)],
        [("v", (BLOCK, D), BF), ("h", (2, BLOCK, D), F32)] if layer == 0 else [("v", (ROWS, D), F32)],
        [((BLOCK, D), F32)] * (layer == 0), 1, name="input_back", cost=1.5, **extra)


def place_body(ids, own_ref, got_ref, out_ref, sems):
    copy = Copies(sems)
    stores = [copy(own_ref, out_ref.at[ids[MINE]]), copy(got_ref, out_ref.at[1 - ids[MINE]])]
    for store in stores:
        store.wait()


def place_call(seq, ids, own, got, **extra):
    return seq(place_body, [("s", ids), ("v", own), ("v", got)], [("h", (2,) + own.shape, own.dtype)], [], 2, "place",
               cost=0.8, **extra)[0]


def fill_call(seq, ids, whole, got):
    def body(ids_ref, got_ref, out_ref, wide, sems):
        wide[...] = got_ref[...].astype(F32)
        Copies(sems)(wide, out_ref.at[1 - ids_ref[MINE]]).wait()

    return seq(body, [("s", ids), ("v", got)], [], [(got.shape, F32)], 1, "fill", cost=1, fill_hbm=[whole])[0]


def add_call(seq, *terms, last=False, **extra):
    def body(*refs):
        total = refs[0][...]
        for ref in refs[1:len(terms)]:
            total = total + ref[...]
        if last:
            gd_out, gb_out, gd_ref, gb_ref, sems = refs[len(terms):]
            for layer in range(LAYERS):
                gd_ref[layer] = total[4 * layer:4 * layer + 2]
                gb_ref[layer] = total[4 * layer + 2:4 * layer + 4, :D]
            copy = Copies(sems)
            stores = [copy(gd_ref, gd_out), copy(gb_ref, gb_out)]
            for store in stores:
                store.wait()
        else:
            refs[len(terms)][...] = total

    shapes = [((LAYERS, 2, RANK), F32), ((LAYERS, 2, D), F32)] if last else []
    outs = [("h", *t) for t in shapes] if last else [("v", terms[0].shape, F32)]
    return seq(body, [("v", t) for t in terms], outs, shapes, len(shapes), "add", **extra)


def prepare_body(ids, x_ref, c_ref, in_ref, out_ref, xs, own, cs, a_in, b_in, own_y, c_send, sems):
    copy = Copies(sems)
    here, core, mine = ids[HERE], ids[CORE], ids[MINE]
    rows = in_ref.shape[1]

    def columns(block):
        return pl.ds(pl.multiple_of(block * CB, CB), CB)

    waits = [copy(c_ref.at[1 - mine], c_send)]
    for layer in range(LAYERS):
        part = pl.ds(layer * rows, rows)
        for q in range(2):
            waits.append(copy(in_ref.at[layer, :, columns(2 * mine + q)], a_in.at[q, part]))
        waits.append(copy(in_ref.at[layer, :, columns(here)], b_in.at[part]))
        waits.append(copy(in_ref.at[layer, :, columns(here)], own_y.at[0, part]))
        waits.append(copy(out_ref.at[layer, core], own_y.at[1 + layer]))
    waits += [copy(x_ref.at[1 - mine], xs), copy(x_ref.at[mine], own)]
    waits[0].wait()
    cs[...] = c_send[...].astype(BF)
    for wait in waits[1:]:
        wait.wait()


def prepare_call(seq, ids, x, c, ffn_in, halves, **extra):
    rows = (BLOCK, D)
    piece = halves.shape[2:]
    return seq(
        prepare_body,
        [("s", ids), ("h", x), ("h", c), ("h", ffn_in), ("h", halves)],
        [("v", rows, BF), ("v", rows, BF), ("v", rows, BF), ("v", (2,) + piece, BF), ("v", piece, BF),
         ("v", (3,) + piece, BF)],
        [(rows, F32)], 3 + 5 * LAYERS, "prepare", cost=2, **extra)


def everywhere(target):
    pairs = []
    for z in range(4):
        for y in range(2):
            for head in range(4):
                z_to, y_to, head_to = target(z, y, head)
                pairs.append(((2 * z + y) * 4 + head, (2 * (z_to % 4) + y_to) * 4 + head_to))
    return pairs


Z_ONE = everywhere(lambda z, y, head: (z + 1 - 2 * (head % 2), y, head))
TWO = everywhere(lambda z, y, head: (z + 2, y, head))
BOTH_SWAP = everywhere(lambda z, y, head: (z, 1 - y, head ^ 2))
Y_SWAP = [(i, i ^ 1) for i in range(8)]
ACROSS = [(i, i ^ 2) for i in range(4)]
BESIDE = [(i, i ^ 1) for i in range(4)]


def z_shift(step):
    return [(2 * z + y, 2 * ((z + step) % 4) + y) for z in range(4) for y in range(2)]


def swap(t, pairs):
    return lax.ppermute(t, "head", pairs)


def both_axes(t, pairs):
    return lax.ppermute(t, ("dp", "head"), pairs)


def across_y(t):
    return lax.ppermute(t, "dp", Y_SWAP)


def lay_call(seq, arrays, outs, moves, name="lay", cost=1.2, **extra):
    def at(ref, part):
        return ref if part is None else ref.at[part]

    def body(*refs):
        copy = Copies(refs[-1])
        waits = [copy(at(refs[1 + i], take), at(refs[1 + len(arrays) + o], put)) for i, take, o, put in moves]
        for wait in waits:
            wait.wait()

    return seq(body, [("s", extra.pop("ids"))] + [("a", t) for t in arrays], [("v", shape, BF) for shape in outs], [],
               len(moves), name, cost=cost, **extra)


def line_moves(ids, ref, side, part, target):
    core, z_near = (ids[CORE], ids[Z_NEAR]) if side == 0 else (ids[OTHER_CORE], ids[Z_BESIDE])
    return [(ref.at[pl.ds(0, 2)] if part is None else ref.at[pl.ds(0, 2), part], target(z_near, pl.ds(0, 2))),
            (ref.at[2] if part is None else ref.at[2, part], target(ids[Z_TWO], core))]


def in_target(dst, slot, y):
    def target(z, piece):
        return dst.at[pl.ds(slot, 2) if not isinstance(piece, jax.Array) else slot + piece, z, y]

    return target


def own_in(layer, ids, refs, dst):
    columns = [pl.ds(pl.multiple_of(ids[SLOTS + slot] * CB, CB), CB) for slot in range(NCB)]
    return [(refs[0].at[layer, :, columns[slot]], dst.at[slot, ids[Z], ids[Y]]) for slot in range(NCB)]


def rest_in(layer, ids, refs, dst):
    part = pl.ds(layer * dst.shape[3], dst.shape[3])
    z, y = ids[Z], (ids[Y], ids[OTHER_Y])
    moves = []
    for side in range(2):
        core = ids[CORE] if side == 0 else ids[OTHER_CORE]
        along, across, own, far, far_across = refs[side::2]
        moves += line_moves(ids, along, side, part, in_target(dst, 0, y[0]))
        moves += line_moves(ids, across, side, part, in_target(dst, 0, y[1]))
        moves.append((own.at[0, part], dst.at[core, z, y[1]]))
        moves += line_moves(ids, far, side, part, in_target(dst, 2, y[0]))
        moves.append((far.at[3, part], dst.at[2 + core, z, y[1]]))
        moves += line_moves(ids, far_across, side, part, in_target(dst, 2, y[1]))
    return moves


def out_target(dst, y):
    def target(z, piece):
        return dst.at[z, y] if not isinstance(piece, jax.Array) else dst.at[z, y, piece]

    return target


def own_out(layer, ids, refs, dst):
    return [(refs[0].at[layer], dst.at[ids[Z], ids[Y]])]


def rest_out(layer, ids, refs, dst):
    moves = []
    for side in range(2):
        along, across, own = refs[side::2]
        moves += line_moves(ids, along, side, None, out_target(dst, ids[Y]))
        moves += line_moves(ids, across, side, None, out_target(dst, ids[OTHER_Y]))
        moves.append((own.at[1 + layer], dst.at[ids[Z], ids[OTHER_Y], ids[CORE] if side == 0 else ids[OTHER_CORE]]))
    return moves


def nothing(ids, refs, dst):
    return []


def plain_in(ids, refs, dst):
    return [(refs[0].at[ids[SLOTS + slot]], dst.at[slot]) for slot in range(NCB)]


def plain_out(ids, refs, dst):
    return [(refs[0], dst)]


def plain_gather(shard_in, shard_out):
    whole_in = lax.all_gather(shard_in, "dp", axis=0, tiled=True)
    blocks = jnp.stack([whole_in[:, cb * CB:(cb + 1) * CB] for cb in range(NCB)])
    whole_out = lax.all_gather(shard_out, "dp", axis=0, tiled=True)
    return blocks, whole_out.reshape(NCB, CB, D)


def local(block_input, part_lengths, query_weight, key_weight, value_weight, out_weight, down_shared, up_shared,
          scale_d, scale_b, ln_gain, ffn_in, ffn_out, out_grad):
    here = lax.axis_index("head")
    place = lax.axis_index("dp")
    mine = here // 2
    dp = lax.axis_size("dp")
    z, y, core = place // 2, place % 2, here % 2
    ids = jnp.stack(
        [here, core, mine, z, y, 1 - y, (z + 2) % 4, (z + 3 + 2 * core) % 4, (z + 1 + 2 * core) % 4, 1 - core]
        + [2 * (mine ^ (slot // 2)) + slot % 2 if dp == 8 else jnp.int32(slot) for slot in range(NCB)]
        + [here, here ^ 2, here ^ 1, here ^ 3]).astype(jnp.int32)
    seq = Sequence()
    halves = ffn_out.reshape(LAYERS, 2, ffn_out.shape[1] // 2, D)
    scales = (scale_d, scale_b)
    if dp == 8:
        rows_in, piece = ffn_in.shape[1], halves.shape[2:]
        line = (3,) + piece

        def z_sends(layer):
            return [(halves, layer), (halves, ((lambda ids_ref: (layer, ids_ref[CORE])), piece))]

        xs, own, cs, a_in, b_in, own_y = prepare_call(seq, ids, block_input, out_grad, ffn_in, halves)
        in_a, in_b = both_axes(a_in, Z_ONE), both_axes(b_in, TWO)
        got, c_got, own_y = swap(xs, ACROSS), swap(cs, ACROSS), across_y(own_y)
        wk, wv, down, up = seq(
            None, [], [], name="fetch", cost=2.5,
            fetch=[(key_weight, 0), (value_weight, 0), (down_shared, None), (up_shared, None)])
        kv, inner, lift_v, xb, wq = kv_call(seq, 0, own, got, wk, wv, down, up, *scales, fetch=[(query_weight, 0)])
        q, qt, lift_q, wo, inner0, lift_v0 = q_call(
            seq, 0, xb, inner, wq, up, *scales, lift_v, fetch=[(out_weight, 0)], save=[1, 6])
        in_z, in_x, a_out, b_out, kv, c_got = lay_call(
            seq, [in_a, in_b, own_y], [line, (4,) + piece],
            [(0, None, 0, pl.ds(0, 2)), (1, None, 0, 2), (0, None, 1, pl.ds(0, 2)), (1, None, 1, 2), (2, 0, 1, 3)],
            ids=ids, fetch=z_sends(0), through=[kv, c_got])
        out_a, out_b = both_axes(a_out, Z_ONE), both_axes(b_out, TWO)
        in_y, in_far = across_y(in_z), swap(in_x, ACROSS)
        far = swap(kv, BESIDE)
        in_z_core, own_y_core = swap(in_z, BESIDE), swap(own_y, BESIDE)
        y, h1, p0, kv0, far0 = attend_call(
            seq, 0, ids, part_lengths, xb, qt, kv, far, wo, ln_gain, save=[4, 5])
        out0_z, a_out, b_out, in_y, in_far, q0, lift_q0, h10 = lay_call(
            seq, [out_a, out_b, q, lift_q, h1], [line], [(0, None, 0, pl.ds(0, 2)), (1, None, 0, 2)],
            ids=ids, fetch=z_sends(1), through=[in_y, in_far], save=[3, 4, 5])
        out_a, out_b = both_axes(a_out, Z_ONE), both_axes(b_out, TWO)
        out0_y, in_y_far = across_y(out0_z), swap(in_y, ACROSS)
        in_y_core, in_far_core, out0_z_core = swap(in_y, BESIDE), swap(in_far, BESIDE), swap(out0_z, BESIDE)
        out1_z, out0_y, in_y_far = lay_call(
            seq, [out_a, out_b], [line], [(0, None, 0, pl.ds(0, 2)), (1, None, 0, 2)],
            ids=ids, through=[out0_y, in_y_far])
        out1_y = across_y(out1_z)
        in_y_far_core, out0_y_core = swap(in_y_far, BESIDE), swap(out0_y, BESIDE)
        out1_z_core = swap(out1_z, BESIDE)
        pieces_in = [in_z, in_z_core, in_y, in_y_core, own_y, own_y_core, in_far, in_far_core, in_y_far, in_y_far_core]

        def matrix_in(layer):
            return Matrix(functools.partial(own_in, layer), [ffn_in], functools.partial(rest_in, layer), pieces_in,
                          (4, 2, rows_in, CB))

        def matrix_out(layer, pieces):
            return Matrix(functools.partial(own_out, layer), [halves], functools.partial(rest_out, layer),
                          pieces + [own_y, own_y_core], (2, 2) + piece)

        x, h20, g0, w_in0, w_out0, w_in, wk, wv, down, up = ffn_call(
            seq, 0, ids,
            [matrix_in(0), matrix_out(0, [out0_z, out0_z_core, out0_y, out0_y_core]), matrix_in(1)], y, ln_gain,
            fetch=[(key_weight, 1), (value_weight, 1), (down_shared, None), (up_shared, None)])
        stored0 = (kv0, far0, q0, inner0, lift_q0, lift_v0, h10, p0)
        kv, inner, lift_v, xb, wq = kv_call(
            seq, 1, x, got, wk, wv, down, up, *scales, fetch=[(query_weight, 1)])
        far = swap(kv, BESIDE)
        q, qt, lift_q, wo = q_call(seq, 1, xb, inner, wq, up, *scales, lift_v, fetch=[(out_weight, 1)])
        y, h1, p, out1_y = attend_call(seq, 1, ids, part_lengths, x, qt, kv, far, wo, ln_gain, through=[out1_y])
        matrix = matrix_out(1, [out1_z, out1_z_core, out1_y, swap(out1_y, BESIDE)])
    else:
        def pick(t, index):
            return lax.dynamic_index_in_dim(t, index, 0, keepdims=False)

        x, got = pick(block_input, mine), swap(pick(block_input, 1 - mine), ACROSS)
        c_got = swap(pick(out_grad, 1 - mine).astype(BF), ACROSS)
        for layer in range(LAYERS):
            pieces = [[t] for t in plain_gather(ffn_in[layer], ffn_out[layer])]
            wk, wv, down, up, wq, wo = seq(
                None, [], [], name="fetch",
                fetch=[(key_weight, layer), (value_weight, layer), (down_shared, None), (up_shared, None),
                       (query_weight, layer), (out_weight, layer)])
            kv, inner, lift_v, xb = kv_call(seq, layer, x, got, wk, wv, down, up, *scales)
            far = swap(kv, BESIDE)
            q, qt, lift_q = q_call(seq, layer, xb, inner, wq, up, *scales, lift_v)
            y, h1, p = attend_call(
                seq, layer, ids, part_lengths, xb if layer == 0 else x, qt, kv, far, wo, ln_gain)
            matrix = Matrix(plain_out, pieces[1], nothing, [], (CB, D))
            if layer == 0:
                x, h20, g0, w_in0, w_out0 = ffn_call(
                    seq, 0, ids, [Matrix(plain_in, pieces[0], nothing, [], (D, CB)), matrix], y, ln_gain)
                kv0, far0, q0, inner0, lift_q0, lift_v0, h10 = seq(
                    None, [("v", t) for t in (kv, far, q, inner, lift_q, lift_v, h1)], [], save=list(range(7)))
                stored0 = (kv0, far0, q0, inner0, lift_q0, lift_v0, h10, p)
            else:
                [w_in] = seq(None, [("s", ids)], [], name="fetch", fetch=[(pieces[0][0], None)])
    output, send, dh, dctx, wq = ffn_both_call(
        seq, 1, ids, w_in, matrix, y, h1, ln_gain, wo, c_got, out_grad, fetch=[(query_weight, 1)])
    other_output = swap(send, ACROSS)
    kv0, far0, q0, inner0, lift_q0, lift_v0, h10, p0 = stored0
    dq, own, send, wv, wk, wo, h1 = attend_back_call(
        seq, dctx, q, kv, far, p, fetch=[(value_weight, 1), (key_weight, 1), (out_weight, 0), (h10, None)])
    got = swap(send, BESIDE)
    dx, dub, gd_q, gb_q = dq_call(seq, 1, dh, dq, lift_q, inner, wq, up, *scales)
    dub, dk, dv, sums = dv_call(
        seq, 1, dub, own, got, lift_v, inner, up, *scales, gd_q, gb_q, jnp.zeros((4 * LAYERS, RANK), F32))
    [cotangent] = dx_call(seq, 1, ids, dx, dub, dk, dv, wk, wv, down)
    dh, dctx, q, kv, far, p = ffn_back_call(
        seq, 0, ids, cotangent, h20, g0, h1, ln_gain, wo, w_in0, w_out0,
        fetch=[(q0, None), (kv0, None), (far0, None), (p0, None)])
    dq, own, send, wq, wv, wk, inner, lift_q, lift_v = attend_back_call(
        seq, dctx, q, kv, far, p,
        fetch=[(query_weight, 0), (value_weight, 0), (key_weight, 0), (inner0, None), (lift_q0, None), (lift_v0, None)])
    got = swap(send, BESIDE)
    dx, dub, gd_q, gb_q = dq_call(seq, 0, dh, dq, lift_q, inner, wq, up, *scales)
    dub, dk, dv, sums = dv_call(seq, 0, dub, own, got, lift_v, inner, up, *scales, gd_q, gb_q, sums)
    if dp == 8:
        [sums] = add_call(seq, sums, swap(sums, BESIDE))
        parts = [swap(sums, ACROSS), across_y(sums), both_axes(sums, BOTH_SWAP)]
        last_rows, input_grad = dx_call(seq, 0, ids, dx, dub, dk, dv, wk, wv, down)
        sums, last_rows = add_call(seq, sums, *parts, through=[last_rows])
        got = swap(last_rows, ACROSS)
        parts = [lax.ppermute(sums, "dp", z_shift(step)) for step in (1, 2, 3)]
    else:
        last_rows, input_grad = dx_call(seq, 0, ids, dx, dub, dk, dv, wk, wv, down)
        got = swap(last_rows, ACROSS)
        sums, parts = lax.psum(sums, ("dp", "head")), []
    block_output = place_call(seq, ids, output, other_output)
    input_grad = fill_call(seq, ids, input_grad, got)
    grad_d, grad_b = add_call(seq, sums, *parts, last=True)
    return block_output, input_grad, grad_d, grad_b


def solution(mesh):
    both = P(None, ("dp", "head"), None)
    in_specs = (both, P(None, "dp", None), P(), P(), P(), P(), P(), P(), P(), P(), P(),
                P(None, "dp", None), P(None, "dp", None), both)
    out_specs = (both, both, P(), P())
    return jax.shard_map(local, mesh=mesh, in_specs=in_specs, out_specs=out_specs, check_vma=False)
```

```python
import functools

import jax
import jax.numpy as jnp
from jax import lax
from jax.experimental import pallas as pl
from jax.experimental.pallas import tpu as pltpu
from jax.sharding import PartitionSpec as P

D = 768
HEADS = 12
HEAD_DIM = 64
FF = 3072
RANK = 1024
LEN = 512
LAYERS = 2
PAIRS = HEADS // 2
PAIR = 2 * HEAD_DIM
BLOCK = LEN // 4
ROWS = 2 * BLOCK
CB = D
NCB = FF // CB
SCALE = HEAD_DIM ** (-0.5)
BF = jnp.bfloat16
F32 = jnp.float32
MIB = 1 << 20

COLOURS = {"v": pltpu.VMEM, "h": pltpu.HBM}
SPACES = {
    "v": pl.BlockSpec(memory_space=pltpu.VMEM),
    "h": pl.BlockSpec(memory_space=pltpu.HBM),
    "s": pl.BlockSpec(memory_space=pltpu.SMEM),
    "a": pl.BlockSpec(memory_space=pl.ANY),
}


HERE, CORE, MINE, Z, Y, OTHER_Y, Z_TWO, Z_NEAR, Z_BESIDE, OTHER_CORE = range(10)
SLOTS, BLOCKS = 10, 14
KV_PARTS = (1, 4)


def dot(left, right):
    return jnp.dot(left, right, preferred_element_type=F32)


def dot_nt(left, right):
    return lax.dot_general(left, right, (((1,), (1,)), ((), ())), preferred_element_type=F32)


def normed(t):
    centred = t - jnp.mean(t, axis=-1, keepdims=True)
    inverse = lax.rsqrt(jnp.mean(centred * centred, axis=-1, keepdims=True) + 1e-05)
    return centred * inverse, inverse


def norm_back(t, gain, cotangent):
    unit, inverse = normed(t)
    scaled = cotangent * gain
    mean_e = jnp.mean(scaled, axis=-1, keepdims=True)
    mean_en = jnp.mean(scaled * unit, axis=-1, keepdims=True)
    return inverse * (scaled - mean_e - unit * mean_en)


class Copies:
    def __init__(self, sems, first=0):
        self.sems, self.count = sems, first

    def __call__(self, src, dst):
        copy = pltpu.make_async_copy(src, dst, self.sems.at[self.count])
        self.count += 1
        copy.start()
        return copy


class Sequence:
    def __init__(self):
        self.token = None

    def __call__(self, body, ins, outs, scratch=(), copies=0, name="keep", fetch=(), fill=(), fill_hbm=(), through=(), limit=12, save=()):
        handed = [pltpu.with_memory_space_constraint(t, pltpu.VMEM) for t in fill]
        handed += [pltpu.with_memory_space_constraint(t, pltpu.HBM) for t in fill_hbm]
        handed += list(through)
        if self.token is not None:
            handed.append(pltpu.with_memory_space_constraint(self.token, pltpu.HBM))
        fetched = [(t.shape if part is None else t.shape[1:] if isinstance(part, int) else part[1], t.dtype)
                   for t, part in fetch]
        n_in, n_fetch, n_hand, n_fill = len(ins), len(fetch), len(handed), len(fill) + len(fill_hbm)
        n_out, n_save = len(outs), len(save)
        first = self.token is None

        def whole(*refs):
            refs = list(refs)
            in_refs, fetch_refs = refs[:n_in], refs[n_in:n_in + n_fetch]
            refs = refs[n_in + n_fetch:]
            refs = refs[n_hand:]
            out_refs, fetch_outs = refs[:n_out], refs[n_out:n_out + n_fetch]
            refs = refs[n_out + n_fetch:]
            fill_refs = refs[:n_fill]
            save_refs = refs[n_hand + first:][:n_save]
            refs = refs[n_hand + first + n_save:]
            scratch_refs, sems = refs[:len(scratch)], refs[len(scratch)]
            copy = Copies(sems, copies)
            waits = []
            for (_, part), source, target in zip(fetch, fetch_refs, fetch_outs, strict=True):
                if part is not None:
                    source = source.at[part if isinstance(part, int) else part[0](in_refs[0])]
                waits.append(copy(source, target))
            for place, target in zip(save, save_refs, strict=True):
                waits.append(copy(in_refs[place], target))
            if body is not None:
                body(*in_refs, *fill_refs, *out_refs, *scratch_refs, sems)
            for wait in waits:
                wait.wait()

        shapes = [COLOURS[space](shape, dtype) for space, shape, dtype in outs]
        shapes += [pltpu.VMEM(shape, dtype) for shape, dtype in fetched]
        shapes += [pltpu.VMEM(t.shape, t.dtype) for t in fill] + [pltpu.HBM(t.shape, t.dtype) for t in fill_hbm]
        shapes += [jax.ShapeDtypeStruct(t.shape, t.dtype) for t in through]
        shapes += [pltpu.HBM((8, 128), F32)]
        shapes += [pltpu.HBM(ins[place][1].shape, ins[place][1].dtype) for place in save]
        results = pl.pallas_call(
            whole,
            out_shape=tuple(shapes),
            in_specs=[SPACES[space] for space, _ in ins] + [SPACES["h"]] * n_fetch + [SPACES["v"]] * len(fill)
            + [SPACES["h"]] * len(fill_hbm) + [SPACES["a"]] * (n_hand - n_fill),
            out_specs=tuple([SPACES[space] for space, _, _ in outs] + [SPACES["v"]] * (n_fetch + len(fill))
                            + [SPACES["h"]] * len(fill_hbm) + [SPACES["a"]] * (n_hand - n_fill + first) + [SPACES["h"]] * n_save),
            scratch_shapes=[pltpu.VMEM(shape, dtype) for shape, dtype in scratch]
            + [pltpu.SemaphoreType.DMA((copies + n_fetch + n_save + 1,))],
            input_output_aliases={n_in + n_fetch + i: n_out + n_fetch + i for i in range(n_hand)},
            compiler_params=pltpu.CompilerParams(vmem_limit_bytes=limit * MIB),
            cost_estimate=pl.CostEstimate(flops=1000, bytes_accessed=1000, transcendentals=0),
            name=name,
        )(*[pltpu.with_memory_space_constraint(t, COLOURS[space]) if space in COLOURS else t for space, t in ins],
          *[pltpu.with_memory_space_constraint(t, pltpu.HBM) for t, _ in fetch],
          *handed)
        results = list(results)
        split = n_out + n_fetch + n_fill + len(through)
        self.token = results[split]
        return results[:split] + results[split + 1:]


def kv_body(layer, x_ref, got_ref, wk, wv, down, up, sd_ref, sb_ref, *rest):
    *kv, inner_out, lift_out, xb_ref, _ = rest
    if layer == 0:
        xb_ref[:BLOCK] = x_ref[...]
        xb_ref[BLOCK:] = got_ref[...]
    else:
        xb_ref[...] = x_ref[...].astype(BF)
    xb = xb_ref[...]
    inner = dot(xb, down[...])
    inner_out[...] = inner
    lift = dot((sd_ref[layer, 1:2, :] * inner).astype(BF), up[...])
    lift_out[...] = lift.astype(BF)
    values = (dot(xb, wv[...]) + sb_ref[layer, 1:2, :] * lift).astype(BF)
    keys = dot(xb, wk[...]).astype(BF)
    for i, part in enumerate(kv):
        rows = slice(i * part.shape[0], (i + 1) * part.shape[0])
        part[:, :D] = keys[rows]
        part[:, D:] = values[rows]


def kv_call(seq, layer, x, got, wk, wv, down, up, sd, sb, **extra):
    return seq(
        functools.partial(kv_body, layer),
        [("v", t) for t in (x, got, wk, wv, down, up, sd, sb)],
        [("v", (ROWS // KV_PARTS[layer], 2 * D), BF)] * KV_PARTS[layer]
        + [("v", (ROWS, RANK), F32), ("v", (ROWS, D), BF), ("v", (ROWS, D), BF)],
        name="keys_values", **extra)


def q_body(layer, x_ref, inner, wq, up, sd_ref, sb_ref, q_ref, qt_ref, lift_out, sems):
    lift = dot((sd_ref[layer, 0:1, :] * inner[...]).astype(BF), up[...])
    lift_out[...] = lift.astype(BF)
    q = (dot(x_ref[...], wq[...]) + sb_ref[layer, 0:1, :] * lift).astype(BF)
    q_ref[...] = q
    qt_ref[...] = q.T


def q_call(seq, layer, x, inner, wq, up, sd, sb, **extra):
    return seq(
        functools.partial(q_body, layer),
        [("v", x), ("v", inner), ("v", wq), ("v", up), ("v", sd), ("v", sb)],
        [("v", (ROWS, D), BF), ("v", (D, ROWS), BF), ("v", (ROWS, D), BF)],
        name="queries", **extra)


def split_heads(t):
    zero = jnp.zeros((HEAD_DIM, t.shape[1]), t.dtype)
    first = jnp.concatenate([t[:HEAD_DIM], zero], axis=0)
    second = jnp.concatenate([zero, t[HEAD_DIM:]], axis=0)
    return jnp.concatenate([first, second], axis=1)


def join_heads(t):
    n = t.shape[1] // 2
    return jnp.concatenate([t[:HEAD_DIM, :n], t[HEAD_DIM:, n:]], axis=0)


def stack_heads(t):
    lane = lax.broadcasted_iota(jnp.int32, (1, PAIR), 1)
    first = (lane < HEAD_DIM).astype(F32).astype(BF)
    second = (lane >= HEAD_DIM).astype(F32).astype(BF)
    return jnp.concatenate([t * first, t * second], axis=0)


def rows_of(parts, cols):
    return jnp.concatenate([part[:, cols] for part in parts], axis=0)


def attend_body(layer, ids, lengths, x_ref, qt_ref, wo, gain_ref, *rest):
    *kv, y_ref, h_ref, p_ref, ctx, _ = rest
    row = lax.broadcasted_iota(jnp.int32, (BLOCK, 2 * ROWS), 0)
    live = lengths[ids[MINE], 0, 0] + lengths[ids[MINE], 0, 1] + 4
    limits = [live - BLOCK * ids[BLOCKS + b] for b in range(4)]
    for pair in range(PAIRS):
        cols = slice(pair * PAIR, (pair + 1) * PAIR)
        vcols = slice(D + pair * PAIR, D + (pair + 1) * PAIR)
        raw = dot(rows_of(kv, cols), split_heads(qt_ref[cols, :])) * SCALE
        scores = jnp.concatenate(
            [jnp.where(row < limits[b], raw[b * BLOCK:(b + 1) * BLOCK], -1000000000.0) for b in range(4)],
            axis=0,
        )
        peak = jnp.max(scores, axis=0, keepdims=True)
        grown = jnp.exp(scores - peak)
        total = jnp.sum(grown, axis=0, keepdims=True)
        p_ref[pair] = (grown * (1.0 / total)).astype(BF)
        ctx_t = join_heads(dot(rows_of(kv, vcols).T, p_ref[pair]))
        ctx[:, cols] = ctx_t.T.astype(BF)
    h = x_ref[...].astype(F32) + dot(ctx[...], wo[...])
    h_ref[...] = h
    y_ref[...] = normed(h)[0] * gain_ref[layer, 0:1, :]


def attend_call(seq, layer, ids, lengths, x, qt, kv, far, wo, gain, **extra):
    return seq(
        functools.partial(attend_body, layer),
        [("s", ids), ("s", lengths)] + [("v", t) for t in (x, qt, wo, gain, *kv, *far)],
        [("v", (ROWS, D), F32), ("v", (ROWS, D), F32), ("v", (PAIRS, LEN, 2 * ROWS), BF)],
        [((ROWS, D), BF)], name="attention", **extra)


def move(pairs):
    for source, target in pairs:
        target[...] = source[...].reshape(target.shape)


def ffn_hidden(yb, w_in, a_ref, g_ref, slots):
    for slot in slots:
        z = dot(yb, w_in[slot].reshape(D, CB))
        cdf = 0.5 * (1.0 + lax.erf(z * (0.5 ** 0.5)))
        g_ref[slot] = (cdf + z * (jnp.exp(-0.5 * z * z) * 0.3989422804014327)).astype(BF)
        a_ref[slot] = (z * cdf).astype(BF)


def ffn_result(ids, total, a_ref, w_out):
    for slot in range(NCB):
        total = total + dot(a_ref[slot], w_out[ids[SLOTS + slot]].reshape(CB, D))
    return total


def ffn_backward(layer, ids, c, h2, g_ref, h1, gain_ref, wo, w_in, w_out, dh_ref, dctx_ref):
    dh2 = norm_back(h2, gain_ref[layer, 1:2, :], c)
    dfb = dh2.astype(BF)
    total = dh2
    for slot in range(NCB):
        da = dot_nt(dfb, w_out[ids[SLOTS + slot]].reshape(CB, D))
        dz = (g_ref[slot].astype(F32) * da).astype(BF)
        total = total + dot_nt(dz, w_in[slot].reshape(D, CB))
    dh1 = norm_back(h1, gain_ref[layer, 0:1, :], total)
    dh_ref[...] = dh1
    dctx_ref[...] = dot_nt(dh1.astype(BF), wo[...]).astype(BF)


FFN_SHAPE = (NCB, ROWS, CB)


def ffn_first_body(ids, y_ref, in_ref, out_ref, cut_ref, in_z, in_y, in_far, own_y, first, out0_z,
                   w_in0, w_in1, w_out0, w_out1, a_ref, g_ref, sems):
    copy = Copies(sems)
    w_in = (w_in0, w_in1)
    owns = [[copy(source, target) for source, target in own_in(layer, ids, in_ref, w_in[layer])] for layer in range(LAYERS)]
    own_out = [copy(out_ref.at[0], w_out0.at[ids[Z], ids[Y]]), copy(cut_ref.at[1], w_out1.at[ids[Z], ids[Y]])]
    lines = [(in_z, 0), (first, 0), (in_y, 0), (first, 6), (own_y, 0), (first, 3), (in_far, 0), (first, 9)]
    move(pieces_in(0, ids, lines, w_in0))
    for wait in owns[0]:
        wait.wait()
    ffn_hidden(y_ref[...].astype(BF), w_in0, a_ref, g_ref, range(NCB // 2))
    move(pieces_in(1, ids, lines, w_in1))
    for side, line in enumerate([(out0_z, 0), (first, 13)]):
        move(line_moves(ids, line, side, slice(None), out_target(w_out0, ids[Y])))
    for side, (ref, start) in enumerate([(own_y, 0), (first, 3)]):
        core = ids[CORE] if side == 0 else ids[OTHER_CORE]
        for layer, dst in enumerate((w_out0, w_out1)):
            move([(ref.at[start + 1 + layer], dst.at[ids[Z], ids[OTHER_Y], core])])
    for wait in owns[1] + own_out:
        wait.wait()


def ffn_second_body(layer, slots, moves, n_refs, ids, y_ref, gain_ref, *rest):
    refs, rest = rest[:n_refs], rest[n_refs:]
    *ws, a_ref, g_ref, x_ref, h_ref, _ = rest
    w_in, w_out = ws[0], ws[-1] if len(ws) == 2 else ws[2]
    move(moves[0](ids, refs, ws))
    ffn_hidden(y_ref[...].astype(BF), w_in, a_ref, g_ref, slots)
    move(moves[1](ids, refs, ws))
    h_ref[...] = ffn_result(ids, y_ref[...], a_ref, w_out)
    x_ref[...] = normed(h_ref[...])[0] * gain_ref[layer, 1:2, :]


def ffn_second_call(seq, layer, ids, slots, moves, refs, y, gain, ws, a, g, **extra):
    return seq(
        functools.partial(ffn_second_body, layer, slots, moves, len(refs)),
        [("s", ids), ("v", y), ("v", gain)] + [("v", t) for t in refs],
        [("v", (ROWS, D), F32), ("v", (ROWS, D), F32)], name="ffn", fill=[*ws, a, g], **extra)


FFN_SHAPE = (NCB, ROWS, CB)


def ffn_both_body(layer, moves, n_refs, ids, y_ref, h1, gain_ref, wo, got_ref, w_in, c_ref, *rest):
    refs, rest = rest[:n_refs], rest[n_refs:]
    w_out, x_ref, send_ref, dh_ref, dctx_ref, a_ref, g_ref, c, sems = rest
    own = Copies(sems)(c_ref.at[ids[MINE]], c.at[pl.ds(0, BLOCK)])
    ffn_hidden(y_ref[...].astype(BF), w_in, a_ref, g_ref, range(NCB))
    move(moves(ids, refs, w_out))
    h2 = ffn_result(ids, y_ref[...], a_ref, w_out)
    dh_ref[...] = h2
    x = normed(h2)[0] * gain_ref[layer, 1:2, :]
    x_ref[...] = x[:BLOCK].astype(BF)
    send_ref[...] = x[BLOCK:].astype(BF)
    own.wait()
    c[BLOCK:] = got_ref[...].astype(F32)
    ffn_backward(layer, ids, c[...], dh_ref[...], g_ref, h1[...], gain_ref, wo, w_in, w_out, dh_ref, dctx_ref)


def ffn_both_call(seq, layer, ids, w_in, w_out, moves, refs, y, h1, gain, wo, got, c, **extra):
    return seq(
        functools.partial(ffn_both_body, layer, moves, len(refs)),
        [("s", ids)] + [("v", t) for t in (y, h1, gain, wo, got, w_in)] + [("h", c)] + [("v", t) for t in refs],
        [("v", (BLOCK, D), BF), ("v", (BLOCK, D), BF), ("v", (ROWS, D), F32), ("v", (ROWS, D), BF)],
        [(FFN_SHAPE, BF), (FFN_SHAPE, BF), ((ROWS, D), F32)], 1, "ffn_both", fill=[w_out], **extra)


def ffn_back_body(layer, ids, c_ref, h2, g, h1, gain_ref, wo, w_in, w_out, dh_ref, dctx_ref, sems):
    ffn_backward(layer, ids, c_ref[...], h2[...], g, h1[...], gain_ref, wo, w_in, w_out, dh_ref, dctx_ref)


def ffn_back_call(seq, layer, ids, c, h2, g, h1, gain, wo, w_in, w_out, **extra):
    return seq(
        functools.partial(ffn_back_body, layer),
        [("s", ids)] + [("v", t) for t in (c, h2, g, h1, gain, wo, w_in, w_out)],
        [("v", (ROWS, D), F32), ("v", (ROWS, D), BF)],
        name="ffn_back", **extra)


def attend_back_body(dctx_ref, q, p_ref, *rest):
    *kv, dq_ref, own_ref, send_ref, _ = rest
    for pair in range(PAIRS):
        cols = slice(pair * PAIR, (pair + 1) * PAIR)
        vcols = slice(D + pair * PAIR, D + (pair + 1) * PAIR)
        dctx = dctx_ref[:, cols]
        dp = dot(rows_of(kv, vcols), split_heads(dctx.T))
        pb = p_ref[pair]
        pf = pb.astype(F32)
        weighted = pf * dp
        ds = (weighted - pf * jnp.sum(weighted, axis=0, keepdims=True)).astype(BF)
        dv = dot(pb, stack_heads(dctx))
        dk = dot(ds, stack_heads(q[:, cols])) * SCALE
        own_ref[:, cols] = dk[:ROWS]
        own_ref[:, vcols] = dv[:ROWS]
        send_ref[:, cols] = dk[ROWS:].astype(BF)
        send_ref[:, vcols] = dv[ROWS:].astype(BF)
        dq_t = join_heads(dot(rows_of(kv, cols).T, ds)) * SCALE
        dq_ref[:, cols] = dq_t.T.astype(BF)


def attend_back_call(seq, dctx, q, kv, far, p, **extra):
    return seq(
        attend_back_body,
        [("v", t) for t in (dctx, q, p, *kv, *far)],
        [("v", (ROWS, D), BF), ("v", (ROWS, 2 * D), F32), ("v", (ROWS, 2 * D), BF)],
        name="attention_back", **extra)


def dq_body(layer, dh_ref, dq_ref, lift, inner, wq, up, sd_ref, sb_ref, dx_ref, dub_ref, gd_ref, gb_ref, sems):
    dq = dq_ref[...]
    dqf = dq.astype(F32)
    gb_ref[...] = jnp.sum(dqf * lift[...].astype(F32), axis=0, keepdims=True)
    dpq = dot_nt((sb_ref[layer, 0:1, :] * dqf).astype(BF), up[...])
    gd_ref[...] = jnp.sum(dpq * inner[...], axis=0, keepdims=True)
    dub_ref[...] = sd_ref[layer, 0:1, :] * dpq
    dx_ref[...] = dh_ref[...] + dot_nt(dq, wq[...])


def dq_call(seq, layer, dh, dq, lift, inner, wq, up, sd, sb, **extra):
    return seq(
        functools.partial(dq_body, layer),
        [("v", dh), ("v", dq), ("v", lift), ("v", inner), ("v", wq), ("v", up), ("v", sd), ("v", sb)],
        [("v", (ROWS, D), F32), ("v", (ROWS, RANK), F32), ("v", (1, RANK), F32), ("v", (1, D), F32)],
        name="queries_back", **extra)


def dv_body(layer, dub_ref, own_ref, got_ref, lift, inner, up, sd_ref, sb_ref, gdq_ref, gbq_ref, before_ref,
            dub_out, dk_ref, dv_ref, sums_ref, sems):
    sums_ref[...] = before_ref[...]
    sums_ref[4 * layer:4 * layer + 1, :] = gdq_ref[...]
    sums_ref[4 * layer + 2:4 * layer + 3, :D] = gbq_ref[...]
    dv = (own_ref[:, D:] + got_ref[:, D:].astype(F32)).astype(BF)
    dv_ref[...] = dv
    dk_ref[...] = (own_ref[:, :D] + got_ref[:, :D].astype(F32)).astype(BF)
    dvf = dv.astype(F32)
    sums_ref[4 * layer + 3:4 * layer + 4, :D] = jnp.sum(dvf * lift[...].astype(F32), axis=0, keepdims=True)
    dpv = dot_nt((sb_ref[layer, 1:2, :] * dvf).astype(BF), up[...])
    sums_ref[4 * layer + 1:4 * layer + 2, :] = jnp.sum(dpv * inner[...], axis=0, keepdims=True)
    dub_out[...] = (dub_ref[...] + sd_ref[layer, 1:2, :] * dpv).astype(BF)


def dv_call(seq, layer, dub, own, got, lift, inner, up, sd, sb, gd, gb, before, **extra):
    return seq(
        functools.partial(dv_body, layer),
        [("v", t) for t in (dub, own, got, lift, inner, up, sd, sb, gd, gb, before)],
        [("v", (ROWS, RANK), BF), ("v", (ROWS, D), BF), ("v", (ROWS, D), BF), ("v", (4 * LAYERS, RANK), F32)],
        name="values_back", **extra)


def dx_body(layer, ids, dx_ref, dub_ref, dk_ref, dv_ref, wk, wv, down, *rest):
    total = dx_ref[...] + dot_nt(dub_ref[...], down[...])
    total = total + dot_nt(dv_ref[...], wv[...])
    total = total + dot_nt(dk_ref[...], wk[...])
    if layer == 0:
        send_ref, grad_ref, own, sems = rest
        own[...] = total[:BLOCK]
        store = Copies(sems)(own, grad_ref.at[ids[MINE]])
        send_ref[...] = total[BLOCK:].astype(BF)
        store.wait()
    else:
        rest[0][...] = total


def dx_call(seq, layer, ids, dx, dub, dk, dv, wk, wv, down, **extra):
    return seq(
        functools.partial(dx_body, layer),
        [("s", ids)] + [("v", t) for t in (dx, dub, dk, dv, wk, wv, down)],
        [("v", (BLOCK, D), BF), ("h", (2, BLOCK, D), F32)] if layer == 0 else [("v", (ROWS, D), F32)],
        [((BLOCK, D), F32)] * (layer == 0), 1, name="input_back", **extra)


def place_body(ids, own_ref, got_ref, out_ref, sems):
    copy = Copies(sems)
    stores = [copy(own_ref, out_ref.at[ids[MINE]]), copy(got_ref, out_ref.at[1 - ids[MINE]])]
    for store in stores:
        store.wait()


def place_call(seq, ids, own, got, **extra):
    return seq(place_body, [("s", ids), ("v", own), ("v", got)], [("h", (2,) + own.shape, own.dtype)], [], 2, "place", **extra)[0]


def fill_call(seq, ids, whole, got):
    def body(ids_ref, got_ref, out_ref, wide, sems):
        wide[...] = got_ref[...].astype(F32)
        Copies(sems)(wide, out_ref.at[1 - ids_ref[MINE]]).wait()

    return seq(body, [("s", ids), ("v", got)], [], [(got.shape, F32)], 1, "fill", fill_hbm=[whole])[0]


def add_call(seq, *terms, last=False, **extra):
    def body(*refs):
        total = refs[0][...]
        for ref in refs[1:len(terms)]:
            total = total + ref[...]
        if last:
            gd_out, gb_out, gd_ref, gb_ref, sems = refs[len(terms):]
            for layer in range(LAYERS):
                gd_ref[layer] = total[4 * layer:4 * layer + 2]
                gb_ref[layer] = total[4 * layer + 2:4 * layer + 4, :D]
            copy = Copies(sems)
            stores = [copy(gd_ref, gd_out), copy(gb_ref, gb_out)]
            for store in stores:
                store.wait()
        else:
            refs[len(terms)][...] = total

    shapes = [((LAYERS, 2, RANK), F32), ((LAYERS, 2, D), F32)] if last else []
    outs = [("h", *t) for t in shapes] if last else [("v", terms[0].shape, F32)]
    return seq(body, [("v", t) for t in terms], outs, shapes, len(shapes), "add", **extra)


def prepare_body(ids, x_ref, c_ref, in_ref, out_ref, xs, own, cs, a_in, b_in, own_y, c_send, sems):
    copy = Copies(sems)
    here, core, mine = ids[HERE], ids[CORE], ids[MINE]
    rows = in_ref.shape[1]

    def columns(block):
        return pl.ds(pl.multiple_of(block * CB, CB), CB)

    waits = [copy(c_ref.at[1 - mine], c_send)]
    for layer in range(LAYERS):
        part = pl.ds(layer * rows, rows)
        for q in range(2):
            waits.append(copy(in_ref.at[layer, :, columns(2 * mine + q)], a_in.at[q, part]))
        waits.append(copy(in_ref.at[layer, :, columns(here)], b_in.at[part]))
        waits.append(copy(in_ref.at[layer, :, columns(here)], own_y.at[0, part]))
        waits.append(copy(out_ref.at[layer, core], own_y.at[1 + layer]))
    waits += [copy(x_ref.at[1 - mine], xs), copy(x_ref.at[mine], own)]
    waits[0].wait()
    cs[...] = c_send[...].astype(BF)
    for wait in waits[1:]:
        wait.wait()


def prepare_call(seq, ids, x, c, ffn_in, halves, **extra):
    rows = (BLOCK, D)
    piece = halves.shape[2:]
    return seq(
        prepare_body,
        [("s", ids), ("h", x), ("h", c), ("h", ffn_in), ("h", halves)],
        [("v", rows, BF), ("v", rows, BF), ("v", rows, BF), ("v", (2,) + piece, BF), ("v", piece, BF),
         ("v", (3,) + piece, BF)],
        [(rows, F32)], 3 + 5 * LAYERS, "prepare", **extra)


def everywhere(target):
    pairs = []
    for z in range(4):
        for y in range(2):
            for head in range(4):
                z_to, y_to, head_to = target(z, y, head)
                pairs.append(((2 * z + y) * 4 + head, (2 * (z_to % 4) + y_to) * 4 + head_to))
    return pairs


Z_ONE = everywhere(lambda z, y, head: (z + 1 - 2 * (head % 2), y, head))
TWO = everywhere(lambda z, y, head: (z + 2, y, head))
BOTH_SWAP = everywhere(lambda z, y, head: (z, 1 - y, head ^ 2))
Y_SWAP = [(i, i ^ 1) for i in range(8)]
ACROSS = [(i, i ^ 2) for i in range(4)]
BESIDE = [(i, i ^ 1) for i in range(4)]


def z_shift(step):
    return [(2 * z + y, 2 * ((z + step) % 4) + y) for z in range(4) for y in range(2)]


def swap(t, pairs):
    return lax.ppermute(t, "head", pairs)


def both_axes(t, pairs):
    return lax.ppermute(t, ("dp", "head"), pairs)


def across_y(t):
    return lax.ppermute(t, "dp", Y_SWAP)


def lay_call(seq, arrays, outs, **extra):
    piece = arrays[0].shape[-2:]

    def length(part):
        return 1 if part is None else part.stop - part.start

    def body(*refs):
        for out, result in zip(outs, refs[len(arrays):], strict=False):
            start = 0
            for index, part in out:
                stop = start + length(part)
                result[start:stop] = refs[index][...][None] if part is None else refs[index][part]
                start = stop

    shapes = [(sum(length(part) for _, part in out),) + piece for out in outs]
    return seq(body, [("v", t) for t in arrays], [("v", shape, BF) for shape in shapes], name="lay", **extra)


def cut_call(seq, ids, cuts):
    cut = cuts.shape[3:]

    def body(ids_ref, cuts_ref, a_ref, b_ref, sems):
        copy = Copies(sems)
        waits = []
        for core, target in ((0, a_ref.at[0]), (1, a_ref.at[1]), (ids_ref[CORE], b_ref)):
            waits.append(copy(cuts_ref.at[1, core, ids_ref[MINE]], target.at[0]))
            waits.append(copy(cuts_ref.at[1, core, pl.ds(2, 2)], target.at[pl.ds(1, 2)]))
        for wait in waits:
            wait.wait()

    return seq(body, [("s", ids), ("h", cuts)], [("v", (2, 3) + cut, BF), ("v", (3,) + cut, BF)], [], 6, "cut")


def cut_lay_call(seq, out_a, out_b, in_y_far, out0_y):
    cut = out_b.shape[1:]
    piece = out0_y.shape[1:]

    def body(a_ref, b_ref, far_ref, y_ref, line_ref, own_ref, common_ref, second_ref, sems):
        for ref, part in ((line_ref, slice(0, 3)), (own_ref, slice(0, 1)), (common_ref, slice(1, 3))):
            ref[:2] = a_ref[:, part].reshape((2,) + ref.shape[1:])
            ref[2] = b_ref[part].reshape(ref.shape[1:])
        second_ref[:3] = far_ref[...]
        second_ref[3:] = y_ref[...]

    return seq(body, [("v", t) for t in (out_a, out_b, in_y_far, out0_y)],
               [("v", (3, 3) + cut, BF), ("v", (3,) + cut, BF), ("v", (3, 2) + cut, BF), ("v", (6,) + piece, BF)], name="lay")


def last_body(own_y, own_x, common_y, own_yx, out_ref, sems):
    out_ref[:, 0] = own_y[...]
    out_ref[:, 1] = own_x[...]
    out_ref[:, 2:4] = common_y[...]
    out_ref[:, 4] = own_yx[...]


def line_moves(ids, line, side, part, target):
    core, z_near = (ids[CORE], ids[Z_NEAR]) if side == 0 else (ids[OTHER_CORE], ids[Z_BESIDE])
    ref, start = line
    return [(ref.at[pl.ds(start, 2), part], target(z_near, pl.ds(0, 2))),
            (ref.at[start + 2, part], target(ids[Z_TWO], core))]


def in_target(dst, slot, y):
    def target(z, piece):
        return dst.at[pl.ds(slot, 2) if not isinstance(piece, jax.Array) else slot + piece, z, y]

    return target


def own_in(layer, ids, ref, dst):
    columns = [pl.ds(pl.multiple_of(ids[SLOTS + slot] * CB, CB), CB) for slot in range(NCB)]
    return [(ref.at[layer, :, columns[slot]], dst.at[slot, ids[Z], ids[Y]]) for slot in range(NCB)]


def pieces_in(layer, ids, lines, dst):
    part = pl.ds(layer * dst.shape[3], dst.shape[3])
    z, y = ids[Z], (ids[Y], ids[OTHER_Y])
    moves = []
    for side in range(2):
        core = ids[CORE] if side == 0 else ids[OTHER_CORE]
        along, across, own, far = lines[side::2]
        moves += line_moves(ids, along, side, part, in_target(dst, 0, y[0]))
        moves += line_moves(ids, across, side, part, in_target(dst, 0, y[1]))
        moves.append((own[0].at[own[1], part], dst.at[core, z, y[1]]))
        moves += line_moves(ids, far, side, part, in_target(dst, 2, y[0]))
        moves.append((far[0].at[far[1] + 3, part], dst.at[2 + core, z, y[1]]))
    return moves


def pieces_in_last(layer, ids, lines, dst):
    part = pl.ds(layer * dst.shape[3], dst.shape[3])
    return [pair for side in range(2) for pair in line_moves(ids, lines[side], side, part, in_target(dst, 2, ids[OTHER_Y]))]


def out_target(dst, y, cut=None):
    def target(z, piece):
        if not isinstance(piece, jax.Array):
            return dst.at[z, y] if cut is None else dst.at[z, y, :, cut]
        return dst.at[z, y, piece] if cut is None else dst.at[z, y, piece, cut]

    return target


def last_pieces(ids, refs, ws):
    in_y_far, second = refs[:2]
    return pieces_in_last(0, ids, [(in_y_far, 0), (second, 0)], ws[0])


def last_pieces_more(ids, refs, ws):
    in_y_far, second, out0_y, out1_z, out1_z_core = refs
    moves = pieces_in_last(1, ids, [(in_y_far, 0), (second, 0)], ws[1])
    for side, line in enumerate([(out0_y, 0), (second, 3)]):
        moves += line_moves(ids, line, side, slice(None), out_target(ws[2], ids[OTHER_Y]))
    return moves + cut_line(ids, out1_z, 0, ws[3]) + cut_line(ids, out1_z_core, 1, ws[3])


def cut_line(ids, ref, side, dst):
    x, y = ids[MINE], ids[Y]
    return (line_moves(ids, (ref, 0), side, 0, out_target(dst, y, x))
            + line_moves(ids, (ref, 0), side, pl.ds(1, 2), out_target(dst, y, pl.ds(2, 2))))


def cut_pieces(ids, refs, dst):
    x, y = ids[MINE], (ids[Y], ids[OTHER_Y])
    moves = []
    for side, ref in enumerate(refs):
        for part, place, cut in ((0, y[1], x), (1, y[0], 1 - x), (pl.ds(2, 2), y[1], pl.ds(2, 2)), (4, y[1], 1 - x)):
            moves += line_moves(ids, (ref, 0), side, part, out_target(dst, place, cut))
    return moves


def nothing(ids, refs, dst):
    return []


def plain_gather(shard_in, shard_out):
    whole_in = lax.all_gather(shard_in, "dp", axis=0, tiled=True)
    blocks = jnp.stack([whole_in[:, cb * CB:(cb + 1) * CB] for cb in range(NCB)])
    whole_out = lax.all_gather(shard_out, "dp", axis=0, tiled=True)
    return blocks, whole_out.reshape(NCB, CB, D)


def local(block_input, part_lengths, query_weight, key_weight, value_weight, out_weight, down_shared, up_shared,
          scale_d, scale_b, ln_gain, ffn_in, ffn_out, out_grad):
    here = lax.axis_index("head")
    place = lax.axis_index("dp")
    mine = here // 2
    dp = lax.axis_size("dp")
    z, y, core = place // 2, place % 2, here % 2
    ids = jnp.stack(
        [here, core, mine, z, y, 1 - y, (z + 2) % 4, (z + 3 + 2 * core) % 4, (z + 1 + 2 * core) % 4, 1 - core]
        + [2 * (mine ^ (slot // 2)) + slot % 2 if dp == 8 else jnp.int32(slot) for slot in range(NCB)]
        + [here, here ^ 2, here ^ 1, here ^ 3]).astype(jnp.int32)
    seq = Sequence()
    halves = ffn_out.reshape(LAYERS, 2, ffn_out.shape[1] // 2, D)
    scales = (scale_d, scale_b)
    if dp == 8:
        rows_in, piece = ffn_in.shape[1], halves.shape[2:]
        cuts = halves.reshape(LAYERS, 2, 4, piece[0] // 4, D)
        cut = cuts.shape[3:]
        line = [(0, slice(0, 2)), (1, None)]

        xs, own, cs, a_in, b_in, own_y = prepare_call(seq, ids, block_input, out_grad, ffn_in, halves)
        in_a, in_b = both_axes(a_in, Z_ONE), both_axes(b_in, TWO)
        got, c_got, own_y = swap(xs, ACROSS), swap(cs, ACROSS), across_y(own_y)
        wk, wv, down, up, a_out, b_out = seq(
            None, [("s", ids)], [], name="fetch",
            fetch=[(key_weight, 0), (value_weight, 0), (down_shared, None), (up_shared, None),
                   (halves, 0), (halves, ((lambda ids_ref: (0, ids_ref[CORE])), piece))])
        *kv, inner0, lift_v0, xb, wq, c_got = kv_call(
            seq, 0, own, got, wk, wv, down, up, *scales, fetch=[(query_weight, 0)], through=[c_got])
        q0, qt, lift_q0, wo = q_call(seq, 0, xb, inner0, wq, up, *scales, fetch=[(out_weight, 0)])
        in_z, in_x, *kv = lay_call(
            seq, [in_a, in_b, own_y], [line, line + [(2, slice(0, 1))]], through=kv)
        out_a, out_b = both_axes(a_out, Z_ONE), both_axes(b_out, TWO)
        in_y, in_far = across_y(in_z), swap(in_x, ACROSS)
        far = [swap(t, BESIDE) for t in kv]
        a_out, b_out = cut_call(seq, ids, cuts)
        y, h10, p0 = attend_call(seq, 0, ids, part_lengths, xb, qt, kv, far, wo, ln_gain)
        out0_z, first = lay_call(
            seq, [out_a, out_b, in_z, own_y, in_y, in_far],
            [line, [(2, slice(0, 3)), (3, slice(0, 3)), (4, slice(0, 3)), (5, slice(0, 4))] + line])
        stored0 = (kv, far, q0, inner0, lift_q0, lift_v0, h10, p0)
        out_a, out_b = both_axes(a_out, Z_ONE), both_axes(b_out, TWO)
        out0_y, in_y_far, first = across_y(out0_z), swap(in_y, ACROSS), swap(first, BESIDE)
        w_in0, w_in, w_out0, w_out, a, g0 = seq(
            ffn_first_body,
            [("s", ids), ("v", y), ("h", ffn_in), ("h", halves), ("h", cuts)]
            + [("v", t) for t in (in_z, in_y, in_far, own_y, first, out0_z)],
            [("v", (NCB, 4, 2, rows_in, CB), BF)] * 2 + [("v", (NCB, 2, 2) + piece, BF), ("v", (NCB, 2, 2, 4) + cut, BF)]
            + [("v", FFN_SHAPE, BF)] * 2, [], 2 * NCB + 2, "ffn_first")
        out1_z, out1_own, out1_common, second = cut_lay_call(seq, out_a, out_b, in_y_far, out0_y)
        out1_own_y, out1_own_x, out1_common_y = across_y(out1_own), swap(out1_own, ACROSS), across_y(out1_common)
        second, out1_z_core = swap(second, BESIDE), swap(out1_z, BESIDE)
        x, h20, wk, wv, down, up, w_in0, w_in, w_out0, w_out, a, g0 = ffn_second_call(
            seq, 0, ids, range(NCB // 2, NCB), (last_pieces, last_pieces_more), [in_y_far, second, out0_y, out1_z, out1_z_core],
            y, ln_gain, [w_in0, w_in, w_out0, w_out], a, g0,
            fetch=[(key_weight, 1), (value_weight, 1), (down_shared, None), (up_shared, None)])
        out1_own_y, out1_own_x = seq(None, [], [], through=[out1_own_y, out1_own_x])
        out1_own_yx = swap(out1_own_y, ACROSS)
        *kv, inner, lift_v, xb, wq = kv_call(
            seq, 1, x, got, wk, wv, down, up, *scales, fetch=[(query_weight, 1)])
        far = [swap(t, BESIDE) for t in kv]
        q, qt, lift_q, wo = q_call(seq, 1, xb, inner, wq, up, *scales, fetch=[(out_weight, 1)])
        y, h1, p = attend_call(seq, 1, ids, part_lengths, x, qt, kv, far, wo, ln_gain)
        [last] = seq(last_body, [("v", t) for t in (out1_own_y, out1_own_x, out1_common_y, out1_own_yx)],
                     [("v", (3, 5) + cut, BF)], name="lay")
        moves, refs = cut_pieces, [last, swap(last, BESIDE)]
    else:
        def pick(t, index):
            return lax.dynamic_index_in_dim(t, index, 0, keepdims=False)

        x, got = pick(block_input, mine), swap(pick(block_input, 1 - mine), ACROSS)
        c_got = swap(pick(out_grad, 1 - mine).astype(BF), ACROSS)
        for layer in range(LAYERS):
            blocks_in, blocks_out = plain_gather(ffn_in[layer], ffn_out[layer])
            wk, wv, down, up, wq, wo, w_in, w_out = seq(
                None, [], [], name="fetch",
                fetch=[(key_weight, layer), (value_weight, layer), (down_shared, None), (up_shared, None),
                       (query_weight, layer), (out_weight, layer), (blocks_in, None), (blocks_out, None)])
            *kv, inner, lift_v, xb = kv_call(seq, layer, x, got, wk, wv, down, up, *scales)
            far = [swap(t, BESIDE) for t in kv]
            q, qt, lift_q = q_call(seq, layer, xb, inner, wq, up, *scales)
            y, h1, p = attend_call(
                seq, layer, ids, part_lengths, xb if layer == 0 else x, qt, kv, far, wo, ln_gain)
            if layer == 0:
                a, g0 = seq(None, [], [("v", FFN_SHAPE, BF)] * 2)
                x, h20, w_in0, w_out0, a, g0 = ffn_second_call(
                    seq, 0, ids, range(NCB), (nothing, nothing), [], y, ln_gain, [w_in, w_out], a, g0)
                stored0 = (kv, far, q, inner, lift_q, lift_v, h1, p)
        moves, refs = nothing, []
    output, send, dh, dctx, wq, _ = ffn_both_call(
        seq, 1, ids, w_in, w_out, moves, refs, y, h1, ln_gain, wo, c_got, out_grad, fetch=[(query_weight, 1)])
    other_output = swap(send, ACROSS)
    dq, own, send, wv, wk, wo = attend_back_call(
        seq, dctx, q, kv, far, p, fetch=[(value_weight, 1), (key_weight, 1), (out_weight, 0)])
    got = swap(send, BESIDE)
    dx, dub, gd_q, gb_q = dq_call(seq, 1, dh, dq, lift_q, inner, wq, up, *scales)
    dub, dk, dv, sums = dv_call(
        seq, 1, dub, own, got, lift_v, inner, up, *scales, gd_q, gb_q, jnp.zeros((4 * LAYERS, RANK), F32))
    [cotangent] = dx_call(seq, 1, ids, dx, dub, dk, dv, wk, wv, down)
    kv, far, q, inner, lift_q, lift_v, h1, p = stored0
    dh, dctx, wq, wv, wk = ffn_back_call(
        seq, 0, ids, cotangent, h20, g0, h1, ln_gain, wo, w_in0, w_out0,
        fetch=[(query_weight, 0), (value_weight, 0), (key_weight, 0)])
    dq, own, send = attend_back_call(seq, dctx, q, kv, far, p)
    got = swap(send, BESIDE)
    dx, dub, gd_q, gb_q = dq_call(seq, 0, dh, dq, lift_q, inner, wq, up, *scales)
    dub, dk, dv, sums = dv_call(seq, 0, dub, own, got, lift_v, inner, up, *scales, gd_q, gb_q, sums)
    if dp == 8:
        [sums] = add_call(seq, sums, swap(sums, BESIDE))
        parts = [swap(sums, ACROSS), across_y(sums), both_axes(sums, BOTH_SWAP)]
        last_rows, input_grad = dx_call(seq, 0, ids, dx, dub, dk, dv, wk, wv, down)
        sums, last_rows = add_call(seq, sums, *parts, through=[last_rows])
        got = swap(last_rows, ACROSS)
        parts = [lax.ppermute(sums, "dp", z_shift(step)) for step in (1, 2, 3)]
    else:
        last_rows, input_grad = dx_call(seq, 0, ids, dx, dub, dk, dv, wk, wv, down)
        got = swap(last_rows, ACROSS)
        sums, parts = lax.psum(sums, ("dp", "head")), []
    block_output = place_call(seq, ids, output, other_output)
    input_grad = fill_call(seq, ids, input_grad, got)
    grad_d, grad_b = add_call(seq, sums, *parts, last=True)
    return block_output, input_grad, grad_d, grad_b


def solution(mesh):
    both = P(None, ("dp", "head"), None)
    in_specs = (both, P(None, "dp", None), P(), P(), P(), P(), P(), P(), P(), P(), P(),
                P(None, "dp", None), P(None, "dp", None), both)
    out_specs = (both, both, P(), P())
    return jax.shard_map(local, mesh=mesh, in_specs=in_specs, out_specs=out_specs, check_vma=False)
```

```python
import functools

import jax
import jax.numpy as jnp
from jax import lax
from jax.experimental import pallas as pl
from jax.experimental.pallas import tpu as pltpu
from jax.sharding import PartitionSpec as P

D = 768
HEADS = 12
HEAD_DIM = 64
FF = 3072
RANK = 1024
LEN = 512
LAYERS = 2
PAIRS = HEADS // 2
PAIR = 2 * HEAD_DIM
BLOCK = LEN // 4
ROWS = 2 * BLOCK
CB = D
NCB = FF // CB
SCALE = HEAD_DIM ** (-0.5)
BF = jnp.bfloat16
F32 = jnp.float32
MIB = 1 << 20

COLOURS = {"v": pltpu.VMEM, "h": pltpu.HBM}
SPACES = {
    "v": pl.BlockSpec(memory_space=pltpu.VMEM),
    "h": pl.BlockSpec(memory_space=pltpu.HBM),
    "s": pl.BlockSpec(memory_space=pltpu.SMEM),
    "a": pl.BlockSpec(memory_space=pl.ANY),
}


HERE, CORE, MINE, Z, Y, OTHER_Y, Z_TWO, Z_NEAR, Z_BESIDE, OTHER_CORE = range(10)
SLOTS, BLOCKS = 10, 14


def indices(dp):
    here, place = lax.axis_index("head"), lax.axis_index("dp")
    mine, core = lax.div(here, 2), lax.rem(here, 2)
    z, y = lax.div(place, 2), lax.rem(place, 2)
    line = [z, y, 1 - y] + [lax.rem(z + step, 4) for step in (2, 3 + 2 * core, 1 + 2 * core)]
    blocks = [here, here ^ 2, here ^ 1, here ^ 3]
    if dp == 8:
        slots = [2 * mine, 2 * mine + 1, 2 - 2 * mine, 3 - 2 * mine]
    else:
        slots = list(range(NCB))
    return [here, core, mine] + line + [1 - core] + slots + blocks


def dot(left, right):
    return jnp.dot(left, right, preferred_element_type=F32)


def dot_nt(left, right):
    return lax.dot_general(left, right, (((1,), (1,)), ((), ())), preferred_element_type=F32)


def normed(t):
    centred = t - jnp.mean(t, axis=-1, keepdims=True)
    inverse = lax.rsqrt(jnp.mean(centred * centred, axis=-1, keepdims=True) + 1e-05)
    return centred * inverse, inverse


def norm_back(t, gain, cotangent):
    unit, inverse = normed(t)
    scaled = cotangent * gain
    mean_e = jnp.mean(scaled, axis=-1, keepdims=True)
    mean_en = jnp.mean(scaled * unit, axis=-1, keepdims=True)
    return inverse * (scaled - mean_e - unit * mean_en)


class Copies:
    def __init__(self, sems, first=0):
        self.sems, self.count = sems, first

    def __call__(self, src, dst):
        copy = pltpu.make_async_copy(src, dst, self.sems.at[self.count])
        self.count += 1
        copy.start()
        return copy


class Sequence:
    def __init__(self, dp):
        self.dp, self.token = dp, None

    def __call__(self, body, ins, outs, scratch=(), copies=0, name="keep", fetch=(), fill=(), fill_hbm=(), through=(), limit=8, save=(), cost=0.001):
        handed = [pltpu.with_memory_space_constraint(t, pltpu.VMEM) for t in fill]
        handed += [pltpu.with_memory_space_constraint(t, pltpu.HBM) for t in fill_hbm]
        handed += list(through)
        if self.token is not None:
            handed.append(pltpu.with_memory_space_constraint(self.token, pltpu.HBM))
        fetched = [(t.shape if part is None else t.shape[1:] if isinstance(part, int) else part[1], t.dtype)
                   for t, part in fetch]
        wants = [i for i, entry in enumerate(ins) if entry is None]
        ins = [entry for entry in ins if entry is not None]
        n_in, n_fetch, n_hand, n_fill = len(ins), len(fetch), len(handed), len(fill) + len(fill_hbm)
        n_out, n_save = len(outs), len(save)
        first = self.token is None

        def whole(*refs):
            refs = list(refs)
            in_refs, fetch_refs = refs[:n_in], refs[n_in:n_in + n_fetch]
            for i in wants:
                in_refs.insert(i, indices(self.dp))
            refs = refs[n_in + n_fetch:]
            refs = refs[n_hand:]
            out_refs, fetch_outs = refs[:n_out], refs[n_out:n_out + n_fetch]
            refs = refs[n_out + n_fetch:]
            fill_refs = refs[:n_fill]
            save_refs = refs[n_hand + first:][:n_save]
            refs = refs[n_hand + first + n_save:]
            scratch_refs, sems = refs[:len(scratch)], refs[len(scratch)]
            copy = Copies(sems, copies)
            waits = []
            for (_, part), source, target in zip(fetch, fetch_refs, fetch_outs, strict=True):
                if part is not None:
                    source = source.at[part if isinstance(part, int) else part[0](in_refs[0])]
                waits.append(copy(source, target))
            for place, target in zip(save, save_refs, strict=True):
                waits.append(copy(in_refs[place], target))
            if body is not None:
                body(*in_refs, *fill_refs, *out_refs, *scratch_refs, sems)
            for wait in waits:
                wait.wait()

        shapes = [COLOURS[space](shape, dtype) for space, shape, dtype in outs]
        shapes += [pltpu.VMEM(shape, dtype) for shape, dtype in fetched]
        shapes += [pltpu.VMEM(t.shape, t.dtype) for t in fill] + [pltpu.HBM(t.shape, t.dtype) for t in fill_hbm]
        shapes += [jax.ShapeDtypeStruct(t.shape, t.dtype) for t in through]
        shapes += [pltpu.HBM((8, 128), F32)]
        shapes += [pltpu.HBM(ins[place][1].shape, ins[place][1].dtype) for place in save]
        results = pl.pallas_call(
            whole,
            out_shape=tuple(shapes),
            in_specs=[SPACES[space] for space, _ in ins] + [SPACES["h"]] * n_fetch + [SPACES["v"]] * len(fill)
            + [SPACES["h"]] * len(fill_hbm) + [SPACES["a"]] * (n_hand - n_fill),
            out_specs=tuple([SPACES[space] for space, _, _ in outs] + [SPACES["v"]] * (n_fetch + len(fill))
                            + [SPACES["h"]] * len(fill_hbm) + [SPACES["a"]] * (n_hand - n_fill + first) + [SPACES["h"]] * n_save),
            scratch_shapes=[pltpu.VMEM(shape, dtype) for shape, dtype in scratch]
            + [pltpu.SemaphoreType.DMA((copies + n_fetch + n_save + 1,))],
            input_output_aliases={n_in + n_fetch + i: n_out + n_fetch + i for i in range(n_hand)},
            compiler_params=pltpu.CompilerParams(vmem_limit_bytes=limit * MIB),
            cost_estimate=pl.CostEstimate(
                flops=int(cost * 1e9), bytes_accessed=int(cost * 3e6), transcendentals=0),
            name=name,
        )(*[pltpu.with_memory_space_constraint(t, COLOURS[space]) if space in COLOURS else t for space, t in ins],
          *[pltpu.with_memory_space_constraint(t, pltpu.HBM) for t, _ in fetch],
          *handed)
        results = list(results)
        split = n_out + n_fetch + n_fill + len(through)
        self.token = results[split]
        return results[:split] + results[split + 1:]


def kv_body(layer, x_ref, got_ref, wk, wv, down, up, sd_ref, sb_ref, *rest):
    keys, values, inner_out, lift_out, xb_ref, _ = rest
    if layer == 0:
        xb_ref[:BLOCK] = x_ref[...]
        xb_ref[BLOCK:] = got_ref[...]
    else:
        xb_ref[...] = x_ref[...].astype(BF)
    xb = xb_ref[...]
    inner = dot(xb, down[...])
    inner_out[...] = inner.astype(BF)
    lift = dot((sd_ref[layer, 1:2, :] * inner).astype(BF), up[...])
    lift_out[...] = lift.astype(BF)
    values[...] = (dot(xb, wv[...]) + sb_ref[layer, 1:2, :] * lift).astype(BF)
    keys[...] = dot(xb, wk[...]).astype(BF)


def kv_call(seq, layer, x, got, wk, wv, down, up, sd, sb, **extra):
    return seq(
        functools.partial(kv_body, layer),
        [("v", t) for t in (x, got, wk, wv, down, up, sd, sb)],
        [("v", (ROWS, D), BF)] * 2 + [("v", (ROWS, RANK), BF), ("v", (ROWS, D), BF), ("v", (ROWS, D), BF)],
        name="keys_values", **extra)


def q_body(layer, x_ref, inner, wq, up, sd_ref, sb_ref, q_ref, qt_ref, lift_out, sems):
    lift = dot((sd_ref[layer, 0:1, :] * inner[...].astype(F32)).astype(BF), up[...])
    lift_out[...] = lift.astype(BF)
    q = (dot(x_ref[...], wq[...]) + sb_ref[layer, 0:1, :] * lift).astype(BF)
    q_ref[...] = q
    qt_ref[...] = (q * SCALE).T


def q_call(seq, layer, x, inner, wq, up, sd, sb, **extra):
    return seq(
        functools.partial(q_body, layer),
        [("v", x), ("v", inner), ("v", wq), ("v", up), ("v", sd), ("v", sb)],
        [("v", (ROWS, D), BF), ("v", (D, ROWS), BF), ("v", (ROWS, D), BF)],
        name="queries", **extra)


def split_heads(t):
    zero = jnp.zeros((HEAD_DIM, t.shape[1]), t.dtype)
    first = jnp.concatenate([t[:HEAD_DIM], zero], axis=0)
    second = jnp.concatenate([zero, t[HEAD_DIM:]], axis=0)
    return jnp.concatenate([first, second], axis=1)


def join_heads(t):
    n = t.shape[1] // 2
    return jnp.concatenate([t[:HEAD_DIM, :n], t[HEAD_DIM:, n:]], axis=0)


def stack_heads(t):
    lane = lax.broadcasted_iota(jnp.int32, (1, PAIR), 1)
    first = (lane < HEAD_DIM).astype(F32).astype(BF)
    second = (lane >= HEAD_DIM).astype(F32).astype(BF)
    return jnp.concatenate([t * first, t * second], axis=0)


def rows_of(near, far, cols):
    return jnp.concatenate([near[:, cols], far[:, cols]], axis=0)


def attend_body(layer, ids, lengths, x_ref, qt_ref, wo, gain_ref, keys, values, far_keys, far_values,
                y_ref, h_ref, e_ref, factor_ref, ctx_t_ref, ctx, sems):
    row = lax.broadcasted_iota(jnp.int32, (BLOCK, 2 * ROWS), 0)
    counts = lengths[ids[MINE]]
    live = counts[:, :1] + counts[:, 1:] + 4
    limits = [live - BLOCK * ids[BLOCKS + b] for b in range(4)]
    for pair in range(PAIRS):
        cols = slice(pair * PAIR, (pair + 1) * PAIR)
        raw = dot(rows_of(keys, far_keys, cols), split_heads(qt_ref[cols, :]))
        scores = jnp.concatenate(
            [jnp.where(row < limits[b], raw[b * BLOCK:(b + 1) * BLOCK], -1000000000.0) for b in range(4)],
            axis=0,
        )
        grown = jnp.exp(scores - jnp.max(scores, axis=0, keepdims=True))
        factor = 1.0 / jnp.sum(grown, axis=0, keepdims=True)
        factor_ref[pair:pair + 1, :] = factor
        e_ref[pair] = grown.astype(BF)
        ctx_t = join_heads(dot(rows_of(values, far_values, cols).T, e_ref[pair]) * factor).astype(BF)
        ctx_t_ref[cols, :] = ctx_t
        ctx[:, cols] = ctx_t.T
    h = x_ref[...].astype(F32) + dot(ctx[...], wo[...])
    h_ref[...] = h
    y_ref[...] = normed(h)[0] * gain_ref[layer, 0:1, :]


def attend_call(seq, layer, lengths, x, qt, kv, wo, gain, **extra):
    return seq(
        functools.partial(attend_body, layer),
        [None] + [("v", t) for t in (lengths, x, qt, wo, gain, *kv)],
        [("v", (ROWS, D), F32), ("v", (ROWS, D), F32), ("v", (PAIRS, LEN, 2 * ROWS), BF), ("v", (PAIRS, 2 * ROWS), F32),
         ("v", (D, ROWS), BF)],
        [((ROWS, D), BF)], name="attention", **extra)


def move(pairs):
    for source, target in pairs:
        target[...] = source[...].reshape(target.shape)


def ffn_hidden(yb, w_in, a_ref, g_ref, slots):
    for slot in slots:
        z = dot(yb, w_in[slot].reshape(D, CB))
        cdf = 0.5 * (1.0 + lax.erf(z * (0.5 ** 0.5)))
        g_ref[slot] = (cdf + z * (jnp.exp(-0.5 * z * z) * 0.3989422804014327)).astype(BF)
        a_ref[slot] = (z * cdf).astype(BF)


def ffn_result(ids, total, a_ref, w_out):
    for slot in range(NCB):
        total = total + dot(a_ref[slot], w_out[ids[SLOTS + slot]].reshape(CB, D))
    return total


def ffn_backward(layer, ids, c, h2, g_ref, h1, gain_ref, w_in, w_out, dh_ref):
    dh2 = norm_back(h2, gain_ref[layer, 1:2, :], c)
    dfb = dh2.astype(BF)
    total = dh2
    for slot in range(NCB):
        da = dot_nt(dfb, w_out[ids[SLOTS + slot]].reshape(CB, D))
        dz = (g_ref[slot].astype(F32) * da).astype(BF)
        total = total + dot_nt(dz, w_in[slot].reshape(D, CB))
    dh1 = norm_back(h1, gain_ref[layer, 0:1, :], total)
    dh_ref[...] = dh1


FFN_SHAPE = (NCB, ROWS, CB)


def ffn_first_body(ids, y_ref, in_ref, cut_ref, in_z, in_y, in_far, own_y, first, out0_z,
                   w_in, w_out, a_ref, g_ref, sems):
    copy = Copies(sems)
    w_in = [w_in.at[layer] for layer in range(LAYERS)]
    w_out = [w_out.at[layer] for layer in range(LAYERS)]
    owns = [[copy(source, target) for source, target in own_in(layer, ids, in_ref, w_in[layer])] for layer in range(LAYERS)]
    own_out = [copy(cut_ref.at[layer], w_out[layer].at[ids[Z], ids[Y]]) for layer in range(LAYERS)]
    lines = [(in_z, 0), (first, 0), (in_y, 0), (first, 6), (own_y, 0), (first, 3), (in_far, 0), (first, 9)]
    move(pieces_in(0, ids, lines, w_in[0]))
    for wait in owns[0]:
        wait.wait()
    ffn_hidden(y_ref[...].astype(BF), w_in[0], a_ref, g_ref, range(NCB // 2))
    move(pieces_in(1, ids, lines, w_in[1]))
    for side, line in enumerate([(out0_z, 0), (first, 13)]):
        move(line_moves(ids, line, side, slice(None), out_target(w_out[0], ids[Y])))
    for side, (ref, start) in enumerate([(own_y, 0), (first, 3)]):
        core = ids[CORE] if side == 0 else ids[OTHER_CORE]
        for layer in range(LAYERS):
            move([(ref.at[start + 1 + layer], w_out[layer].at[ids[Z], ids[OTHER_Y], core])])
    for wait in owns[1] + own_out:
        wait.wait()


def ffn_second_body(layer, slots, moves, n_refs, ids, y_ref, gain_ref, *rest):
    refs, rest = rest[:n_refs], rest[n_refs:]
    w_in, w_out, a_ref, g_ref, x_ref, h_ref, _ = rest
    move(moves[0](ids, refs, w_in, w_out))
    ffn_hidden(y_ref[...].astype(BF), w_in.at[layer], a_ref, g_ref, slots)
    move(moves[1](ids, refs, w_in, w_out))
    h_ref[...] = ffn_result(ids, y_ref[...], a_ref, w_out.at[layer])
    x_ref[...] = normed(h_ref[...])[0] * gain_ref[layer, 1:2, :]


def ffn_second_call(seq, layer, slots, moves, refs, y, gain, w_in, w_out, a, g, **extra):
    return seq(
        functools.partial(ffn_second_body, layer, slots, moves, len(refs)),
        [None, ("v", y), ("v", gain)] + [("v", t) for t in refs],
        [("v", (ROWS, D), F32), ("v", (ROWS, D), F32)], name="ffn", fill=[w_in, w_out, a, g], **extra)


FFN_SHAPE = (NCB, ROWS, CB)


def ffn_both_body(layer, moves, n_refs, ids, y_ref, h1, gain_ref, got_ref, c_ref, *rest):
    refs, rest = rest[:n_refs], rest[n_refs:]
    w_in, w_out, x_ref, send_ref, dh_ref, a_ref, g_ref, c, sems = rest
    own = Copies(sems)(c_ref.at[ids[MINE]], c.at[pl.ds(0, BLOCK)])
    w_in, w_out = w_in.at[layer], w_out.at[layer]
    move(moves(ids, refs, w_in, w_out))
    ffn_hidden(y_ref[...].astype(BF), w_in, a_ref, g_ref, range(NCB))
    h2 = ffn_result(ids, y_ref[...], a_ref, w_out)
    dh_ref[...] = h2
    x = normed(h2)[0] * gain_ref[layer, 1:2, :]
    x_ref[...] = x[:BLOCK].astype(BF)
    send_ref[...] = x[BLOCK:].astype(BF)
    own.wait()
    c[BLOCK:] = got_ref[...].astype(F32)
    ffn_backward(layer, ids, c[...], dh_ref[...], g_ref, h1[...], gain_ref, w_in, w_out, dh_ref)


def ffn_both_call(seq, layer, w_in, w_out, moves, refs, y, h1, gain, got, c, **extra):
    return seq(
        functools.partial(ffn_both_body, layer, moves, len(refs)),
        [None] + [("v", t) for t in (y, h1, gain, got)] + [("h", c)] + [("v", t) for t in refs],
        [("v", (BLOCK, D), BF), ("v", (BLOCK, D), BF), ("v", (ROWS, D), F32)],
        [(FFN_SHAPE, BF), (FFN_SHAPE, BF), ((ROWS, D), F32)], 1, "ffn_both", fill=[w_in, w_out], **extra)


def ffn_back_body(layer, ids, c_ref, h2, g, h1, gain_ref, w_in, w_out, dh_ref, sems):
    ffn_backward(layer, ids, c_ref[...], h2[...], g, h1[...], gain_ref, w_in.at[layer], w_out.at[layer], dh_ref)


def ffn_back_call(seq, layer, c, h2, g, h1, gain, w_in, w_out, **extra):
    return seq(
        functools.partial(ffn_back_body, layer),
        [None] + [("v", t) for t in (c, h2, g, h1, gain, w_in, w_out)],
        [("v", (ROWS, D), F32)], name="ffn_back", **extra)


def attend_back_body(ids, dh_ref, wo, q, e_ref, factor_ref, ctx_t_ref, keys, values, far_keys, far_values, *rest):
    stores = []
    if len(rest) > 5:
        own_rows, other_rows, dq_ref, own_ref, send_ref, output_ref, dctx_ref, sems = rest
        rest = dq_ref, own_ref, send_ref, dctx_ref
        copy = Copies(sems)
        stores = [copy(own_rows, output_ref.at[ids[MINE]]), copy(other_rows, output_ref.at[1 - ids[MINE]])]
    dq_ref, own_ref, send_ref, dctx_ref = rest[:4]
    dctx_ref[...] = dot_nt(dh_ref[...].astype(BF), wo[...]).astype(BF)
    for pair in range(PAIRS):
        cols = slice(pair * PAIR, (pair + 1) * PAIR)
        vcols = slice(D + pair * PAIR, D + (pair + 1) * PAIR)
        factor = factor_ref[pair:pair + 1, :]
        dctx = split_heads(dctx_ref[:, cols].T).astype(F32)
        ctx = split_heads(ctx_t_ref[cols, :]).astype(F32)
        scaled = dctx * factor
        inner = jnp.sum(scaled * ctx, axis=0, keepdims=True)
        scaled = scaled.astype(BF)
        e = e_ref[pair]
        ds = (e.astype(F32) * (dot(rows_of(values, far_values, cols), scaled) - inner)).astype(BF)
        dv = dot(e, scaled.T)
        dk = dot(ds, stack_heads(q[:, cols])) * SCALE
        own_ref[:, cols] = dk[:ROWS]
        own_ref[:, vcols] = dv[:ROWS]
        send_ref[:, cols] = dk[ROWS:].astype(BF)
        send_ref[:, vcols] = dv[ROWS:].astype(BF)
        dq_t = join_heads(dot(rows_of(keys, far_keys, cols).T, ds)) * SCALE
        dq_ref[:, cols] = dq_t.T.astype(BF)
    for store in stores:
        store.wait()


def attend_back_call(seq, dh, wo, q, kv, weights, output=(), **extra):
    return seq(
        attend_back_body,
        [None] + [("v", t) for t in (dh, wo, q, *weights, *kv, *output)],
        [("v", (ROWS, D), BF), ("v", (ROWS, 2 * D), F32), ("v", (ROWS, 2 * D), BF)]
        + [("h", (2, BLOCK, D), BF)] * (len(output) > 0), [((ROWS, D), BF)], 2, "attention_back", **extra)


def dq_body(layer, dh_ref, dq_ref, lift, inner, wq, up, sd_ref, sb_ref, dx_ref, dub_ref, gd_ref, gb_ref, sems):
    dq = dq_ref[...]
    dqf = dq.astype(F32)
    gb_ref[...] = jnp.sum(dqf * lift[...].astype(F32), axis=0, keepdims=True)
    dpq = dot_nt((sb_ref[layer, 0:1, :] * dqf).astype(BF), up[...])
    gd_ref[...] = jnp.sum(dpq * inner[...].astype(F32), axis=0, keepdims=True)
    dub_ref[...] = sd_ref[layer, 0:1, :] * dpq
    dx_ref[...] = dh_ref[...] + dot_nt(dq, wq[...])


def dq_call(seq, layer, dh, dq, lift, inner, wq, up, sd, sb, **extra):
    return seq(
        functools.partial(dq_body, layer),
        [("v", dh), ("v", dq), ("v", lift), ("v", inner), ("v", wq), ("v", up), ("v", sd), ("v", sb)],
        [("v", (ROWS, D), F32), ("v", (ROWS, RANK), F32), ("v", (1, RANK), F32), ("v", (1, D), F32)],
        name="queries_back", **extra)


def dv_body(layer, dub_ref, own_ref, got_ref, lift, inner, up, sd_ref, sb_ref, gdq_ref, gbq_ref, before_ref,
            dub_out, dk_ref, dv_ref, sums_ref, sems):
    sums_ref[...] = before_ref[...]
    sums_ref[4 * layer:4 * layer + 1, :] = gdq_ref[...]
    sums_ref[4 * layer + 2:4 * layer + 3, :D] = gbq_ref[...]
    dv = (own_ref[:, D:] + got_ref[:, D:].astype(F32)).astype(BF)
    dv_ref[...] = dv
    dk_ref[...] = (own_ref[:, :D] + got_ref[:, :D].astype(F32)).astype(BF)
    dvf = dv.astype(F32)
    sums_ref[4 * layer + 3:4 * layer + 4, :D] = jnp.sum(dvf * lift[...].astype(F32), axis=0, keepdims=True)
    dpv = dot_nt((sb_ref[layer, 1:2, :] * dvf).astype(BF), up[...])
    sums_ref[4 * layer + 1:4 * layer + 2, :] = jnp.sum(dpv * inner[...].astype(F32), axis=0, keepdims=True)
    dub_out[...] = (dub_ref[...] + sd_ref[layer, 1:2, :] * dpv).astype(BF)


def dv_call(seq, layer, dub, own, got, lift, inner, up, sd, sb, gd, gb, before, **extra):
    return seq(
        functools.partial(dv_body, layer),
        [("v", t) for t in (dub, own, got, lift, inner, up, sd, sb, gd, gb, before)],
        [("v", (ROWS, RANK), BF), ("v", (ROWS, D), BF), ("v", (ROWS, D), BF), ("v", (4 * LAYERS, RANK), F32)],
        name="values_back", **extra)


def dx_body(layer, ids, dx_ref, dub_ref, dk_ref, dv_ref, wk, wv, down, *rest):
    total = dx_ref[...] + dot_nt(dub_ref[...], down[...])
    total = total + dot_nt(dv_ref[...], wv[...])
    total = total + dot_nt(dk_ref[...], wk[...])
    if layer == 0:
        send_ref, grad_ref, own, sems = rest
        own[...] = total[:BLOCK]
        store = Copies(sems)(own, grad_ref.at[ids[MINE]])
        send_ref[...] = total[BLOCK:].astype(BF)
        store.wait()
    else:
        rest[0][...] = total


def dx_call(seq, layer, dx, dub, dk, dv, wk, wv, down, **extra):
    return seq(
        functools.partial(dx_body, layer),
        [None] + [("v", t) for t in (dx, dub, dk, dv, wk, wv, down)],
        [("v", (BLOCK, D), BF), ("h", (2, BLOCK, D), F32)] if layer == 0 else [("v", (ROWS, D), F32)],
        [((BLOCK, D), F32)] * (layer == 0), 1, name="input_back", **extra)


def add_call(seq, *terms, **extra):
    def body(*refs):
        total = refs[0][...]
        for ref in refs[1:len(terms)]:
            total = total + ref[...]
        refs[len(terms)][...] = total

    return seq(body, [("v", t) for t in terms], [("v", terms[0].shape, F32)], name="add", **extra)


def finish_call(seq, terms, got, input_grad):
    def body(ids_ref, *refs):
        got_ref, *terms_refs = refs[:1 + len(terms)]
        grad_ref, gd_out, gb_out, wide, gd_ref, gb_ref, sems = refs[1 + len(terms):]
        copy = Copies(sems)
        wide[...] = got_ref[...].astype(F32)
        stores = [copy(wide, grad_ref.at[1 - ids_ref[MINE]])]
        total = terms_refs[0][...]
        for ref in terms_refs[1:]:
            total = total + ref[...]
        for layer in range(LAYERS):
            gd_ref[layer] = total[4 * layer:4 * layer + 2]
            gb_ref[layer] = total[4 * layer + 2:4 * layer + 4, :D]
        stores += [copy(gd_ref, gd_out), copy(gb_ref, gb_out)]
        for store in stores:
            store.wait()

    shapes = [((LAYERS, 2, RANK), F32), ((LAYERS, 2, D), F32)]
    return seq(body, [None, ("v", got)] + [("v", t) for t in terms], [("h", *t) for t in shapes],
               [(got.shape, F32)] + shapes, 3, "finish", fill_hbm=[input_grad])


def prepare_body(ids, x_ref, c_ref, in_ref, out_ref, xs, own, cs, a_in, b_in, own_y, c_send, sems):
    copy = Copies(sems)
    here, core, mine = ids[HERE], ids[CORE], ids[MINE]
    rows = in_ref.shape[1]

    def columns(block):
        return pl.ds(pl.multiple_of(block * CB, CB), CB)

    waits = [copy(c_ref.at[1 - mine], c_send)]
    for layer in range(LAYERS):
        part = pl.ds(layer * rows, rows)
        for q in range(2):
            waits.append(copy(in_ref.at[layer, :, columns(2 * mine + q)], a_in.at[q, part]))
        waits.append(copy(in_ref.at[layer, :, columns(here)], b_in.at[part]))
        waits.append(copy(in_ref.at[layer, :, columns(here)], own_y.at[0, part]))
        waits.append(copy(out_ref.at[layer, core], own_y.at[1 + layer]))
    waits += [copy(x_ref.at[1 - mine], xs), copy(x_ref.at[mine], own)]
    waits[0].wait()
    cs[...] = c_send[...].astype(BF)
    for wait in waits[1:]:
        wait.wait()


def prepare_call(seq, x, c, ffn_in, halves, **extra):
    rows = (BLOCK, D)
    piece = halves.shape[2:]
    return seq(
        prepare_body,
        [None, ("h", x), ("h", c), ("h", ffn_in), ("h", halves)],
        [("v", rows, BF), ("v", rows, BF), ("v", rows, BF), ("v", (2,) + piece, BF), ("v", piece, BF),
         ("v", (3,) + piece, BF)],
        [(rows, F32)], 3 + 5 * LAYERS, "prepare", **extra)


def everywhere(target):
    pairs = []
    for z in range(4):
        for y in range(2):
            for head in range(4):
                z_to, y_to, head_to = target(z, y, head)
                pairs.append(((2 * z + y) * 4 + head, (2 * (z_to % 4) + y_to) * 4 + head_to))
    return pairs


Z_ONE = everywhere(lambda z, y, head: (z + 1 - 2 * (head % 2), y, head))
TWO = everywhere(lambda z, y, head: (z + 2, y, head))
Y_SWAP = [(i, i ^ 1) for i in range(8)]
BOTH_SWAP = everywhere(lambda z, y, head: (z, 1 - y, head ^ 2))
Z_ALL = [everywhere(lambda z, y, head, other=other: (z ^ other, y, head)) for other in (3, 2, 1)]
ACROSS = [(i, i ^ 2) for i in range(4)]
BESIDE = [(i, i ^ 1) for i in range(4)]


def swap(t, pairs):
    return lax.ppermute(t, "head", pairs)


def both_axes(t, pairs):
    return lax.ppermute(t, ("dp", "head"), pairs)


def across_y(t):
    return lax.ppermute(t, "dp", Y_SWAP)


def lay_call(seq, arrays, outs, **extra):
    piece = arrays[0].shape[-2:]

    def length(part):
        return 1 if part is None else part.stop - part.start

    def body(*refs):
        for out, result in zip(outs, refs[len(arrays):], strict=False):
            start = 0
            for index, part in out:
                stop = start + length(part)
                result[start:stop] = refs[index][...][None] if part is None else refs[index][part]
                start = stop

    shapes = [(sum(length(part) for _, part in out),) + piece for out in outs]
    return seq(body, [("v", t) for t in arrays], [("v", shape, BF) for shape in shapes], name="lay", **extra)


def cut_call(seq, cuts):
    cut = cuts.shape[3:]

    def body(ids_ref, cuts_ref, a_ref, b_ref, sems):
        copy = Copies(sems)
        waits = []
        for core, target in ((0, a_ref.at[0]), (1, a_ref.at[1]), (ids_ref[CORE], b_ref)):
            waits.append(copy(cuts_ref.at[1, core, ids_ref[MINE]], target.at[0]))
            waits.append(copy(cuts_ref.at[1, core, pl.ds(2, 2)], target.at[pl.ds(1, 2)]))
        for wait in waits:
            wait.wait()

    return seq(body, [None, ("h", cuts)], [("v", (2, 3) + cut, BF), ("v", (3,) + cut, BF)], [], 6, "cut")


def cut_lay_call(seq, out_a, out_b, in_y_far, out0_y):
    cut = out_b.shape[1:]

    def body_z(a_ref, b_ref, line_ref, sems):
        line_ref[:2] = a_ref[...]
        line_ref[2] = b_ref[...]

    [line] = seq(body_z, [("v", out_a), ("v", out_b)], [("v", (3, 3) + cut, BF)], name="lay")
    return cut_lay_rest_call(seq, line, in_y_far, out0_y)


def cut_lay_rest_call(seq, line, in_y_far, out0_y):
    cut = line.shape[2:]
    piece = out0_y.shape[1:]

    def body(z_ref, far_ref, y_ref, line_ref, own_ref, common_ref, second_ref, sems):
        rows = piece[0] // LAYERS
        line_ref[:, :3] = z_ref[...]
        line_ref[:, 3:] = far_ref[:, rows:].reshape((3, 2) + cut)
        own_ref[...] = z_ref[:, 0]
        common_ref[...] = z_ref[:, 1:]
        second_ref[:, :rows] = far_ref[:, :rows]
        second_ref[:, rows:] = y_ref[...]

    return seq(body, [("v", t) for t in (line, in_y_far, out0_y)],
               [("v", (3, 5) + cut, BF), ("v", (3,) + cut, BF), ("v", (3, 2) + cut, BF),
                ("v", (3, piece[0] // LAYERS + piece[0]) + piece[1:], BF)], name="lay")


def first_lay_call(seq, arrays):
    piece = arrays[0].shape[-2:]
    extra = -(-2 * ROWS // piece[0])

    def body(out0_z, in_z, own_y, in_y, in_far, keys, values, first_ref, sems):
        for start, ref in ((0, in_z), (3, own_y), (6, in_y), (9, in_far), (13, out0_z)):
            first_ref[start:start + ref.shape[0]] = ref[...]
        both = jnp.concatenate([keys[...], values[...]], axis=0)
        for i in range(extra):
            rows = min(piece[0], 2 * ROWS - i * piece[0])
            first_ref[16 + i, :rows] = both[i * piece[0]:i * piece[0] + rows]

    return seq(body, [("v", t) for t in arrays], [("v", (16 + extra,) + piece, BF)], name="lay")


def far_body(first_ref, keys, values, sems):
    rows, count = first_ref.shape[1], first_ref.shape[0] - 16
    both = first_ref[16:].reshape(count * rows, D)
    keys[...] = both[:ROWS]
    values[...] = both[ROWS:2 * ROWS]


def stack_body(first, second, out_ref, sems):
    count = out_ref.shape[1] - 1
    out_ref[:, count] = second[...]
    out_ref[:, :count] = first[...].reshape((out_ref.shape[0], count) + out_ref.shape[2:])


def line_moves(ids, line, side, part, target):
    core, z_near = (ids[CORE], ids[Z_NEAR]) if side == 0 else (ids[OTHER_CORE], ids[Z_BESIDE])
    ref, start = line
    return [(ref.at[pl.ds(start, 2), part], target(z_near, pl.ds(0, 2))),
            (ref.at[start + 2, part], target(ids[Z_TWO], core))]


def in_target(dst, slot, y):
    def target(z, piece):
        return dst.at[pl.ds(slot, 2) if not isinstance(piece, jax.Array) else slot + piece, z, y]

    return target


def own_in(layer, ids, ref, dst):
    columns = [pl.ds(pl.multiple_of(ids[SLOTS + slot] * CB, CB), CB) for slot in range(NCB)]
    return [(ref.at[layer, :, columns[slot]], dst.at[slot, ids[Z], ids[Y]]) for slot in range(NCB)]


def pieces_in(layer, ids, lines, dst):
    part = pl.ds(layer * dst.shape[3], dst.shape[3])
    z, y = ids[Z], (ids[Y], ids[OTHER_Y])
    moves = []
    for side in range(2):
        core = ids[CORE] if side == 0 else ids[OTHER_CORE]
        along, across, own, far = lines[side::2]
        moves += line_moves(ids, along, side, part, in_target(dst, 0, y[0]))
        moves += line_moves(ids, across, side, part, in_target(dst, 0, y[1]))
        moves.append((own[0].at[own[1], part], dst.at[core, z, y[1]]))
        moves += line_moves(ids, far, side, part, in_target(dst, 2, y[0]))
        moves.append((far[0].at[far[1] + 3, part], dst.at[2 + core, z, y[1]]))
    return moves


def out_target(dst, y, cut=None):
    def target(z, piece):
        if not isinstance(piece, jax.Array):
            return dst.at[z, y] if cut is None else dst.at[z, y, :, cut]
        return dst.at[z, y, piece] if cut is None else dst.at[z, y, piece, cut]

    return target


def last_pieces(ids, refs, w_in, w_out):
    rows = pl.ds(0, w_in.shape[4])
    return [pair for side in range(2)
            for pair in line_moves(ids, (refs[side], 0), side, rows, in_target(w_in.at[0], 2, ids[OTHER_Y]))]


def last_pieces_more(ids, refs, w_in, w_out):
    in_y_far, second, out0_y, out1_z = refs
    rows = w_in.shape[4]
    moves = line_moves(ids, (out0_y, 0), 0, slice(None), out_target(w_out.at[0], ids[OTHER_Y]))
    moves += line_moves(ids, (second, 0), 1, pl.ds(rows, second.shape[1] - rows), out_target(w_out.at[0], ids[OTHER_Y]))
    moves += line_moves(ids, (in_y_far, 0), 0, pl.ds(rows, rows), in_target(w_in.at[1], 2, ids[OTHER_Y]))
    return moves + cut_line(ids, out1_z, 0, w_out.at[1])


def cut_line(ids, ref, side, dst):
    x, y = ids[MINE], ids[Y]
    return (line_moves(ids, (ref, 0), side, 0, out_target(dst, y, x))
            + line_moves(ids, (ref, 0), side, pl.ds(1, 2), out_target(dst, y, pl.ds(2, 2))))


def cut_pieces(ids, refs, w_in, w_out):
    core_line, *refs = refs
    x, y = ids[MINE], (ids[Y], ids[OTHER_Y])
    moves = line_moves(ids, (core_line, 0), 1, pl.ds(3, 2), in_target(w_in, 2, y[1])) + cut_line(ids, core_line, 1, w_out)
    for side in range(2):
        for ref, part, place, cut in ((refs[side], 0, y[1], x), (refs[side], 1, y[0], 1 - x),
                                      (refs[2 + side], pl.ds(0, 2), y[1], pl.ds(2, 2)), (refs[2 + side], 2, y[1], 1 - x)):
            moves += line_moves(ids, (ref, 0), side, part, out_target(w_out, place, cut))
    return moves


def nothing(*_):
    return []


def plain_gather(ffn_in, ffn_out):
    whole_in = lax.all_gather(ffn_in, "dp", axis=1, tiled=True)
    whole_out = lax.all_gather(ffn_out, "dp", axis=1, tiled=True)
    return jnp.stack([whole_in[:, :, cb * CB:(cb + 1) * CB] for cb in range(NCB)], axis=1), whole_out.reshape(LAYERS, NCB, CB, D)


def local(block_input, part_lengths, query_weight, key_weight, value_weight, out_weight, down_shared, up_shared,
          scale_d, scale_b, ln_gain, ffn_in, ffn_out, out_grad):
    mine = lax.axis_index("head") // 2
    dp = lax.axis_size("dp")
    seq = Sequence(dp)
    halves = ffn_out.reshape(LAYERS, 2, ffn_out.shape[1] // 2, D)
    scales = (scale_d, scale_b)
    if dp == 8:
        rows_in, piece = ffn_in.shape[1], halves.shape[2:]
        cuts = halves.reshape(LAYERS, 2, 4, piece[0] // 4, D)
        cut = cuts.shape[3:]
        line = [(0, slice(0, 2)), (1, None)]

        xs, own, cs, a_in, b_in, own_y = prepare_call(seq, block_input, out_grad, ffn_in, halves)
        in_a, in_b = both_axes(a_in, Z_ONE), both_axes(b_in, TWO)
        got, c_got, own_y = swap(xs, ACROSS), swap(cs, ACROSS), across_y(own_y)
        wk0, wv0, down, up, a_out, b_out = seq(
            None, [None], [], name="fetch",
            fetch=[(key_weight, 0), (value_weight, 0), (down_shared, None), (up_shared, None),
                   (halves, 0), (halves, ((lambda ids_ref: (0, ids_ref[CORE])), piece))])
        keys, values, inner0, lift_v0, xb, wq0, c_got = kv_call(
            seq, 0, own, got, wk0, wv0, down, up, *scales, fetch=[(query_weight, 0)], through=[c_got])
        q0, qt, lift_q0, wo0 = q_call(seq, 0, xb, inner0, wq0, up, *scales, fetch=[(out_weight, 0)])
        in_z, in_x = lay_call(seq, [in_a, in_b, own_y], [line, line + [(2, slice(0, 1))]])
        out_a, out_b = both_axes(a_out, Z_ONE), both_axes(b_out, TWO)
        in_y, in_far = across_y(in_z), swap(in_x, ACROSS)
        a_out, b_out = cut_call(seq, cuts)
        [out0_z] = lay_call(seq, [out_a, out_b], [line])
        [first] = first_lay_call(seq, [out0_z, in_z, own_y, in_y, in_far, keys, values])
        out_a, out_b = both_axes(a_out, Z_ONE), both_axes(b_out, TWO)
        out0_y, in_y_far, first = across_y(out0_z), swap(in_y, ACROSS), swap(first, BESIDE)
        kv = (keys, values, *seq(far_body, [("v", first)], [("v", (ROWS, D), BF)] * 2, name="far"))
        y, h10, *p0 = attend_call(seq, 0, part_lengths, xb, qt, kv, wo0, ln_gain)
        stored0 = (kv, q0, inner0, lift_q0, lift_v0, h10, p0, wk0, wv0, wq0, wo0)
        w_in, w_out, a, g0, wk, wv, wq, wo = seq(
            ffn_first_body,
            [None, ("v", y), ("h", ffn_in), ("h", cuts)]
            + [("v", t) for t in (in_z, in_y, in_far, own_y, first, out0_z)],
            [("v", (LAYERS, NCB, 4, 2, rows_in, CB), BF), ("v", (LAYERS, NCB, 2, 2, 4) + cut, BF)]
            + [("v", FFN_SHAPE, BF)] * 2, [], 2 * NCB + 2, "ffn_first",
            fetch=[(t, 1) for t in (key_weight, value_weight, query_weight, out_weight)])
        out1_z, out1_own, out1_common, second = cut_lay_call(seq, out_a, out_b, in_y_far, out0_y)
        out1_own_y, out1_own_x, out1_common_y = across_y(out1_own), swap(out1_own, ACROSS), across_y(out1_common)
        second, out1_z_core = swap(second, BESIDE), swap(out1_z, BESIDE)
        x, h20, w_in, w_out, a, g0 = ffn_second_call(
            seq, 0, range(NCB // 2, NCB), (last_pieces, last_pieces_more), [in_y_far, second, out0_y, out1_z],
            y, ln_gain, w_in, w_out, a, g0)
        [third] = seq(stack_body, [("v", out1_own_y), ("v", out1_own_x)], [("v", (3, 2) + cut, BF)], name="lay")
        out1_own_yx, third_core = swap(out1_own_y, ACROSS), swap(third, BESIDE)
        keys, values, inner, lift_v, xb, out1_z_core = kv_call(
            seq, 1, x, got, wk, wv, down, up, *scales, through=[out1_z_core])
        kv = (keys, values, swap(keys, BESIDE), swap(values, BESIDE))
        q, qt, lift_q = q_call(seq, 1, xb, inner, wq, up, *scales)
        y, h1, *p = attend_call(seq, 1, part_lengths, x, qt, kv, wo, ln_gain)
        last, third_core = seq(stack_body, [("v", out1_common_y), ("v", out1_own_yx)], [("v", (3, 3) + cut, BF)], name="lay",
                               through=[third_core])
        moves, refs = cut_pieces, [out1_z_core, third, third_core, last, swap(last, BESIDE)]
    else:
        def pick(t, index):
            return lax.dynamic_index_in_dim(t, index, 0, keepdims=False)

        x, got = pick(block_input, mine), swap(pick(block_input, 1 - mine), ACROSS)
        c_got = swap(pick(out_grad, 1 - mine).astype(BF), ACROSS)
        blocks_in, blocks_out = plain_gather(ffn_in, ffn_out)
        for layer in range(LAYERS):
            wk, wv, down, up, wq, wo = seq(
                None, [], [], name="fetch",
                fetch=[(key_weight, layer), (value_weight, layer), (down_shared, None), (up_shared, None),
                       (query_weight, layer), (out_weight, layer)])
            keys, values, inner, lift_v, xb = kv_call(seq, layer, x, got, wk, wv, down, up, *scales)
            kv = (keys, values, swap(keys, BESIDE), swap(values, BESIDE))
            q, qt, lift_q = q_call(seq, layer, xb, inner, wq, up, *scales)
            y, h1, *p = attend_call(
                seq, layer, part_lengths, xb if layer == 0 else x, qt, kv, wo, ln_gain)
            if layer == 0:
                a, g0 = seq(None, [], [("v", FFN_SHAPE, BF)] * 2)
                w_in, w_out = seq(None, [], [], name="fetch", fetch=[(blocks_in, None), (blocks_out, None)])
                x, h20, w_in, w_out, a, g0 = ffn_second_call(
                    seq, 0, range(NCB), (nothing, nothing), [], y, ln_gain, w_in, w_out, a, g0)
                stored0 = (kv, q, inner, lift_q, lift_v, h1, p, wk, wv, wq, wo)
        moves, refs = nothing, []
    output, send, dh, w_in, w_out = ffn_both_call(seq, 1, w_in, w_out, moves, refs, y, h1, ln_gain, c_got, out_grad)
    other_output = swap(send, ACROSS)
    dq, own, send = attend_back_call(seq, dh, wo, q, kv, p)
    got = swap(send, BESIDE)
    dx, dub, gd_q, gb_q = dq_call(seq, 1, dh, dq, lift_q, inner, wq, up, *scales)
    dub, dk, dv, sums = dv_call(
        seq, 1, dub, own, got, lift_v, inner, up, *scales, gd_q, gb_q, jnp.zeros((4 * LAYERS, RANK), F32))
    [cotangent] = dx_call(seq, 1, dx, dub, dk, dv, wk, wv, down)
    kv, q, inner, lift_q, lift_v, h1, p, wk, wv, wq, wo = stored0
    [dh] = ffn_back_call(seq, 0, cotangent, h20, g0, h1, ln_gain, w_in, w_out)
    dq, own, send, block_output = attend_back_call(seq, dh, wo, q, kv, p, (output, other_output))
    got = swap(send, BESIDE)
    dx, dub, gd_q, gb_q = dq_call(seq, 0, dh, dq, lift_q, inner, wq, up, *scales)
    dub, dk, dv, sums = dv_call(seq, 0, dub, own, got, lift_v, inner, up, *scales, gd_q, gb_q, sums)
    if dp == 8:
        [sums] = add_call(seq, sums, swap(sums, BESIDE))
        parts = [both_axes(sums, BOTH_SWAP), swap(sums, ACROSS), across_y(sums)]
        last_rows, input_grad = dx_call(seq, 0, dx, dub, dk, dv, wk, wv, down)
        sums, last_rows = add_call(seq, sums, *parts, through=[last_rows])
        got = swap(last_rows, ACROSS)
        parts = [both_axes(sums, along) for along in Z_ALL]
    else:
        last_rows, input_grad = dx_call(seq, 0, dx, dub, dk, dv, wk, wv, down)
        got = swap(last_rows, ACROSS)
        sums, parts = lax.psum(sums, ("dp", "head")), []
    grad_d, grad_b, input_grad = finish_call(seq, [sums, *parts], got, input_grad)
    return block_output, input_grad, grad_d, grad_b


def solution(mesh):
    both = P(None, ("dp", "head"), None)
    in_specs = (both, P(None, "dp", None), P(), P(), P(), P(), P(), P(), P(), P(), P(),
                P(None, "dp", None), P(None, "dp", None), both)
    out_specs = (both, both, P(), P())
    return jax.shard_map(local, mesh=mesh, in_specs=in_specs, out_specs=out_specs, check_vma=False)
```

```python
import functools

import jax
import jax.numpy as jnp
from jax import lax
from jax.experimental import pallas as pl
from jax.experimental.pallas import tpu as pltpu
from jax.sharding import PartitionSpec as P

D = 768
HEADS = 12
HEAD_DIM = 64
FF = 3072
RANK = 1024
LEN = 512
LAYERS = 2
PAIRS = HEADS // 2
PAIR = 2 * HEAD_DIM
BLOCK = LEN // 4
ROWS = 2 * BLOCK
CB = D
NCB = FF // CB
SCALE = HEAD_DIM ** (-0.5)
BF = jnp.bfloat16
F32 = jnp.float32
MIB = 1 << 20

COLOURS = {"v": pltpu.VMEM, "h": pltpu.HBM}
SPACES = {
    "v": pl.BlockSpec(memory_space=pltpu.VMEM),
    "h": pl.BlockSpec(memory_space=pltpu.HBM),
    "s": pl.BlockSpec(memory_space=pltpu.SMEM),
    "a": pl.BlockSpec(memory_space=pl.ANY),
}


HERE, CORE, MINE, Z, Y, OTHER_Y, Z_TWO, Z_NEAR, Z_BESIDE, OTHER_CORE = range(10)
SLOTS, BLOCKS = 10, 14


def indices(dp):
    here, place = lax.axis_index("head"), lax.axis_index("dp")
    mine, core = lax.div(here, 2), lax.rem(here, 2)
    z, y = lax.div(place, 2), lax.rem(place, 2)
    line = [z, y, 1 - y] + [lax.rem(z + step, 4) for step in (2, 3 + 2 * core, 1 + 2 * core)]
    blocks = [here, here ^ 2, here ^ 1, here ^ 3]
    if dp == 8:
        slots = [2 * mine, 2 * mine + 1, 2 - 2 * mine, 3 - 2 * mine]
    else:
        slots = list(range(NCB))
    return [here, core, mine] + line + [1 - core] + slots + blocks


def dot(left, right):
    return jnp.dot(left, right, preferred_element_type=F32)


def dot_nt(left, right):
    return lax.dot_general(left, right, (((1,), (1,)), ((), ())), preferred_element_type=F32)


def normed(t):
    centred = t - jnp.mean(t, axis=-1, keepdims=True)
    inverse = lax.rsqrt(jnp.mean(centred * centred, axis=-1, keepdims=True) + 1e-05)
    return centred * inverse, inverse


def norm_back(t, gain, cotangent):
    unit, inverse = normed(t)
    scaled = cotangent * gain
    mean_e = jnp.mean(scaled, axis=-1, keepdims=True)
    mean_en = jnp.mean(scaled * unit, axis=-1, keepdims=True)
    return inverse * (scaled - mean_e - unit * mean_en)


class Copies:
    def __init__(self, sems, first=0):
        self.sems, self.count = sems, first

    def __call__(self, src, dst):
        copy = pltpu.make_async_copy(src, dst, self.sems.at[self.count])
        self.count += 1
        copy.start()
        return copy


class Sequence:
    def __init__(self, dp):
        self.dp, self.token = dp, None

    def __call__(self, body, ins, outs, scratch=(), copies=0, name="keep", fetch=(), fill=(), fill_hbm=(), through=(), limit=8, save=(), cost=0.001):
        handed = [pltpu.with_memory_space_constraint(t, pltpu.VMEM) for t in fill]
        handed += [pltpu.with_memory_space_constraint(t, pltpu.HBM) for t in fill_hbm]
        handed += list(through)
        if self.token is not None:
            handed.append(pltpu.with_memory_space_constraint(self.token, pltpu.HBM))
        fetched = [(t.shape if part is None else t.shape[1:] if isinstance(part, int) else part[1], t.dtype)
                   for t, part in fetch]
        wants = [i for i, entry in enumerate(ins) if entry is None]
        ins = [entry for entry in ins if entry is not None]
        n_in, n_fetch, n_hand, n_fill = len(ins), len(fetch), len(handed), len(fill) + len(fill_hbm)
        n_out, n_save = len(outs), len(save)
        first = self.token is None

        def whole(*refs):
            refs = list(refs)
            in_refs, fetch_refs = refs[:n_in], refs[n_in:n_in + n_fetch]
            for i in wants:
                in_refs.insert(i, indices(self.dp))
            refs = refs[n_in + n_fetch:]
            refs = refs[n_hand:]
            out_refs, fetch_outs = refs[:n_out], refs[n_out:n_out + n_fetch]
            refs = refs[n_out + n_fetch:]
            fill_refs = refs[:n_fill]
            save_refs = refs[n_hand + first:][:n_save]
            refs = refs[n_hand + first + n_save:]
            scratch_refs, sems = refs[:len(scratch)], refs[len(scratch)]
            copy = Copies(sems, copies)
            waits = []
            for (_, part), source, target in zip(fetch, fetch_refs, fetch_outs, strict=True):
                if part is not None:
                    source = source.at[part if isinstance(part, int) else part[0](in_refs[0])]
                waits.append(copy(source, target))
            for place, target in zip(save, save_refs, strict=True):
                waits.append(copy(in_refs[place], target))
            if body is not None:
                body(*in_refs, *fill_refs, *out_refs, *scratch_refs, sems)
            for wait in waits:
                wait.wait()

        shapes = [COLOURS[space](shape, dtype) for space, shape, dtype in outs]
        shapes += [pltpu.VMEM(shape, dtype) for shape, dtype in fetched]
        shapes += [pltpu.VMEM(t.shape, t.dtype) for t in fill] + [pltpu.HBM(t.shape, t.dtype) for t in fill_hbm]
        shapes += [jax.ShapeDtypeStruct(t.shape, t.dtype) for t in through]
        shapes += [pltpu.HBM((8, 128), F32)]
        shapes += [pltpu.HBM(ins[place][1].shape, ins[place][1].dtype) for place in save]
        results = pl.pallas_call(
            whole,
            out_shape=tuple(shapes),
            in_specs=[SPACES[space] for space, _ in ins] + [SPACES["h"]] * n_fetch + [SPACES["v"]] * len(fill)
            + [SPACES["h"]] * len(fill_hbm) + [SPACES["a"]] * (n_hand - n_fill),
            out_specs=tuple([SPACES[space] for space, _, _ in outs] + [SPACES["v"]] * (n_fetch + len(fill))
                            + [SPACES["h"]] * len(fill_hbm) + [SPACES["a"]] * (n_hand - n_fill + first) + [SPACES["h"]] * n_save),
            scratch_shapes=[pltpu.VMEM(shape, dtype) for shape, dtype in scratch]
            + [pltpu.SemaphoreType.DMA((copies + n_fetch + n_save + 1,))],
            input_output_aliases={n_in + n_fetch + i: n_out + n_fetch + i for i in range(n_hand)},
            compiler_params=pltpu.CompilerParams(vmem_limit_bytes=limit * MIB),
            cost_estimate=pl.CostEstimate(
                flops=int(cost * 1e9), bytes_accessed=int(cost * 3e6), transcendentals=0),
            name=name,
        )(*[pltpu.with_memory_space_constraint(t, COLOURS[space]) if space in COLOURS else t for space, t in ins],
          *[pltpu.with_memory_space_constraint(t, pltpu.HBM) for t, _ in fetch],
          *handed)
        results = list(results)
        split = n_out + n_fetch + n_fill + len(through)
        self.token = results[split]
        return results[:split] + results[split + 1:]


def kv_body(layer, x_ref, got_ref, wk, wv, down, up, sd_ref, sb_ref, *rest):
    keys, values, inner_out, lift_out, xb_ref, _ = rest
    if layer == 0:
        xb_ref[:BLOCK] = x_ref[...]
        xb_ref[BLOCK:] = got_ref[0]
    else:
        xb_ref[...] = x_ref[...].astype(BF)
    xb = xb_ref[...]
    inner = dot(xb, down[...])
    inner_out[...] = inner.astype(BF)
    lift = dot((sd_ref[layer, 1:2, :] * inner).astype(BF), up[...])
    lift_out[...] = lift.astype(BF)
    values[...] = (dot(xb, wv[...]) + sb_ref[layer, 1:2, :] * lift).astype(BF)
    keys[...] = dot(xb, wk[...]).astype(BF)


def kv_call(seq, layer, x, got, wk, wv, down, up, sd, sb, **extra):
    return seq(
        functools.partial(kv_body, layer),
        [("v", t) for t in (x, got, wk, wv, down, up, sd, sb)],
        [("v", (ROWS, D), BF)] * 2 + [("v", (ROWS, RANK), BF), ("v", (ROWS, D), BF), ("v", (ROWS, D), BF)],
        name="keys_values", **extra)


def q_body(layer, x_ref, inner, wq, up, sd_ref, sb_ref, q_ref, qt_ref, lift_out, sems):
    lift = dot((sd_ref[layer, 0:1, :] * inner[...].astype(F32)).astype(BF), up[...])
    lift_out[...] = lift.astype(BF)
    q = (dot(x_ref[...], wq[...]) + sb_ref[layer, 0:1, :] * lift).astype(BF)
    q_ref[...] = q
    qt_ref[...] = (q * SCALE).T


def q_call(seq, layer, x, inner, wq, up, sd, sb, **extra):
    return seq(
        functools.partial(q_body, layer),
        [("v", x), ("v", inner), ("v", wq), ("v", up), ("v", sd), ("v", sb)],
        [("v", (ROWS, D), BF), ("v", (D, ROWS), BF), ("v", (ROWS, D), BF)],
        name="queries", **extra)


def split_heads(t):
    zero = jnp.zeros((HEAD_DIM, t.shape[1]), t.dtype)
    first = jnp.concatenate([t[:HEAD_DIM], zero], axis=0)
    second = jnp.concatenate([zero, t[HEAD_DIM:]], axis=0)
    return jnp.concatenate([first, second], axis=1)


def join_heads(t):
    n = t.shape[1] // 2
    return jnp.concatenate([t[:HEAD_DIM, :n], t[HEAD_DIM:, n:]], axis=0)


def stack_heads(t):
    lane = lax.broadcasted_iota(jnp.int32, (1, PAIR), 1)
    first = (lane < HEAD_DIM).astype(F32).astype(BF)
    second = (lane >= HEAD_DIM).astype(F32).astype(BF)
    return jnp.concatenate([t * first, t * second], axis=0)


def rows_of(near, far, cols):
    return jnp.concatenate([near[:, cols], far[:, cols]], axis=0)


def attend_body(layer, ids, lengths, x_ref, qt_ref, wo, gain_ref, keys, values, far_keys, far_values,
                y_ref, h_ref, e_ref, factor_ref, ctx_t_ref, ctx, sems):
    row = lax.broadcasted_iota(jnp.int32, (BLOCK, 2 * ROWS), 0)
    counts = lengths[ids[MINE]]
    live = counts[:, :1] + counts[:, 1:] + 4
    limits = [live - BLOCK * ids[BLOCKS + b] for b in range(4)]
    for pair in range(PAIRS):
        cols = slice(pair * PAIR, (pair + 1) * PAIR)
        raw = dot(rows_of(keys, far_keys, cols), split_heads(qt_ref[cols, :]))
        scores = jnp.concatenate(
            [jnp.where(row < limits[b], raw[b * BLOCK:(b + 1) * BLOCK], -1000000000.0) for b in range(4)],
            axis=0,
        )
        grown = jnp.exp(scores - jnp.max(scores, axis=0, keepdims=True))
        factor = 1.0 / jnp.sum(grown, axis=0, keepdims=True)
        factor_ref[pair:pair + 1, :] = factor
        e_ref[pair] = grown.astype(BF)
        ctx_t = join_heads(dot(rows_of(values, far_values, cols).T, e_ref[pair]) * factor)
        ctx_t_ref[cols, :] = ctx_t
        ctx[:, cols] = ctx_t.astype(BF).T
    h = x_ref[...].astype(F32) + dot(ctx[...], wo[...])
    h_ref[...] = h
    y_ref[...] = normed(h)[0] * gain_ref[layer, 0:1, :]


def attend_call(seq, layer, lengths, x, qt, kv, wo, gain, **extra):
    return seq(
        functools.partial(attend_body, layer),
        [None] + [("v", t) for t in (lengths, x, qt, wo, gain, *kv)],
        [("v", (ROWS, D), F32), ("v", (ROWS, D), F32), ("v", (PAIRS, LEN, 2 * ROWS), BF), ("v", (PAIRS, 2 * ROWS), F32),
         ("v", (D, ROWS), F32)],
        [((ROWS, D), BF)], name="attention", **extra)


def move(pairs):
    for source, target in pairs:
        target[...] = source[...].reshape(target.shape)


def ffn_hidden(yb, w_in, a_ref, g_ref, slots):
    for slot in slots:
        z = dot(yb, w_in[slot].reshape(D, CB))
        cdf = 0.5 * (1.0 + lax.erf(z * (0.5 ** 0.5)))
        g_ref[slot] = (cdf + z * (jnp.exp(-0.5 * z * z) * 0.3989422804014327)).astype(BF)
        a_ref[slot] = (z * cdf).astype(BF)


def ffn_result(ids, total, a_ref, w_out):
    for slot in range(NCB):
        total = total + dot(a_ref[slot], w_out[ids[SLOTS + slot]].reshape(CB, D))
    return total


def ffn_backward(layer, ids, c, h2, g_ref, h1, gain_ref, w_in, w_out, dh_ref):
    dh2 = norm_back(h2, gain_ref[layer, 1:2, :], c)
    dfb = dh2.astype(BF)
    total = dh2
    for slot in range(NCB):
        da = dot_nt(dfb, w_out[ids[SLOTS + slot]].reshape(CB, D))
        dz = (g_ref[slot].astype(F32) * da).astype(BF)
        total = total + dot_nt(dz, w_in[slot].reshape(D, CB))
    dh1 = norm_back(h1, gain_ref[layer, 0:1, :], total)
    dh_ref[...] = dh1


FFN_SHAPE = (NCB, ROWS, CB)


def ffn_first_body(ids, y_ref, in_ref, cut_ref, in_z, in_y, in_far, own_y, first, out0_z,
                   w_in, w_out, a_ref, g_ref, sems):
    copy = Copies(sems)
    w_in = [w_in.at[layer] for layer in range(LAYERS)]
    w_out = [w_out.at[layer] for layer in range(LAYERS)]
    owns = [[copy(source, target) for source, target in own_in(layer, ids, in_ref, w_in[layer])] for layer in range(LAYERS)]
    own_out = [copy(cut_ref.at[layer], w_out[layer].at[ids[Z], ids[Y]]) for layer in range(LAYERS)]
    lines = [(in_z, 0), (first, 0), (in_y, 0), (first, 6), (own_y, 0), (first, 3), (in_far, 0), (first, 9)]
    move(pieces_in(0, ids, lines, w_in[0]))
    for wait in owns[0]:
        wait.wait()
    ffn_hidden(y_ref[...].astype(BF), w_in[0], a_ref, g_ref, range(NCB // 2))
    move(pieces_in(1, ids, lines, w_in[1]))
    for side, line in enumerate([(out0_z, 0), (first, 13)]):
        move(line_moves(ids, line, side, slice(None), out_target(w_out[0], ids[Y])))
    for side, (ref, start) in enumerate([(own_y, 0), (first, 3)]):
        core = ids[CORE] if side == 0 else ids[OTHER_CORE]
        for layer in range(LAYERS):
            move([(ref.at[start + 1 + layer], w_out[layer].at[ids[Z], ids[OTHER_Y], core])])
    for wait in owns[1] + own_out:
        wait.wait()


def ffn_second_body(layer, slots, moves, n_refs, ids, y_ref, gain_ref, *rest):
    refs, rest = rest[:n_refs], rest[n_refs:]
    w_in, w_out, a_ref, g_ref, x_ref, h_ref, _ = rest
    move(moves[0](ids, refs, w_in, w_out))
    ffn_hidden(y_ref[...].astype(BF), w_in.at[layer], a_ref, g_ref, slots)
    move(moves[1](ids, refs, w_in, w_out))
    h_ref[...] = ffn_result(ids, y_ref[...], a_ref, w_out.at[layer])
    x_ref[...] = normed(h_ref[...])[0] * gain_ref[layer, 1:2, :]


def ffn_second_call(seq, layer, slots, moves, refs, y, gain, w_in, w_out, a, g, **extra):
    return seq(
        functools.partial(ffn_second_body, layer, slots, moves, len(refs)),
        [None, ("v", y), ("v", gain)] + [("v", t) for t in refs],
        [("v", (ROWS, D), F32), ("v", (ROWS, D), F32)], name="ffn", fill=[w_in, w_out, a, g], **extra)


FFN_SHAPE = (NCB, ROWS, CB)


def ffn_hidden_body(layer, moves, n_refs, ids, y_ref, *rest):
    refs, (w_in, a_ref, g_ref, _) = rest[:n_refs], rest[n_refs:]
    move(moves(ids, refs, w_in.at[layer]))
    ffn_hidden(y_ref[...].astype(BF), w_in.at[layer], a_ref, g_ref, range(NCB))


def ffn_hidden_call(seq, layer, w_in, moves, refs, y, **extra):
    return seq(
        functools.partial(ffn_hidden_body, layer, moves, len(refs)),
        [None, ("v", y)] + [("v", t) for t in refs], [("v", FFN_SHAPE, BF)] * 2, name="ffn_hidden", fill=[w_in], **extra)


def ffn_both_body(layer, moves, n_refs, ids, y_ref, h1, gain_ref, got_ref, w_in, a_ref, g_ref, c_ref, *rest):
    refs, rest = rest[:n_refs], rest[n_refs:]
    w_out, x_ref, send_ref, dh_ref, c, sems = rest
    own = Copies(sems)(c_ref.at[ids[MINE]], c.at[pl.ds(0, BLOCK)])
    w_in, w_out = w_in.at[layer], w_out.at[layer]
    move(moves(ids, refs, w_out))
    h2 = ffn_result(ids, y_ref[...], a_ref, w_out)
    dh_ref[...] = h2
    x = normed(h2)[0] * gain_ref[layer, 1:2, :]
    x_ref[...] = x[:BLOCK].astype(BF)
    send_ref[...] = x[BLOCK:].astype(BF)
    own.wait()
    c[BLOCK:] = got_ref[1].astype(F32)
    ffn_backward(layer, ids, c[...], dh_ref[...], g_ref, h1[...], gain_ref, w_in, w_out, dh_ref)


def ffn_both_call(seq, layer, w_in, w_out, a, g, moves, refs, y, h1, gain, got, c, **extra):
    return seq(
        functools.partial(ffn_both_body, layer, moves, len(refs)),
        [None] + [("v", t) for t in (y, h1, gain, got, w_in, a, g)] + [("h", c)] + [("v", t) for t in refs],
        [("v", (BLOCK, D), BF), ("v", (BLOCK, D), BF), ("v", (ROWS, D), F32)],
        [((ROWS, D), F32)], 1, "ffn_both", fill=[w_out], **extra)


def ffn_back_body(layer, ids, c_ref, h2, g, h1, gain_ref, w_in, w_out, dh_ref, sems):
    ffn_backward(layer, ids, c_ref[...], h2[...], g, h1[...], gain_ref, w_in.at[layer], w_out.at[layer], dh_ref)


def ffn_back_call(seq, layer, c, h2, g, h1, gain, w_in, w_out, **extra):
    return seq(
        functools.partial(ffn_back_body, layer),
        [None] + [("v", t) for t in (c, h2, g, h1, gain, w_in, w_out)],
        [("v", (ROWS, D), F32)], name="ffn_back", **extra)


def attend_back_body(ids, dh_ref, wo, q, e_ref, factor_ref, ctx_t_ref, keys, values, far_keys, far_values, *rest):
    stores = []
    if len(rest) > 5:
        own_rows, other_rows, dq_ref, own_ref, send_ref, output_ref, dctx_ref, sems = rest
        rest = dq_ref, own_ref, send_ref, dctx_ref
        copy = Copies(sems)
        stores = [copy(own_rows, output_ref.at[ids[MINE]]), copy(other_rows, output_ref.at[1 - ids[MINE]])]
    dq_ref, own_ref, send_ref, dctx_ref = rest[:4]
    dctx_ref[...] = dot_nt(dh_ref[...].astype(BF), wo[...]).astype(BF)
    for pair in range(PAIRS):
        cols = slice(pair * PAIR, (pair + 1) * PAIR)
        vcols = slice(D + pair * PAIR, D + (pair + 1) * PAIR)
        factor = factor_ref[pair:pair + 1, :]
        scaled = (split_heads(dctx_ref[:, cols].T).astype(F32) * factor).astype(BF)
        inner = jnp.sum(scaled.astype(F32) * split_heads(ctx_t_ref[cols, :]), axis=0, keepdims=True)
        e = e_ref[pair]
        ds = (e.astype(F32) * (dot(rows_of(values, far_values, cols), scaled) - inner)).astype(BF)
        dv = dot(e, scaled.T)
        dk = dot(ds, stack_heads(q[:, cols])) * SCALE
        own_ref[:, cols] = dk[:ROWS]
        own_ref[:, vcols] = dv[:ROWS]
        send_ref[:, cols] = dk[ROWS:].astype(BF)
        send_ref[:, vcols] = dv[ROWS:].astype(BF)
        dq_t = join_heads(dot(rows_of(keys, far_keys, cols).T, ds)) * SCALE
        dq_ref[:, cols] = dq_t.T.astype(BF)
    for store in stores:
        store.wait()


def attend_back_call(seq, dh, wo, q, kv, weights, output=(), **extra):
    return seq(
        attend_back_body,
        [None] + [("v", t) for t in (dh, wo, q, *weights, *kv, *output)],
        [("v", (ROWS, D), BF), ("v", (ROWS, 2 * D), F32), ("v", (ROWS, 2 * D), BF)]
        + [("h", (2, BLOCK, D), BF)] * (len(output) > 0), [((ROWS, D), BF)], 2, "attention_back", **extra)


def dq_body(layer, dh_ref, dq_ref, lift, inner, wq, up, sd_ref, sb_ref, dx_ref, dub_ref, gd_ref, gb_ref, sems):
    dq = dq_ref[...]
    dqf = dq.astype(F32)
    gb_ref[...] = jnp.sum(dqf * lift[...].astype(F32), axis=0, keepdims=True)
    dpq = dot_nt((sb_ref[layer, 0:1, :] * dqf).astype(BF), up[...])
    gd_ref[...] = jnp.sum(dpq * inner[...].astype(F32), axis=0, keepdims=True)
    dub_ref[...] = sd_ref[layer, 0:1, :] * dpq
    dx_ref[...] = dh_ref[...] + dot_nt(dq, wq[...])


def dq_call(seq, layer, dh, dq, lift, inner, wq, up, sd, sb, **extra):
    return seq(
        functools.partial(dq_body, layer),
        [("v", dh), ("v", dq), ("v", lift), ("v", inner), ("v", wq), ("v", up), ("v", sd), ("v", sb)],
        [("v", (ROWS, D), F32), ("v", (ROWS, RANK), F32), ("v", (1, RANK), F32), ("v", (1, D), F32)],
        name="queries_back", **extra)


def dv_body(layer, dub_ref, own_ref, got_ref, lift, inner, up, sd_ref, sb_ref, gdq_ref, gbq_ref, before_ref,
            dub_out, dk_ref, dv_ref, sums_ref, sems):
    sums_ref[...] = before_ref[...]
    sums_ref[4 * layer:4 * layer + 1, :] = gdq_ref[...]
    sums_ref[4 * layer + 2:4 * layer + 3, :D] = gbq_ref[...]
    dv = (own_ref[:, D:] + got_ref[:, D:].astype(F32)).astype(BF)
    dv_ref[...] = dv
    dk_ref[...] = (own_ref[:, :D] + got_ref[:, :D].astype(F32)).astype(BF)
    dvf = dv.astype(F32)
    sums_ref[4 * layer + 3:4 * layer + 4, :D] = jnp.sum(dvf * lift[...].astype(F32), axis=0, keepdims=True)
    dpv = dot_nt((sb_ref[layer, 1:2, :] * dvf).astype(BF), up[...])
    sums_ref[4 * layer + 1:4 * layer + 2, :] = jnp.sum(dpv * inner[...].astype(F32), axis=0, keepdims=True)
    dub_out[...] = (dub_ref[...] + sd_ref[layer, 1:2, :] * dpv).astype(BF)


def dv_call(seq, layer, dub, own, got, lift, inner, up, sd, sb, gd, gb, before, **extra):
    return seq(
        functools.partial(dv_body, layer),
        [("v", t) for t in (dub, own, got, lift, inner, up, sd, sb, gd, gb, before)],
        [("v", (ROWS, RANK), BF), ("v", (ROWS, D), BF), ("v", (ROWS, D), BF), ("v", (4 * LAYERS, RANK), F32)],
        name="values_back", **extra)


def dx_body(layer, ids, dx_ref, dub_ref, dk_ref, dv_ref, wk, wv, down, *rest):
    total = dx_ref[...] + dot_nt(dub_ref[...], down[...])
    total = total + dot_nt(dv_ref[...], wv[...])
    total = total + dot_nt(dk_ref[...], wk[...])
    if layer == 0:
        send_ref, grad_ref, own, sems = rest
        own[...] = total[:BLOCK]
        store = Copies(sems)(own, grad_ref.at[ids[MINE]])
        send_ref[...] = total[BLOCK:].astype(BF)
        store.wait()
    else:
        rest[0][...] = total


def dx_call(seq, layer, dx, dub, dk, dv, wk, wv, down, **extra):
    return seq(
        functools.partial(dx_body, layer),
        [None] + [("v", t) for t in (dx, dub, dk, dv, wk, wv, down)],
        [("v", (BLOCK, D), BF), ("h", (2, BLOCK, D), F32)] if layer == 0 else [("v", (ROWS, D), F32)],
        [((BLOCK, D), F32)] * (layer == 0), 1, name="input_back", **extra)


def add_call(seq, *terms, **extra):
    def body(*refs):
        total = refs[0][...]
        for ref in refs[1:len(terms)]:
            total = total + ref[...]
        refs[len(terms)][...] = total

    return seq(body, [("v", t) for t in terms], [("v", terms[0].shape, F32)], name="add", **extra)


def finish_call(seq, terms, got, input_grad):
    def body(ids_ref, *refs):
        got_ref, *terms_refs = refs[:1 + len(terms)]
        grad_ref, gd_out, gb_out, wide, gd_ref, gb_ref, sems = refs[1 + len(terms):]
        copy = Copies(sems)
        wide[...] = got_ref[...].astype(F32)
        stores = [copy(wide, grad_ref.at[1 - ids_ref[MINE]])]
        total = terms_refs[0][...]
        for ref in terms_refs[1:]:
            total = total + ref[...]
        for layer in range(LAYERS):
            gd_ref[layer] = total[4 * layer:4 * layer + 2]
            gb_ref[layer] = total[4 * layer + 2:4 * layer + 4, :D]
        stores += [copy(gd_ref, gd_out), copy(gb_ref, gb_out)]
        for store in stores:
            store.wait()

    shapes = [((LAYERS, 2, RANK), F32), ((LAYERS, 2, D), F32)]
    return seq(body, [None, ("v", got)] + [("v", t) for t in terms], [("h", *t) for t in shapes],
               [(got.shape, F32)] + shapes, 3, "finish", fill_hbm=[input_grad])


def prepare_body(ids, x_ref, c_ref, in_ref, out_ref, own, sent, a_in, b_in, own_a, own_b, c_send, sems):
    copy = Copies(sems)
    here, core, mine = ids[HERE], ids[CORE], ids[MINE]
    rows = in_ref.shape[1]

    def columns(block):
        return pl.ds(pl.multiple_of(block * CB, CB), CB)

    waits = [copy(c_ref.at[1 - mine], c_send)]
    for layer in range(LAYERS):
        part = pl.ds(layer * rows, rows)
        for q in range(2):
            waits.append(copy(in_ref.at[layer, :, columns(2 * mine + q)], a_in.at[q, part]))
        waits.append(copy(in_ref.at[layer, :, columns(here)], b_in.at[part]))
        waits.append(copy(in_ref.at[layer, :, columns(here)], own_a.at[part]))
    piece = own_a.shape[0] - rows
    half = pl.ds(0, rows), pl.ds(rows, rows)
    waits.append(copy(out_ref.at[0, core, half[0]], own_a.at[pl.ds(piece, rows)]))
    waits.append(copy(out_ref.at[0, core, half[1]], own_b.at[half[0]]))
    waits.append(copy(out_ref.at[1, core], own_b.at[pl.ds(rows, piece)]))
    waits += [copy(x_ref.at[1 - mine], sent.at[0]), copy(x_ref.at[mine], own)]
    waits[0].wait()
    sent[1] = c_send[...].astype(BF)
    for wait in waits[1:]:
        wait.wait()


def prepare_call(seq, x, c, ffn_in, halves, **extra):
    rows = (BLOCK, D)
    piece = halves.shape[2:]
    return seq(
        prepare_body,
        [None, ("h", x), ("h", c), ("h", ffn_in), ("h", halves)],
        [("v", rows, BF), ("v", (2,) + rows, BF), ("v", (2,) + piece, BF), ("v", piece, BF)]
        + [("v", (piece[0] * 3 // 2,) + piece[1:], BF)] * 2,
        [(rows, F32)], 6 + 4 * LAYERS, "prepare", **extra)


def everywhere(target):
    pairs = []
    for z in range(4):
        for y in range(2):
            for head in range(4):
                z_to, y_to, head_to = target(z, y, head)
                pairs.append(((2 * z + y) * 4 + head, (2 * (z_to % 4) + y_to) * 4 + head_to))
    return pairs


Z_ONE = everywhere(lambda z, y, head: (z + 1 - 2 * (head % 2), y, head))
TWO = everywhere(lambda z, y, head: (z + 2, y, head))
Y_SWAP = [(i, i ^ 1) for i in range(8)]
BOTH_SWAP = everywhere(lambda z, y, head: (z, 1 - y, head ^ 2))
Z_ALL = [everywhere(lambda z, y, head, other=other: (z ^ other, y, head)) for other in (3, 2, 1)]
ACROSS = [(i, i ^ 2) for i in range(4)]
BESIDE = [(i, i ^ 1) for i in range(4)]


def swap(t, pairs):
    return lax.ppermute(t, "head", pairs)


def both_axes(t, pairs):
    return lax.ppermute(t, ("dp", "head"), pairs)


def across_y(t):
    return lax.ppermute(t, "dp", Y_SWAP)


def lay_call(seq, arrays, outs, **extra):
    piece = arrays[0].shape[-2:]

    def length(part):
        return 1 if part is None else part.stop - part.start

    def body(*refs):
        for out, result in zip(outs, refs[len(arrays):], strict=False):
            start = 0
            for index, part in out:
                stop = start + length(part)
                result[start:stop] = refs[index][...][None] if part is None else refs[index][part]
                start = stop

    shapes = [(sum(length(part) for _, part in out),) + piece for out in outs]
    return seq(body, [("v", t) for t in arrays], [("v", shape, BF) for shape in shapes], name="lay", **extra)


def cut_call(seq, cuts):
    cut = cuts.shape[3:]

    def body(ids_ref, cuts_ref, a_ref, b_ref, sems):
        copy = Copies(sems)
        waits = []
        for core, target in ((0, a_ref.at[0]), (1, a_ref.at[1]), (ids_ref[CORE], b_ref)):
            waits.append(copy(cuts_ref.at[1, core, ids_ref[MINE]], target.at[0]))
            waits.append(copy(cuts_ref.at[1, core, pl.ds(2, 2)], target.at[pl.ds(1, 2)]))
        for wait in waits:
            wait.wait()

    return seq(body, [None, ("h", cuts)], [("v", (2, 3) + cut, BF), ("v", (3,) + cut, BF)], [], 6, "cut")


def cut_lay_call(seq, out_a, out_b, in_y_far, out0_y):
    cut = out_b.shape[1:]

    def body_z(a_ref, b_ref, line_ref, sems):
        line_ref[:2] = a_ref[...]
        line_ref[2] = b_ref[...]

    [line] = seq(body_z, [("v", out_a), ("v", out_b)], [("v", (3, 3) + cut, BF)], name="lay")
    return cut_lay_rest_call(seq, line, in_y_far, out0_y)


def cut_lay_rest_call(seq, line, in_y_far, out0_y):
    cut = line.shape[2:]
    piece = out0_y.shape[1:]

    def body(z_ref, far_ref, y_ref, line_ref, own_ref, common_ref, second_ref, sems):
        rows = piece[0] // LAYERS
        line_ref[:, :3] = z_ref[...]
        line_ref[:, 3:] = far_ref[:, rows:].reshape((3, 2) + cut)
        own_ref[...] = z_ref[:, 0]
        common_ref[...] = z_ref[:, 1:]
        second_ref[:, :rows] = far_ref[:, :rows]
        second_ref[:, rows:] = y_ref[...]

    return seq(body, [("v", t) for t in (line, in_y_far, out0_y)],
               [("v", (3, 5) + cut, BF), ("v", (3,) + cut, BF), ("v", (3, 2) + cut, BF),
                ("v", (3, piece[0] // LAYERS + piece[0]) + piece[1:], BF)], name="lay")


def window_lay_call(seq, in_a, in_b, own_a, own_b):
    piece = in_b.shape

    def body(a_ref, b_ref, own_a_ref, own_b_ref, z_ref, x_ref, own_ref, sems):
        full, half = piece[0], piece[0] // 2
        own_ref[0] = own_a_ref[:full]
        own_ref[1, :half] = own_a_ref[full:]
        own_ref[1, half:] = own_b_ref[:half]
        own_ref[2] = own_b_ref[half:]
        for ref in (z_ref, x_ref):
            ref[:2] = a_ref[...]
            ref[2] = b_ref[...]
        x_ref[3] = own_a_ref[:full]

    return seq(body, [("v", t) for t in (in_a, in_b, own_a, own_b)],
               [("v", (count,) + piece, BF) for count in (3, 4, 3)], name="lay")


def first_lay_call(seq, arrays):
    piece = arrays[0].shape[-2:]
    extra = -(-2 * ROWS // piece[0])

    def body(out0_z, in_z, own_y, in_y, in_far, keys, values, first_ref, sems):
        for start, ref in ((0, in_z), (3, own_y), (6, in_y), (9, in_far), (13, out0_z)):
            first_ref[start:start + ref.shape[0]] = ref[...]
        both = jnp.concatenate([keys[...], values[...]], axis=0)
        for i in range(extra):
            rows = min(piece[0], 2 * ROWS - i * piece[0])
            first_ref[16 + i, :rows] = both[i * piece[0]:i * piece[0] + rows]

    return seq(body, [("v", t) for t in arrays], [("v", (16 + extra,) + piece, BF)], name="lay")


def far_body(first_ref, keys, values, sems):
    rows, count = first_ref.shape[1], first_ref.shape[0] - 16
    both = first_ref[16:].reshape(count * rows, D)
    keys[...] = both[:ROWS]
    values[...] = both[ROWS:2 * ROWS]


def last_body(own_y, common_y, own_yx, out_ref, sems):
    out_ref[:, 0] = own_y[...]
    out_ref[:, 1:3] = common_y[...]
    out_ref[:, 3] = own_yx[...]


def line_moves(ids, line, side, part, target):
    core, z_near = (ids[CORE], ids[Z_NEAR]) if side == 0 else (ids[OTHER_CORE], ids[Z_BESIDE])
    ref, start = line
    return [(ref.at[pl.ds(start, 2), part], target(z_near, pl.ds(0, 2))),
            (ref.at[start + 2, part], target(ids[Z_TWO], core))]


def in_target(dst, slot, y):
    def target(z, piece):
        return dst.at[pl.ds(slot, 2) if not isinstance(piece, jax.Array) else slot + piece, z, y]

    return target


def own_in(layer, ids, ref, dst):
    columns = [pl.ds(pl.multiple_of(ids[SLOTS + slot] * CB, CB), CB) for slot in range(NCB)]
    return [(ref.at[layer, :, columns[slot]], dst.at[slot, ids[Z], ids[Y]]) for slot in range(NCB)]


def pieces_in(layer, ids, lines, dst):
    part = pl.ds(layer * dst.shape[3], dst.shape[3])
    z, y = ids[Z], (ids[Y], ids[OTHER_Y])
    moves = []
    for side in range(2):
        core = ids[CORE] if side == 0 else ids[OTHER_CORE]
        along, across, own, far = lines[side::2]
        moves += line_moves(ids, along, side, part, in_target(dst, 0, y[0]))
        moves += line_moves(ids, across, side, part, in_target(dst, 0, y[1]))
        moves.append((own[0].at[own[1], part], dst.at[core, z, y[1]]))
        moves += line_moves(ids, far, side, part, in_target(dst, 2, y[0]))
        moves.append((far[0].at[far[1] + 3, part], dst.at[2 + core, z, y[1]]))
    return moves


def out_target(dst, y, cut=None):
    def target(z, piece):
        if not isinstance(piece, jax.Array):
            return dst.at[z, y] if cut is None else dst.at[z, y, :, cut]
        return dst.at[z, y, piece] if cut is None else dst.at[z, y, piece, cut]

    return target


def last_pieces(ids, refs, w_in, w_out):
    rows = pl.ds(0, w_in.shape[4])
    return [pair for side in range(2)
            for pair in line_moves(ids, (refs[side], 0), side, rows, in_target(w_in.at[0], 2, ids[OTHER_Y]))]


def last_pieces_more(ids, refs, w_in, w_out):
    in_y_far, second, out0_y, out1_z = refs
    rows = w_in.shape[4]
    moves = line_moves(ids, (out0_y, 0), 0, slice(None), out_target(w_out.at[0], ids[OTHER_Y]))
    moves += line_moves(ids, (second, 0), 1, pl.ds(rows, second.shape[1] - rows), out_target(w_out.at[0], ids[OTHER_Y]))
    moves += line_moves(ids, (in_y_far, 0), 0, pl.ds(rows, rows), in_target(w_in.at[1], 2, ids[OTHER_Y]))
    return moves + cut_line(ids, out1_z, 0, w_out.at[1])


def cut_line(ids, ref, side, dst):
    x, y = ids[MINE], ids[Y]
    return (line_moves(ids, (ref, 0), side, 0, out_target(dst, y, x))
            + line_moves(ids, (ref, 0), side, pl.ds(1, 2), out_target(dst, y, pl.ds(2, 2))))


def line_pieces(ids, refs, w_in):
    return line_moves(ids, (refs[0], 0), 1, pl.ds(3, 2), in_target(w_in, 2, ids[OTHER_Y]))


def cut_pieces(ids, refs, w_out):
    core_line, *refs = refs
    x, y = ids[MINE], (ids[Y], ids[OTHER_Y])
    moves = cut_line(ids, core_line, 1, w_out)
    for side in range(2):
        moves += line_moves(ids, (refs[side], 0), side, slice(None), out_target(w_out, y[0], 1 - x))
        for part, cut in ((0, x), (pl.ds(1, 2), pl.ds(2, 2)), (3, 1 - x)):
            moves += line_moves(ids, (refs[2 + side], 0), side, part, out_target(w_out, y[1], cut))
    return moves


def nothing(*_):
    return []


def plain_gather(ffn_in, ffn_out):
    whole_in = lax.all_gather(ffn_in, "dp", axis=1, tiled=True)
    whole_out = lax.all_gather(ffn_out, "dp", axis=1, tiled=True)
    return jnp.stack([whole_in[:, :, cb * CB:(cb + 1) * CB] for cb in range(NCB)], axis=1), whole_out.reshape(LAYERS, NCB, CB, D)


def local(block_input, part_lengths, query_weight, key_weight, value_weight, out_weight, down_shared, up_shared,
          scale_d, scale_b, ln_gain, ffn_in, ffn_out, out_grad):
    mine = lax.axis_index("head") // 2
    dp = lax.axis_size("dp")
    seq = Sequence(dp)
    halves = ffn_out.reshape(LAYERS, 2, ffn_out.shape[1] // 2, D)
    scales = (scale_d, scale_b)
    if dp == 8:
        rows_in, piece = ffn_in.shape[1], halves.shape[2:]
        cuts = halves.reshape(LAYERS, 2, 4, piece[0] // 4, D)
        cut = cuts.shape[3:]
        line = [(0, slice(0, 2)), (1, None)]

        own, sent, a_in, b_in, own_a, own_b = prepare_call(seq, block_input, out_grad, ffn_in, halves)
        in_a, in_b = both_axes(a_in, Z_ONE), both_axes(b_in, TWO)
        got, own_a, own_b = swap(sent, ACROSS), across_y(own_a), across_y(own_b)
        wk0, wv0, down, up, a_out, b_out = seq(
            None, [None], [], name="fetch",
            fetch=[(key_weight, 0), (value_weight, 0), (down_shared, None), (up_shared, None),
                   (halves, 0), (halves, ((lambda ids_ref: (0, ids_ref[CORE])), piece))])
        keys, values, inner0, lift_v0, xb, wq0 = kv_call(
            seq, 0, own, got, wk0, wv0, down, up, *scales, fetch=[(query_weight, 0)])
        q0, qt, lift_q0, wo0 = q_call(seq, 0, xb, inner0, wq0, up, *scales, fetch=[(out_weight, 0)])
        in_z, in_x, own_y = window_lay_call(seq, in_a, in_b, own_a, own_b)
        out_a, out_b = both_axes(a_out, Z_ONE), both_axes(b_out, TWO)
        in_y, in_far = across_y(in_z), swap(in_x, ACROSS)
        a_out, b_out = cut_call(seq, cuts)
        [out0_z] = lay_call(seq, [out_a, out_b], [line])
        [first] = first_lay_call(seq, [out0_z, in_z, own_y, in_y, in_far, keys, values])
        out_a, out_b = both_axes(a_out, Z_ONE), both_axes(b_out, TWO)
        out0_y, in_y_far, first = across_y(out0_z), swap(in_y, ACROSS), swap(first, BESIDE)
        kv = (keys, values, *seq(far_body, [("v", first)], [("v", (ROWS, D), BF)] * 2, name="far"))
        y, h10, *p0 = attend_call(seq, 0, part_lengths, xb, qt, kv, wo0, ln_gain)
        stored0 = (kv, q0, inner0, lift_q0, lift_v0, h10, p0, wk0, wv0, wq0, wo0)
        w_in, w_out, a, g0, wk, wv, wq, wo = seq(
            ffn_first_body,
            [None, ("v", y), ("h", ffn_in), ("h", cuts)]
            + [("v", t) for t in (in_z, in_y, in_far, own_y, first, out0_z)],
            [("v", (LAYERS, NCB, 4, 2, rows_in, CB), BF), ("v", (LAYERS, NCB, 2, 2, 4) + cut, BF)]
            + [("v", FFN_SHAPE, BF)] * 2, [], 2 * NCB + 2, "ffn_first",
            fetch=[(t, 1) for t in (key_weight, value_weight, query_weight, out_weight)])
        out1_z, out1_own, out1_common, second = cut_lay_call(seq, out_a, out_b, in_y_far, out0_y)
        out1_own_y, out1_own_x, out1_common_y = across_y(out1_own), swap(out1_own, ACROSS), across_y(out1_common)
        second, out1_z_core = swap(second, BESIDE), swap(out1_z, BESIDE)
        x, h20, w_in, w_out, a, g0 = ffn_second_call(
            seq, 0, range(NCB // 2, NCB), (last_pieces, last_pieces_more), [in_y_far, second, out0_y, out1_z],
            y, ln_gain, w_in, w_out, a, g0)
        keys, values, inner, lift_v, xb, out1_z_core = kv_call(
            seq, 1, x, got, wk, wv, down, up, *scales, through=[out1_z_core])
        [out1_own_x] = seq(None, [], [], through=[out1_own_x])
        out1_own_yx, third_core = swap(out1_own_y, ACROSS), swap(out1_own_x, BESIDE)
        kv = (keys, values, swap(keys, BESIDE), swap(values, BESIDE))
        q, qt, lift_q = q_call(seq, 1, xb, inner, wq, up, *scales)
        y, h1, *p = attend_call(seq, 1, part_lengths, x, qt, kv, wo, ln_gain)
        last, third_core = seq(last_body, [("v", t) for t in (out1_own_y, out1_common_y, out1_own_yx)],
                               [("v", (3, 4) + cut, BF)], name="lay", through=[third_core])
        last_core = swap(last, BESIDE)
        a, g, w_in = ffn_hidden_call(seq, 1, w_in, line_pieces, [out1_z_core], y)
        moves, refs = cut_pieces, [out1_z_core, out1_own_x, third_core, last, last_core]
    else:
        def pick(t, index):
            return lax.dynamic_index_in_dim(t, index, 0, keepdims=False)

        x = pick(block_input, mine)
        got = swap(jnp.stack([pick(block_input, 1 - mine), pick(out_grad, 1 - mine).astype(BF)]), ACROSS)
        blocks_in, blocks_out = plain_gather(ffn_in, ffn_out)
        for layer in range(LAYERS):
            wk, wv, down, up, wq, wo = seq(
                None, [], [], name="fetch",
                fetch=[(key_weight, layer), (value_weight, layer), (down_shared, None), (up_shared, None),
                       (query_weight, layer), (out_weight, layer)])
            keys, values, inner, lift_v, xb = kv_call(seq, layer, x, got, wk, wv, down, up, *scales)
            kv = (keys, values, swap(keys, BESIDE), swap(values, BESIDE))
            q, qt, lift_q = q_call(seq, layer, xb, inner, wq, up, *scales)
            y, h1, *p = attend_call(
                seq, layer, part_lengths, xb if layer == 0 else x, qt, kv, wo, ln_gain)
            if layer == 0:
                a, g0 = seq(None, [], [("v", FFN_SHAPE, BF)] * 2)
                w_in, w_out = seq(None, [], [], name="fetch", fetch=[(blocks_in, None), (blocks_out, None)])
                x, h20, w_in, w_out, a, g0 = ffn_second_call(
                    seq, 0, range(NCB), (nothing, nothing), [], y, ln_gain, w_in, w_out, a, g0)
                stored0 = (kv, q, inner, lift_q, lift_v, h1, p, wk, wv, wq, wo)
        a, g, w_in = ffn_hidden_call(seq, 1, w_in, nothing, [], y)
        moves, refs = nothing, []
    output, send, dh, w_out = ffn_both_call(seq, 1, w_in, w_out, a, g, moves, refs, y, h1, ln_gain, got, out_grad)
    other_output = swap(send, ACROSS)
    dq, own, send = attend_back_call(seq, dh, wo, q, kv, p)
    got = swap(send, BESIDE)
    dx, dub, gd_q, gb_q = dq_call(seq, 1, dh, dq, lift_q, inner, wq, up, *scales)
    dub, dk, dv, sums = dv_call(
        seq, 1, dub, own, got, lift_v, inner, up, *scales, gd_q, gb_q, jnp.zeros((4 * LAYERS, RANK), F32))
    [cotangent] = dx_call(seq, 1, dx, dub, dk, dv, wk, wv, down)
    kv, q, inner, lift_q, lift_v, h1, p, wk, wv, wq, wo = stored0
    [dh] = ffn_back_call(seq, 0, cotangent, h20, g0, h1, ln_gain, w_in, w_out)
    dq, own, send, block_output = attend_back_call(seq, dh, wo, q, kv, p, (output, other_output))
    got = swap(send, BESIDE)
    dx, dub, gd_q, gb_q = dq_call(seq, 0, dh, dq, lift_q, inner, wq, up, *scales)
    dub, dk, dv, sums = dv_call(seq, 0, dub, own, got, lift_v, inner, up, *scales, gd_q, gb_q, sums)
    if dp == 8:
        [sums] = add_call(seq, sums, swap(sums, BESIDE))
        parts = [both_axes(sums, BOTH_SWAP), swap(sums, ACROSS), across_y(sums)]
        last_rows, input_grad = dx_call(seq, 0, dx, dub, dk, dv, wk, wv, down)
        sums, last_rows = add_call(seq, sums, *parts, through=[last_rows])
        got = swap(last_rows, ACROSS)
        parts = [both_axes(sums, along) for along in Z_ALL]
    else:
        last_rows, input_grad = dx_call(seq, 0, dx, dub, dk, dv, wk, wv, down)
        got = swap(last_rows, ACROSS)
        sums, parts = lax.psum(sums, ("dp", "head")), []
    grad_d, grad_b, input_grad = finish_call(seq, [sums, *parts], got, input_grad)
    return block_output, input_grad, grad_d, grad_b


def solution(mesh):
    both = P(None, ("dp", "head"), None)
    in_specs = (both, P(None, "dp", None), P(), P(), P(), P(), P(), P(), P(), P(), P(),
                P(None, "dp", None), P(None, "dp", None), both)
    out_specs = (both, both, P(), P())
    return jax.shard_map(local, mesh=mesh, in_specs=in_specs, out_specs=out_specs, check_vma=False)
```

```python
import functools

import jax
import jax.numpy as jnp
from jax import lax
from jax.experimental import pallas as pl
from jax.experimental.pallas import tpu as pltpu
from jax.sharding import PartitionSpec as P

D = 768
HEADS = 12
HEAD_DIM = 64
FF = 3072
RANK = 1024
LEN = 512
LAYERS = 2
PAIRS = HEADS // 2
PAIR = 2 * HEAD_DIM
BLOCK = LEN // 4
ROWS = 2 * BLOCK
CB = D
NCB = FF // CB
SCALE = HEAD_DIM ** (-0.5)
BF = jnp.bfloat16
F32 = jnp.float32
MIB = 1 << 20

COLOURS = {"v": pltpu.VMEM, "h": pltpu.HBM}
SPACES = {
    "v": pl.BlockSpec(memory_space=pltpu.VMEM),
    "h": pl.BlockSpec(memory_space=pltpu.HBM),
    "s": pl.BlockSpec(memory_space=pltpu.SMEM),
    "a": pl.BlockSpec(memory_space=pl.ANY),
}


HERE, CORE, MINE, Z, Y, OTHER_Y, Z_TWO, Z_NEAR, Z_BESIDE, OTHER_CORE = range(10)
SLOTS, BLOCKS = 10, 14


def indices(dp):
    here, place = lax.axis_index("head"), lax.axis_index("dp")
    mine, core = lax.div(here, 2), lax.rem(here, 2)
    z, y = lax.div(place, 2), lax.rem(place, 2)
    line = [z, y, 1 - y] + [lax.rem(z + step, 4) for step in (2, 3 + 2 * core, 1 + 2 * core)]
    blocks = [here, here ^ 2, here ^ 1, here ^ 3]
    if dp == 8:
        slots = [2 * mine, 2 * mine + 1, 2 - 2 * mine, 3 - 2 * mine]
    else:
        slots = list(range(NCB))
    return [here, core, mine] + line + [1 - core] + slots + blocks


def dot(left, right):
    return jnp.dot(left, right, preferred_element_type=F32)


def dot_nt(left, right):
    return lax.dot_general(left, right, (((1,), (1,)), ((), ())), preferred_element_type=F32)


def normed(t):
    centred = t - jnp.mean(t, axis=-1, keepdims=True)
    inverse = lax.rsqrt(jnp.mean(centred * centred, axis=-1, keepdims=True) + 1e-05)
    return centred * inverse, inverse


def norm_back(t, gain, cotangent):
    unit, inverse = normed(t)
    scaled = cotangent * gain
    mean_e = jnp.mean(scaled, axis=-1, keepdims=True)
    mean_en = jnp.mean(scaled * unit, axis=-1, keepdims=True)
    return inverse * (scaled - mean_e - unit * mean_en)


class Copies:
    def __init__(self, sems, first=0):
        self.sems, self.count = sems, first

    def __call__(self, src, dst):
        copy = pltpu.make_async_copy(src, dst, self.sems.at[self.count])
        self.count += 1
        copy.start()
        return copy


class Sequence:
    def __init__(self, dp):
        self.dp, self.token = dp, None

    def __call__(self, body, ins, outs, scratch=(), copies=0, name="keep", fetch=(), fill=(), fill_hbm=(), through=(), limit=8, save=(), cost=0.001):
        handed = [pltpu.with_memory_space_constraint(t, pltpu.VMEM) for t in fill]
        handed += [pltpu.with_memory_space_constraint(t, pltpu.HBM) for t in fill_hbm]
        handed += list(through)
        if self.token is not None:
            handed.append(pltpu.with_memory_space_constraint(self.token, pltpu.HBM))
        fetched = [(t.shape if part is None else t.shape[1:] if isinstance(part, int) else part[1], t.dtype)
                   for t, part in fetch]
        wants = [i for i, entry in enumerate(ins) if entry is None]
        ins = [entry for entry in ins if entry is not None]
        n_in, n_fetch, n_hand, n_fill = len(ins), len(fetch), len(handed), len(fill) + len(fill_hbm)
        n_out, n_save = len(outs), len(save)
        first = self.token is None

        def whole(*refs):
            refs = list(refs)
            in_refs, fetch_refs = refs[:n_in], refs[n_in:n_in + n_fetch]
            for i in wants:
                in_refs.insert(i, indices(self.dp))
            refs = refs[n_in + n_fetch:]
            refs = refs[n_hand:]
            out_refs, fetch_outs = refs[:n_out], refs[n_out:n_out + n_fetch]
            refs = refs[n_out + n_fetch:]
            fill_refs = refs[:n_fill]
            save_refs = refs[n_hand + first:][:n_save]
            refs = refs[n_hand + first + n_save:]
            scratch_refs, sems = refs[:len(scratch)], refs[len(scratch)]
            copy = Copies(sems, copies)
            waits = []
            for (_, part), source, target in zip(fetch, fetch_refs, fetch_outs, strict=True):
                if part is not None:
                    source = source.at[part if isinstance(part, int) else part[0](in_refs[0])]
                waits.append(copy(source, target))
            for place, target in zip(save, save_refs, strict=True):
                waits.append(copy(in_refs[place], target))
            if body is not None:
                body(*in_refs, *fill_refs, *out_refs, *scratch_refs, sems)
            for wait in waits:
                wait.wait()

        shapes = [COLOURS[space](shape, dtype) for space, shape, dtype in outs]
        shapes += [pltpu.VMEM(shape, dtype) for shape, dtype in fetched]
        shapes += [pltpu.VMEM(t.shape, t.dtype) for t in fill] + [pltpu.HBM(t.shape, t.dtype) for t in fill_hbm]
        shapes += [jax.ShapeDtypeStruct(t.shape, t.dtype) for t in through]
        shapes += [pltpu.HBM((8, 128), F32)]
        shapes += [pltpu.HBM(ins[place][1].shape, ins[place][1].dtype) for place in save]
        results = pl.pallas_call(
            whole,
            out_shape=tuple(shapes),
            in_specs=[SPACES[space] for space, _ in ins] + [SPACES["h"]] * n_fetch + [SPACES["v"]] * len(fill)
            + [SPACES["h"]] * len(fill_hbm) + [SPACES["a"]] * (n_hand - n_fill),
            out_specs=tuple([SPACES[space] for space, _, _ in outs] + [SPACES["v"]] * (n_fetch + len(fill))
                            + [SPACES["h"]] * len(fill_hbm) + [SPACES["a"]] * (n_hand - n_fill + first) + [SPACES["h"]] * n_save),
            scratch_shapes=[pltpu.VMEM(shape, dtype) for shape, dtype in scratch]
            + [pltpu.SemaphoreType.DMA((copies + n_fetch + n_save + 1,))],
            input_output_aliases={n_in + n_fetch + i: n_out + n_fetch + i for i in range(n_hand)},
            compiler_params=pltpu.CompilerParams(vmem_limit_bytes=limit * MIB),
            cost_estimate=pl.CostEstimate(
                flops=int(cost * 1e9), bytes_accessed=int(cost * 3e6), transcendentals=0),
            name=name,
        )(*[pltpu.with_memory_space_constraint(t, COLOURS[space]) if space in COLOURS else t for space, t in ins],
          *[pltpu.with_memory_space_constraint(t, pltpu.HBM) for t, _ in fetch],
          *handed)
        results = list(results)
        split = n_out + n_fetch + n_fill + len(through)
        self.token = results[split]
        return results[:split] + results[split + 1:]


def kv_body(layer, x_ref, got_ref, wk, wv, down, up, sd_ref, sb_ref, *rest):
    keys, values, inner_out, lift_out, xb_ref, _ = rest
    if layer == 0:
        xb_ref[:BLOCK] = x_ref[...]
        xb_ref[BLOCK:] = got_ref[0]
    else:
        xb_ref[...] = x_ref[...].astype(BF)
    xb = xb_ref[...]
    inner = dot(xb, down[...])
    inner_out[...] = inner.astype(BF)
    lift = dot((sd_ref[layer, 1:2, :] * inner).astype(BF), up[...])
    lift_out[...] = lift.astype(BF)
    values[...] = (dot(xb, wv[...]) + sb_ref[layer, 1:2, :] * lift).astype(BF)
    keys[...] = dot(xb, wk[...]).astype(BF)


def kv_call(seq, layer, x, got, wk, wv, down, up, sd, sb, **extra):
    return seq(
        functools.partial(kv_body, layer),
        [("v", t) for t in (x, got, wk, wv, down, up, sd, sb)],
        [("v", (ROWS, D), BF)] * 2 + [("v", (ROWS, RANK), BF), ("v", (ROWS, D), BF), ("v", (ROWS, D), BF)],
        name="keys_values", **extra)


def q_body(layer, x_ref, inner, wq, up, sd_ref, sb_ref, q_ref, qt_ref, lift_out, sems):
    lift = dot((sd_ref[layer, 0:1, :] * inner[...].astype(F32)).astype(BF), up[...])
    lift_out[...] = lift.astype(BF)
    q = (dot(x_ref[...], wq[...]) + sb_ref[layer, 0:1, :] * lift).astype(BF)
    q_ref[...] = q
    qt_ref[...] = (q * SCALE).T


def q_call(seq, layer, x, inner, wq, up, sd, sb, **extra):
    return seq(
        functools.partial(q_body, layer),
        [("v", x), ("v", inner), ("v", wq), ("v", up), ("v", sd), ("v", sb)],
        [("v", (ROWS, D), BF), ("v", (D, ROWS), BF), ("v", (ROWS, D), BF)],
        name="queries", **extra)


def split_heads(t):
    zero = jnp.zeros((HEAD_DIM, t.shape[1]), t.dtype)
    first = jnp.concatenate([t[:HEAD_DIM], zero], axis=0)
    second = jnp.concatenate([zero, t[HEAD_DIM:]], axis=0)
    return jnp.concatenate([first, second], axis=1)


def join_heads(t):
    n = t.shape[1] // 2
    return jnp.concatenate([t[:HEAD_DIM, :n], t[HEAD_DIM:, n:]], axis=0)


def stack_heads(t):
    lane = lax.broadcasted_iota(jnp.int32, (1, PAIR), 1)
    first = (lane < HEAD_DIM).astype(F32).astype(BF)
    second = (lane >= HEAD_DIM).astype(F32).astype(BF)
    return jnp.concatenate([t * first, t * second], axis=0)


def rows_of(near, far, cols):
    return jnp.concatenate([near[:, cols], far[:, cols]], axis=0)


def attend_body(layer, ids, lengths, x_ref, qt_ref, wo, gain_ref, keys, values, far_keys, far_values,
                y_ref, h_ref, e_ref, factor_ref, ctx_t_ref, ctx, sems):
    row = lax.broadcasted_iota(jnp.int32, (BLOCK, 2 * ROWS), 0)
    counts = lengths[ids[MINE]]
    live = counts[:, :1] + counts[:, 1:] + 4
    limits = [live - BLOCK * ids[BLOCKS + b] for b in range(4)]
    for pair in range(PAIRS):
        cols = slice(pair * PAIR, (pair + 1) * PAIR)
        raw = dot(rows_of(keys, far_keys, cols), split_heads(qt_ref[cols, :]))
        scores = jnp.concatenate(
            [jnp.where(row < limits[b], raw[b * BLOCK:(b + 1) * BLOCK], -1000000000.0) for b in range(4)],
            axis=0,
        )
        grown = jnp.exp(scores - jnp.max(scores, axis=0, keepdims=True))
        factor = 1.0 / jnp.sum(grown, axis=0, keepdims=True)
        factor_ref[pair:pair + 1, :] = factor
        e_ref[pair] = grown.astype(BF)
        ctx_t = join_heads(dot(rows_of(values, far_values, cols).T, e_ref[pair]) * factor)
        ctx_t_ref[cols, :] = ctx_t
        ctx[:, cols] = ctx_t.astype(BF).T
    h = x_ref[...].astype(F32) + dot(ctx[...], wo[...])
    h_ref[...] = h
    y_ref[...] = normed(h)[0] * gain_ref[layer, 0:1, :]


def attend_call(seq, layer, lengths, x, qt, kv, wo, gain, **extra):
    return seq(
        functools.partial(attend_body, layer),
        [None] + [("v", t) for t in (lengths, x, qt, wo, gain, *kv)],
        [("v", (ROWS, D), F32), ("v", (ROWS, D), F32), ("v", (PAIRS, LEN, 2 * ROWS), BF), ("v", (PAIRS, 2 * ROWS), F32),
         ("v", (D, ROWS), F32)],
        [((ROWS, D), BF)], name="attention", **extra)


def move(pairs):
    for source, target in pairs:
        target[...] = source[...].reshape(target.shape)


def ffn_hidden(yb, w_in, a_ref, g_ref, slots):
    for slot in slots:
        z = dot(yb, w_in[slot].reshape(D, CB))
        cdf = 0.5 * (1.0 + lax.erf(z * (0.5 ** 0.5)))
        g_ref[slot] = (cdf + z * (jnp.exp(-0.5 * z * z) * 0.3989422804014327)).astype(BF)
        a_ref[slot] = (z * cdf).astype(BF)


def ffn_result(ids, total, a_ref, w_out):
    for slot in range(NCB):
        total = total + dot(a_ref[slot], w_out[ids[SLOTS + slot]].reshape(CB, D))
    return total


def ffn_backward(layer, ids, c, h2, g_ref, h1, gain_ref, w_in, w_out, dh_ref):
    dh2 = norm_back(h2, gain_ref[layer, 1:2, :], c)
    dfb = dh2.astype(BF)
    total = dh2
    for slot in range(NCB):
        da = dot_nt(dfb, w_out[ids[SLOTS + slot]].reshape(CB, D))
        dz = (g_ref[slot].astype(F32) * da).astype(BF)
        total = total + dot_nt(dz, w_in[slot].reshape(D, CB))
    dh1 = norm_back(h1, gain_ref[layer, 0:1, :], total)
    dh_ref[...] = dh1


FFN_SHAPE = (NCB, ROWS, CB)


def ffn_first_body(ids, y_ref, in_ref, cut_ref, in_z, in_y, in_far, own_y, first, out0_z,
                   w_in, w_out, a_ref, g_ref, sems):
    copy = Copies(sems)
    w_in = [w_in.at[layer] for layer in range(LAYERS)]
    w_out = [w_out.at[layer] for layer in range(LAYERS)]
    owns = [[copy(source, target) for source, target in own_in(layer, ids, in_ref, w_in[layer])] for layer in range(LAYERS)]
    own_out = [copy(cut_ref.at[layer], w_out[layer].at[ids[Z], ids[Y]]) for layer in range(LAYERS)]
    lines = [(in_z, 0), (first, 0), (in_y, 0), (first, 6), (own_y, 0), (first, 3), (in_far, 0), (first, 9)]
    move(pieces_in(0, ids, lines, w_in[0]))
    for wait in owns[0]:
        wait.wait()
    ffn_hidden(y_ref[...].astype(BF), w_in[0], a_ref, g_ref, range(NCB // 2))
    move(pieces_in(1, ids, lines, w_in[1]))
    for side, line in enumerate([(out0_z, 0), (first, 13)]):
        move(line_moves(ids, line, side, slice(None), out_target(w_out[0], ids[Y])))
    for side, (ref, start) in enumerate([(own_y, 0), (first, 3)]):
        core = ids[CORE] if side == 0 else ids[OTHER_CORE]
        for layer in range(LAYERS):
            move([(ref.at[start + 1 + layer], w_out[layer].at[ids[Z], ids[OTHER_Y], core])])
    for wait in owns[1] + own_out:
        wait.wait()


def ffn_second_body(layer, slots, moves, n_refs, ids, y_ref, gain_ref, *rest):
    refs, rest = rest[:n_refs], rest[n_refs:]
    w_in, w_out, a_ref, g_ref, x_ref, h_ref, _ = rest
    move(moves[0](ids, refs, w_in, w_out))
    ffn_hidden(y_ref[...].astype(BF), w_in.at[layer], a_ref, g_ref, slots)
    move(moves[1](ids, refs, w_in, w_out))
    h_ref[...] = ffn_result(ids, y_ref[...], a_ref, w_out.at[layer])
    x_ref[...] = normed(h_ref[...])[0] * gain_ref[layer, 1:2, :]


def ffn_second_call(seq, layer, slots, moves, refs, y, gain, w_in, w_out, a, g, **extra):
    return seq(
        functools.partial(ffn_second_body, layer, slots, moves, len(refs)),
        [None, ("v", y), ("v", gain)] + [("v", t) for t in refs],
        [("v", (ROWS, D), F32), ("v", (ROWS, D), F32)], name="ffn", fill=[w_in, w_out, a, g], **extra)


FFN_SHAPE = (NCB, ROWS, CB)


def ffn_hidden_body(layer, moves, n_refs, ids, y_ref, *rest):
    refs, (w_in, a_ref, g_ref, _) = rest[:n_refs], rest[n_refs:]
    move(moves(ids, refs, w_in.at[layer]))
    ffn_hidden(y_ref[...].astype(BF), w_in.at[layer], a_ref, g_ref, range(NCB))


def ffn_hidden_call(seq, layer, w_in, moves, refs, y, **extra):
    return seq(
        functools.partial(ffn_hidden_body, layer, moves, len(refs)),
        [None, ("v", y)] + [("v", t) for t in refs], [("v", FFN_SHAPE, BF)] * 2, name="ffn_hidden", fill=[w_in], **extra)


def ffn_both_body(layer, moves, n_refs, ids, y_ref, h1, gain_ref, got_ref, w_in, a_ref, g_ref, c_ref, *rest):
    refs, rest = rest[:n_refs], rest[n_refs:]
    w_out, x_ref, send_ref, dh_ref, c, sems = rest
    own = Copies(sems)(c_ref.at[ids[MINE]], c.at[pl.ds(0, BLOCK)])
    w_in, w_out = w_in.at[layer], w_out.at[layer]
    move(moves(ids, refs, w_out))
    h2 = ffn_result(ids, y_ref[...], a_ref, w_out)
    dh_ref[...] = h2
    x = normed(h2)[0] * gain_ref[layer, 1:2, :]
    x_ref[...] = x[:BLOCK].astype(BF)
    send_ref[...] = x[BLOCK:].astype(BF)
    own.wait()
    c[BLOCK:] = got_ref[1].astype(F32)
    ffn_backward(layer, ids, c[...], dh_ref[...], g_ref, h1[...], gain_ref, w_in, w_out, dh_ref)


def ffn_both_call(seq, layer, w_in, w_out, a, g, moves, refs, y, h1, gain, got, c, **extra):
    return seq(
        functools.partial(ffn_both_body, layer, moves, len(refs)),
        [None] + [("v", t) for t in (y, h1, gain, got, w_in, a, g)] + [("h", c)] + [("v", t) for t in refs],
        [("v", (BLOCK, D), BF), ("v", (BLOCK, D), BF), ("v", (ROWS, D), F32)],
        [((ROWS, D), F32)], 1, "ffn_both", fill=[w_out], **extra)


def ffn_back_body(layer, ids, c_ref, h2, g, h1, gain_ref, w_in, w_out, dh_ref, sems):
    ffn_backward(layer, ids, c_ref[...], h2[...], g, h1[...], gain_ref, w_in.at[layer], w_out.at[layer], dh_ref)


def ffn_back_call(seq, layer, c, h2, g, h1, gain, w_in, w_out, **extra):
    return seq(
        functools.partial(ffn_back_body, layer),
        [None] + [("v", t) for t in (c, h2, g, h1, gain, w_in, w_out)],
        [("v", (ROWS, D), F32)], name="ffn_back", **extra)


def attend_back_body(dh_ref, wo, q, factor_ref, ctx_t_ref, keys, values, far_keys, far_values,
                     e_ref, own_ref, send_ref, dctx_ref, sems):
    dctx_ref[...] = dot_nt(dh_ref[...].astype(BF), wo[...]).astype(BF)
    for pair in range(PAIRS):
        cols = slice(pair * PAIR, (pair + 1) * PAIR)
        vcols = slice(D + pair * PAIR, D + (pair + 1) * PAIR)
        factor = factor_ref[pair:pair + 1, :]
        scaled = (split_heads(dctx_ref[:, cols].T).astype(F32) * factor).astype(BF)
        inner = jnp.sum(scaled.astype(F32) * split_heads(ctx_t_ref[cols, :]), axis=0, keepdims=True)
        e = e_ref[pair]
        ds = (e.astype(F32) * (dot(rows_of(values, far_values, cols), scaled) - inner)).astype(BF)
        dv = dot(e, scaled.T)
        dk = dot(ds[ROWS:], stack_heads(q[:, cols])) * SCALE
        own_ref[:, cols] = dv[:ROWS]
        send_ref[:, cols] = dk.astype(BF)
        send_ref[:, vcols] = dv[ROWS:].astype(BF)
        e_ref[pair] = ds


def attend_back_call(seq, dh, wo, q, kv, weights, **extra):
    e, *rest = weights
    return seq(
        attend_back_body,
        [("v", t) for t in (dh, wo, q, *rest, *kv)],
        [("v", (ROWS, D), F32), ("v", (ROWS, 2 * D), BF)],
        [((ROWS, D), BF)], name="attention_back", fill=[e], **extra)


def dq_body(layer, dh_ref, ds_ref, q, keys, far_keys, lift, inner, wq, up, sd_ref, sb_ref,
            dx_ref, dub_ref, dk_ref, gd_ref, gb_ref, dq_ref, sems):
    for pair in range(PAIRS):
        cols = slice(pair * PAIR, (pair + 1) * PAIR)
        dq_t = join_heads(dot(rows_of(keys, far_keys, cols).T, ds_ref[pair])) * SCALE
        dq_ref[:, cols] = dq_t.T.astype(BF)
        dk_ref[:, cols] = dot(ds_ref[pair, :ROWS], stack_heads(q[:, cols])) * SCALE
    dq = dq_ref[...]
    dqf = dq.astype(F32)
    gb_ref[...] = jnp.sum(dqf * lift[...].astype(F32), axis=0, keepdims=True)
    dpq = dot_nt((sb_ref[layer, 0:1, :] * dqf).astype(BF), up[...])
    gd_ref[...] = jnp.sum(dpq * inner[...].astype(F32), axis=0, keepdims=True)
    dub_ref[...] = sd_ref[layer, 0:1, :] * dpq
    dx_ref[...] = dh_ref[...] + dot_nt(dq, wq[...])


def dq_call(seq, layer, dh, ds, q, kv, lift, inner, wq, up, sd, sb, **extra):
    return seq(
        functools.partial(dq_body, layer),
        [("v", t) for t in (dh, ds, q, kv[0], kv[2], lift, inner, wq, up, sd, sb)],
        [("v", (ROWS, D), F32), ("v", (ROWS, RANK), F32), ("v", (ROWS, D), F32), ("v", (1, RANK), F32), ("v", (1, D), F32)],
        [((ROWS, D), BF)], name="queries_back", **extra)


def dv_body(layer, dub_ref, own_ref, got_ref, lift, inner, up, sd_ref, sb_ref, gdq_ref, gbq_ref, before_ref,
            dub_out, dv_ref, sums_ref, sems):
    sums_ref[...] = before_ref[...]
    sums_ref[4 * layer:4 * layer + 1, :] = gdq_ref[...]
    sums_ref[4 * layer + 2:4 * layer + 3, :D] = gbq_ref[...]
    dv = (own_ref[...] + got_ref[:, D:].astype(F32)).astype(BF)
    dv_ref[...] = dv
    dvf = dv.astype(F32)
    sums_ref[4 * layer + 3:4 * layer + 4, :D] = jnp.sum(dvf * lift[...].astype(F32), axis=0, keepdims=True)
    dpv = dot_nt((sb_ref[layer, 1:2, :] * dvf).astype(BF), up[...])
    sums_ref[4 * layer + 1:4 * layer + 2, :] = jnp.sum(dpv * inner[...].astype(F32), axis=0, keepdims=True)
    dub_out[...] = (dub_ref[...] + sd_ref[layer, 1:2, :] * dpv).astype(BF)


def dv_call(seq, layer, dub, own, got, lift, inner, up, sd, sb, gd, gb, before, **extra):
    return seq(
        functools.partial(dv_body, layer),
        [("v", t) for t in (dub, own, got, lift, inner, up, sd, sb, gd, gb, before)],
        [("v", (ROWS, RANK), BF), ("v", (ROWS, D), BF), ("v", (4 * LAYERS, RANK), F32)],
        name="values_back", **extra)


def dx_body(layer, dx_ref, dub_ref, dk_ref, got_ref, dv_ref, wk, wv, down, *rest):
    total = dx_ref[...] + dot_nt(dub_ref[...], down[...])
    total = total + dot_nt(dv_ref[...], wv[...])
    dk = (dk_ref[...] + got_ref[:, :D].astype(F32)).astype(BF)
    total = total + dot_nt(dk, wk[...])
    if layer == 0:
        own_ref, send_ref, _ = rest
        own_ref[...] = total[:BLOCK]
        send_ref[...] = total[BLOCK:].astype(BF)
    else:
        rest[0][...] = total


def dx_call(seq, layer, dx, dub, dk, got, dv, wk, wv, down, **extra):
    return seq(
        functools.partial(dx_body, layer),
        [("v", t) for t in (dx, dub, dk, got, dv, wk, wv, down)],
        [("v", (BLOCK, D), F32), ("v", (BLOCK, D), BF)] if layer == 0 else [("v", (ROWS, D), F32)],
        name="input_back", **extra)


def add_call(seq, *terms, **extra):
    def body(*refs):
        total = refs[0][...]
        for ref in refs[1:len(terms)]:
            total = total + ref[...]
        refs[len(terms)][...] = total

    return seq(body, [("v", t) for t in terms], [("v", terms[0].shape, F32)], name="add", **extra)


def store_call(seq, output, other_output, rows, got):
    def body(ids_ref, output_ref, other_ref, rows_ref, got_ref, block_ref, grad_ref, wide, sems):
        copy = Copies(sems)
        mine = ids_ref[MINE]
        stores = [copy(rows_ref, grad_ref.at[mine]), copy(output_ref, block_ref.at[mine]), copy(other_ref, block_ref.at[1 - mine])]
        wide[...] = got_ref[...].astype(F32)
        stores.append(copy(wide, grad_ref.at[1 - mine]))
        for store in stores:
            store.wait()

    return seq(body, [None] + [("v", t) for t in (output, other_output, rows, got)],
               [("h", (2,) + t.shape, t.dtype) for t in (output, rows)], [(got.shape, F32)], 4, "store")


def finish_call(seq, terms):
    def body(*refs):
        *terms_refs, gd_out, gb_out, gd_ref, gb_ref, sems = refs
        copy = Copies(sems)
        total = terms_refs[0][...]
        for ref in terms_refs[1:]:
            total = total + ref[...]
        for layer in range(LAYERS):
            gd_ref[layer] = total[4 * layer:4 * layer + 2]
            gb_ref[layer] = total[4 * layer + 2:4 * layer + 4, :D]
        stores = [copy(gd_ref, gd_out), copy(gb_ref, gb_out)]
        for store in stores:
            store.wait()

    shapes = [((LAYERS, 2, RANK), F32), ((LAYERS, 2, D), F32)]
    return seq(body, [("v", t) for t in terms], [("h", *t) for t in shapes], shapes, 2, "finish")


def prepare_body(ids, x_ref, c_ref, in_ref, out_ref, own, sent, a_in, b_in, own_a, own_b, c_send, sems):
    copy = Copies(sems)
    here, core, mine = ids[HERE], ids[CORE], ids[MINE]
    rows = in_ref.shape[1]

    def columns(block):
        return pl.ds(pl.multiple_of(block * CB, CB), CB)

    waits = [copy(c_ref.at[1 - mine], c_send)]
    for layer in range(LAYERS):
        part = pl.ds(layer * rows, rows)
        for q in range(2):
            waits.append(copy(in_ref.at[layer, :, columns(2 * mine + q)], a_in.at[q, part]))
        waits.append(copy(in_ref.at[layer, :, columns(here)], b_in.at[part]))
        waits.append(copy(in_ref.at[layer, :, columns(here)], own_a.at[part]))
    piece = own_a.shape[0] - rows
    half = pl.ds(0, rows), pl.ds(rows, rows)
    waits.append(copy(out_ref.at[0, core, half[0]], own_a.at[pl.ds(piece, rows)]))
    waits.append(copy(out_ref.at[0, core, half[1]], own_b.at[half[0]]))
    waits.append(copy(out_ref.at[1, core], own_b.at[pl.ds(rows, piece)]))
    waits += [copy(x_ref.at[1 - mine], sent.at[0]), copy(x_ref.at[mine], own)]
    waits[0].wait()
    sent[1] = c_send[...].astype(BF)
    for wait in waits[1:]:
        wait.wait()


def prepare_call(seq, x, c, ffn_in, halves, **extra):
    rows = (BLOCK, D)
    piece = halves.shape[2:]
    return seq(
        prepare_body,
        [None, ("h", x), ("h", c), ("h", ffn_in), ("h", halves)],
        [("v", rows, BF), ("v", (2,) + rows, BF), ("v", (2,) + piece, BF), ("v", piece, BF)]
        + [("v", (piece[0] * 3 // 2,) + piece[1:], BF)] * 2,
        [(rows, F32)], 6 + 4 * LAYERS, "prepare", **extra)


def everywhere(target):
    pairs = []
    for z in range(4):
        for y in range(2):
            for head in range(4):
                z_to, y_to, head_to = target(z, y, head)
                pairs.append(((2 * z + y) * 4 + head, (2 * (z_to % 4) + y_to) * 4 + head_to))
    return pairs


Z_ONE = everywhere(lambda z, y, head: (z + 1 - 2 * (head % 2), y, head))
TWO = everywhere(lambda z, y, head: (z + 2, y, head))
Y_SWAP = [(i, i ^ 1) for i in range(8)]
BOTH_SWAP = everywhere(lambda z, y, head: (z, 1 - y, head ^ 2))
Z_ALL = [everywhere(lambda z, y, head, other=other: (z ^ other, y, head)) for other in (3, 2, 1)]
ACROSS = [(i, i ^ 2) for i in range(4)]
BESIDE = [(i, i ^ 1) for i in range(4)]


def swap(t, pairs):
    return lax.ppermute(t, "head", pairs)


def both_axes(t, pairs):
    return lax.ppermute(t, ("dp", "head"), pairs)


def across_y(t):
    return lax.ppermute(t, "dp", Y_SWAP)


def lay_call(seq, arrays, outs, **extra):
    piece = arrays[0].shape[-2:]

    def length(part):
        return 1 if part is None else part.stop - part.start

    def body(*refs):
        for out, result in zip(outs, refs[len(arrays):], strict=False):
            start = 0
            for index, part in out:
                stop = start + length(part)
                result[start:stop] = refs[index][...][None] if part is None else refs[index][part]
                start = stop

    shapes = [(sum(length(part) for _, part in out),) + piece for out in outs]
    return seq(body, [("v", t) for t in arrays], [("v", shape, BF) for shape in shapes], name="lay", **extra)


def cut_call(seq, cuts):
    cut = cuts.shape[3:]

    def body(ids_ref, cuts_ref, a_ref, b_ref, sems):
        copy = Copies(sems)
        waits = []
        for core, target in ((0, a_ref.at[0]), (1, a_ref.at[1]), (ids_ref[CORE], b_ref)):
            waits.append(copy(cuts_ref.at[1, core, ids_ref[MINE]], target.at[0]))
            waits.append(copy(cuts_ref.at[1, core, pl.ds(2, 2)], target.at[pl.ds(1, 2)]))
        for wait in waits:
            wait.wait()

    return seq(body, [None, ("h", cuts)], [("v", (2, 3) + cut, BF), ("v", (3,) + cut, BF)], [], 6, "cut")


def cut_lay_call(seq, out_a, out_b, in_y_far, out0_y):
    cut = out_b.shape[1:]

    def body_z(a_ref, b_ref, line_ref, sems):
        line_ref[:2] = a_ref[...]
        line_ref[2] = b_ref[...]

    [line] = seq(body_z, [("v", out_a), ("v", out_b)], [("v", (3, 3) + cut, BF)], name="lay")
    return cut_lay_rest_call(seq, line, in_y_far, out0_y)


def cut_lay_rest_call(seq, line, in_y_far, out0_y):
    cut = line.shape[2:]
    piece = out0_y.shape[1:]

    def body(z_ref, far_ref, y_ref, line_ref, own_ref, common_ref, second_ref, sems):
        rows = piece[0] // LAYERS
        line_ref[:, :3] = z_ref[...]
        line_ref[:, 3:] = far_ref[:, rows:].reshape((3, 2) + cut)
        own_ref[...] = z_ref[:, 0]
        common_ref[...] = z_ref[:, 1:]
        second_ref[:, :rows] = far_ref[:, :rows]
        second_ref[:, rows:] = y_ref[...]

    return seq(body, [("v", t) for t in (line, in_y_far, out0_y)],
               [("v", (3, 5) + cut, BF), ("v", (3,) + cut, BF), ("v", (3, 2) + cut, BF),
                ("v", (3, piece[0] // LAYERS + piece[0]) + piece[1:], BF)], name="lay")


def window_lay_call(seq, in_a, in_b, own_a, own_b):
    piece = in_b.shape

    def body(a_ref, b_ref, own_a_ref, own_b_ref, z_ref, x_ref, own_ref, sems):
        full, half = piece[0], piece[0] // 2
        own_ref[0] = own_a_ref[:full]
        own_ref[1, :half] = own_a_ref[full:]
        own_ref[1, half:] = own_b_ref[:half]
        own_ref[2] = own_b_ref[half:]
        for ref in (z_ref, x_ref):
            ref[:2] = a_ref[...]
            ref[2] = b_ref[...]
        x_ref[3] = own_a_ref[:full]

    return seq(body, [("v", t) for t in (in_a, in_b, own_a, own_b)],
               [("v", (count,) + piece, BF) for count in (3, 4, 3)], name="lay")


def first_lay_call(seq, arrays):
    piece = arrays[0].shape[-2:]
    extra = -(-2 * ROWS // piece[0])

    def body(out0_z, in_z, own_y, in_y, in_far, keys, values, first_ref, sems):
        for start, ref in ((0, in_z), (3, own_y), (6, in_y), (9, in_far), (13, out0_z)):
            first_ref[start:start + ref.shape[0]] = ref[...]
        both = jnp.concatenate([keys[...], values[...]], axis=0)
        for i in range(extra):
            rows = min(piece[0], 2 * ROWS - i * piece[0])
            first_ref[16 + i, :rows] = both[i * piece[0]:i * piece[0] + rows]

    return seq(body, [("v", t) for t in arrays], [("v", (16 + extra,) + piece, BF)], name="lay")


def far_body(first_ref, keys, values, sems):
    rows, count = first_ref.shape[1], first_ref.shape[0] - 16
    both = first_ref[16:].reshape(count * rows, D)
    keys[...] = both[:ROWS]
    values[...] = both[ROWS:2 * ROWS]


def last_body(own_y, common_y, own_yx, out_ref, sems):
    out_ref[:, 0] = own_y[...]
    out_ref[:, 1:3] = common_y[...]
    out_ref[:, 3] = own_yx[...]


def line_moves(ids, line, side, part, target):
    core, z_near = (ids[CORE], ids[Z_NEAR]) if side == 0 else (ids[OTHER_CORE], ids[Z_BESIDE])
    ref, start = line
    return [(ref.at[pl.ds(start, 2), part], target(z_near, pl.ds(0, 2))),
            (ref.at[start + 2, part], target(ids[Z_TWO], core))]


def in_target(dst, slot, y):
    def target(z, piece):
        return dst.at[pl.ds(slot, 2) if not isinstance(piece, jax.Array) else slot + piece, z, y]

    return target


def own_in(layer, ids, ref, dst):
    columns = [pl.ds(pl.multiple_of(ids[SLOTS + slot] * CB, CB), CB) for slot in range(NCB)]
    return [(ref.at[layer, :, columns[slot]], dst.at[slot, ids[Z], ids[Y]]) for slot in range(NCB)]


def pieces_in(layer, ids, lines, dst):
    part = pl.ds(layer * dst.shape[3], dst.shape[3])
    z, y = ids[Z], (ids[Y], ids[OTHER_Y])
    moves = []
    for side in range(2):
        core = ids[CORE] if side == 0 else ids[OTHER_CORE]
        along, across, own, far = lines[side::2]
        moves += line_moves(ids, along, side, part, in_target(dst, 0, y[0]))
        moves += line_moves(ids, across, side, part, in_target(dst, 0, y[1]))
        moves.append((own[0].at[own[1], part], dst.at[core, z, y[1]]))
        moves += line_moves(ids, far, side, part, in_target(dst, 2, y[0]))
        moves.append((far[0].at[far[1] + 3, part], dst.at[2 + core, z, y[1]]))
    return moves


def out_target(dst, y, cut=None):
    def target(z, piece):
        if not isinstance(piece, jax.Array):
            return dst.at[z, y] if cut is None else dst.at[z, y, :, cut]
        return dst.at[z, y, piece] if cut is None else dst.at[z, y, piece, cut]

    return target


def last_pieces(ids, refs, w_in, w_out):
    rows = pl.ds(0, w_in.shape[4])
    return [pair for side in range(2)
            for pair in line_moves(ids, (refs[side], 0), side, rows, in_target(w_in.at[0], 2, ids[OTHER_Y]))]


def last_pieces_more(ids, refs, w_in, w_out):
    in_y_far, second, out0_y, out1_z = refs
    rows = w_in.shape[4]
    moves = line_moves(ids, (out0_y, 0), 0, slice(None), out_target(w_out.at[0], ids[OTHER_Y]))
    moves += line_moves(ids, (second, 0), 1, pl.ds(rows, second.shape[1] - rows), out_target(w_out.at[0], ids[OTHER_Y]))
    moves += line_moves(ids, (in_y_far, 0), 0, pl.ds(rows, rows), in_target(w_in.at[1], 2, ids[OTHER_Y]))
    return moves + cut_line(ids, out1_z, 0, w_out.at[1])


def cut_line(ids, ref, side, dst):
    x, y = ids[MINE], ids[Y]
    return (line_moves(ids, (ref, 0), side, 0, out_target(dst, y, x))
            + line_moves(ids, (ref, 0), side, pl.ds(1, 2), out_target(dst, y, pl.ds(2, 2))))


def line_pieces(ids, refs, w_in):
    return line_moves(ids, (refs[0], 0), 1, pl.ds(3, 2), in_target(w_in, 2, ids[OTHER_Y]))


def cut_pieces(ids, refs, w_out):
    core_line, *refs = refs
    x, y = ids[MINE], (ids[Y], ids[OTHER_Y])
    moves = cut_line(ids, core_line, 1, w_out)
    for side in range(2):
        moves += line_moves(ids, (refs[side], 0), side, slice(None), out_target(w_out, y[0], 1 - x))
        for part, cut in ((0, x), (pl.ds(1, 2), pl.ds(2, 2)), (3, 1 - x)):
            moves += line_moves(ids, (refs[2 + side], 0), side, part, out_target(w_out, y[1], cut))
    return moves


def nothing(*_):
    return []


def plain_gather(ffn_in, ffn_out):
    whole_in = lax.all_gather(ffn_in, "dp", axis=1, tiled=True)
    whole_out = lax.all_gather(ffn_out, "dp", axis=1, tiled=True)
    return jnp.stack([whole_in[:, :, cb * CB:(cb + 1) * CB] for cb in range(NCB)], axis=1), whole_out.reshape(LAYERS, NCB, CB, D)


def local(block_input, part_lengths, query_weight, key_weight, value_weight, out_weight, down_shared, up_shared,
          scale_d, scale_b, ln_gain, ffn_in, ffn_out, out_grad):
    mine = lax.axis_index("head") // 2
    dp = lax.axis_size("dp")
    seq = Sequence(dp)
    halves = ffn_out.reshape(LAYERS, 2, ffn_out.shape[1] // 2, D)
    scales = (scale_d, scale_b)
    if dp == 8:
        rows_in, piece = ffn_in.shape[1], halves.shape[2:]
        cuts = halves.reshape(LAYERS, 2, 4, piece[0] // 4, D)
        cut = cuts.shape[3:]
        line = [(0, slice(0, 2)), (1, None)]

        own, sent, a_in, b_in, own_a, own_b = prepare_call(seq, block_input, out_grad, ffn_in, halves)
        in_a, in_b = both_axes(a_in, Z_ONE), both_axes(b_in, TWO)
        got, own_a, own_b = swap(sent, ACROSS), across_y(own_a), across_y(own_b)
        wk0, wv0, down, up, a_out, b_out = seq(
            None, [None], [], name="fetch",
            fetch=[(key_weight, 0), (value_weight, 0), (down_shared, None), (up_shared, None),
                   (halves, 0), (halves, ((lambda ids_ref: (0, ids_ref[CORE])), piece))])
        keys, values, inner0, lift_v0, xb, wq0 = kv_call(
            seq, 0, own, got, wk0, wv0, down, up, *scales, fetch=[(query_weight, 0)])
        q0, qt, lift_q0, wo0 = q_call(seq, 0, xb, inner0, wq0, up, *scales, fetch=[(out_weight, 0)])
        in_z, in_x, own_y = window_lay_call(seq, in_a, in_b, own_a, own_b)
        out_a, out_b = both_axes(a_out, Z_ONE), both_axes(b_out, TWO)
        in_y, in_far = across_y(in_z), swap(in_x, ACROSS)
        a_out, b_out = cut_call(seq, cuts)
        [out0_z] = lay_call(seq, [out_a, out_b], [line])
        [first] = first_lay_call(seq, [out0_z, in_z, own_y, in_y, in_far, keys, values])
        out_a, out_b = both_axes(a_out, Z_ONE), both_axes(b_out, TWO)
        out0_y, in_y_far, first = across_y(out0_z), swap(in_y, ACROSS), swap(first, BESIDE)
        kv = (keys, values, *seq(far_body, [("v", first)], [("v", (ROWS, D), BF)] * 2, name="far"))
        y, h10, *p0 = attend_call(seq, 0, part_lengths, xb, qt, kv, wo0, ln_gain)
        stored0 = (kv, q0, inner0, lift_q0, lift_v0, h10, p0, wk0, wv0, wq0, wo0)
        w_in, w_out, a, g0, wk, wv, wq, wo = seq(
            ffn_first_body,
            [None, ("v", y), ("h", ffn_in), ("h", cuts)]
            + [("v", t) for t in (in_z, in_y, in_far, own_y, first, out0_z)],
            [("v", (LAYERS, NCB, 4, 2, rows_in, CB), BF), ("v", (LAYERS, NCB, 2, 2, 4) + cut, BF)]
            + [("v", FFN_SHAPE, BF)] * 2, [], 2 * NCB + 2, "ffn_first",
            fetch=[(t, 1) for t in (key_weight, value_weight, query_weight, out_weight)])
        out1_z, out1_own, out1_common, second = cut_lay_call(seq, out_a, out_b, in_y_far, out0_y)
        out1_own_y, out1_own_x, out1_common_y = across_y(out1_own), swap(out1_own, ACROSS), across_y(out1_common)
        second, out1_z_core = swap(second, BESIDE), swap(out1_z, BESIDE)
        x, h20, w_in, w_out, a, g0 = ffn_second_call(
            seq, 0, range(NCB // 2, NCB), (last_pieces, last_pieces_more), [in_y_far, second, out0_y, out1_z],
            y, ln_gain, w_in, w_out, a, g0)
        keys, values, inner, lift_v, xb, out1_z_core = kv_call(
            seq, 1, x, got, wk, wv, down, up, *scales, through=[out1_z_core])
        [out1_own_x] = seq(None, [], [], through=[out1_own_x])
        out1_own_yx, third_core = swap(out1_own_y, ACROSS), swap(out1_own_x, BESIDE)
        kv = (keys, values, swap(keys, BESIDE), swap(values, BESIDE))
        q, qt, lift_q = q_call(seq, 1, xb, inner, wq, up, *scales)
        y, h1, *p = attend_call(seq, 1, part_lengths, x, qt, kv, wo, ln_gain)
        last, third_core = seq(last_body, [("v", t) for t in (out1_own_y, out1_common_y, out1_own_yx)],
                               [("v", (3, 4) + cut, BF)], name="lay", through=[third_core])
        last_core = swap(last, BESIDE)
        a, g, w_in = ffn_hidden_call(seq, 1, w_in, line_pieces, [out1_z_core], y)
        moves, refs = cut_pieces, [out1_z_core, out1_own_x, third_core, last, last_core]
    else:
        def pick(t, index):
            return lax.dynamic_index_in_dim(t, index, 0, keepdims=False)

        x = pick(block_input, mine)
        got = swap(jnp.stack([pick(block_input, 1 - mine), pick(out_grad, 1 - mine).astype(BF)]), ACROSS)
        blocks_in, blocks_out = plain_gather(ffn_in, ffn_out)
        for layer in range(LAYERS):
            wk, wv, down, up, wq, wo = seq(
                None, [], [], name="fetch",
                fetch=[(key_weight, layer), (value_weight, layer), (down_shared, None), (up_shared, None),
                       (query_weight, layer), (out_weight, layer)])
            keys, values, inner, lift_v, xb = kv_call(seq, layer, x, got, wk, wv, down, up, *scales)
            kv = (keys, values, swap(keys, BESIDE), swap(values, BESIDE))
            q, qt, lift_q = q_call(seq, layer, xb, inner, wq, up, *scales)
            y, h1, *p = attend_call(
                seq, layer, part_lengths, xb if layer == 0 else x, qt, kv, wo, ln_gain)
            if layer == 0:
                a, g0 = seq(None, [], [("v", FFN_SHAPE, BF)] * 2)
                w_in, w_out = seq(None, [], [], name="fetch", fetch=[(blocks_in, None), (blocks_out, None)])
                x, h20, w_in, w_out, a, g0 = ffn_second_call(
                    seq, 0, range(NCB), (nothing, nothing), [], y, ln_gain, w_in, w_out, a, g0)
                stored0 = (kv, q, inner, lift_q, lift_v, h1, p, wk, wv, wq, wo)
        a, g, w_in = ffn_hidden_call(seq, 1, w_in, nothing, [], y)
        moves, refs = nothing, []
    output, other_output, dh, w_out = ffn_both_call(seq, 1, w_in, w_out, a, g, moves, refs, y, h1, ln_gain, got, out_grad)
    own, send, ds = attend_back_call(seq, dh, wo, q, kv, p)
    got = swap(send, BESIDE)
    dx, dub, dk, gd_q, gb_q = dq_call(seq, 1, dh, ds, q, kv, lift_q, inner, wq, up, *scales)
    dub, dv, sums = dv_call(
        seq, 1, dub, own, got, lift_v, inner, up, *scales, gd_q, gb_q, jnp.zeros((4 * LAYERS, RANK), F32))
    [cotangent] = dx_call(seq, 1, dx, dub, dk, got, dv, wk, wv, down)
    kv, q, inner, lift_q, lift_v, h1, p, wk, wv, wq, wo = stored0
    [dh] = ffn_back_call(seq, 0, cotangent, h20, g0, h1, ln_gain, w_in, w_out)
    own, send, ds, other_output = attend_back_call(seq, dh, wo, q, kv, p, through=[other_output])
    got, other_output = swap(send, BESIDE), swap(other_output, ACROSS)
    dx, dub, dk, gd_q, gb_q = dq_call(seq, 0, dh, ds, q, kv, lift_q, inner, wq, up, *scales)
    dub, dv, sums = dv_call(seq, 0, dub, own, got, lift_v, inner, up, *scales, gd_q, gb_q, sums)
    if dp == 8:
        [sums] = add_call(seq, sums, swap(sums, BESIDE))
        parts = [both_axes(sums, BOTH_SWAP), swap(sums, ACROSS), across_y(sums)]
        rows, last_rows = dx_call(seq, 0, dx, dub, dk, got, dv, wk, wv, down)
        sums, last_rows = add_call(seq, sums, *parts, through=[last_rows])
        got = swap(last_rows, ACROSS)
        parts = [both_axes(sums, along) for along in Z_ALL]
    else:
        rows, last_rows = dx_call(seq, 0, dx, dub, dk, got, dv, wk, wv, down)
        got = swap(last_rows, ACROSS)
        sums, parts = lax.psum(sums, ("dp", "head")), []
    block_output, input_grad = store_call(seq, output, other_output, rows, got)
    grad_d, grad_b = finish_call(seq, [sums, *parts])
    return block_output, input_grad, grad_d, grad_b


def solution(mesh):
    both = P(None, ("dp", "head"), None)
    in_specs = (both, P(None, "dp", None), P(), P(), P(), P(), P(), P(), P(), P(), P(),
                P(None, "dp", None), P(None, "dp", None), both)
    out_specs = (both, both, P(), P())
    return jax.shard_map(local, mesh=mesh, in_specs=in_specs, out_specs=out_specs, check_vma=False)
```

```python
import functools

import jax
import jax.numpy as jnp
from jax import lax
from jax.experimental import pallas as pl
from jax.experimental.pallas import tpu as pltpu
from jax.sharding import PartitionSpec as P

D = 768
HEADS = 12
HEAD_DIM = 64
FF = 3072
RANK = 1024
LEN = 512
LAYERS = 2
PAIRS = HEADS // 2
PAIR = 2 * HEAD_DIM
BLOCK = LEN // 4
ROWS = 2 * BLOCK
CB = D
NCB = FF // CB
SCALE = HEAD_DIM ** (-0.5)
BF = jnp.bfloat16
F32 = jnp.float32
MIB = 1 << 20

COLOURS = {"v": pltpu.VMEM, "h": pltpu.HBM}
SPACES = {
    "v": pl.BlockSpec(memory_space=pltpu.VMEM),
    "h": pl.BlockSpec(memory_space=pltpu.HBM),
    "s": pl.BlockSpec(memory_space=pltpu.SMEM),
    "a": pl.BlockSpec(memory_space=pl.ANY),
}


HERE, CORE, MINE, Z, Y, OTHER_Y, Z_TWO, Z_NEAR, Z_BESIDE, OTHER_CORE = range(10)
SLOTS, BLOCKS = 10, 14


def indices(dp):
    here, place = lax.axis_index("head"), lax.axis_index("dp")
    mine, core = lax.div(here, 2), lax.rem(here, 2)
    z, y = lax.div(place, 2), lax.rem(place, 2)
    line = [z, y, 1 - y] + [lax.rem(z + step, 4) for step in (2, 3 + 2 * core, 1 + 2 * core)]
    blocks = [here, here ^ 2, here ^ 1, here ^ 3]
    if dp == 8:
        slots = [2 * mine, 2 * mine + 1, 2 - 2 * mine, 3 - 2 * mine]
    else:
        slots = list(range(NCB))
    return [here, core, mine] + line + [1 - core] + slots + blocks


def dot(left, right):
    return jnp.dot(left, right, preferred_element_type=F32)


def dot_nt(left, right):
    return lax.dot_general(left, right, (((1,), (1,)), ((), ())), preferred_element_type=F32)


def normed(t):
    centred = t - jnp.mean(t, axis=-1, keepdims=True)
    inverse = lax.rsqrt(jnp.mean(centred * centred, axis=-1, keepdims=True) + 1e-05)
    return centred * inverse, inverse


def norm_back(t, gain, cotangent):
    unit, inverse = normed(t)
    scaled = cotangent * gain
    mean_e = jnp.mean(scaled, axis=-1, keepdims=True)
    mean_en = jnp.mean(scaled * unit, axis=-1, keepdims=True)
    return inverse * (scaled - mean_e - unit * mean_en)


class Copies:
    def __init__(self, sems, first=0):
        self.sems, self.count = sems, first

    def __call__(self, src, dst):
        copy = pltpu.make_async_copy(src, dst, self.sems.at[self.count])
        self.count += 1
        copy.start()
        return copy


class Sequence:
    def __init__(self, dp):
        self.dp, self.token = dp, None

    def __call__(self, body, ins, outs, scratch=(), copies=0, name="keep", fetch=(), fill=(), fill_hbm=(), through=(), limit=8, save=(), cost=0.001):
        handed = [pltpu.with_memory_space_constraint(t, pltpu.VMEM) for t in fill]
        handed += [pltpu.with_memory_space_constraint(t, pltpu.HBM) for t in fill_hbm]
        handed += list(through)
        if self.token is not None:
            handed.append(pltpu.with_memory_space_constraint(self.token, pltpu.HBM))
        fetched = [(t.shape if part is None else t.shape[1:] if isinstance(part, int) else part[1], t.dtype)
                   for t, part in fetch]
        wants = [i for i, entry in enumerate(ins) if entry is None]
        ins = [entry for entry in ins if entry is not None]
        n_in, n_fetch, n_hand, n_fill = len(ins), len(fetch), len(handed), len(fill) + len(fill_hbm)
        n_out, n_save = len(outs), len(save)
        first = self.token is None

        def whole(*refs):
            refs = list(refs)
            in_refs, fetch_refs = refs[:n_in], refs[n_in:n_in + n_fetch]
            for i in wants:
                in_refs.insert(i, indices(self.dp))
            refs = refs[n_in + n_fetch:]
            refs = refs[n_hand:]
            out_refs, fetch_outs = refs[:n_out], refs[n_out:n_out + n_fetch]
            refs = refs[n_out + n_fetch:]
            fill_refs = refs[:n_fill]
            save_refs = refs[n_hand + first:][:n_save]
            refs = refs[n_hand + first + n_save:]
            scratch_refs, sems = refs[:len(scratch)], refs[len(scratch)]
            copy = Copies(sems, copies)
            waits = []
            for (_, part), source, target in zip(fetch, fetch_refs, fetch_outs, strict=True):
                if part is not None:
                    source = source.at[part if isinstance(part, int) else part[0](in_refs[0])]
                waits.append(copy(source, target))
            for place, target in zip(save, save_refs, strict=True):
                waits.append(copy(in_refs[place], target))
            if body is not None:
                body(*in_refs, *fill_refs, *out_refs, *scratch_refs, sems)
            for wait in waits:
                wait.wait()

        shapes = [COLOURS[space](shape, dtype) for space, shape, dtype in outs]
        shapes += [pltpu.VMEM(shape, dtype) for shape, dtype in fetched]
        shapes += [pltpu.VMEM(t.shape, t.dtype) for t in fill] + [pltpu.HBM(t.shape, t.dtype) for t in fill_hbm]
        shapes += [jax.ShapeDtypeStruct(t.shape, t.dtype) for t in through]
        shapes += [pltpu.HBM((8, 128), F32)]
        shapes += [pltpu.HBM(ins[place][1].shape, ins[place][1].dtype) for place in save]
        results = pl.pallas_call(
            whole,
            out_shape=tuple(shapes),
            in_specs=[SPACES[space] for space, _ in ins] + [SPACES["h"]] * n_fetch + [SPACES["v"]] * len(fill)
            + [SPACES["h"]] * len(fill_hbm) + [SPACES["a"]] * (n_hand - n_fill),
            out_specs=tuple([SPACES[space] for space, _, _ in outs] + [SPACES["v"]] * (n_fetch + len(fill))
                            + [SPACES["h"]] * len(fill_hbm) + [SPACES["a"]] * (n_hand - n_fill + first) + [SPACES["h"]] * n_save),
            scratch_shapes=[pltpu.VMEM(shape, dtype) for shape, dtype in scratch]
            + [pltpu.SemaphoreType.DMA((copies + n_fetch + n_save + 1,))],
            input_output_aliases={n_in + n_fetch + i: n_out + n_fetch + i for i in range(n_hand)},
            compiler_params=pltpu.CompilerParams(vmem_limit_bytes=limit * MIB),
            cost_estimate=pl.CostEstimate(
                flops=int(cost * 1e9), bytes_accessed=int(cost * 3e6), transcendentals=0),
            name=name,
        )(*[pltpu.with_memory_space_constraint(t, COLOURS[space]) if space in COLOURS else t for space, t in ins],
          *[pltpu.with_memory_space_constraint(t, pltpu.HBM) for t, _ in fetch],
          *handed)
        results = list(results)
        split = n_out + n_fetch + n_fill + len(through)
        self.token = results[split]
        return results[:split] + results[split + 1:]


def kv_body(layer, x_ref, got_ref, wk, wv, down, up, sd_ref, sb_ref, *rest):
    keys, values, inner_out, lift_out, xb_ref, _ = rest
    if layer == 0:
        xb_ref[:BLOCK] = x_ref[...]
        xb_ref[BLOCK:] = got_ref[0]
    else:
        xb_ref[...] = x_ref[...].astype(BF)
    xb = xb_ref[...]
    inner = dot(xb, down[...])
    inner_out[...] = inner.astype(BF)
    lift = dot((sd_ref[layer, 1:2, :] * inner).astype(BF), up[...])
    lift_out[...] = lift.astype(BF)
    values[...] = (dot(xb, wv[...]) + sb_ref[layer, 1:2, :] * lift).astype(BF)
    keys[...] = dot(xb, wk[...]).astype(BF)


def kv_call(seq, layer, x, got, wk, wv, down, up, sd, sb, **extra):
    return seq(
        functools.partial(kv_body, layer),
        [("v", t) for t in (x, got, wk, wv, down, up, sd, sb)],
        [("v", (ROWS, D), BF)] * 2 + [("v", (ROWS, RANK), BF), ("v", (ROWS, D), BF), ("v", (ROWS, D), BF)],
        name="keys_values", **extra)


def q_body(layer, x_ref, inner, wq, up, sd_ref, sb_ref, q_ref, qt_ref, lift_out, sems):
    lift = dot((sd_ref[layer, 0:1, :] * inner[...].astype(F32)).astype(BF), up[...])
    lift_out[...] = lift.astype(BF)
    q = (dot(x_ref[...], wq[...]) + sb_ref[layer, 0:1, :] * lift).astype(BF)
    q_ref[...] = q
    qt_ref[...] = (q * SCALE).T


def q_call(seq, layer, x, inner, wq, up, sd, sb, **extra):
    return seq(
        functools.partial(q_body, layer),
        [("v", x), ("v", inner), ("v", wq), ("v", up), ("v", sd), ("v", sb)],
        [("v", (ROWS, D), BF), ("v", (D, ROWS), BF), ("v", (ROWS, D), BF)],
        name="queries", **extra)


def split_heads(t):
    zero = jnp.zeros((HEAD_DIM, t.shape[1]), t.dtype)
    first = jnp.concatenate([t[:HEAD_DIM], zero], axis=0)
    second = jnp.concatenate([zero, t[HEAD_DIM:]], axis=0)
    return jnp.concatenate([first, second], axis=1)


def join_heads(t):
    n = t.shape[1] // 2
    return jnp.concatenate([t[:HEAD_DIM, :n], t[HEAD_DIM:, n:]], axis=0)


def stack_heads(t):
    lane = lax.broadcasted_iota(jnp.int32, (1, PAIR), 1)
    first = (lane < HEAD_DIM).astype(F32).astype(BF)
    second = (lane >= HEAD_DIM).astype(F32).astype(BF)
    return jnp.concatenate([t * first, t * second], axis=0)


def rows_of(near, far, cols):
    return jnp.concatenate([near[:, cols], far[:, cols]], axis=0)


def attend_body(layer, ids, lengths, x_ref, qt_ref, wo, gain_ref, keys, values, far_keys, far_values,
                y_ref, h_ref, e_ref, factor_ref, ctx_t_ref, ctx, sems):
    row = lax.broadcasted_iota(jnp.int32, (BLOCK, 2 * ROWS), 0)
    counts = lengths[ids[MINE]]
    live = counts[:, :1] + counts[:, 1:] + 4
    limits = [live - BLOCK * ids[BLOCKS + b] for b in range(4)]
    for pair in range(PAIRS):
        cols = slice(pair * PAIR, (pair + 1) * PAIR)
        raw = dot(rows_of(keys, far_keys, cols), split_heads(qt_ref[cols, :]))
        scores = jnp.concatenate(
            [jnp.where(row < limits[b], raw[b * BLOCK:(b + 1) * BLOCK], -1000000000.0) for b in range(4)],
            axis=0,
        )
        grown = jnp.exp(scores - jnp.max(scores, axis=0, keepdims=True))
        factor = 1.0 / jnp.sum(grown, axis=0, keepdims=True)
        factor_ref[pair:pair + 1, :] = factor
        e_ref[pair] = grown.astype(BF)
        ctx_t = join_heads(dot(rows_of(values, far_values, cols).T, e_ref[pair]) * factor)
        ctx_t_ref[cols, :] = ctx_t
        ctx[:, cols] = ctx_t.astype(BF).T
    h = x_ref[...].astype(F32) + dot(ctx[...], wo[...])
    h_ref[...] = h
    y_ref[...] = normed(h)[0] * gain_ref[layer, 0:1, :]


def attend_call(seq, layer, lengths, x, qt, kv, wo, gain, **extra):
    return seq(
        functools.partial(attend_body, layer),
        [None] + [("v", t) for t in (lengths, x, qt, wo, gain, *kv)],
        [("v", (ROWS, D), F32), ("v", (ROWS, D), F32), ("v", (PAIRS, LEN, 2 * ROWS), BF), ("v", (PAIRS, 2 * ROWS), F32),
         ("v", (D, ROWS), F32)],
        [((ROWS, D), BF)], name="attention", **extra)


def move(pairs):
    for source, target in pairs:
        target[...] = source[...].reshape(target.shape)


def ffn_hidden(yb, w_in, a_ref, g_ref, slots):
    for slot in slots:
        z = dot(yb, w_in[slot].reshape(D, CB))
        cdf = 0.5 * (1.0 + lax.erf(z * (0.5 ** 0.5)))
        g_ref[slot] = (cdf + z * (jnp.exp(-0.5 * z * z) * 0.3989422804014327)).astype(BF)
        a_ref[slot] = (z * cdf).astype(BF)


def ffn_result(ids, total, a_ref, w_out, y=None):
    size = CB if y is None else CB // 2
    for slot in range(NCB):
        if y is None:
            hidden, rows = a_ref[slot], w_out[ids[SLOTS + slot]]
        else:
            hidden = a_ref[slot, :, pl.ds(pl.multiple_of(y * size, size), size)]
            rows = w_out[ids[SLOTS + slot], y]
        total = total + dot(hidden, rows.reshape(size, D))
    return total


def ffn_backward(layer, ids, c, h2, g_ref, h1, gain_ref, w_in, w_out, dh_ref):
    dh2 = norm_back(h2, gain_ref[layer, 1:2, :], c)
    dfb = dh2.astype(BF)
    total = dh2
    for slot in range(NCB):
        da = dot_nt(dfb, w_out[ids[SLOTS + slot]].reshape(CB, D))
        dz = (g_ref[slot].astype(F32) * da).astype(BF)
        total = total + dot_nt(dz, w_in[slot].reshape(D, CB))
    dh1 = norm_back(h1, gain_ref[layer, 0:1, :], total)
    dh_ref[...] = dh1


FFN_SHAPE = (NCB, ROWS, CB)


def ffn_first_body(ids, y_ref, in_ref, cut_ref, in_z, in_y, in_far, own_y, first, out0_z,
                   w_in, w_out, a_ref, g_ref, sems):
    copy = Copies(sems)
    w_in = [w_in.at[layer] for layer in range(LAYERS)]
    w_out = [w_out.at[layer] for layer in range(LAYERS)]
    owns = [[copy(source, target) for source, target in own_in(layer, ids, in_ref, w_in[layer])] for layer in range(LAYERS)]
    own_out = [copy(cut_ref.at[layer], w_out[layer].at[ids[Z], ids[Y]]) for layer in range(LAYERS)]
    lines = [(in_z, 0), (first, 0), (in_y, 0), (first, 6), (own_y, 0), (first, 3), (in_far, 0), (first, 9)]
    move(pieces_in(0, ids, lines, w_in[0]))
    for wait in owns[0]:
        wait.wait()
    ffn_hidden(y_ref[...].astype(BF), w_in[0], a_ref, g_ref, range(NCB // 2))
    move(pieces_in(1, ids, lines, w_in[1]))
    for side, line in enumerate([(out0_z, 0), (first, 13)]):
        move(line_moves(ids, line, side, slice(None), out_target(w_out[0], ids[Y])))
    for side, (ref, start) in enumerate([(own_y, 0), (first, 3)]):
        core = ids[CORE] if side == 0 else ids[OTHER_CORE]
        for layer in range(LAYERS):
            move([(ref.at[start + 1 + layer], w_out[layer].at[ids[Z], ids[OTHER_Y], core])])
    for wait in owns[1] + own_out:
        wait.wait()


def ffn_second_body(layer, slots, moves, n_refs, ids, y_ref, gain_ref, *rest):
    refs, rest = rest[:n_refs], rest[n_refs:]
    w_in, w_out, a_ref, g_ref, x_ref, h_ref, _ = rest
    move(moves[0](ids, refs, w_in, w_out))
    ffn_hidden(y_ref[...].astype(BF), w_in.at[layer], a_ref, g_ref, slots)
    move(moves[1](ids, refs, w_in, w_out))
    h_ref[...] = ffn_result(ids, y_ref[...], a_ref, w_out.at[layer])
    x_ref[...] = normed(h_ref[...])[0] * gain_ref[layer, 1:2, :]


def ffn_second_call(seq, layer, slots, moves, refs, y, gain, w_in, w_out, a, g, **extra):
    return seq(
        functools.partial(ffn_second_body, layer, slots, moves, len(refs)),
        [None, ("v", y), ("v", gain)] + [("v", t) for t in refs],
        [("v", (ROWS, D), F32), ("v", (ROWS, D), F32)], name="ffn", fill=[w_in, w_out, a, g], **extra)


FFN_SHAPE = (NCB, ROWS, CB)


def ffn_hidden_body(layer, slots, moves, n_refs, ids, y_ref, *rest):
    refs, (w_in, a_ref, g_ref, _) = rest[:n_refs], rest[n_refs:]
    move(moves(ids, refs, w_in.at[layer]))
    ffn_hidden(y_ref[...].astype(BF), w_in.at[layer], a_ref, g_ref, slots)


def ffn_hidden_call(seq, layer, slots, w_in, moves, refs, y, **extra):
    return seq(
        functools.partial(ffn_hidden_body, layer, slots, moves, len(refs)),
        [None, ("v", y)] + [("v", t) for t in refs], [("v", FFN_SHAPE, BF)] * 2, name="ffn_hidden", fill=[w_in], **extra)


def ffn_near_body(layer, slots, moves, n_refs, ids, y_ref, w_in, *rest):
    refs, (w_out, a_ref, g_ref, near_ref, _) = rest[:n_refs], rest[n_refs:]
    ffn_hidden(y_ref[...].astype(BF), w_in.at[layer], a_ref, g_ref, slots)
    w_out = w_out.at[layer]
    move(moves(ids, refs, w_out))
    near_ref[...] = ffn_result(ids, y_ref[...], a_ref, w_out, ids[Y])


def ffn_near_call(seq, layer, slots, w_in, w_out, a, g, moves, refs, y, **extra):
    return seq(
        functools.partial(ffn_near_body, layer, slots, moves, len(refs)),
        [None, ("v", y), ("v", w_in)] + [("v", t) for t in refs],
        [("v", (ROWS, D), F32)], name="ffn_near", fill=[w_out, a, g], **extra)


def ffn_both_body(layer, moves, n_refs, near, ids, y_ref, h1, gain_ref, got_ref, w_in, a_ref, g_ref, c_ref, *rest):
    refs, rest = rest[:n_refs], rest[n_refs:]
    w_out, x_ref, send_ref, dh_ref, c, sems = rest
    own = Copies(sems)(c_ref.at[ids[MINE]], c.at[pl.ds(0, BLOCK)])
    w_in, w_out = w_in.at[layer], w_out.at[layer]
    move(moves(ids, refs, w_out))
    h2 = ffn_result(ids, y_ref[...], a_ref, w_out, ids[OTHER_Y] if near else None)
    dh_ref[...] = h2
    x = normed(h2)[0] * gain_ref[layer, 1:2, :]
    x_ref[...] = x[:BLOCK].astype(BF)
    send_ref[...] = x[BLOCK:].astype(BF)
    own.wait()
    c[BLOCK:] = got_ref[1].astype(F32)
    ffn_backward(layer, ids, c[...], dh_ref[...], g_ref, h1[...], gain_ref, w_in, w_out, dh_ref)


def ffn_both_call(seq, layer, w_in, w_out, a, g, moves, refs, near, y, h1, gain, got, c, **extra):
    return seq(
        functools.partial(ffn_both_body, layer, moves, len(refs), near),
        [None] + [("v", t) for t in (y, h1, gain, got, w_in, a, g)] + [("h", c)] + [("v", t) for t in refs],
        [("v", (BLOCK, D), BF), ("v", (BLOCK, D), BF), ("v", (ROWS, D), F32)],
        [((ROWS, D), F32)], 1, "ffn_both", fill=[w_out], **extra)


def ffn_back_body(layer, ids, c_ref, h2, g, h1, gain_ref, w_in, w_out, dh_ref, sems):
    ffn_backward(layer, ids, c_ref[...], h2[...], g, h1[...], gain_ref, w_in.at[layer], w_out.at[layer], dh_ref)


def ffn_back_call(seq, layer, c, h2, g, h1, gain, w_in, w_out, **extra):
    return seq(
        functools.partial(ffn_back_body, layer),
        [None] + [("v", t) for t in (c, h2, g, h1, gain, w_in, w_out)],
        [("v", (ROWS, D), F32)], name="ffn_back", **extra)


def attend_back_body(dh_ref, wo, q, factor_ref, ctx_t_ref, keys, values, far_keys, far_values,
                     e_ref, own_ref, send_ref, dctx_ref, sems):
    dctx_ref[...] = dot_nt(dh_ref[...].astype(BF), wo[...]).astype(BF)
    for pair in range(PAIRS):
        cols = slice(pair * PAIR, (pair + 1) * PAIR)
        vcols = slice(D + pair * PAIR, D + (pair + 1) * PAIR)
        factor = factor_ref[pair:pair + 1, :]
        scaled = (split_heads(dctx_ref[:, cols].T).astype(F32) * factor).astype(BF)
        inner = jnp.sum(scaled.astype(F32) * split_heads(ctx_t_ref[cols, :]), axis=0, keepdims=True)
        e = e_ref[pair]
        ds = (e.astype(F32) * (dot(rows_of(values, far_values, cols), scaled) - inner)).astype(BF)
        dv = dot(e, scaled.T)
        dk = dot(ds[ROWS:], stack_heads(q[:, cols])) * SCALE
        own_ref[:, cols] = dv[:ROWS]
        send_ref[:, cols] = dk.astype(BF)
        send_ref[:, vcols] = dv[ROWS:].astype(BF)
        e_ref[pair] = ds


def attend_back_call(seq, dh, wo, q, kv, weights, **extra):
    e, *rest = weights
    return seq(
        attend_back_body,
        [("v", t) for t in (dh, wo, q, *rest, *kv)],
        [("v", (ROWS, D), F32), ("v", (ROWS, 2 * D), BF)],
        [((ROWS, D), BF)], name="attention_back", fill=[e], **extra)


def dq_body(layer, dh_ref, ds_ref, q, keys, far_keys, lift, inner, wq, up, sd_ref, sb_ref,
            dx_ref, dub_ref, dk_ref, gd_ref, gb_ref, dq_ref, sems):
    for pair in range(PAIRS):
        cols = slice(pair * PAIR, (pair + 1) * PAIR)
        dq_t = join_heads(dot(rows_of(keys, far_keys, cols).T, ds_ref[pair])) * SCALE
        dq_ref[:, cols] = dq_t.T.astype(BF)
        dk_ref[:, cols] = dot(ds_ref[pair, :ROWS], stack_heads(q[:, cols])) * SCALE
    dq = dq_ref[...]
    dqf = dq.astype(F32)
    gb_ref[...] = jnp.sum(dqf * lift[...].astype(F32), axis=0, keepdims=True)
    dpq = dot_nt((sb_ref[layer, 0:1, :] * dqf).astype(BF), up[...])
    gd_ref[...] = jnp.sum(dpq * inner[...].astype(F32), axis=0, keepdims=True)
    dub_ref[...] = sd_ref[layer, 0:1, :] * dpq
    dx_ref[...] = dh_ref[...] + dot_nt(dq, wq[...])


def dq_call(seq, layer, dh, ds, q, kv, lift, inner, wq, up, sd, sb, **extra):
    return seq(
        functools.partial(dq_body, layer),
        [("v", t) for t in (dh, ds, q, kv[0], kv[2], lift, inner, wq, up, sd, sb)],
        [("v", (ROWS, D), F32), ("v", (ROWS, RANK), F32), ("v", (ROWS, D), F32), ("v", (1, RANK), F32), ("v", (1, D), F32)],
        [((ROWS, D), BF)], name="queries_back", **extra)


def dv_body(layer, dub_ref, own_ref, got_ref, lift, inner, up, sd_ref, sb_ref, gdq_ref, gbq_ref, before_ref,
            dub_out, dv_ref, sums_ref, sems):
    sums_ref[...] = before_ref[...]
    sums_ref[4 * layer:4 * layer + 1, :] = gdq_ref[...]
    sums_ref[4 * layer + 2:4 * layer + 3, :D] = gbq_ref[...]
    dv = (own_ref[...] + got_ref[:, D:].astype(F32)).astype(BF)
    dv_ref[...] = dv
    dvf = dv.astype(F32)
    sums_ref[4 * layer + 3:4 * layer + 4, :D] = jnp.sum(dvf * lift[...].astype(F32), axis=0, keepdims=True)
    dpv = dot_nt((sb_ref[layer, 1:2, :] * dvf).astype(BF), up[...])
    sums_ref[4 * layer + 1:4 * layer + 2, :] = jnp.sum(dpv * inner[...].astype(F32), axis=0, keepdims=True)
    dub_out[...] = (dub_ref[...] + sd_ref[layer, 1:2, :] * dpv).astype(BF)


def dv_call(seq, layer, dub, own, got, lift, inner, up, sd, sb, gd, gb, before, **extra):
    return seq(
        functools.partial(dv_body, layer),
        [("v", t) for t in (dub, own, got, lift, inner, up, sd, sb, gd, gb, before)],
        [("v", (ROWS, RANK), BF), ("v", (ROWS, D), BF), ("v", (4 * LAYERS, RANK), F32)],
        name="values_back", **extra)


def dx_body(layer, dx_ref, dub_ref, dk_ref, got_ref, dv_ref, wk, wv, down, *rest):
    total = dx_ref[...] + dot_nt(dub_ref[...], down[...])
    total = total + dot_nt(dv_ref[...], wv[...])
    dk = (dk_ref[...] + got_ref[:, :D].astype(F32)).astype(BF)
    total = total + dot_nt(dk, wk[...])
    if layer == 0:
        own_ref, send_ref, _ = rest
        own_ref[...] = total[:BLOCK]
        send_ref[...] = total[BLOCK:].astype(BF)
    else:
        rest[0][...] = total


def dx_call(seq, layer, dx, dub, dk, got, dv, wk, wv, down, **extra):
    return seq(
        functools.partial(dx_body, layer),
        [("v", t) for t in (dx, dub, dk, got, dv, wk, wv, down)],
        [("v", (BLOCK, D), F32), ("v", (BLOCK, D), BF)] if layer == 0 else [("v", (ROWS, D), F32)],
        name="input_back", **extra)


def add_call(seq, *terms, **extra):
    def body(*refs):
        total = refs[0][...]
        for ref in refs[1:len(terms)]:
            total = total + ref[...]
        refs[len(terms)][...] = total

    return seq(body, [("v", t) for t in terms], [("v", terms[0].shape, F32)], name="add", **extra)


def store_call(seq, output, other_output, rows, got):
    def body(ids_ref, output_ref, other_ref, rows_ref, got_ref, block_ref, grad_ref, wide, sems):
        copy = Copies(sems)
        mine = ids_ref[MINE]
        stores = [copy(rows_ref, grad_ref.at[mine]), copy(output_ref, block_ref.at[mine]), copy(other_ref, block_ref.at[1 - mine])]
        wide[...] = got_ref[...].astype(F32)
        stores.append(copy(wide, grad_ref.at[1 - mine]))
        for store in stores:
            store.wait()

    return seq(body, [None] + [("v", t) for t in (output, other_output, rows, got)],
               [("h", (2,) + t.shape, t.dtype) for t in (output, rows)], [(got.shape, F32)], 4, "store")


def finish_call(seq, terms):
    def body(*refs):
        *terms_refs, gd_out, gb_out, gd_ref, gb_ref, sems = refs
        copy = Copies(sems)
        total = terms_refs[0][...]
        for ref in terms_refs[1:]:
            total = total + ref[...]
        for layer in range(LAYERS):
            gd_ref[layer] = total[4 * layer:4 * layer + 2]
            gb_ref[layer] = total[4 * layer + 2:4 * layer + 4, :D]
        stores = [copy(gd_ref, gd_out), copy(gb_ref, gb_out)]
        for store in stores:
            store.wait()

    shapes = [((LAYERS, 2, RANK), F32), ((LAYERS, 2, D), F32)]
    return seq(body, [("v", t) for t in terms], [("h", *t) for t in shapes], shapes, 2, "finish")


def prepare_body(ids, x_ref, c_ref, in_ref, out_ref, own, sent, a_in, b_in, own_a, own_b, c_send, sems):
    copy = Copies(sems)
    here, core, mine = ids[HERE], ids[CORE], ids[MINE]
    rows = in_ref.shape[1]

    def columns(block):
        return pl.ds(pl.multiple_of(block * CB, CB), CB)

    waits = [copy(c_ref.at[1 - mine], c_send)]
    for layer in range(LAYERS):
        part = pl.ds(layer * rows, rows)
        for q in range(2):
            waits.append(copy(in_ref.at[layer, :, columns(2 * mine + q)], a_in.at[q, part]))
        waits.append(copy(in_ref.at[layer, :, columns(here)], b_in.at[part]))
        waits.append(copy(in_ref.at[layer, :, columns(here)], own_a.at[part]))
    piece = own_a.shape[0] - rows
    half = pl.ds(0, rows), pl.ds(rows, rows)
    waits.append(copy(out_ref.at[0, core, half[0]], own_a.at[pl.ds(piece, rows)]))
    waits.append(copy(out_ref.at[0, core, half[1]], own_b.at[half[0]]))
    waits.append(copy(out_ref.at[1, core], own_b.at[pl.ds(rows, piece)]))
    waits += [copy(x_ref.at[1 - mine], sent.at[0]), copy(x_ref.at[mine], own)]
    waits[0].wait()
    sent[1] = c_send[...].astype(BF)
    for wait in waits[1:]:
        wait.wait()


def prepare_call(seq, x, c, ffn_in, halves, **extra):
    rows = (BLOCK, D)
    piece = halves.shape[2:]
    return seq(
        prepare_body,
        [None, ("h", x), ("h", c), ("h", ffn_in), ("h", halves)],
        [("v", rows, BF), ("v", (2,) + rows, BF), ("v", (2,) + piece, BF), ("v", piece, BF)]
        + [("v", (piece[0] * 3 // 2,) + piece[1:], BF)] * 2,
        [(rows, F32)], 6 + 4 * LAYERS, "prepare", **extra)


def everywhere(target):
    pairs = []
    for z in range(4):
        for y in range(2):
            for head in range(4):
                z_to, y_to, head_to = target(z, y, head)
                pairs.append(((2 * z + y) * 4 + head, (2 * (z_to % 4) + y_to) * 4 + head_to))
    return pairs


Z_ONE = everywhere(lambda z, y, head: (z + 1 - 2 * (head % 2), y, head))
TWO = everywhere(lambda z, y, head: (z + 2, y, head))
Y_SWAP = [(i, i ^ 1) for i in range(8)]
BOTH_SWAP = everywhere(lambda z, y, head: (z, 1 - y, head ^ 2))
Z_ALL = [everywhere(lambda z, y, head, other=other: (z ^ other, y, head)) for other in (3, 2, 1)]
ACROSS = [(i, i ^ 2) for i in range(4)]
BESIDE = [(i, i ^ 1) for i in range(4)]


def swap(t, pairs):
    return lax.ppermute(t, "head", pairs)


def both_axes(t, pairs):
    return lax.ppermute(t, ("dp", "head"), pairs)


def across_y(t):
    return lax.ppermute(t, "dp", Y_SWAP)


def lay_call(seq, arrays, outs, **extra):
    piece = arrays[0].shape[-2:]

    def length(part):
        return 1 if part is None else part.stop - part.start

    def body(*refs):
        for out, result in zip(outs, refs[len(arrays):], strict=False):
            start = 0
            for index, part in out:
                stop = start + length(part)
                result[start:stop] = refs[index][...][None] if part is None else refs[index][part]
                start = stop

    shapes = [(sum(length(part) for _, part in out),) + piece for out in outs]
    return seq(body, [("v", t) for t in arrays], [("v", shape, BF) for shape in shapes], name="lay", **extra)


def cut_call(seq, cuts):
    cut = cuts.shape[3:]

    def body(ids_ref, cuts_ref, a_ref, b_ref, sems):
        copy = Copies(sems)
        waits = []
        for core, target in ((0, a_ref.at[0]), (1, a_ref.at[1]), (ids_ref[CORE], b_ref)):
            waits.append(copy(cuts_ref.at[1, core, ids_ref[MINE]], target.at[0]))
            waits.append(copy(cuts_ref.at[1, core, pl.ds(2, 2)], target.at[pl.ds(1, 2)]))
        for wait in waits:
            wait.wait()

    return seq(body, [None, ("h", cuts)], [("v", (2, 3) + cut, BF), ("v", (3,) + cut, BF)], [], 6, "cut")


def cut_lay_call(seq, out_a, out_b, in_y_far, out0_y):
    cut = out_b.shape[1:]

    def body_z(a_ref, b_ref, line_ref, sems):
        line_ref[:2] = a_ref[...]
        line_ref[2] = b_ref[...]

    [line] = seq(body_z, [("v", out_a), ("v", out_b)], [("v", (3, 3) + cut, BF)], name="lay")
    return cut_lay_rest_call(seq, line, in_y_far, out0_y)


def cut_lay_rest_call(seq, line, in_y_far, out0_y):
    cut = line.shape[2:]
    piece = out0_y.shape[1:]

    def body(z_ref, far_ref, y_ref, line_ref, own_ref, common_ref, second_ref, sems):
        rows = piece[0] // LAYERS
        line_ref[:, :3] = z_ref[...]
        line_ref[:, 3:] = far_ref[:, rows:].reshape((3, 2) + cut)
        own_ref[...] = z_ref[:, 0]
        common_ref[...] = z_ref[:, 1:]
        second_ref[:, :rows] = far_ref[:, :rows]
        second_ref[:, rows:] = y_ref[...]

    return seq(body, [("v", t) for t in (line, in_y_far, out0_y)],
               [("v", (3, 5) + cut, BF), ("v", (3,) + cut, BF), ("v", (3, 2) + cut, BF),
                ("v", (3, piece[0] // LAYERS + piece[0]) + piece[1:], BF)], name="lay")


def window_lay_call(seq, in_a, in_b, own_a, own_b):
    piece = in_b.shape

    def body(a_ref, b_ref, own_a_ref, own_b_ref, z_ref, x_ref, own_ref, sems):
        full, half = piece[0], piece[0] // 2
        own_ref[0] = own_a_ref[:full]
        own_ref[1, :half] = own_a_ref[full:]
        own_ref[1, half:] = own_b_ref[:half]
        own_ref[2] = own_b_ref[half:]
        for ref in (z_ref, x_ref):
            ref[:2] = a_ref[...]
            ref[2] = b_ref[...]
        x_ref[3] = own_a_ref[:full]

    return seq(body, [("v", t) for t in (in_a, in_b, own_a, own_b)],
               [("v", (count,) + piece, BF) for count in (3, 4, 3)], name="lay")


def first_lay_call(seq, arrays):
    piece = arrays[0].shape[-2:]
    extra = -(-2 * ROWS // piece[0])

    def body(out0_z, in_z, own_y, in_y, in_far, keys, values, first_ref, sems):
        for start, ref in ((0, in_z), (3, own_y), (6, in_y), (9, in_far), (13, out0_z)):
            first_ref[start:start + ref.shape[0]] = ref[...]
        both = jnp.concatenate([keys[...], values[...]], axis=0)
        for i in range(extra):
            rows = min(piece[0], 2 * ROWS - i * piece[0])
            first_ref[16 + i, :rows] = both[i * piece[0]:i * piece[0] + rows]

    return seq(body, [("v", t) for t in arrays], [("v", (16 + extra,) + piece, BF)], name="lay")


def far_body(first_ref, keys, values, sems):
    rows, count = first_ref.shape[1], first_ref.shape[0] - 16
    both = first_ref[16:].reshape(count * rows, D)
    keys[...] = both[:ROWS]
    values[...] = both[ROWS:2 * ROWS]


def last_body(own_y, common_y, own_yx, out_ref, sems):
    out_ref[:, 0] = own_y[...]
    out_ref[:, 1:3] = common_y[...]
    out_ref[:, 3] = own_yx[...]


def line_moves(ids, line, side, part, target):
    core, z_near = (ids[CORE], ids[Z_NEAR]) if side == 0 else (ids[OTHER_CORE], ids[Z_BESIDE])
    ref, start = line
    return [(ref.at[pl.ds(start, 2), part], target(z_near, pl.ds(0, 2))),
            (ref.at[start + 2, part], target(ids[Z_TWO], core))]


def in_target(dst, slot, y):
    def target(z, piece):
        return dst.at[pl.ds(slot, 2) if not isinstance(piece, jax.Array) else slot + piece, z, y]

    return target


def own_in(layer, ids, ref, dst):
    columns = [pl.ds(pl.multiple_of(ids[SLOTS + slot] * CB, CB), CB) for slot in range(NCB)]
    return [(ref.at[layer, :, columns[slot]], dst.at[slot, ids[Z], ids[Y]]) for slot in range(NCB)]


def pieces_in(layer, ids, lines, dst):
    part = pl.ds(layer * dst.shape[3], dst.shape[3])
    z, y = ids[Z], (ids[Y], ids[OTHER_Y])
    moves = []
    for side in range(2):
        core = ids[CORE] if side == 0 else ids[OTHER_CORE]
        along, across, own, far = lines[side::2]
        moves += line_moves(ids, along, side, part, in_target(dst, 0, y[0]))
        moves += line_moves(ids, across, side, part, in_target(dst, 0, y[1]))
        moves.append((own[0].at[own[1], part], dst.at[core, z, y[1]]))
        moves += line_moves(ids, far, side, part, in_target(dst, 2, y[0]))
        moves.append((far[0].at[far[1] + 3, part], dst.at[2 + core, z, y[1]]))
    return moves


def out_target(dst, y, cut=None):
    def target(z, piece):
        if not isinstance(piece, jax.Array):
            return dst.at[z, y] if cut is None else dst.at[z, y, :, cut]
        return dst.at[z, y, piece] if cut is None else dst.at[z, y, piece, cut]

    return target


def last_pieces(ids, refs, w_in, w_out):
    rows = pl.ds(0, w_in.shape[4])
    return [pair for side in range(2)
            for pair in line_moves(ids, (refs[side], 0), side, rows, in_target(w_in.at[0], 2, ids[OTHER_Y]))]


def last_pieces_more(ids, refs, w_in, w_out):
    in_y_far, second, out0_y, out1_z = refs
    rows = w_in.shape[4]
    moves = line_moves(ids, (out0_y, 0), 0, slice(None), out_target(w_out.at[0], ids[OTHER_Y]))
    moves += line_moves(ids, (second, 0), 1, pl.ds(rows, second.shape[1] - rows), out_target(w_out.at[0], ids[OTHER_Y]))
    moves += line_moves(ids, (in_y_far, 0), 0, pl.ds(rows, rows), in_target(w_in.at[1], 2, ids[OTHER_Y]))
    return moves + cut_line(ids, out1_z, 0, w_out.at[1])


def cut_line(ids, ref, side, dst):
    x, y = ids[MINE], ids[Y]
    return (line_moves(ids, (ref, 0), side, 0, out_target(dst, y, x))
            + line_moves(ids, (ref, 0), side, pl.ds(1, 2), out_target(dst, y, pl.ds(2, 2))))


def line_pieces(ids, refs, w_in):
    return line_moves(ids, (refs[0], 0), 1, pl.ds(3, 2), in_target(w_in, 2, ids[OTHER_Y]))


def near_pieces(ids, refs, w_out):
    core_line, *refs, last = refs
    moves = cut_line(ids, core_line, 1, w_out)
    for side in range(2):
        moves += line_moves(ids, (refs[side], 0), side, slice(None), out_target(w_out, ids[Y], 1 - ids[MINE]))
    return moves + cut_pieces(ids, [last], w_out, 0)


def cut_pieces(ids, refs, w_out, side=1):
    x, moves = ids[MINE], []
    for part, cut in ((0, x), (pl.ds(1, 2), pl.ds(2, 2)), (3, 1 - x)):
        moves += line_moves(ids, (refs[0], 0), side, part, out_target(w_out, ids[OTHER_Y], cut))
    return moves


def nothing(*_):
    return []


def plain_gather(ffn_in, ffn_out):
    whole_in = lax.all_gather(ffn_in, "dp", axis=1, tiled=True)
    whole_out = lax.all_gather(ffn_out, "dp", axis=1, tiled=True)
    return jnp.stack([whole_in[:, :, cb * CB:(cb + 1) * CB] for cb in range(NCB)], axis=1), whole_out.reshape(LAYERS, NCB, CB, D)


def local(block_input, part_lengths, query_weight, key_weight, value_weight, out_weight, down_shared, up_shared,
          scale_d, scale_b, ln_gain, ffn_in, ffn_out, out_grad):
    mine = lax.axis_index("head") // 2
    dp = lax.axis_size("dp")
    seq = Sequence(dp)
    halves = ffn_out.reshape(LAYERS, 2, ffn_out.shape[1] // 2, D)
    scales = (scale_d, scale_b)
    if dp == 8:
        rows_in, piece = ffn_in.shape[1], halves.shape[2:]
        cuts = halves.reshape(LAYERS, 2, 4, piece[0] // 4, D)
        cut = cuts.shape[3:]
        line = [(0, slice(0, 2)), (1, None)]

        own, sent, a_in, b_in, own_a, own_b = prepare_call(seq, block_input, out_grad, ffn_in, halves)
        in_a, in_b = both_axes(a_in, Z_ONE), both_axes(b_in, TWO)
        got, own_a, own_b = swap(sent, ACROSS), across_y(own_a), across_y(own_b)
        wk0, wv0, down, up, a_out, b_out = seq(
            None, [None], [], name="fetch",
            fetch=[(key_weight, 0), (value_weight, 0), (down_shared, None), (up_shared, None),
                   (halves, 0), (halves, ((lambda ids_ref: (0, ids_ref[CORE])), piece))])
        keys, values, inner0, lift_v0, xb, wq0 = kv_call(
            seq, 0, own, got, wk0, wv0, down, up, *scales, fetch=[(query_weight, 0)])
        q0, qt, lift_q0, wo0 = q_call(seq, 0, xb, inner0, wq0, up, *scales, fetch=[(out_weight, 0)])
        in_z, in_x, own_y = window_lay_call(seq, in_a, in_b, own_a, own_b)
        out_a, out_b = both_axes(a_out, Z_ONE), both_axes(b_out, TWO)
        in_y, in_far = across_y(in_z), swap(in_x, ACROSS)
        a_out, b_out = cut_call(seq, cuts)
        [out0_z] = lay_call(seq, [out_a, out_b], [line])
        [first] = first_lay_call(seq, [out0_z, in_z, own_y, in_y, in_far, keys, values])
        out_a, out_b = both_axes(a_out, Z_ONE), both_axes(b_out, TWO)
        out0_y, in_y_far, first = across_y(out0_z), swap(in_y, ACROSS), swap(first, BESIDE)
        kv = (keys, values, *seq(far_body, [("v", first)], [("v", (ROWS, D), BF)] * 2, name="far"))
        y, h10, *p0 = attend_call(seq, 0, part_lengths, xb, qt, kv, wo0, ln_gain)
        stored0 = (kv, q0, inner0, lift_q0, lift_v0, h10, p0, wk0, wv0, wq0, wo0)
        w_in, w_out, a, g0, wk, wv, wq, wo = seq(
            ffn_first_body,
            [None, ("v", y), ("h", ffn_in), ("h", cuts)]
            + [("v", t) for t in (in_z, in_y, in_far, own_y, first, out0_z)],
            [("v", (LAYERS, NCB, 4, 2, rows_in, CB), BF), ("v", (LAYERS, NCB, 2, 2, 4) + cut, BF)]
            + [("v", FFN_SHAPE, BF)] * 2, [], 2 * NCB + 2, "ffn_first",
            fetch=[(t, 1) for t in (key_weight, value_weight, query_weight, out_weight)])
        out1_z, out1_own, out1_common, second = cut_lay_call(seq, out_a, out_b, in_y_far, out0_y)
        out1_own_y, out1_own_x, out1_common_y = across_y(out1_own), swap(out1_own, ACROSS), across_y(out1_common)
        second, out1_z_core = swap(second, BESIDE), swap(out1_z, BESIDE)
        x, h20, w_in, w_out, a, g0 = ffn_second_call(
            seq, 0, range(NCB // 2, NCB), (last_pieces, last_pieces_more), [in_y_far, second, out0_y, out1_z],
            y, ln_gain, w_in, w_out, a, g0)
        keys, values, inner, lift_v, xb, out1_z_core = kv_call(
            seq, 1, x, got, wk, wv, down, up, *scales, through=[out1_z_core])
        [out1_own_x] = seq(None, [], [], through=[out1_own_x])
        out1_own_yx, third_core = swap(out1_own_y, ACROSS), swap(out1_own_x, BESIDE)
        kv = (keys, values, swap(keys, BESIDE), swap(values, BESIDE))
        q, qt, lift_q = q_call(seq, 1, xb, inner, wq, up, *scales)
        y, h1, *p = attend_call(seq, 1, part_lengths, x, qt, kv, wo, ln_gain)
        a, g, w_in = ffn_hidden_call(seq, 1, range(NCB - 1), w_in, line_pieces, [out1_z_core], y)
        last, third_core = seq(last_body, [("v", t) for t in (out1_own_y, out1_common_y, out1_own_yx)],
                               [("v", (3, 4) + cut, BF)], name="lay", through=[third_core])
        last_core = swap(last, BESIDE)
        y, w_out, a, g = ffn_near_call(
            seq, 1, range(NCB - 1, NCB), w_in, w_out, a, g, near_pieces, [out1_z_core, out1_own_x, third_core, last], y)
        moves, refs = cut_pieces, [last_core]
    else:
        def pick(t, index):
            return lax.dynamic_index_in_dim(t, index, 0, keepdims=False)

        x = pick(block_input, mine)
        got = swap(jnp.stack([pick(block_input, 1 - mine), pick(out_grad, 1 - mine).astype(BF)]), ACROSS)
        blocks_in, blocks_out = plain_gather(ffn_in, ffn_out)
        for layer in range(LAYERS):
            wk, wv, down, up, wq, wo = seq(
                None, [], [], name="fetch",
                fetch=[(key_weight, layer), (value_weight, layer), (down_shared, None), (up_shared, None),
                       (query_weight, layer), (out_weight, layer)])
            keys, values, inner, lift_v, xb = kv_call(seq, layer, x, got, wk, wv, down, up, *scales)
            kv = (keys, values, swap(keys, BESIDE), swap(values, BESIDE))
            q, qt, lift_q = q_call(seq, layer, xb, inner, wq, up, *scales)
            y, h1, *p = attend_call(
                seq, layer, part_lengths, xb if layer == 0 else x, qt, kv, wo, ln_gain)
            if layer == 0:
                a, g0 = seq(None, [], [("v", FFN_SHAPE, BF)] * 2)
                w_in, w_out = seq(None, [], [], name="fetch", fetch=[(blocks_in, None), (blocks_out, None)])
                x, h20, w_in, w_out, a, g0 = ffn_second_call(
                    seq, 0, range(NCB), (nothing, nothing), [], y, ln_gain, w_in, w_out, a, g0)
                stored0 = (kv, q, inner, lift_q, lift_v, h1, p, wk, wv, wq, wo)
        a, g, w_in = ffn_hidden_call(seq, 1, range(NCB), w_in, nothing, [], y)
        moves, refs = nothing, []
    output, other_output, dh, w_out = ffn_both_call(
        seq, 1, w_in, w_out, a, g, moves, refs, dp == 8, y, h1, ln_gain, got, out_grad)
    own, send, ds = attend_back_call(seq, dh, wo, q, kv, p)
    got = swap(send, BESIDE)
    dx, dub, dk, gd_q, gb_q = dq_call(seq, 1, dh, ds, q, kv, lift_q, inner, wq, up, *scales)
    dub, dv, sums = dv_call(
        seq, 1, dub, own, got, lift_v, inner, up, *scales, gd_q, gb_q, jnp.zeros((4 * LAYERS, RANK), F32))
    [cotangent] = dx_call(seq, 1, dx, dub, dk, got, dv, wk, wv, down)
    kv, q, inner, lift_q, lift_v, h1, p, wk, wv, wq, wo = stored0
    [dh] = ffn_back_call(seq, 0, cotangent, h20, g0, h1, ln_gain, w_in, w_out)
    own, send, ds, other_output = attend_back_call(seq, dh, wo, q, kv, p, through=[other_output])
    got, other_output = swap(send, BESIDE), swap(other_output, ACROSS)
    dx, dub, dk, gd_q, gb_q = dq_call(seq, 0, dh, ds, q, kv, lift_q, inner, wq, up, *scales)
    dub, dv, sums = dv_call(seq, 0, dub, own, got, lift_v, inner, up, *scales, gd_q, gb_q, sums)
    if dp == 8:
        [sums] = add_call(seq, sums, swap(sums, BESIDE))
        parts = [both_axes(sums, BOTH_SWAP), swap(sums, ACROSS), across_y(sums)]
        rows, last_rows = dx_call(seq, 0, dx, dub, dk, got, dv, wk, wv, down)
        sums, last_rows = add_call(seq, sums, *parts, through=[last_rows])
        got = swap(last_rows, ACROSS)
        parts = [both_axes(sums, along) for along in Z_ALL]
    else:
        rows, last_rows = dx_call(seq, 0, dx, dub, dk, got, dv, wk, wv, down)
        got = swap(last_rows, ACROSS)
        sums, parts = lax.psum(sums, ("dp", "head")), []
    block_output, input_grad = store_call(seq, output, other_output, rows, got)
    grad_d, grad_b = finish_call(seq, [sums, *parts])
    return block_output, input_grad, grad_d, grad_b


def solution(mesh):
    both = P(None, ("dp", "head"), None)
    in_specs = (both, P(None, "dp", None), P(), P(), P(), P(), P(), P(), P(), P(), P(),
                P(None, "dp", None), P(None, "dp", None), both)
    out_specs = (both, both, P(), P())
    return jax.shard_map(local, mesh=mesh, in_specs=in_specs, out_specs=out_specs, check_vma=False)
```

```python
import functools

import jax
import jax.numpy as jnp
from jax import lax
from jax.experimental import pallas as pl
from jax.experimental.pallas import tpu as pltpu
from jax.sharding import PartitionSpec as P

D = 768
HEADS = 12
HEAD_DIM = 64
FF = 3072
RANK = 1024
LEN = 512
LAYERS = 2
PAIRS = HEADS // 2
PAIR = 2 * HEAD_DIM
BLOCK = LEN // 4
ROWS = 2 * BLOCK
CB = D
NCB = FF // CB
SCALE = HEAD_DIM ** (-0.5)
BF = jnp.bfloat16
F32 = jnp.float32
MIB = 1 << 20

COLOURS = {"v": pltpu.VMEM, "h": pltpu.HBM}
SPACES = {
    "v": pl.BlockSpec(memory_space=pltpu.VMEM),
    "h": pl.BlockSpec(memory_space=pltpu.HBM),
    "s": pl.BlockSpec(memory_space=pltpu.SMEM),
    "a": pl.BlockSpec(memory_space=pl.ANY),
}


HERE, CORE, MINE, Z, Y, OTHER_Y, Z_TWO, Z_NEAR, Z_BESIDE, OTHER_CORE = range(10)
SLOTS, BLOCKS = 10, 14


def indices(dp):
    here, place = lax.axis_index("head"), lax.axis_index("dp")
    mine, core = lax.div(here, 2), lax.rem(here, 2)
    z, y = lax.div(place, 2), lax.rem(place, 2)
    line = [z, y, 1 - y] + [lax.rem(z + step, 4) for step in (2, 3 + 2 * core, 1 + 2 * core)]
    blocks = [here, here ^ 2, here ^ 1, here ^ 3]
    if dp == 8:
        slots = [2 * mine, 2 * mine + 1, 2 - 2 * mine, 3 - 2 * mine]
    else:
        slots = list(range(NCB))
    return [here, core, mine] + line + [1 - core] + slots + blocks


def dot(left, right):
    return jnp.dot(left, right, preferred_element_type=F32)


def dot_nt(left, right):
    return lax.dot_general(left, right, (((1,), (1,)), ((), ())), preferred_element_type=F32)


def normed(t):
    centred = t - jnp.mean(t, axis=-1, keepdims=True)
    inverse = lax.rsqrt(jnp.mean(centred * centred, axis=-1, keepdims=True) + 1e-05)
    return centred * inverse, inverse


def norm_back(t, gain, cotangent):
    unit, inverse = normed(t)
    scaled = cotangent * gain
    mean_e = jnp.mean(scaled, axis=-1, keepdims=True)
    mean_en = jnp.mean(scaled * unit, axis=-1, keepdims=True)
    return inverse * (scaled - mean_e - unit * mean_en)


class Copies:
    def __init__(self, sems, first=0):
        self.sems, self.count = sems, first

    def __call__(self, src, dst):
        copy = pltpu.make_async_copy(src, dst, self.sems.at[self.count])
        self.count += 1
        copy.start()
        return copy


class Sequence:
    def __init__(self, dp):
        self.dp, self.token = dp, None

    def __call__(self, body, ins, outs, scratch=(), copies=0, name="keep", fetch=(), fill=(), fill_hbm=(), through=(), limit=8, save=(), cost=0.001):
        handed = [pltpu.with_memory_space_constraint(t, pltpu.VMEM) for t in fill]
        handed += [pltpu.with_memory_space_constraint(t, pltpu.HBM) for t in fill_hbm]
        handed += list(through)
        if self.token is not None:
            handed.append(pltpu.with_memory_space_constraint(self.token, pltpu.HBM))
        fetched = [(t.shape if part is None else t.shape[1:] if isinstance(part, int) else part[1], t.dtype)
                   for t, part in fetch]
        wants = [i for i, entry in enumerate(ins) if entry is None]
        ins = [entry for entry in ins if entry is not None]
        n_in, n_fetch, n_hand, n_fill = len(ins), len(fetch), len(handed), len(fill) + len(fill_hbm)
        n_out, n_save = len(outs), len(save)
        first = self.token is None

        def whole(*refs):
            refs = list(refs)
            in_refs, fetch_refs = refs[:n_in], refs[n_in:n_in + n_fetch]
            for i in wants:
                in_refs.insert(i, indices(self.dp))
            refs = refs[n_in + n_fetch:]
            refs = refs[n_hand:]
            out_refs, fetch_outs = refs[:n_out], refs[n_out:n_out + n_fetch]
            refs = refs[n_out + n_fetch:]
            fill_refs = refs[:n_fill]
            save_refs = refs[n_hand + first:][:n_save]
            refs = refs[n_hand + first + n_save:]
            scratch_refs, sems = refs[:len(scratch)], refs[len(scratch)]
            copy = Copies(sems, copies)
            waits = []
            for (_, part), source, target in zip(fetch, fetch_refs, fetch_outs, strict=True):
                if part is not None:
                    source = source.at[part if isinstance(part, int) else part[0](in_refs[0])]
                waits.append(copy(source, target))
            for place, target in zip(save, save_refs, strict=True):
                waits.append(copy(in_refs[place], target))
            if body is not None:
                body(*in_refs, *fill_refs, *out_refs, *scratch_refs, sems)
            for wait in waits:
                wait.wait()

        shapes = [COLOURS[space](shape, dtype) for space, shape, dtype in outs]
        shapes += [pltpu.VMEM(shape, dtype) for shape, dtype in fetched]
        shapes += [pltpu.VMEM(t.shape, t.dtype) for t in fill] + [pltpu.HBM(t.shape, t.dtype) for t in fill_hbm]
        shapes += [jax.ShapeDtypeStruct(t.shape, t.dtype) for t in through]
        shapes += [pltpu.HBM((8, 128), F32)]
        shapes += [pltpu.HBM(ins[place][1].shape, ins[place][1].dtype) for place in save]
        results = pl.pallas_call(
            whole,
            out_shape=tuple(shapes),
            in_specs=[SPACES[space] for space, _ in ins] + [SPACES["h"]] * n_fetch + [SPACES["v"]] * len(fill)
            + [SPACES["h"]] * len(fill_hbm) + [SPACES["a"]] * (n_hand - n_fill),
            out_specs=tuple([SPACES[space] for space, _, _ in outs] + [SPACES["v"]] * (n_fetch + len(fill))
                            + [SPACES["h"]] * len(fill_hbm) + [SPACES["a"]] * (n_hand - n_fill + first) + [SPACES["h"]] * n_save),
            scratch_shapes=[pltpu.VMEM(shape, dtype) for shape, dtype in scratch]
            + [pltpu.SemaphoreType.DMA((copies + n_fetch + n_save + 1,))],
            input_output_aliases={n_in + n_fetch + i: n_out + n_fetch + i for i in range(n_hand)},
            compiler_params=pltpu.CompilerParams(vmem_limit_bytes=limit * MIB),
            cost_estimate=pl.CostEstimate(
                flops=int(cost * 1e9), bytes_accessed=int(cost * 3e6), transcendentals=0),
            name=name,
        )(*[pltpu.with_memory_space_constraint(t, COLOURS[space]) if space in COLOURS else t for space, t in ins],
          *[pltpu.with_memory_space_constraint(t, pltpu.HBM) for t, _ in fetch],
          *handed)
        results = list(results)
        split = n_out + n_fetch + n_fill + len(through)
        self.token = results[split]
        return results[:split] + results[split + 1:]


def kv_body(layer, x_ref, got_ref, wk, wv, down, up, sd_ref, sb_ref, *rest):
    keys, values, inner_out, lift_out, xb_ref, _ = rest
    if layer == 0:
        xb_ref[:BLOCK] = x_ref[...]
        xb_ref[BLOCK:] = got_ref[0]
    else:
        xb_ref[...] = x_ref[...].astype(BF)
    xb = xb_ref[...]
    inner = dot(xb, down[...])
    inner_out[...] = inner.astype(BF)
    lift = dot((sd_ref[layer, 1:2, :] * inner).astype(BF), up[...])
    lift_out[...] = lift.astype(BF)
    values[...] = (dot(xb, wv[...]) + sb_ref[layer, 1:2, :] * lift).astype(BF)
    keys[...] = dot(xb, wk[...]).astype(BF)


def kv_call(seq, layer, x, got, wk, wv, down, up, sd, sb, **extra):
    return seq(
        functools.partial(kv_body, layer),
        [("v", t) for t in (x, got, wk, wv, down, up, sd, sb)],
        [("v", (ROWS, D), BF)] * 2 + [("v", (ROWS, RANK), BF), ("v", (ROWS, D), BF), ("v", (ROWS, D), BF)],
        name="keys_values", **extra)


def q_body(layer, x_ref, inner, wq, up, sd_ref, sb_ref, q_ref, qt_ref, lift_out, sems):
    lift = dot((sd_ref[layer, 0:1, :] * inner[...].astype(F32)).astype(BF), up[...])
    lift_out[...] = lift.astype(BF)
    q = (dot(x_ref[...], wq[...]) + sb_ref[layer, 0:1, :] * lift).astype(BF)
    q_ref[...] = q
    qt_ref[...] = (q * SCALE).T


def q_call(seq, layer, x, inner, wq, up, sd, sb, **extra):
    return seq(
        functools.partial(q_body, layer),
        [("v", x), ("v", inner), ("v", wq), ("v", up), ("v", sd), ("v", sb)],
        [("v", (ROWS, D), BF), ("v", (D, ROWS), BF), ("v", (ROWS, D), BF)],
        name="queries", **extra)


def split_heads(t):
    zero = jnp.zeros((HEAD_DIM, t.shape[1]), t.dtype)
    first = jnp.concatenate([t[:HEAD_DIM], zero], axis=0)
    second = jnp.concatenate([zero, t[HEAD_DIM:]], axis=0)
    return jnp.concatenate([first, second], axis=1)


def join_heads(t):
    n = t.shape[1] // 2
    return jnp.concatenate([t[:HEAD_DIM, :n], t[HEAD_DIM:, n:]], axis=0)


def stack_heads(t):
    lane = lax.broadcasted_iota(jnp.int32, (1, PAIR), 1)
    first = (lane < HEAD_DIM).astype(F32).astype(BF)
    second = (lane >= HEAD_DIM).astype(F32).astype(BF)
    return jnp.concatenate([t * first, t * second], axis=0)


def rows_of(near, far, cols):
    return jnp.concatenate([near[:, cols], far[:, cols]], axis=0)


def attend_body(layer, ids, lengths, x_ref, qt_ref, wo, gain_ref, keys, values, far_keys, far_values,
                y_ref, h_ref, e_ref, factor_ref, ctx_t_ref, ctx, sems):
    row = lax.broadcasted_iota(jnp.int32, (BLOCK, 2 * ROWS), 0)
    counts = lengths[ids[MINE]]
    live = counts[:, :1] + counts[:, 1:] + 4
    limits = [live - BLOCK * ids[BLOCKS + b] for b in range(4)]
    for pair in range(PAIRS):
        cols = slice(pair * PAIR, (pair + 1) * PAIR)
        raw = dot(rows_of(keys, far_keys, cols), split_heads(qt_ref[cols, :]))
        scores = jnp.concatenate(
            [jnp.where(row < limits[b], raw[b * BLOCK:(b + 1) * BLOCK], -1000000000.0) for b in range(4)],
            axis=0,
        )
        grown = jnp.exp(scores - jnp.max(scores, axis=0, keepdims=True))
        factor = 1.0 / jnp.sum(grown, axis=0, keepdims=True)
        factor_ref[pair:pair + 1, :] = factor
        e_ref[pair] = grown.astype(BF)
        ctx_t = join_heads(dot(rows_of(values, far_values, cols).T, e_ref[pair]) * factor)
        ctx_t_ref[cols, :] = ctx_t
        ctx[:, cols] = ctx_t.astype(BF).T
    h = x_ref[...].astype(F32) + dot(ctx[...], wo[...])
    h_ref[...] = h
    y_ref[...] = normed(h)[0] * gain_ref[layer, 0:1, :]


def attend_call(seq, layer, lengths, x, qt, kv, wo, gain, **extra):
    return seq(
        functools.partial(attend_body, layer),
        [None] + [("v", t) for t in (lengths, x, qt, wo, gain, *kv)],
        [("v", (ROWS, D), F32), ("v", (ROWS, D), F32), ("v", (PAIRS, LEN, 2 * ROWS), BF), ("v", (PAIRS, 2 * ROWS), F32),
         ("v", (D, ROWS), F32)],
        [((ROWS, D), BF)], name="attention", **extra)


def move(pairs):
    for source, target in pairs:
        target[...] = source[...].reshape(target.shape)


def ffn_hidden(yb, w_in, a_ref, g_ref, slots):
    for slot in slots:
        z = dot(yb, w_in[slot].reshape(D, CB))
        cdf = 0.5 * (1.0 + lax.erf(z * (0.5 ** 0.5)))
        g_ref[slot] = (cdf + z * (jnp.exp(-0.5 * z * z) * 0.3989422804014327)).astype(BF)
        a_ref[slot] = (z * cdf).astype(BF)


def ffn_result(ids, total, a_ref, w_out, y=None):
    size = CB if y is None else CB // 2
    for slot in range(NCB):
        if y is None:
            hidden, rows = a_ref[slot], w_out[ids[SLOTS + slot]]
        else:
            hidden = a_ref[slot, :, pl.ds(pl.multiple_of(y * size, size), size)]
            rows = w_out[ids[SLOTS + slot], y]
        total = total + dot(hidden, rows.reshape(size, D))
    return total


def ffn_backward(layer, ids, c, h2, g_ref, h1, gain_ref, w_in, w_out, dh_ref):
    dh2 = norm_back(h2, gain_ref[layer, 1:2, :], c)
    dfb = dh2.astype(BF)
    total = dh2
    for slot in range(NCB):
        da = dot_nt(dfb, w_out[ids[SLOTS + slot]].reshape(CB, D))
        dz = (g_ref[slot].astype(F32) * da).astype(BF)
        total = total + dot_nt(dz, w_in[slot].reshape(D, CB))
    dh1 = norm_back(h1, gain_ref[layer, 0:1, :], total)
    dh_ref[...] = dh1


FFN_SHAPE = (NCB, ROWS, CB)


def ffn_first_body(ids, y_ref, in_ref, cut_ref, in_z, in_y, in_far, own_y, first, out0_z,
                   w_in, w_out, a_ref, g_ref, sems):
    copy = Copies(sems)
    w_in = [w_in.at[layer] for layer in range(LAYERS)]
    w_out = [w_out.at[layer] for layer in range(LAYERS)]
    owns = [[copy(source, target) for source, target in own_in(layer, ids, in_ref, w_in[layer])] for layer in range(LAYERS)]
    own_out = [copy(cut_ref.at[layer], w_out[layer].at[ids[Z], ids[Y]]) for layer in range(LAYERS)]
    lines = [(in_z, 0), (first, 0), (in_y, 0), (first, 6), (own_y, 0), (first, 3), (in_far, 0), (first, 9)]
    move(pieces_in(0, ids, lines, w_in[0]))
    for wait in owns[0]:
        wait.wait()
    ffn_hidden(y_ref[...].astype(BF), w_in[0], a_ref, g_ref, range(NCB // 2))
    move(pieces_in(1, ids, lines, w_in[1]))
    for side, line in enumerate([(out0_z, 0), (first, 13)]):
        move(line_moves(ids, line, side, slice(None), out_target(w_out[0], ids[Y])))
    for side, (ref, start) in enumerate([(own_y, 0), (first, 3)]):
        core = ids[CORE] if side == 0 else ids[OTHER_CORE]
        for layer in range(LAYERS):
            move([(ref.at[start + 1 + layer], w_out[layer].at[ids[Z], ids[OTHER_Y], core])])
    for wait in owns[1] + own_out:
        wait.wait()


def ffn_second_body(layer, slots, moves, n_refs, ids, y_ref, gain_ref, *rest):
    refs, rest = rest[:n_refs], rest[n_refs:]
    w_in, w_out, a_ref, g_ref, x_ref, h_ref, _ = rest
    move(moves[0](ids, refs, w_in, w_out))
    ffn_hidden(y_ref[...].astype(BF), w_in.at[layer], a_ref, g_ref, slots)
    move(moves[1](ids, refs, w_in, w_out))
    h_ref[...] = ffn_result(ids, y_ref[...], a_ref, w_out.at[layer])
    x_ref[...] = normed(h_ref[...])[0] * gain_ref[layer, 1:2, :]


def ffn_second_call(seq, layer, slots, moves, refs, y, gain, w_in, w_out, a, g, **extra):
    return seq(
        functools.partial(ffn_second_body, layer, slots, moves, len(refs)),
        [None, ("v", y), ("v", gain)] + [("v", t) for t in refs],
        [("v", (ROWS, D), F32), ("v", (ROWS, D), F32)], name="ffn", fill=[w_in, w_out, a, g], **extra)


FFN_SHAPE = (NCB, ROWS, CB)


def ffn_hidden_body(layer, slots, moves, n_refs, ids, y_ref, *rest):
    refs, (w_in, a_ref, g_ref, _) = rest[:n_refs], rest[n_refs:]
    move(moves(ids, refs, w_in.at[layer]))
    ffn_hidden(y_ref[...].astype(BF), w_in.at[layer], a_ref, g_ref, slots)


def ffn_hidden_call(seq, layer, slots, w_in, moves, refs, y, **extra):
    return seq(
        functools.partial(ffn_hidden_body, layer, slots, moves, len(refs)),
        [None, ("v", y)] + [("v", t) for t in refs], [("v", FFN_SHAPE, BF)] * 2, name="ffn_hidden", fill=[w_in], **extra)


def ffn_near_body(layer, slots, moves, n_refs, ids, y_ref, w_in, *rest):
    refs, (w_out, a_ref, g_ref, near_ref, _) = rest[:n_refs], rest[n_refs:]
    ffn_hidden(y_ref[...].astype(BF), w_in.at[layer], a_ref, g_ref, slots)
    w_out = w_out.at[layer]
    move(moves(ids, refs, w_out))
    near_ref[...] = ffn_result(ids, y_ref[...], a_ref, w_out, ids[Y])


def ffn_near_call(seq, layer, slots, w_in, w_out, a, g, moves, refs, y, **extra):
    return seq(
        functools.partial(ffn_near_body, layer, slots, moves, len(refs)),
        [None, ("v", y), ("v", w_in)] + [("v", t) for t in refs],
        [("v", (ROWS, D), F32)], name="ffn_near", fill=[w_out, a, g], **extra)


def ffn_both_body(layer, moves, n_refs, near, ids, y_ref, h1, gain_ref, got_ref, w_in, a_ref, g_ref, c_ref, *rest):
    refs, rest = rest[:n_refs], rest[n_refs:]
    w_out, x_ref, send_ref, dh_ref, c, sems = rest
    own = Copies(sems)(c_ref.at[ids[MINE]], c.at[pl.ds(0, BLOCK)])
    w_in, w_out = w_in.at[layer], w_out.at[layer]
    move(moves(ids, refs, w_out))
    h2 = ffn_result(ids, y_ref[...], a_ref, w_out, ids[OTHER_Y] if near else None)
    dh_ref[...] = h2
    x = normed(h2)[0] * gain_ref[layer, 1:2, :]
    x_ref[...] = x[:BLOCK].astype(BF)
    send_ref[...] = x[BLOCK:].astype(BF)
    own.wait()
    c[BLOCK:] = got_ref[1].astype(F32)
    ffn_backward(layer, ids, c[...], dh_ref[...], g_ref, h1[...], gain_ref, w_in, w_out, dh_ref)


def ffn_both_call(seq, layer, w_in, w_out, a, g, moves, refs, near, y, h1, gain, got, c, **extra):
    return seq(
        functools.partial(ffn_both_body, layer, moves, len(refs), near),
        [None] + [("v", t) for t in (y, h1, gain, got, w_in, a, g)] + [("h", c)] + [("v", t) for t in refs],
        [("v", (BLOCK, D), BF), ("v", (BLOCK, D), BF), ("v", (ROWS, D), F32)],
        [((ROWS, D), F32)], 1, "ffn_both", fill=[w_out], **extra)


def ffn_back_body(layer, ids, c_ref, h2, g, h1, gain_ref, w_in, w_out, dh_ref, sems):
    ffn_backward(layer, ids, c_ref[...], h2[...], g, h1[...], gain_ref, w_in.at[layer], w_out.at[layer], dh_ref)


def ffn_back_call(seq, layer, c, h2, g, h1, gain, w_in, w_out, **extra):
    return seq(
        functools.partial(ffn_back_body, layer),
        [None] + [("v", t) for t in (c, h2, g, h1, gain, w_in, w_out)],
        [("v", (ROWS, D), F32)], name="ffn_back", **extra)


def attend_back_body(dh_ref, wo, q, factor_ref, ctx_t_ref, keys, values, far_keys, far_values,
                     e_ref, own_ref, send_ref, dctx_ref, sems):
    dctx_ref[...] = dot_nt(dh_ref[...].astype(BF), wo[...]).astype(BF)
    for pair in range(PAIRS):
        cols = slice(pair * PAIR, (pair + 1) * PAIR)
        vcols = slice(D + pair * PAIR, D + (pair + 1) * PAIR)
        factor = factor_ref[pair:pair + 1, :]
        scaled = (split_heads(dctx_ref[:, cols].T).astype(F32) * factor).astype(BF)
        inner = jnp.sum(scaled.astype(F32) * split_heads(ctx_t_ref[cols, :]), axis=0, keepdims=True)
        e = e_ref[pair]
        ds = (e.astype(F32) * (dot(rows_of(values, far_values, cols), scaled) - inner)).astype(BF)
        dv = dot(e, scaled.T)
        dk = dot(ds[ROWS:], stack_heads(q[:, cols])) * SCALE
        own_ref[:, cols] = dv[:ROWS]
        send_ref[:, cols] = dk.astype(BF)
        send_ref[:, vcols] = dv[ROWS:].astype(BF)
        e_ref[pair] = ds


def attend_back_call(seq, dh, wo, q, kv, weights, **extra):
    e, *rest = weights
    return seq(
        attend_back_body,
        [("v", t) for t in (dh, wo, q, *rest, *kv)],
        [("v", (ROWS, D), F32), ("v", (ROWS, 2 * D), BF)],
        [((ROWS, D), BF)], name="attention_back", fill=[e], **extra)


def dq_body(layer, dh_ref, ds_ref, q, keys, far_keys, lift, inner, wq, up, sd_ref, sb_ref,
            dx_ref, dub_ref, dk_ref, gd_ref, gb_ref, dq_ref, sems):
    for pair in range(PAIRS):
        cols = slice(pair * PAIR, (pair + 1) * PAIR)
        dq_t = join_heads(dot(rows_of(keys, far_keys, cols).T, ds_ref[pair])) * SCALE
        dq_ref[:, cols] = dq_t.T.astype(BF)
        dk_ref[:, cols] = dot(ds_ref[pair, :ROWS], stack_heads(q[:, cols])) * SCALE
    dq = dq_ref[...]
    dqf = dq.astype(F32)
    gb_ref[...] = jnp.sum(dqf * lift[...].astype(F32), axis=0, keepdims=True)
    dpq = dot_nt((sb_ref[layer, 0:1, :] * dqf).astype(BF), up[...])
    gd_ref[...] = jnp.sum(dpq * inner[...].astype(F32), axis=0, keepdims=True)
    dub_ref[...] = sd_ref[layer, 0:1, :] * dpq
    dx_ref[...] = dh_ref[...] + dot_nt(dq, wq[...])


def dq_call(seq, layer, dh, ds, q, kv, lift, inner, wq, up, sd, sb, **extra):
    return seq(
        functools.partial(dq_body, layer),
        [("v", t) for t in (dh, ds, q, kv[0], kv[2], lift, inner, wq, up, sd, sb)],
        [("v", (ROWS, D), F32), ("v", (ROWS, RANK), F32), ("v", (ROWS, D), F32), ("v", (1, RANK), F32), ("v", (1, D), F32)],
        [((ROWS, D), BF)], name="queries_back", **extra)


def dv_body(layer, dub_ref, own_ref, got_ref, lift, inner, up, sd_ref, sb_ref, gdq_ref, gbq_ref, before_ref,
            dub_out, dv_ref, sums_ref, sems):
    sums_ref[...] = before_ref[...]
    sums_ref[4 * layer:4 * layer + 1, :] = gdq_ref[...]
    sums_ref[4 * layer + 2:4 * layer + 3, :D] = gbq_ref[...]
    dv = (own_ref[...] + got_ref[:, D:].astype(F32)).astype(BF)
    dv_ref[...] = dv
    dvf = dv.astype(F32)
    sums_ref[4 * layer + 3:4 * layer + 4, :D] = jnp.sum(dvf * lift[...].astype(F32), axis=0, keepdims=True)
    dpv = dot_nt((sb_ref[layer, 1:2, :] * dvf).astype(BF), up[...])
    sums_ref[4 * layer + 1:4 * layer + 2, :] = jnp.sum(dpv * inner[...].astype(F32), axis=0, keepdims=True)
    dub_out[...] = (dub_ref[...] + sd_ref[layer, 1:2, :] * dpv).astype(BF)


def dv_call(seq, layer, dub, own, got, lift, inner, up, sd, sb, gd, gb, before, **extra):
    return seq(
        functools.partial(dv_body, layer),
        [("v", t) for t in (dub, own, got, lift, inner, up, sd, sb, gd, gb, before)],
        [("v", (ROWS, RANK), BF), ("v", (ROWS, D), BF), ("v", (4 * LAYERS, RANK), F32)],
        name="values_back", **extra)


def dx_body(layer, dx_ref, dub_ref, dk_ref, got_ref, dv_ref, wk, wv, down, *rest):
    total = dx_ref[...] + dot_nt(dub_ref[...], down[...])
    total = total + dot_nt(dv_ref[...], wv[...])
    dk = (dk_ref[...] + got_ref[:, :D].astype(F32)).astype(BF)
    total = total + dot_nt(dk, wk[...])
    if layer == 0:
        own_ref, send_ref, _ = rest
        own_ref[...] = total[:BLOCK]
        send_ref[...] = total[BLOCK:].astype(BF)
    else:
        rest[0][...] = total


def dx_call(seq, layer, dx, dub, dk, got, dv, wk, wv, down, **extra):
    return seq(
        functools.partial(dx_body, layer),
        [("v", t) for t in (dx, dub, dk, got, dv, wk, wv, down)],
        [("v", (BLOCK, D), F32), ("v", (BLOCK, D), BF)] if layer == 0 else [("v", (ROWS, D), F32)],
        name="input_back", **extra)


def add_call(seq, *terms, **extra):
    def body(*refs):
        total = refs[0][...]
        for ref in refs[1:len(terms)]:
            total = total + ref[...]
        refs[len(terms)][...] = total

    return seq(body, [("v", t) for t in terms], [("v", terms[0].shape, F32)], name="add", **extra)


def store_call(seq, output, other_output, rows, got):
    def body(ids_ref, output_ref, other_ref, rows_ref, got_ref, block_ref, grad_ref, wide, sems):
        copy = Copies(sems)
        mine = ids_ref[MINE]
        stores = [copy(rows_ref, grad_ref.at[mine]), copy(output_ref, block_ref.at[mine]), copy(other_ref, block_ref.at[1 - mine])]
        wide[...] = got_ref[...].astype(F32)
        stores.append(copy(wide, grad_ref.at[1 - mine]))
        for store in stores:
            store.wait()

    return seq(body, [None] + [("v", t) for t in (output, other_output, rows, got)],
               [("h", (2,) + t.shape, t.dtype) for t in (output, rows)], [(got.shape, F32)], 4, "store")


def finish_call(seq, terms):
    def body(*refs):
        *terms_refs, gd_out, gb_out, gd_ref, gb_ref, sems = refs
        copy = Copies(sems)
        total = terms_refs[0][...]
        for ref in terms_refs[1:]:
            total = total + ref[...]
        for layer in range(LAYERS):
            gd_ref[layer] = total[4 * layer:4 * layer + 2]
            gb_ref[layer] = total[4 * layer + 2:4 * layer + 4, :D]
        stores = [copy(gd_ref, gd_out), copy(gb_ref, gb_out)]
        for store in stores:
            store.wait()

    shapes = [((LAYERS, 2, RANK), F32), ((LAYERS, 2, D), F32)]
    return seq(body, [("v", t) for t in terms], [("h", *t) for t in shapes], shapes, 2, "finish")


def columns(block):
    return pl.ds(pl.multiple_of(block * CB, CB), CB)


def prepare_line_body(ids, in_ref, a_in, sems):
    copy, rows, waits = Copies(sems), in_ref.shape[1], []
    for layer in range(LAYERS):
        for q in range(2):
            waits.append(copy(in_ref.at[layer, :, columns(2 * ids[MINE] + q)], a_in.at[q, pl.ds(layer * rows, rows)]))
    for wait in waits:
        wait.wait()


def prepare_body(ids, x_ref, c_ref, in_ref, out_ref, own, sent, b_in, own_a, own_b, c_send, sems):
    copy = Copies(sems)
    here, core, mine = ids[HERE], ids[CORE], ids[MINE]
    rows = in_ref.shape[1]
    waits = [copy(c_ref.at[1 - mine], c_send)]
    for layer in range(LAYERS):
        part = pl.ds(layer * rows, rows)
        waits.append(copy(in_ref.at[layer, :, columns(here)], b_in.at[part]))
        waits.append(copy(in_ref.at[layer, :, columns(here)], own_a.at[part]))
    piece = own_a.shape[0] - rows
    half = pl.ds(0, rows), pl.ds(rows, rows)
    waits.append(copy(out_ref.at[0, core, half[0]], own_a.at[pl.ds(piece, rows)]))
    waits.append(copy(out_ref.at[0, core, half[1]], own_b.at[half[0]]))
    waits.append(copy(out_ref.at[1, core], own_b.at[pl.ds(rows, piece)]))
    waits += [copy(x_ref.at[1 - mine], sent.at[0]), copy(x_ref.at[mine], own)]
    waits[0].wait()
    sent[1] = c_send[...].astype(BF)
    for wait in waits[1:]:
        wait.wait()


def prepare_call(seq, x, c, ffn_in, halves):
    rows = (BLOCK, D)
    piece = halves.shape[2:]
    [a_in] = seq(prepare_line_body, [None, ("h", ffn_in)], [("v", (2,) + piece, BF)], [], 2 * LAYERS, "prepare")
    own, sent, *rest = seq(
        prepare_body,
        [None, ("h", x), ("h", c), ("h", ffn_in), ("h", halves)],
        [("v", rows, BF), ("v", (2,) + rows, BF), ("v", piece, BF)]
        + [("v", (piece[0] * 3 // 2,) + piece[1:], BF)] * 2,
        [(rows, F32)], 6 + 2 * LAYERS, "prepare")
    return own, sent, a_in, *rest


def everywhere(target):
    pairs = []
    for z in range(4):
        for y in range(2):
            for head in range(4):
                z_to, y_to, head_to = target(z, y, head)
                pairs.append(((2 * z + y) * 4 + head, (2 * (z_to % 4) + y_to) * 4 + head_to))
    return pairs


Z_ONE = everywhere(lambda z, y, head: (z + 1 - 2 * (head % 2), y, head))
TWO = everywhere(lambda z, y, head: (z + 2, y, head))
Y_SWAP = [(i, i ^ 1) for i in range(8)]
BOTH_SWAP = everywhere(lambda z, y, head: (z, 1 - y, head ^ 2))
Z_ALL = [everywhere(lambda z, y, head, other=other: (z ^ other, y, head)) for other in (3, 2, 1)]
ACROSS = [(i, i ^ 2) for i in range(4)]
BESIDE = [(i, i ^ 1) for i in range(4)]


def swap(t, pairs):
    return lax.ppermute(t, "head", pairs)


def both_axes(t, pairs):
    return lax.ppermute(t, ("dp", "head"), pairs)


def across_y(t):
    return lax.ppermute(t, "dp", Y_SWAP)


def lay_call(seq, arrays, outs, **extra):
    piece = arrays[0].shape[-2:]

    def length(part):
        return 1 if part is None else part.stop - part.start

    def body(*refs):
        for out, result in zip(outs, refs[len(arrays):], strict=False):
            start = 0
            for index, part in out:
                stop = start + length(part)
                result[start:stop] = refs[index][...][None] if part is None else refs[index][part]
                start = stop

    shapes = [(sum(length(part) for _, part in out),) + piece for out in outs]
    return seq(body, [("v", t) for t in arrays], [("v", shape, BF) for shape in shapes], name="lay", **extra)


def cut_call(seq, cuts):
    cut = cuts.shape[3:]

    def body(ids_ref, cuts_ref, a_ref, b_ref, sems):
        copy = Copies(sems)
        waits = []
        for core, target in ((0, a_ref.at[0]), (1, a_ref.at[1]), (ids_ref[CORE], b_ref)):
            waits.append(copy(cuts_ref.at[1, core, ids_ref[MINE]], target.at[0]))
            waits.append(copy(cuts_ref.at[1, core, pl.ds(2, 2)], target.at[pl.ds(1, 2)]))
        for wait in waits:
            wait.wait()

    return seq(body, [None, ("h", cuts)], [("v", (2, 3) + cut, BF), ("v", (3,) + cut, BF)], [], 6, "cut")


def cut_lay_call(seq, out_a, out_b, in_y_far, out0_y):
    cut = out_b.shape[1:]

    def body_z(a_ref, b_ref, line_ref, sems):
        line_ref[:2] = a_ref[...]
        line_ref[2] = b_ref[...]

    [line] = seq(body_z, [("v", out_a), ("v", out_b)], [("v", (3, 3) + cut, BF)], name="lay")
    return cut_lay_rest_call(seq, line, in_y_far, out0_y)


def cut_lay_rest_call(seq, line, in_y_far, out0_y):
    cut = line.shape[2:]
    piece = out0_y.shape[1:]

    def body(z_ref, far_ref, y_ref, line_ref, own_ref, common_ref, second_ref, sems):
        rows = piece[0] // LAYERS
        line_ref[:, :3] = z_ref[...]
        line_ref[:, 3:] = far_ref[:, rows:].reshape((3, 2) + cut)
        own_ref[...] = z_ref[:, 0]
        common_ref[...] = z_ref[:, 1:]
        second_ref[:, :rows] = far_ref[:, :rows]
        second_ref[:, rows:] = y_ref[...]

    return seq(body, [("v", t) for t in (line, in_y_far, out0_y)],
               [("v", (3, 5) + cut, BF), ("v", (3,) + cut, BF), ("v", (3, 2) + cut, BF),
                ("v", (3, piece[0] // LAYERS + piece[0]) + piece[1:], BF)], name="lay")


def window_lay_call(seq, in_a, in_b, own_a, own_b):
    piece = in_b.shape

    def body(a_ref, b_ref, own_a_ref, own_b_ref, z_ref, x_ref, own_ref, sems):
        full, half = piece[0], piece[0] // 2
        own_ref[0] = own_a_ref[:full]
        own_ref[1, :half] = own_a_ref[full:]
        own_ref[1, half:] = own_b_ref[:half]
        own_ref[2] = own_b_ref[half:]
        for ref in (z_ref, x_ref):
            ref[:2] = a_ref[...]
            ref[2] = b_ref[...]
        x_ref[3] = own_a_ref[:full]

    return seq(body, [("v", t) for t in (in_a, in_b, own_a, own_b)],
               [("v", (count,) + piece, BF) for count in (3, 4, 3)], name="lay")


def first_lay_call(seq, arrays):
    piece = arrays[0].shape[-2:]
    extra = -(-2 * ROWS // piece[0])

    def body(out0_z, in_z, own_y, in_y, in_far, keys, values, first_ref, sems):
        for start, ref in ((0, in_z), (3, own_y), (6, in_y), (9, in_far), (13, out0_z)):
            first_ref[start:start + ref.shape[0]] = ref[...]
        both = jnp.concatenate([keys[...], values[...]], axis=0)
        for i in range(extra):
            rows = min(piece[0], 2 * ROWS - i * piece[0])
            first_ref[16 + i, :rows] = both[i * piece[0]:i * piece[0] + rows]

    return seq(body, [("v", t) for t in arrays], [("v", (16 + extra,) + piece, BF)], name="lay")


def far_body(first_ref, keys, values, sems):
    rows, count = first_ref.shape[1], first_ref.shape[0] - 16
    both = first_ref[16:].reshape(count * rows, D)
    keys[...] = both[:ROWS]
    values[...] = both[ROWS:2 * ROWS]


def last_body(own_y, common_y, own_yx, out_ref, sems):
    out_ref[:, 0] = own_y[...]
    out_ref[:, 1:3] = common_y[...]
    out_ref[:, 3] = own_yx[...]


def line_moves(ids, line, side, part, target):
    core, z_near = (ids[CORE], ids[Z_NEAR]) if side == 0 else (ids[OTHER_CORE], ids[Z_BESIDE])
    ref, start = line
    return [(ref.at[pl.ds(start, 2), part], target(z_near, pl.ds(0, 2))),
            (ref.at[start + 2, part], target(ids[Z_TWO], core))]


def in_target(dst, slot, y):
    def target(z, piece):
        return dst.at[pl.ds(slot, 2) if not isinstance(piece, jax.Array) else slot + piece, z, y]

    return target


def own_in(layer, ids, ref, dst):
    columns = [pl.ds(pl.multiple_of(ids[SLOTS + slot] * CB, CB), CB) for slot in range(NCB)]
    return [(ref.at[layer, :, columns[slot]], dst.at[slot, ids[Z], ids[Y]]) for slot in range(NCB)]


def pieces_in(layer, ids, lines, dst):
    part = pl.ds(layer * dst.shape[3], dst.shape[3])
    z, y = ids[Z], (ids[Y], ids[OTHER_Y])
    moves = []
    for side in range(2):
        core = ids[CORE] if side == 0 else ids[OTHER_CORE]
        along, across, own, far = lines[side::2]
        moves += line_moves(ids, along, side, part, in_target(dst, 0, y[0]))
        moves += line_moves(ids, across, side, part, in_target(dst, 0, y[1]))
        moves.append((own[0].at[own[1], part], dst.at[core, z, y[1]]))
        moves += line_moves(ids, far, side, part, in_target(dst, 2, y[0]))
        moves.append((far[0].at[far[1] + 3, part], dst.at[2 + core, z, y[1]]))
    return moves


def out_target(dst, y, cut=None):
    def target(z, piece):
        if not isinstance(piece, jax.Array):
            return dst.at[z, y] if cut is None else dst.at[z, y, :, cut]
        return dst.at[z, y, piece] if cut is None else dst.at[z, y, piece, cut]

    return target


def last_pieces(ids, refs, w_in, w_out):
    rows = pl.ds(0, w_in.shape[4])
    return [pair for side in range(2)
            for pair in line_moves(ids, (refs[side], 0), side, rows, in_target(w_in.at[0], 2, ids[OTHER_Y]))]


def last_pieces_more(ids, refs, w_in, w_out):
    in_y_far, second, out0_y, out1_z = refs
    rows = w_in.shape[4]
    moves = line_moves(ids, (out0_y, 0), 0, slice(None), out_target(w_out.at[0], ids[OTHER_Y]))
    moves += line_moves(ids, (second, 0), 1, pl.ds(rows, second.shape[1] - rows), out_target(w_out.at[0], ids[OTHER_Y]))
    moves += line_moves(ids, (in_y_far, 0), 0, pl.ds(rows, rows), in_target(w_in.at[1], 2, ids[OTHER_Y]))
    return moves + cut_line(ids, out1_z, 0, w_out.at[1])


def cut_line(ids, ref, side, dst):
    x, y = ids[MINE], ids[Y]
    return (line_moves(ids, (ref, 0), side, 0, out_target(dst, y, x))
            + line_moves(ids, (ref, 0), side, pl.ds(1, 2), out_target(dst, y, pl.ds(2, 2))))


def line_pieces(ids, refs, w_in):
    return line_moves(ids, (refs[0], 0), 1, pl.ds(3, 2), in_target(w_in, 2, ids[OTHER_Y]))


def near_pieces(ids, refs, w_out):
    core_line, *refs, last = refs
    moves = cut_line(ids, core_line, 1, w_out)
    for side in range(2):
        moves += line_moves(ids, (refs[side], 0), side, slice(None), out_target(w_out, ids[Y], 1 - ids[MINE]))
    return moves + cut_pieces(ids, [last], w_out, 0)


def cut_pieces(ids, refs, w_out, side=1):
    x, moves = ids[MINE], []
    for part, cut in ((0, x), (pl.ds(1, 2), pl.ds(2, 2)), (3, 1 - x)):
        moves += line_moves(ids, (refs[0], 0), side, part, out_target(w_out, ids[OTHER_Y], cut))
    return moves


def nothing(*_):
    return []


def plain_gather(ffn_in, ffn_out):
    whole_in = lax.all_gather(ffn_in, "dp", axis=1, tiled=True)
    whole_out = lax.all_gather(ffn_out, "dp", axis=1, tiled=True)
    return jnp.stack([whole_in[:, :, cb * CB:(cb + 1) * CB] for cb in range(NCB)], axis=1), whole_out.reshape(LAYERS, NCB, CB, D)


def local(block_input, part_lengths, query_weight, key_weight, value_weight, out_weight, down_shared, up_shared,
          scale_d, scale_b, ln_gain, ffn_in, ffn_out, out_grad):
    mine = lax.axis_index("head") // 2
    dp = lax.axis_size("dp")
    seq = Sequence(dp)
    halves = ffn_out.reshape(LAYERS, 2, ffn_out.shape[1] // 2, D)
    scales = (scale_d, scale_b)
    if dp == 8:
        rows_in, piece = ffn_in.shape[1], halves.shape[2:]
        cuts = halves.reshape(LAYERS, 2, 4, piece[0] // 4, D)
        cut = cuts.shape[3:]
        line = [(0, slice(0, 2)), (1, None)]

        own, sent, a_in, b_in, own_a, own_b = prepare_call(seq, block_input, out_grad, ffn_in, halves)
        in_a, in_b = both_axes(a_in, Z_ONE), both_axes(b_in, TWO)
        got, own_a, own_b = swap(sent, ACROSS), across_y(own_a), across_y(own_b)
        wk0, wv0, down, up, a_out, b_out = seq(
            None, [None], [], name="fetch",
            fetch=[(key_weight, 0), (value_weight, 0), (down_shared, None), (up_shared, None),
                   (halves, 0), (halves, ((lambda ids_ref: (0, ids_ref[CORE])), piece))])
        keys, values, inner0, lift_v0, xb, wq0 = kv_call(
            seq, 0, own, got, wk0, wv0, down, up, *scales, fetch=[(query_weight, 0)])
        q0, qt, lift_q0, wo0 = q_call(seq, 0, xb, inner0, wq0, up, *scales, fetch=[(out_weight, 0)])
        in_z, in_x, own_y = window_lay_call(seq, in_a, in_b, own_a, own_b)
        out_a, out_b = both_axes(a_out, Z_ONE), both_axes(b_out, TWO)
        in_y, in_far = across_y(in_z), swap(in_x, ACROSS)
        a_out, b_out = cut_call(seq, cuts)
        [out0_z] = lay_call(seq, [out_a, out_b], [line])
        [first] = first_lay_call(seq, [out0_z, in_z, own_y, in_y, in_far, keys, values])
        out_a, out_b = both_axes(a_out, Z_ONE), both_axes(b_out, TWO)
        out0_y, in_y_far, first = across_y(out0_z), swap(in_y, ACROSS), swap(first, BESIDE)
        kv = (keys, values, *seq(far_body, [("v", first)], [("v", (ROWS, D), BF)] * 2, name="far"))
        y, h10, *p0 = attend_call(seq, 0, part_lengths, xb, qt, kv, wo0, ln_gain)
        stored0 = (kv, q0, inner0, lift_q0, lift_v0, h10, p0, wk0, wv0, wq0, wo0)
        w_in, w_out, a, g0, wk, wv, wq, wo = seq(
            ffn_first_body,
            [None, ("v", y), ("h", ffn_in), ("h", cuts)]
            + [("v", t) for t in (in_z, in_y, in_far, own_y, first, out0_z)],
            [("v", (LAYERS, NCB, 4, 2, rows_in, CB), BF), ("v", (LAYERS, NCB, 2, 2, 4) + cut, BF)]
            + [("v", FFN_SHAPE, BF)] * 2, [], 2 * NCB + 2, "ffn_first",
            fetch=[(t, 1) for t in (key_weight, value_weight, query_weight, out_weight)])
        out1_z, out1_own, out1_common, second = cut_lay_call(seq, out_a, out_b, in_y_far, out0_y)
        out1_own_y, out1_own_x, out1_common_y = across_y(out1_own), swap(out1_own, ACROSS), across_y(out1_common)
        second, out1_z_core = swap(second, BESIDE), swap(out1_z, BESIDE)
        x, h20, w_in, w_out, a, g0 = ffn_second_call(
            seq, 0, range(NCB // 2, NCB), (last_pieces, last_pieces_more), [in_y_far, second, out0_y, out1_z],
            y, ln_gain, w_in, w_out, a, g0)
        keys, values, inner, lift_v, xb, out1_z_core = kv_call(
            seq, 1, x, got, wk, wv, down, up, *scales, through=[out1_z_core])
        [out1_own_x] = seq(None, [], [], through=[out1_own_x])
        out1_own_yx, third_core = swap(out1_own_y, ACROSS), swap(out1_own_x, BESIDE)
        kv = (keys, values, swap(keys, BESIDE), swap(values, BESIDE))
        q, qt, lift_q = q_call(seq, 1, xb, inner, wq, up, *scales)
        y, h1, *p = attend_call(seq, 1, part_lengths, x, qt, kv, wo, ln_gain)
        a, g, w_in = ffn_hidden_call(seq, 1, range(NCB - 1), w_in, line_pieces, [out1_z_core], y)
        last, third_core = seq(last_body, [("v", t) for t in (out1_own_y, out1_common_y, out1_own_yx)],
                               [("v", (3, 4) + cut, BF)], name="lay", through=[third_core])
        last_core = swap(last, BESIDE)
        y, w_out, a, g = ffn_near_call(
            seq, 1, range(NCB - 1, NCB), w_in, w_out, a, g, near_pieces, [out1_z_core, out1_own_x, third_core, last], y)
        moves, refs = cut_pieces, [last_core]
    else:
        def pick(t, index):
            return lax.dynamic_index_in_dim(t, index, 0, keepdims=False)

        x = pick(block_input, mine)
        got = swap(jnp.stack([pick(block_input, 1 - mine), pick(out_grad, 1 - mine).astype(BF)]), ACROSS)
        blocks_in, blocks_out = plain_gather(ffn_in, ffn_out)
        for layer in range(LAYERS):
            wk, wv, down, up, wq, wo = seq(
                None, [], [], name="fetch",
                fetch=[(key_weight, layer), (value_weight, layer), (down_shared, None), (up_shared, None),
                       (query_weight, layer), (out_weight, layer)])
            keys, values, inner, lift_v, xb = kv_call(seq, layer, x, got, wk, wv, down, up, *scales)
            kv = (keys, values, swap(keys, BESIDE), swap(values, BESIDE))
            q, qt, lift_q = q_call(seq, layer, xb, inner, wq, up, *scales)
            y, h1, *p = attend_call(
                seq, layer, part_lengths, xb if layer == 0 else x, qt, kv, wo, ln_gain)
            if layer == 0:
                a, g0 = seq(None, [], [("v", FFN_SHAPE, BF)] * 2)
                w_in, w_out = seq(None, [], [], name="fetch", fetch=[(blocks_in, None), (blocks_out, None)])
                x, h20, w_in, w_out, a, g0 = ffn_second_call(
                    seq, 0, range(NCB), (nothing, nothing), [], y, ln_gain, w_in, w_out, a, g0)
                stored0 = (kv, q, inner, lift_q, lift_v, h1, p, wk, wv, wq, wo)
        a, g, w_in = ffn_hidden_call(seq, 1, range(NCB), w_in, nothing, [], y)
        moves, refs = nothing, []
    output, other_output, dh, w_out = ffn_both_call(
        seq, 1, w_in, w_out, a, g, moves, refs, dp == 8, y, h1, ln_gain, got, out_grad)
    own, send, ds = attend_back_call(seq, dh, wo, q, kv, p)
    got = swap(send, BESIDE)
    dx, dub, dk, gd_q, gb_q = dq_call(seq, 1, dh, ds, q, kv, lift_q, inner, wq, up, *scales)
    dub, dv, sums = dv_call(
        seq, 1, dub, own, got, lift_v, inner, up, *scales, gd_q, gb_q, jnp.zeros((4 * LAYERS, RANK), F32))
    [cotangent] = dx_call(seq, 1, dx, dub, dk, got, dv, wk, wv, down)
    kv, q, inner, lift_q, lift_v, h1, p, wk, wv, wq, wo = stored0
    [dh] = ffn_back_call(seq, 0, cotangent, h20, g0, h1, ln_gain, w_in, w_out)
    own, send, ds, other_output = attend_back_call(seq, dh, wo, q, kv, p, through=[other_output])
    got, other_output = swap(send, BESIDE), swap(other_output, ACROSS)
    dx, dub, dk, gd_q, gb_q = dq_call(seq, 0, dh, ds, q, kv, lift_q, inner, wq, up, *scales)
    dub, dv, sums = dv_call(seq, 0, dub, own, got, lift_v, inner, up, *scales, gd_q, gb_q, sums)
    if dp == 8:
        [sums] = add_call(seq, sums, swap(sums, BESIDE))
        parts = [both_axes(sums, BOTH_SWAP), swap(sums, ACROSS), across_y(sums)]
        rows, last_rows = dx_call(seq, 0, dx, dub, dk, got, dv, wk, wv, down)
        got = swap(last_rows, ACROSS)
        [sums] = add_call(seq, sums, *parts, cost=10)
        parts = [both_axes(sums, along) for along in Z_ALL]
    else:
        rows, last_rows = dx_call(seq, 0, dx, dub, dk, got, dv, wk, wv, down)
        got = swap(last_rows, ACROSS)
        sums, parts = lax.psum(sums, ("dp", "head")), []
    block_output, input_grad = store_call(seq, output, other_output, rows, got)
    grad_d, grad_b = finish_call(seq, [sums, *parts])
    return block_output, input_grad, grad_d, grad_b


def solution(mesh):
    both = P(None, ("dp", "head"), None)
    in_specs = (both, P(None, "dp", None), P(), P(), P(), P(), P(), P(), P(), P(), P(),
                P(None, "dp", None), P(None, "dp", None), both)
    out_specs = (both, both, P(), P())
    return jax.shard_map(local, mesh=mesh, in_specs=in_specs, out_specs=out_specs, check_vma=False)
```

```python
import functools

import jax
import jax.numpy as jnp
from jax import lax
from jax.experimental import pallas as pl
from jax.experimental.pallas import tpu as pltpu
from jax.sharding import PartitionSpec as P

D = 768
HEADS = 12
HEAD_DIM = 64
FF = 3072
RANK = 1024
LEN = 512
LAYERS = 2
PAIRS = HEADS // 2
PAIR = 2 * HEAD_DIM
BLOCK = LEN // 4
ROWS = 2 * BLOCK
CB = D
NCB = FF // CB
SCALE = HEAD_DIM ** (-0.5)
BF = jnp.bfloat16
F32 = jnp.float32
MIB = 1 << 20

COLOURS = {"v": pltpu.VMEM, "h": pltpu.HBM}
SPACES = {
    "v": pl.BlockSpec(memory_space=pltpu.VMEM),
    "h": pl.BlockSpec(memory_space=pltpu.HBM),
    "s": pl.BlockSpec(memory_space=pltpu.SMEM),
    "a": pl.BlockSpec(memory_space=pl.ANY),
}


HERE, CORE, MINE, Z, Y, OTHER_Y, Z_TWO, Z_NEAR, Z_BESIDE, OTHER_CORE = range(10)
SLOTS, BLOCKS = 10, 14


def indices(dp):
    here, place = lax.axis_index("head"), lax.axis_index("dp")
    mine, core = lax.div(here, 2), lax.rem(here, 2)
    z, y = lax.div(place, 2), lax.rem(place, 2)
    line = [z, y, 1 - y] + [lax.rem(z + step, 4) for step in (2, 3 + 2 * core, 1 + 2 * core)]
    blocks = [here, here ^ 2, here ^ 1, here ^ 3]
    if dp == 8:
        slots = [2 * mine, 2 * mine + 1, 2 - 2 * mine, 3 - 2 * mine]
    else:
        slots = list(range(NCB))
    return [here, core, mine] + line + [1 - core] + slots + blocks


def dot(left, right):
    return jnp.dot(left, right, preferred_element_type=F32)


def dot_nt(left, right):
    return lax.dot_general(left, right, (((1,), (1,)), ((), ())), preferred_element_type=F32)


def normed(t):
    centred = t - jnp.mean(t, axis=-1, keepdims=True)
    inverse = lax.rsqrt(jnp.mean(centred * centred, axis=-1, keepdims=True) + 1e-05)
    return centred * inverse, inverse


def norm_back(t, gain, cotangent):
    unit, inverse = normed(t)
    scaled = cotangent * gain
    mean_e = jnp.mean(scaled, axis=-1, keepdims=True)
    mean_en = jnp.mean(scaled * unit, axis=-1, keepdims=True)
    return inverse * (scaled - mean_e - unit * mean_en)


class Copies:
    def __init__(self, sems, first=0):
        self.sems, self.count = sems, first

    def __call__(self, src, dst):
        copy = pltpu.make_async_copy(src, dst, self.sems.at[self.count])
        self.count += 1
        copy.start()
        return copy


class Sequence:
    def __init__(self, dp):
        self.dp, self.token = dp, None

    def __call__(self, body, ins, outs, scratch=(), copies=0, name="keep", fetch=(), fill=(), fill_hbm=(), through=(), limit=8, save=(), cost=0.001):
        handed = [pltpu.with_memory_space_constraint(t, pltpu.VMEM) for t in fill]
        handed += [pltpu.with_memory_space_constraint(t, pltpu.HBM) for t in fill_hbm]
        handed += list(through)
        if self.token is not None:
            handed.append(pltpu.with_memory_space_constraint(self.token, pltpu.HBM))
        fetched = [(t.shape if part is None else t.shape[1:] if isinstance(part, int) else part[1], t.dtype)
                   for t, part in fetch]
        wants = [i for i, entry in enumerate(ins) if entry is None]
        ins = [entry for entry in ins if entry is not None]
        n_in, n_fetch, n_hand, n_fill = len(ins), len(fetch), len(handed), len(fill) + len(fill_hbm)
        n_out, n_save = len(outs), len(save)
        first = self.token is None

        def whole(*refs):
            refs = list(refs)
            in_refs, fetch_refs = refs[:n_in], refs[n_in:n_in + n_fetch]
            for i in wants:
                in_refs.insert(i, indices(self.dp))
            refs = refs[n_in + n_fetch:]
            refs = refs[n_hand:]
            out_refs, fetch_outs = refs[:n_out], refs[n_out:n_out + n_fetch]
            refs = refs[n_out + n_fetch:]
            fill_refs = refs[:n_fill]
            save_refs = refs[n_hand + first:][:n_save]
            refs = refs[n_hand + first + n_save:]
            scratch_refs, sems = refs[:len(scratch)], refs[len(scratch)]
            copy = Copies(sems, copies)
            waits = []
            for (_, part), source, target in zip(fetch, fetch_refs, fetch_outs, strict=True):
                if part is not None:
                    source = source.at[part if isinstance(part, int) else part[0](in_refs[0])]
                waits.append(copy(source, target))
            for place, target in zip(save, save_refs, strict=True):
                waits.append(copy(in_refs[place], target))
            if body is not None:
                body(*in_refs, *fill_refs, *out_refs, *scratch_refs, sems)
            for wait in waits:
                wait.wait()

        shapes = [COLOURS[space](shape, dtype) for space, shape, dtype in outs]
        shapes += [pltpu.VMEM(shape, dtype) for shape, dtype in fetched]
        shapes += [pltpu.VMEM(t.shape, t.dtype) for t in fill] + [pltpu.HBM(t.shape, t.dtype) for t in fill_hbm]
        shapes += [jax.ShapeDtypeStruct(t.shape, t.dtype) for t in through]
        shapes += [pltpu.HBM((8, 128), F32)]
        shapes += [pltpu.HBM(ins[place][1].shape, ins[place][1].dtype) for place in save]
        results = pl.pallas_call(
            whole,
            out_shape=tuple(shapes),
            in_specs=[SPACES[space] for space, _ in ins] + [SPACES["h"]] * n_fetch + [SPACES["v"]] * len(fill)
            + [SPACES["h"]] * len(fill_hbm) + [SPACES["a"]] * (n_hand - n_fill),
            out_specs=tuple([SPACES[space] for space, _, _ in outs] + [SPACES["v"]] * (n_fetch + len(fill))
                            + [SPACES["h"]] * len(fill_hbm) + [SPACES["a"]] * (n_hand - n_fill + first) + [SPACES["h"]] * n_save),
            scratch_shapes=[pltpu.VMEM(shape, dtype) for shape, dtype in scratch]
            + [pltpu.SemaphoreType.DMA((copies + n_fetch + n_save + 1,))],
            input_output_aliases={n_in + n_fetch + i: n_out + n_fetch + i for i in range(n_hand)},
            compiler_params=pltpu.CompilerParams(vmem_limit_bytes=limit * MIB),
            cost_estimate=pl.CostEstimate(
                flops=int(cost * 1e9), bytes_accessed=int(cost * 3e6), transcendentals=0),
            name=name,
        )(*[pltpu.with_memory_space_constraint(t, COLOURS[space]) if space in COLOURS else t for space, t in ins],
          *[pltpu.with_memory_space_constraint(t, pltpu.HBM) for t, _ in fetch],
          *handed)
        results = list(results)
        split = n_out + n_fetch + n_fill + len(through)
        self.token = results[split]
        return results[:split] + results[split + 1:]


def kv_body(layer, x_ref, got_ref, wk, wv, down, up, sd_ref, sb_ref, *rest):
    keys, values, inner_out, lift_out, xb_ref, _ = rest
    if layer == 0:
        xb_ref[:BLOCK] = x_ref[...]
        xb_ref[BLOCK:] = got_ref[0]
    else:
        xb_ref[...] = x_ref[...].astype(BF)
    xb = xb_ref[...]
    inner = dot(xb, down[...])
    inner_out[...] = inner.astype(BF)
    lift = dot((sd_ref[layer, 1:2, :] * inner).astype(BF), up[...])
    lift_out[...] = lift.astype(BF)
    values[...] = (dot(xb, wv[...]) + sb_ref[layer, 1:2, :] * lift).astype(BF)
    keys[...] = dot(xb, wk[...]).astype(BF)


def kv_call(seq, layer, x, got, wk, wv, down, up, sd, sb, **extra):
    return seq(
        functools.partial(kv_body, layer),
        [("v", t) for t in (x, got, wk, wv, down, up, sd, sb)],
        [("v", (ROWS, D), BF)] * 2 + [("v", (ROWS, RANK), BF), ("v", (ROWS, D), BF), ("v", (ROWS, D), BF)],
        name="keys_values", **extra)


def q_body(layer, x_ref, inner, wq, up, sd_ref, sb_ref, q_ref, qt_ref, lift_out, sems):
    lift = dot((sd_ref[layer, 0:1, :] * inner[...].astype(F32)).astype(BF), up[...])
    lift_out[...] = lift.astype(BF)
    q = (dot(x_ref[...], wq[...]) + sb_ref[layer, 0:1, :] * lift).astype(BF)
    q_ref[...] = q
    qt_ref[...] = (q * SCALE).T


def q_call(seq, layer, x, inner, wq, up, sd, sb, **extra):
    return seq(
        functools.partial(q_body, layer),
        [("v", x), ("v", inner), ("v", wq), ("v", up), ("v", sd), ("v", sb)],
        [("v", (ROWS, D), BF), ("v", (D, ROWS), BF), ("v", (ROWS, D), BF)],
        name="queries", **extra)


def split_heads(t):
    zero = jnp.zeros((HEAD_DIM, t.shape[1]), t.dtype)
    first = jnp.concatenate([t[:HEAD_DIM], zero], axis=0)
    second = jnp.concatenate([zero, t[HEAD_DIM:]], axis=0)
    return jnp.concatenate([first, second], axis=1)


def join_heads(t):
    n = t.shape[1] // 2
    return jnp.concatenate([t[:HEAD_DIM, :n], t[HEAD_DIM:, n:]], axis=0)


def stack_heads(t):
    lane = lax.broadcasted_iota(jnp.int32, (1, PAIR), 1)
    first = (lane < HEAD_DIM).astype(F32).astype(BF)
    second = (lane >= HEAD_DIM).astype(F32).astype(BF)
    return jnp.concatenate([t * first, t * second], axis=0)


def rows_of(near, far, cols):
    return jnp.concatenate([near[:, cols], far[:, cols]], axis=0)


def attend_body(layer, ids, lengths, x_ref, qt_ref, wo, gain_ref, keys, values, far_keys, far_values,
                y_ref, h_ref, e_ref, factor_ref, ctx_t_ref, ctx, sems):
    row = lax.broadcasted_iota(jnp.int32, (BLOCK, 2 * ROWS), 0)
    counts = lengths[ids[MINE]]
    live = counts[:, :1] + counts[:, 1:] + 4
    limits = [live - BLOCK * ids[BLOCKS + b] for b in range(4)]
    for pair in range(PAIRS):
        cols = slice(pair * PAIR, (pair + 1) * PAIR)
        raw = dot(rows_of(keys, far_keys, cols), split_heads(qt_ref[cols, :]))
        scores = jnp.concatenate(
            [jnp.where(row < limits[b], raw[b * BLOCK:(b + 1) * BLOCK], -1000000000.0) for b in range(4)],
            axis=0,
        )
        grown = jnp.exp(scores - jnp.max(scores, axis=0, keepdims=True))
        factor = 1.0 / jnp.sum(grown, axis=0, keepdims=True)
        factor_ref[pair:pair + 1, :] = factor
        e_ref[pair] = grown.astype(BF)
        ctx_t = join_heads(dot(rows_of(values, far_values, cols).T, e_ref[pair]) * factor)
        ctx_t_ref[cols, :] = ctx_t
        ctx[:, cols] = ctx_t.astype(BF).T
    h = x_ref[...].astype(F32) + dot(ctx[...], wo[...])
    h_ref[...] = h
    y_ref[...] = normed(h)[0] * gain_ref[layer, 0:1, :]


def attend_call(seq, layer, lengths, x, qt, kv, wo, gain, **extra):
    return seq(
        functools.partial(attend_body, layer),
        [None] + [("v", t) for t in (lengths, x, qt, wo, gain, *kv)],
        [("v", (ROWS, D), F32), ("v", (ROWS, D), F32), ("v", (PAIRS, LEN, 2 * ROWS), BF), ("v", (PAIRS, 2 * ROWS), F32),
         ("v", (D, ROWS), F32)],
        [((ROWS, D), BF)], name="attention", **extra)


def move(pairs):
    for source, target in pairs:
        target[...] = source[...].reshape(target.shape)


def ffn_hidden(yb, w_in, a_ref, g_ref, slots):
    for slot in slots:
        z = dot(yb, w_in[slot].reshape(D, CB))
        cdf = 0.5 * (1.0 + lax.erf(z * (0.5 ** 0.5)))
        g_ref[slot] = (cdf + z * (jnp.exp(-0.5 * z * z) * 0.3989422804014327)).astype(BF)
        a_ref[slot] = (z * cdf).astype(BF)


def ffn_result(ids, total, a_ref, w_out, y=None):
    size = CB if y is None else CB // 2
    for slot in range(NCB):
        if y is None:
            hidden, rows = a_ref[slot], w_out[ids[SLOTS + slot]]
        else:
            hidden = a_ref[slot, :, pl.ds(pl.multiple_of(y * size, size), size)]
            rows = w_out[ids[SLOTS + slot], y]
        total = total + dot(hidden, rows.reshape(size, D))
    return total


def ffn_backward(layer, ids, c, h2, g_ref, h1, gain_ref, w_in, w_out, dh_ref):
    dh2 = norm_back(h2, gain_ref[layer, 1:2, :], c)
    dfb = dh2.astype(BF)
    total = dh2
    for slot in range(NCB):
        da = dot_nt(dfb, w_out[ids[SLOTS + slot]].reshape(CB, D))
        dz = (g_ref[slot].astype(F32) * da).astype(BF)
        total = total + dot_nt(dz, w_in[slot].reshape(D, CB))
    dh1 = norm_back(h1, gain_ref[layer, 0:1, :], total)
    dh_ref[...] = dh1


FFN_SHAPE = (NCB, ROWS, CB)


def ffn_first_body(ids, y_ref, in_ref, cut_ref, in_z, in_y, in_far, own_y, first, out0_z,
                   w_in, w_out, a_ref, g_ref, sems):
    copy = Copies(sems)
    w_in = [w_in.at[layer] for layer in range(LAYERS)]
    w_out = [w_out.at[layer] for layer in range(LAYERS)]
    owns = [[copy(source, target) for source, target in own_in(layer, ids, in_ref, w_in[layer])] for layer in range(LAYERS)]
    own_out = [copy(cut_ref.at[layer], w_out[layer].at[ids[Z], ids[Y]]) for layer in range(LAYERS)]
    lines = [(in_z, 0), (first, 0), (in_y, 0), (first, 6), (own_y, 0), (first, 3), (in_far, 0), (first, 9)]
    move(pieces_in(0, ids, lines, w_in[0]))
    for wait in owns[0]:
        wait.wait()
    ffn_hidden(y_ref[...].astype(BF), w_in[0], a_ref, g_ref, range(NCB // 2))
    move(pieces_in(1, ids, lines, w_in[1]))
    for side, line in enumerate([(out0_z, 0), (first, 13)]):
        move(line_moves(ids, line, side, slice(None), out_target(w_out[0], ids[Y])))
    for side, (ref, start) in enumerate([(own_y, 0), (first, 3)]):
        core = ids[CORE] if side == 0 else ids[OTHER_CORE]
        for layer in range(LAYERS):
            move([(ref.at[start + 1 + layer], w_out[layer].at[ids[Z], ids[OTHER_Y], core])])
    for wait in owns[1] + own_out:
        wait.wait()


def ffn_second_body(layer, slots, moves, n_refs, ids, y_ref, gain_ref, *rest):
    refs, rest = rest[:n_refs], rest[n_refs:]
    w_in, w_out, a_ref, g_ref, x_ref, h_ref, _ = rest
    move(moves[0](ids, refs, w_in, w_out))
    ffn_hidden(y_ref[...].astype(BF), w_in.at[layer], a_ref, g_ref, slots)
    move(moves[1](ids, refs, w_in, w_out))
    h_ref[...] = ffn_result(ids, y_ref[...], a_ref, w_out.at[layer])
    x_ref[...] = normed(h_ref[...])[0] * gain_ref[layer, 1:2, :]


def ffn_second_call(seq, layer, slots, moves, refs, y, gain, w_in, w_out, a, g, **extra):
    return seq(
        functools.partial(ffn_second_body, layer, slots, moves, len(refs)),
        [None, ("v", y), ("v", gain)] + [("v", t) for t in refs],
        [("v", (ROWS, D), F32), ("v", (ROWS, D), F32)], name="ffn", fill=[w_in, w_out, a, g], **extra)


FFN_SHAPE = (NCB, ROWS, CB)


def ffn_hidden_body(layer, slots, moves, n_refs, ids, y_ref, *rest):
    refs, (w_in, a_ref, g_ref, _) = rest[:n_refs], rest[n_refs:]
    move(moves(ids, refs, w_in.at[layer]))
    ffn_hidden(y_ref[...].astype(BF), w_in.at[layer], a_ref, g_ref, slots)


def ffn_hidden_call(seq, layer, slots, w_in, moves, refs, y, **extra):
    return seq(
        functools.partial(ffn_hidden_body, layer, slots, moves, len(refs)),
        [None, ("v", y)] + [("v", t) for t in refs], [("v", FFN_SHAPE, BF)] * 2, name="ffn_hidden", fill=[w_in], **extra)


def ffn_near_body(layer, slots, moves, n_refs, ids, y_ref, w_in, *rest):
    refs, (w_out, a_ref, g_ref, near_ref, _) = rest[:n_refs], rest[n_refs:]
    ffn_hidden(y_ref[...].astype(BF), w_in.at[layer], a_ref, g_ref, slots)
    w_out = w_out.at[layer]
    move(moves(ids, refs, w_out))
    near_ref[...] = ffn_result(ids, y_ref[...], a_ref, w_out, ids[Y])


def ffn_near_call(seq, layer, slots, w_in, w_out, a, g, moves, refs, y, **extra):
    return seq(
        functools.partial(ffn_near_body, layer, slots, moves, len(refs)),
        [None, ("v", y), ("v", w_in)] + [("v", t) for t in refs],
        [("v", (ROWS, D), F32)], name="ffn_near", fill=[w_out, a, g], **extra)


def ffn_both_body(layer, moves, n_refs, near, ids, y_ref, h1, gain_ref, got_ref, w_in, a_ref, g_ref, c_ref, *rest):
    refs, rest = rest[:n_refs], rest[n_refs:]
    w_out, x_ref, send_ref, dh_ref, c, sems = rest
    own = Copies(sems)(c_ref.at[ids[MINE]], c.at[pl.ds(0, BLOCK)])
    w_in, w_out = w_in.at[layer], w_out.at[layer]
    move(moves(ids, refs, w_out))
    h2 = ffn_result(ids, y_ref[...], a_ref, w_out, ids[OTHER_Y] if near else None)
    dh_ref[...] = h2
    x = normed(h2)[0] * gain_ref[layer, 1:2, :]
    x_ref[...] = x[:BLOCK].astype(BF)
    send_ref[...] = x[BLOCK:].astype(BF)
    own.wait()
    c[BLOCK:] = got_ref[1].astype(F32)
    ffn_backward(layer, ids, c[...], dh_ref[...], g_ref, h1[...], gain_ref, w_in, w_out, dh_ref)


def ffn_both_call(seq, layer, w_in, w_out, a, g, moves, refs, near, y, h1, gain, got, c, **extra):
    return seq(
        functools.partial(ffn_both_body, layer, moves, len(refs), near),
        [None] + [("v", t) for t in (y, h1, gain, got, w_in, a, g)] + [("h", c)] + [("v", t) for t in refs],
        [("v", (BLOCK, D), BF), ("v", (BLOCK, D), BF), ("v", (ROWS, D), F32)],
        [((ROWS, D), F32)], 1, "ffn_both", fill=[w_out], **extra)


def ffn_back_body(layer, ids, c_ref, h2, g, h1, gain_ref, w_in, w_out, dh_ref, sems):
    ffn_backward(layer, ids, c_ref[...], h2[...], g, h1[...], gain_ref, w_in.at[layer], w_out.at[layer], dh_ref)


def ffn_back_call(seq, layer, c, h2, g, h1, gain, w_in, w_out, **extra):
    return seq(
        functools.partial(ffn_back_body, layer),
        [None] + [("v", t) for t in (c, h2, g, h1, gain, w_in, w_out)],
        [("v", (ROWS, D), F32)], name="ffn_back", **extra)


def attend_back_body(dh_ref, wo, q, factor_ref, ctx_t_ref, keys, values, far_keys, far_values,
                     e_ref, own_ref, send_ref, dctx_ref, sems):
    dctx_ref[...] = dot_nt(dh_ref[...].astype(BF), wo[...]).astype(BF)
    for pair in range(PAIRS):
        cols = slice(pair * PAIR, (pair + 1) * PAIR)
        vcols = slice(D + pair * PAIR, D + (pair + 1) * PAIR)
        factor = factor_ref[pair:pair + 1, :]
        scaled = (split_heads(dctx_ref[:, cols].T).astype(F32) * factor).astype(BF)
        inner = jnp.sum(scaled.astype(F32) * split_heads(ctx_t_ref[cols, :]), axis=0, keepdims=True)
        e = e_ref[pair]
        ds = (e.astype(F32) * (dot(rows_of(values, far_values, cols), scaled) - inner)).astype(BF)
        dv = dot(e, scaled.T)
        dk = dot(ds[ROWS:], stack_heads(q[:, cols])) * SCALE
        own_ref[:, cols] = dv[:ROWS]
        send_ref[:, cols] = dk.astype(BF)
        send_ref[:, vcols] = dv[ROWS:].astype(BF)
        e_ref[pair] = ds


def attend_back_call(seq, dh, wo, q, kv, weights, **extra):
    e, *rest = weights
    return seq(
        attend_back_body,
        [("v", t) for t in (dh, wo, q, *rest, *kv)],
        [("v", (ROWS, D), F32), ("v", (ROWS, 2 * D), BF)],
        [((ROWS, D), BF)], name="attention_back", fill=[e], **extra)


def dq_body(layer, dh_ref, ds_ref, q, keys, far_keys, lift, inner, wq, up, sd_ref, sb_ref,
            dx_ref, dub_ref, dk_ref, gd_ref, gb_ref, dq_ref, sems):
    for pair in range(PAIRS):
        cols = slice(pair * PAIR, (pair + 1) * PAIR)
        dq_t = join_heads(dot(rows_of(keys, far_keys, cols).T, ds_ref[pair])) * SCALE
        dq_ref[:, cols] = dq_t.T.astype(BF)
        dk_ref[:, cols] = dot(ds_ref[pair, :ROWS], stack_heads(q[:, cols])) * SCALE
    dq = dq_ref[...]
    dqf = dq.astype(F32)
    gb_ref[...] = jnp.sum(dqf * lift[...].astype(F32), axis=0, keepdims=True)
    dpq = dot_nt((sb_ref[layer, 0:1, :] * dqf).astype(BF), up[...])
    gd_ref[...] = jnp.sum(dpq * inner[...].astype(F32), axis=0, keepdims=True)
    dub_ref[...] = sd_ref[layer, 0:1, :] * dpq
    dx_ref[...] = dh_ref[...] + dot_nt(dq, wq[...])


def dq_call(seq, layer, dh, ds, q, kv, lift, inner, wq, up, sd, sb, **extra):
    return seq(
        functools.partial(dq_body, layer),
        [("v", t) for t in (dh, ds, q, kv[0], kv[2], lift, inner, wq, up, sd, sb)],
        [("v", (ROWS, D), F32), ("v", (ROWS, RANK), F32), ("v", (ROWS, D), F32), ("v", (1, RANK), F32), ("v", (1, D), F32)],
        [((ROWS, D), BF)], name="queries_back", **extra)


def dv_body(layer, dub_ref, own_ref, got_ref, lift, inner, up, sd_ref, sb_ref, gdq_ref, gbq_ref, before_ref,
            dub_out, dv_ref, sums_ref, sems):
    sums_ref[...] = before_ref[...]
    sums_ref[4 * layer:4 * layer + 1, :] = gdq_ref[...]
    sums_ref[4 * layer + 2:4 * layer + 3, :D] = gbq_ref[...]
    dv = (own_ref[...] + got_ref[:, D:].astype(F32)).astype(BF)
    dv_ref[...] = dv
    dvf = dv.astype(F32)
    sums_ref[4 * layer + 3:4 * layer + 4, :D] = jnp.sum(dvf * lift[...].astype(F32), axis=0, keepdims=True)
    dpv = dot_nt((sb_ref[layer, 1:2, :] * dvf).astype(BF), up[...])
    sums_ref[4 * layer + 1:4 * layer + 2, :] = jnp.sum(dpv * inner[...].astype(F32), axis=0, keepdims=True)
    dub_out[...] = (dub_ref[...] + sd_ref[layer, 1:2, :] * dpv).astype(BF)


def dv_call(seq, layer, dub, own, got, lift, inner, up, sd, sb, gd, gb, before, **extra):
    return seq(
        functools.partial(dv_body, layer),
        [("v", t) for t in (dub, own, got, lift, inner, up, sd, sb, gd, gb, before)],
        [("v", (ROWS, RANK), BF), ("v", (ROWS, D), BF), ("v", (4 * LAYERS, RANK), F32)],
        name="values_back", **extra)


def dx_body(layer, dx_ref, dub_ref, dk_ref, got_ref, dv_ref, wk, wv, down, *rest):
    total = dx_ref[...] + dot_nt(dub_ref[...], down[...])
    total = total + dot_nt(dv_ref[...], wv[...])
    dk = (dk_ref[...] + got_ref[:, :D].astype(F32)).astype(BF)
    total = total + dot_nt(dk, wk[...])
    if layer == 0:
        own_ref, send_ref, _ = rest
        own_ref[...] = total[:BLOCK]
        send_ref[...] = total[BLOCK:].astype(BF)
    else:
        rest[0][...] = total


def dx_call(seq, layer, dx, dub, dk, got, dv, wk, wv, down, **extra):
    return seq(
        functools.partial(dx_body, layer),
        [("v", t) for t in (dx, dub, dk, got, dv, wk, wv, down)],
        [("v", (BLOCK, D), F32), ("v", (BLOCK, D), BF)] if layer == 0 else [("v", (ROWS, D), F32)],
        name="input_back", **extra)


def add_call(seq, *terms, **extra):
    def body(*refs):
        total = refs[0][...]
        for ref in refs[1:len(terms)]:
            total = total + ref[...]
        refs[len(terms)][...] = total

    return seq(body, [("v", t) for t in terms], [("v", terms[0].shape, F32)], name="add", **extra)


def store_call(seq, output, other_output, rows):
    def body(ids_ref, output_ref, other_ref, rows_ref, block_ref, grad_ref, sems):
        copy = Copies(sems)
        mine = ids_ref[MINE]
        stores = [copy(rows_ref, grad_ref.at[mine]), copy(output_ref, block_ref.at[mine]), copy(other_ref, block_ref.at[1 - mine])]
        for store in stores:
            store.wait()

    return seq(body, [None] + [("v", t) for t in (output, other_output, rows)],
               [("h", (2,) + t.shape, t.dtype) for t in (output, rows)], [], 3, "store")


def finish_call(seq, terms, got, input_grad):
    def body(ids_ref, got_ref, *refs):
        *terms_refs, grad_ref, gd_out, gb_out, wide, gd_ref, gb_ref, sems = refs
        copy = Copies(sems)
        wide[...] = got_ref[...].astype(F32)
        stores = [copy(wide, grad_ref.at[1 - ids_ref[MINE]])]
        total = terms_refs[0][...]
        for ref in terms_refs[1:]:
            total = total + ref[...]
        for layer in range(LAYERS):
            gd_ref[layer] = total[4 * layer:4 * layer + 2]
            gb_ref[layer] = total[4 * layer + 2:4 * layer + 4, :D]
        stores += [copy(gd_ref, gd_out), copy(gb_ref, gb_out)]
        for store in stores:
            store.wait()

    shapes = [((LAYERS, 2, RANK), F32), ((LAYERS, 2, D), F32)]
    return seq(body, [None, ("v", got)] + [("v", t) for t in terms], [("h", *t) for t in shapes],
               [(got.shape, F32)] + shapes, 3, "finish", fill_hbm=[input_grad])


def columns(block):
    return pl.ds(pl.multiple_of(block * CB, CB), CB)


def prepare_line_body(ids, in_ref, a_in, sems):
    copy, rows, waits = Copies(sems), in_ref.shape[1], []
    for layer in range(LAYERS):
        for q in range(2):
            waits.append(copy(in_ref.at[layer, :, columns(2 * ids[MINE] + q)], a_in.at[q, pl.ds(layer * rows, rows)]))
    for wait in waits:
        wait.wait()


def prepare_body(ids, x_ref, c_ref, in_ref, out_ref, own, sent, b_in, own_a, own_b, c_send, sems):
    copy = Copies(sems)
    here, core, mine = ids[HERE], ids[CORE], ids[MINE]
    rows = in_ref.shape[1]
    waits = [copy(c_ref.at[1 - mine], c_send)]
    for layer in range(LAYERS):
        part = pl.ds(layer * rows, rows)
        waits.append(copy(in_ref.at[layer, :, columns(here)], b_in.at[part]))
        waits.append(copy(in_ref.at[layer, :, columns(here)], own_a.at[part]))
    piece = own_a.shape[0] - rows
    half = pl.ds(0, rows), pl.ds(rows, rows)
    waits.append(copy(out_ref.at[0, core, half[0]], own_a.at[pl.ds(piece, rows)]))
    waits.append(copy(out_ref.at[0, core, half[1]], own_b.at[half[0]]))
    waits.append(copy(out_ref.at[1, core], own_b.at[pl.ds(rows, piece)]))
    waits += [copy(x_ref.at[1 - mine], sent.at[0]), copy(x_ref.at[mine], own)]
    waits[0].wait()
    sent[1] = c_send[...].astype(BF)
    for wait in waits[1:]:
        wait.wait()


def prepare_call(seq, x, c, ffn_in, halves):
    rows = (BLOCK, D)
    piece = halves.shape[2:]
    [a_in] = seq(prepare_line_body, [None, ("h", ffn_in)], [("v", (2,) + piece, BF)], [], 2 * LAYERS, "prepare")
    own, sent, *rest = seq(
        prepare_body,
        [None, ("h", x), ("h", c), ("h", ffn_in), ("h", halves)],
        [("v", rows, BF), ("v", (2,) + rows, BF), ("v", piece, BF)]
        + [("v", (piece[0] * 3 // 2,) + piece[1:], BF)] * 2,
        [(rows, F32)], 6 + 2 * LAYERS, "prepare")
    return own, sent, a_in, *rest


def everywhere(target):
    pairs = []
    for z in range(4):
        for y in range(2):
            for head in range(4):
                z_to, y_to, head_to = target(z, y, head)
                pairs.append(((2 * z + y) * 4 + head, (2 * (z_to % 4) + y_to) * 4 + head_to))
    return pairs


Z_ONE = everywhere(lambda z, y, head: (z + 1 - 2 * (head % 2), y, head))
TWO = everywhere(lambda z, y, head: (z + 2, y, head))
Y_SWAP = [(i, i ^ 1) for i in range(8)]
BOTH_SWAP = everywhere(lambda z, y, head: (z, 1 - y, head ^ 2))
Z_ALL = [everywhere(lambda z, y, head, other=other: (z ^ other, y, head)) for other in (2, 3, 1)]
ACROSS = [(i, i ^ 2) for i in range(4)]
BESIDE = [(i, i ^ 1) for i in range(4)]


def swap(t, pairs):
    return lax.ppermute(t, "head", pairs)


def both_axes(t, pairs):
    return lax.ppermute(t, ("dp", "head"), pairs)


def across_y(t):
    return lax.ppermute(t, "dp", Y_SWAP)


def lay_call(seq, arrays, outs, **extra):
    piece = arrays[0].shape[-2:]

    def length(part):
        return 1 if part is None else part.stop - part.start

    def body(*refs):
        for out, result in zip(outs, refs[len(arrays):], strict=False):
            start = 0
            for index, part in out:
                stop = start + length(part)
                result[start:stop] = refs[index][...][None] if part is None else refs[index][part]
                start = stop

    shapes = [(sum(length(part) for _, part in out),) + piece for out in outs]
    return seq(body, [("v", t) for t in arrays], [("v", shape, BF) for shape in shapes], name="lay", **extra)


def cut_call(seq, cuts):
    cut = cuts.shape[3:]

    def body(ids_ref, cuts_ref, a_ref, b_ref, sems):
        copy = Copies(sems)
        waits = []
        for core, target in ((0, a_ref.at[0]), (1, a_ref.at[1]), (ids_ref[CORE], b_ref)):
            waits.append(copy(cuts_ref.at[1, core, ids_ref[MINE]], target.at[0]))
            waits.append(copy(cuts_ref.at[1, core, pl.ds(2, 2)], target.at[pl.ds(1, 2)]))
        for wait in waits:
            wait.wait()

    return seq(body, [None, ("h", cuts)], [("v", (2, 3) + cut, BF), ("v", (3,) + cut, BF)], [], 6, "cut")


def cut_lay_call(seq, out_a, out_b, in_y_far, out0_y):
    cut = out_b.shape[1:]

    def body_z(a_ref, b_ref, line_ref, sems):
        line_ref[:2] = a_ref[...]
        line_ref[2] = b_ref[...]

    [line] = seq(body_z, [("v", out_a), ("v", out_b)], [("v", (3, 3) + cut, BF)], name="lay")
    return cut_lay_rest_call(seq, line, in_y_far, out0_y)


def cut_lay_rest_call(seq, line, in_y_far, out0_y):
    cut = line.shape[2:]
    piece = out0_y.shape[1:]

    def body(z_ref, far_ref, y_ref, line_ref, own_ref, common_ref, second_ref, sems):
        rows = piece[0] // LAYERS
        line_ref[:, :3] = z_ref[...]
        line_ref[:, 3:] = far_ref[:, rows:].reshape((3, 2) + cut)
        own_ref[...] = z_ref[:, 0]
        common_ref[...] = z_ref[:, 1:]
        second_ref[:, :rows] = far_ref[:, :rows]
        second_ref[:, rows:] = y_ref[...]

    return seq(body, [("v", t) for t in (line, in_y_far, out0_y)],
               [("v", (3, 5) + cut, BF), ("v", (3,) + cut, BF), ("v", (3, 2) + cut, BF),
                ("v", (3, piece[0] // LAYERS + piece[0]) + piece[1:], BF)], name="lay")


def window_lay_call(seq, in_a, in_b, own_a, own_b):
    piece = in_b.shape

    def body(a_ref, b_ref, own_a_ref, own_b_ref, z_ref, x_ref, own_ref, sems):
        full, half = piece[0], piece[0] // 2
        own_ref[0] = own_a_ref[:full]
        own_ref[1, :half] = own_a_ref[full:]
        own_ref[1, half:] = own_b_ref[:half]
        own_ref[2] = own_b_ref[half:]
        for ref in (z_ref, x_ref):
            ref[:2] = a_ref[...]
            ref[2] = b_ref[...]
        x_ref[3] = own_a_ref[:full]

    return seq(body, [("v", t) for t in (in_a, in_b, own_a, own_b)],
               [("v", (count,) + piece, BF) for count in (3, 4, 3)], name="lay")


def first_lay_call(seq, arrays):
    piece = arrays[0].shape[-2:]
    extra = -(-2 * ROWS // piece[0])

    def body(out0_z, in_z, own_y, in_y, in_far, keys, values, first_ref, sems):
        for start, ref in ((0, in_z), (3, own_y), (6, in_y), (9, in_far), (13, out0_z)):
            first_ref[start:start + ref.shape[0]] = ref[...]
        both = jnp.concatenate([keys[...], values[...]], axis=0)
        for i in range(extra):
            rows = min(piece[0], 2 * ROWS - i * piece[0])
            first_ref[16 + i, :rows] = both[i * piece[0]:i * piece[0] + rows]

    return seq(body, [("v", t) for t in arrays], [("v", (16 + extra,) + piece, BF)], name="lay")


def far_body(first_ref, keys, values, sems):
    rows, count = first_ref.shape[1], first_ref.shape[0] - 16
    both = first_ref[16:].reshape(count * rows, D)
    keys[...] = both[:ROWS]
    values[...] = both[ROWS:2 * ROWS]


def last_body(own_y, common_y, own_yx, out_ref, sems):
    out_ref[:, 0] = own_y[...]
    out_ref[:, 1:3] = common_y[...]
    out_ref[:, 3] = own_yx[...]


def line_moves(ids, line, side, part, target):
    core, z_near = (ids[CORE], ids[Z_NEAR]) if side == 0 else (ids[OTHER_CORE], ids[Z_BESIDE])
    ref, start = line
    return [(ref.at[pl.ds(start, 2), part], target(z_near, pl.ds(0, 2))),
            (ref.at[start + 2, part], target(ids[Z_TWO], core))]


def in_target(dst, slot, y):
    def target(z, piece):
        return dst.at[pl.ds(slot, 2) if not isinstance(piece, jax.Array) else slot + piece, z, y]

    return target


def own_in(layer, ids, ref, dst):
    columns = [pl.ds(pl.multiple_of(ids[SLOTS + slot] * CB, CB), CB) for slot in range(NCB)]
    return [(ref.at[layer, :, columns[slot]], dst.at[slot, ids[Z], ids[Y]]) for slot in range(NCB)]


def pieces_in(layer, ids, lines, dst):
    part = pl.ds(layer * dst.shape[3], dst.shape[3])
    z, y = ids[Z], (ids[Y], ids[OTHER_Y])
    moves = []
    for side in range(2):
        core = ids[CORE] if side == 0 else ids[OTHER_CORE]
        along, across, own, far = lines[side::2]
        moves += line_moves(ids, along, side, part, in_target(dst, 0, y[0]))
        moves += line_moves(ids, across, side, part, in_target(dst, 0, y[1]))
        moves.append((own[0].at[own[1], part], dst.at[core, z, y[1]]))
        moves += line_moves(ids, far, side, part, in_target(dst, 2, y[0]))
        moves.append((far[0].at[far[1] + 3, part], dst.at[2 + core, z, y[1]]))
    return moves


def out_target(dst, y, cut=None):
    def target(z, piece):
        if not isinstance(piece, jax.Array):
            return dst.at[z, y] if cut is None else dst.at[z, y, :, cut]
        return dst.at[z, y, piece] if cut is None else dst.at[z, y, piece, cut]

    return target


def last_pieces(ids, refs, w_in, w_out):
    rows = pl.ds(0, w_in.shape[4])
    return [pair for side in range(2)
            for pair in line_moves(ids, (refs[side], 0), side, rows, in_target(w_in.at[0], 2, ids[OTHER_Y]))]


def last_pieces_more(ids, refs, w_in, w_out):
    in_y_far, second, out0_y, out1_z = refs
    rows = w_in.shape[4]
    moves = line_moves(ids, (out0_y, 0), 0, slice(None), out_target(w_out.at[0], ids[OTHER_Y]))
    moves += line_moves(ids, (second, 0), 1, pl.ds(rows, second.shape[1] - rows), out_target(w_out.at[0], ids[OTHER_Y]))
    moves += line_moves(ids, (in_y_far, 0), 0, pl.ds(rows, rows), in_target(w_in.at[1], 2, ids[OTHER_Y]))
    return moves + cut_line(ids, out1_z, 0, w_out.at[1])


def cut_line(ids, ref, side, dst):
    x, y = ids[MINE], ids[Y]
    return (line_moves(ids, (ref, 0), side, 0, out_target(dst, y, x))
            + line_moves(ids, (ref, 0), side, pl.ds(1, 2), out_target(dst, y, pl.ds(2, 2))))


def line_pieces(ids, refs, w_in):
    return line_moves(ids, (refs[0], 0), 1, pl.ds(3, 2), in_target(w_in, 2, ids[OTHER_Y]))


def near_pieces(ids, refs, w_out):
    core_line, *refs, last = refs
    moves = cut_line(ids, core_line, 1, w_out)
    for side in range(2):
        moves += line_moves(ids, (refs[side], 0), side, slice(None), out_target(w_out, ids[Y], 1 - ids[MINE]))
    return moves + cut_pieces(ids, [last], w_out, 0)


def cut_pieces(ids, refs, w_out, side=1):
    x, moves = ids[MINE], []
    for part, cut in ((0, x), (pl.ds(1, 2), pl.ds(2, 2)), (3, 1 - x)):
        moves += line_moves(ids, (refs[0], 0), side, part, out_target(w_out, ids[OTHER_Y], cut))
    return moves


def nothing(*_):
    return []


def plain_gather(ffn_in, ffn_out):
    whole_in = lax.all_gather(ffn_in, "dp", axis=1, tiled=True)
    whole_out = lax.all_gather(ffn_out, "dp", axis=1, tiled=True)
    return jnp.stack([whole_in[:, :, cb * CB:(cb + 1) * CB] for cb in range(NCB)], axis=1), whole_out.reshape(LAYERS, NCB, CB, D)


def local(block_input, part_lengths, query_weight, key_weight, value_weight, out_weight, down_shared, up_shared,
          scale_d, scale_b, ln_gain, ffn_in, ffn_out, out_grad):
    mine = lax.axis_index("head") // 2
    dp = lax.axis_size("dp")
    seq = Sequence(dp)
    halves = ffn_out.reshape(LAYERS, 2, ffn_out.shape[1] // 2, D)
    scales = (scale_d, scale_b)
    if dp == 8:
        rows_in, piece = ffn_in.shape[1], halves.shape[2:]
        cuts = halves.reshape(LAYERS, 2, 4, piece[0] // 4, D)
        cut = cuts.shape[3:]
        line = [(0, slice(0, 2)), (1, None)]

        own, sent, a_in, b_in, own_a, own_b = prepare_call(seq, block_input, out_grad, ffn_in, halves)
        in_a, in_b = both_axes(a_in, Z_ONE), both_axes(b_in, TWO)
        got, own_a, own_b = swap(sent, ACROSS), across_y(own_a), across_y(own_b)
        wk0, wv0, down, up, a_out, b_out = seq(
            None, [None], [], name="fetch",
            fetch=[(key_weight, 0), (value_weight, 0), (down_shared, None), (up_shared, None),
                   (halves, 0), (halves, ((lambda ids_ref: (0, ids_ref[CORE])), piece))])
        keys, values, inner0, lift_v0, xb, wq0 = kv_call(
            seq, 0, own, got, wk0, wv0, down, up, *scales, fetch=[(query_weight, 0)])
        q0, qt, lift_q0, wo0 = q_call(seq, 0, xb, inner0, wq0, up, *scales, fetch=[(out_weight, 0)])
        in_z, in_x, own_y = window_lay_call(seq, in_a, in_b, own_a, own_b)
        out_a, out_b = both_axes(a_out, Z_ONE), both_axes(b_out, TWO)
        in_y, in_far = across_y(in_z), swap(in_x, ACROSS)
        a_out, b_out = cut_call(seq, cuts)
        [out0_z] = lay_call(seq, [out_a, out_b], [line])
        [first] = first_lay_call(seq, [out0_z, in_z, own_y, in_y, in_far, keys, values])
        out_a, out_b = both_axes(a_out, Z_ONE), both_axes(b_out, TWO)
        out0_y, in_y_far, first = across_y(out0_z), swap(in_y, ACROSS), swap(first, BESIDE)
        kv = (keys, values, *seq(far_body, [("v", first)], [("v", (ROWS, D), BF)] * 2, name="far"))
        y, h10, *p0 = attend_call(seq, 0, part_lengths, xb, qt, kv, wo0, ln_gain)
        stored0 = (kv, q0, inner0, lift_q0, lift_v0, h10, p0, wk0, wv0, wq0, wo0)
        w_in, w_out, a, g0, wk, wv, wq, wo = seq(
            ffn_first_body,
            [None, ("v", y), ("h", ffn_in), ("h", cuts)]
            + [("v", t) for t in (in_z, in_y, in_far, own_y, first, out0_z)],
            [("v", (LAYERS, NCB, 4, 2, rows_in, CB), BF), ("v", (LAYERS, NCB, 2, 2, 4) + cut, BF)]
            + [("v", FFN_SHAPE, BF)] * 2, [], 2 * NCB + 2, "ffn_first",
            fetch=[(t, 1) for t in (key_weight, value_weight, query_weight, out_weight)])
        out1_z, out1_own, out1_common, second = cut_lay_call(seq, out_a, out_b, in_y_far, out0_y)
        out1_own_y, out1_own_x, out1_common_y = across_y(out1_own), swap(out1_own, ACROSS), across_y(out1_common)
        second, out1_z_core = swap(second, BESIDE), swap(out1_z, BESIDE)
        x, h20, w_in, w_out, a, g0 = ffn_second_call(
            seq, 0, range(NCB // 2, NCB), (last_pieces, last_pieces_more), [in_y_far, second, out0_y, out1_z],
            y, ln_gain, w_in, w_out, a, g0)
        keys, values, inner, lift_v, xb, out1_z_core = kv_call(
            seq, 1, x, got, wk, wv, down, up, *scales, through=[out1_z_core])
        [out1_own_x] = seq(None, [], [], through=[out1_own_x])
        out1_own_yx, third_core = swap(out1_own_y, ACROSS), swap(out1_own_x, BESIDE)
        kv = (keys, values, swap(keys, BESIDE), swap(values, BESIDE))
        q, qt, lift_q = q_call(seq, 1, xb, inner, wq, up, *scales)
        y, h1, *p = attend_call(seq, 1, part_lengths, x, qt, kv, wo, ln_gain)
        a, g, w_in = ffn_hidden_call(seq, 1, range(NCB - 1), w_in, line_pieces, [out1_z_core], y)
        last, third_core = seq(last_body, [("v", t) for t in (out1_own_y, out1_common_y, out1_own_yx)],
                               [("v", (3, 4) + cut, BF)], name="lay", through=[third_core])
        last_core = swap(last, BESIDE)
        y, w_out, a, g = ffn_near_call(
            seq, 1, range(NCB - 1, NCB), w_in, w_out, a, g, near_pieces, [out1_z_core, out1_own_x, third_core, last], y)
        moves, refs = cut_pieces, [last_core]
    else:
        def pick(t, index):
            return lax.dynamic_index_in_dim(t, index, 0, keepdims=False)

        x = pick(block_input, mine)
        got = swap(jnp.stack([pick(block_input, 1 - mine), pick(out_grad, 1 - mine).astype(BF)]), ACROSS)
        blocks_in, blocks_out = plain_gather(ffn_in, ffn_out)
        for layer in range(LAYERS):
            wk, wv, down, up, wq, wo = seq(
                None, [], [], name="fetch",
                fetch=[(key_weight, layer), (value_weight, layer), (down_shared, None), (up_shared, None),
                       (query_weight, layer), (out_weight, layer)])
            keys, values, inner, lift_v, xb = kv_call(seq, layer, x, got, wk, wv, down, up, *scales)
            kv = (keys, values, swap(keys, BESIDE), swap(values, BESIDE))
            q, qt, lift_q = q_call(seq, layer, xb, inner, wq, up, *scales)
            y, h1, *p = attend_call(
                seq, layer, part_lengths, xb if layer == 0 else x, qt, kv, wo, ln_gain)
            if layer == 0:
                a, g0 = seq(None, [], [("v", FFN_SHAPE, BF)] * 2)
                w_in, w_out = seq(None, [], [], name="fetch", fetch=[(blocks_in, None), (blocks_out, None)])
                x, h20, w_in, w_out, a, g0 = ffn_second_call(
                    seq, 0, range(NCB), (nothing, nothing), [], y, ln_gain, w_in, w_out, a, g0)
                stored0 = (kv, q, inner, lift_q, lift_v, h1, p, wk, wv, wq, wo)
        a, g, w_in = ffn_hidden_call(seq, 1, range(NCB), w_in, nothing, [], y)
        moves, refs = nothing, []
    output, other_output, dh, w_out = ffn_both_call(
        seq, 1, w_in, w_out, a, g, moves, refs, dp == 8, y, h1, ln_gain, got, out_grad)
    own, send, ds = attend_back_call(seq, dh, wo, q, kv, p)
    got = swap(send, BESIDE)
    dx, dub, dk, gd_q, gb_q = dq_call(seq, 1, dh, ds, q, kv, lift_q, inner, wq, up, *scales)
    dub, dv, sums = dv_call(
        seq, 1, dub, own, got, lift_v, inner, up, *scales, gd_q, gb_q, jnp.zeros((4 * LAYERS, RANK), F32))
    [cotangent] = dx_call(seq, 1, dx, dub, dk, got, dv, wk, wv, down)
    kv, q, inner, lift_q, lift_v, h1, p, wk, wv, wq, wo = stored0
    [dh] = ffn_back_call(seq, 0, cotangent, h20, g0, h1, ln_gain, w_in, w_out)
    own, send, ds, other_output = attend_back_call(seq, dh, wo, q, kv, p, through=[other_output])
    got, other_output = swap(send, BESIDE), swap(other_output, ACROSS)
    dx, dub, dk, gd_q, gb_q = dq_call(seq, 0, dh, ds, q, kv, lift_q, inner, wq, up, *scales)
    dub, dv, sums = dv_call(seq, 0, dub, own, got, lift_v, inner, up, *scales, gd_q, gb_q, sums)
    if dp == 8:
        [sums] = add_call(seq, sums, swap(sums, BESIDE))
        parts = [both_axes(sums, BOTH_SWAP), swap(sums, ACROSS), across_y(sums)]
        rows, last_rows = dx_call(seq, 0, dx, dub, dk, got, dv, wk, wv, down)
        got = swap(last_rows, ACROSS)
        [sums] = add_call(seq, sums, *parts, cost=10)
        parts = [both_axes(sums, along) for along in Z_ALL]
    else:
        rows, last_rows = dx_call(seq, 0, dx, dub, dk, got, dv, wk, wv, down)
        got = swap(last_rows, ACROSS)
        sums, parts = lax.psum(sums, ("dp", "head")), []
    block_output, input_grad = store_call(seq, output, other_output, rows)
    grad_d, grad_b, input_grad = finish_call(seq, [sums, *parts], got, input_grad)
    return block_output, input_grad, grad_d, grad_b


def solution(mesh):
    both = P(None, ("dp", "head"), None)
    in_specs = (both, P(None, "dp", None), P(), P(), P(), P(), P(), P(), P(), P(), P(),
                P(None, "dp", None), P(None, "dp", None), both)
    out_specs = (both, both, P(), P())
    return jax.shard_map(local, mesh=mesh, in_specs=in_specs, out_specs=out_specs, check_vma=False)
```

```python
import functools

import jax
import jax.numpy as jnp
from jax import lax
from jax.experimental import pallas as pl
from jax.experimental.pallas import tpu as pltpu
from jax.sharding import PartitionSpec as P

D = 768
HEADS = 12
HEAD_DIM = 64
FF = 3072
RANK = 1024
LEN = 512
LAYERS = 2
PAIRS = HEADS // 2
PAIR = 2 * HEAD_DIM
BLOCK = LEN // 4
ROWS = 2 * BLOCK
CB = D
NCB = FF // CB
SCALE = HEAD_DIM ** (-0.5)
BF = jnp.bfloat16
F32 = jnp.float32
MIB = 1 << 20

COLOURS = {"v": pltpu.VMEM, "h": pltpu.HBM}
SPACES = {
    "v": pl.BlockSpec(memory_space=pltpu.VMEM),
    "h": pl.BlockSpec(memory_space=pltpu.HBM),
    "s": pl.BlockSpec(memory_space=pltpu.SMEM),
    "a": pl.BlockSpec(memory_space=pl.ANY),
}


HERE, CORE, MINE, Z, Y, OTHER_Y, Z_TWO, Z_NEAR, Z_BESIDE, OTHER_CORE = range(10)
SLOTS, BLOCKS = 10, 14


def indices(dp):
    here, place = lax.axis_index("head"), lax.axis_index("dp")
    mine, core = lax.div(here, 2), lax.rem(here, 2)
    z, y = lax.div(place, 2), lax.rem(place, 2)
    line = [z, y, 1 - y] + [lax.rem(z + step, 4) for step in (2, 3 + 2 * core, 1 + 2 * core)]
    blocks = [here, here ^ 2, here ^ 1, here ^ 3]
    if dp == 8:
        slots = [2 * mine, 2 * mine + 1, 2 - 2 * mine, 3 - 2 * mine]
    else:
        slots = list(range(NCB))
    return [here, core, mine] + line + [1 - core] + slots + blocks


def dot(left, right):
    return jnp.dot(left, right, preferred_element_type=F32)


def dot_nt(left, right):
    return lax.dot_general(left, right, (((1,), (1,)), ((), ())), preferred_element_type=F32)


def normed(t):
    centred = t - jnp.mean(t, axis=-1, keepdims=True)
    inverse = lax.rsqrt(jnp.mean(centred * centred, axis=-1, keepdims=True) + 1e-05)
    return centred * inverse, inverse


def norm_back(t, gain, cotangent):
    unit, inverse = normed(t)
    scaled = cotangent * gain
    mean_e = jnp.mean(scaled, axis=-1, keepdims=True)
    mean_en = jnp.mean(scaled * unit, axis=-1, keepdims=True)
    return inverse * (scaled - mean_e - unit * mean_en)


class Copies:
    def __init__(self, sems, first=0):
        self.sems, self.count = sems, first

    def __call__(self, src, dst):
        copy = pltpu.make_async_copy(src, dst, self.sems.at[self.count])
        self.count += 1
        copy.start()
        return copy


class Sequence:
    def __init__(self, dp):
        self.dp, self.token = dp, None

    def __call__(self, body, ins, outs, scratch=(), copies=0, name="keep", fetch=(), fill=(), fill_hbm=(), through=(), limit=8, save=(), cost=0.001):
        handed = [pltpu.with_memory_space_constraint(t, pltpu.VMEM) for t in fill]
        handed += [pltpu.with_memory_space_constraint(t, pltpu.HBM) for t in fill_hbm]
        handed += list(through)
        if self.token is not None:
            handed.append(pltpu.with_memory_space_constraint(self.token, pltpu.HBM))
        fetched = [(t.shape if part is None else t.shape[1:] if isinstance(part, int) else part[1], t.dtype)
                   for t, part in fetch]
        wants = [i for i, entry in enumerate(ins) if entry is None]
        ins = [entry for entry in ins if entry is not None]
        n_in, n_fetch, n_hand, n_fill = len(ins), len(fetch), len(handed), len(fill) + len(fill_hbm)
        n_out, n_save = len(outs), len(save)
        first = self.token is None

        def whole(*refs):
            refs = list(refs)
            in_refs, fetch_refs = refs[:n_in], refs[n_in:n_in + n_fetch]
            for i in wants:
                in_refs.insert(i, indices(self.dp))
            refs = refs[n_in + n_fetch:]
            refs = refs[n_hand:]
            out_refs, fetch_outs = refs[:n_out], refs[n_out:n_out + n_fetch]
            refs = refs[n_out + n_fetch:]
            fill_refs = refs[:n_fill]
            save_refs = refs[n_hand + first:][:n_save]
            refs = refs[n_hand + first + n_save:]
            scratch_refs, sems = refs[:len(scratch)], refs[len(scratch)]
            copy = Copies(sems, copies)
            waits = []
            for (_, part), source, target in zip(fetch, fetch_refs, fetch_outs, strict=True):
                if part is not None:
                    source = source.at[part if isinstance(part, int) else part[0](in_refs[0])]
                waits.append(copy(source, target))
            for place, target in zip(save, save_refs, strict=True):
                waits.append(copy(in_refs[place], target))
            if body is not None:
                body(*in_refs, *fill_refs, *out_refs, *scratch_refs, sems)
            for wait in waits:
                wait.wait()

        shapes = [COLOURS[space](shape, dtype) for space, shape, dtype in outs]
        shapes += [pltpu.VMEM(shape, dtype) for shape, dtype in fetched]
        shapes += [pltpu.VMEM(t.shape, t.dtype) for t in fill] + [pltpu.HBM(t.shape, t.dtype) for t in fill_hbm]
        shapes += [jax.ShapeDtypeStruct(t.shape, t.dtype) for t in through]
        shapes += [pltpu.HBM((8, 128), F32)]
        shapes += [pltpu.HBM(ins[place][1].shape, ins[place][1].dtype) for place in save]
        results = pl.pallas_call(
            whole,
            out_shape=tuple(shapes),
            in_specs=[SPACES[space] for space, _ in ins] + [SPACES["h"]] * n_fetch + [SPACES["v"]] * len(fill)
            + [SPACES["h"]] * len(fill_hbm) + [SPACES["a"]] * (n_hand - n_fill),
            out_specs=tuple([SPACES[space] for space, _, _ in outs] + [SPACES["v"]] * (n_fetch + len(fill))
                            + [SPACES["h"]] * len(fill_hbm) + [SPACES["a"]] * (n_hand - n_fill + first) + [SPACES["h"]] * n_save),
            scratch_shapes=[pltpu.VMEM(shape, dtype) for shape, dtype in scratch]
            + [pltpu.SemaphoreType.DMA((copies + n_fetch + n_save + 1,))],
            input_output_aliases={n_in + n_fetch + i: n_out + n_fetch + i for i in range(n_hand)},
            compiler_params=pltpu.CompilerParams(vmem_limit_bytes=limit * MIB),
            cost_estimate=pl.CostEstimate(
                flops=int(cost * 1e9), bytes_accessed=int(cost * 3e6), transcendentals=0),
            name=name,
        )(*[pltpu.with_memory_space_constraint(t, COLOURS[space]) if space in COLOURS else t for space, t in ins],
          *[pltpu.with_memory_space_constraint(t, pltpu.HBM) for t, _ in fetch],
          *handed)
        results = list(results)
        split = n_out + n_fetch + n_fill + len(through)
        self.token = results[split]
        return results[:split] + results[split + 1:]


def kv_body(layer, x_ref, got_ref, wk, wv, down, up, sd_ref, sb_ref, *rest):
    keys, values, inner_out, lift_out, xb_ref, _ = rest
    if layer == 0:
        xb_ref[:BLOCK] = x_ref[...]
        xb_ref[BLOCK:] = got_ref[0]
    else:
        xb_ref[...] = x_ref[...].astype(BF)
    xb = xb_ref[...]
    inner = dot(xb, down[...])
    inner_out[...] = inner.astype(BF)
    lift = dot((sd_ref[layer, 1:2, :] * inner).astype(BF), up[...])
    lift_out[...] = lift.astype(BF)
    values[...] = (dot(xb, wv[...]) + sb_ref[layer, 1:2, :] * lift).astype(BF)
    keys[...] = dot(xb, wk[...]).astype(BF)


def kv_call(seq, layer, x, got, wk, wv, down, up, sd, sb, **extra):
    return seq(
        functools.partial(kv_body, layer),
        [("v", t) for t in (x, got, wk, wv, down, up, sd, sb)],
        [("v", (ROWS, D), BF)] * 2 + [("v", (ROWS, RANK), BF), ("v", (ROWS, D), BF), ("v", (ROWS, D), BF)],
        name="keys_values", **extra)


def q_body(layer, x_ref, inner, wq, up, sd_ref, sb_ref, q_ref, qt_ref, lift_out, sems):
    lift = dot((sd_ref[layer, 0:1, :] * inner[...].astype(F32)).astype(BF), up[...])
    lift_out[...] = lift.astype(BF)
    q = (dot(x_ref[...], wq[...]) + sb_ref[layer, 0:1, :] * lift).astype(BF)
    q_ref[...] = q
    qt_ref[...] = (q * SCALE).T


def q_call(seq, layer, x, inner, wq, up, sd, sb, **extra):
    return seq(
        functools.partial(q_body, layer),
        [("v", x), ("v", inner), ("v", wq), ("v", up), ("v", sd), ("v", sb)],
        [("v", (ROWS, D), BF), ("v", (D, ROWS), BF), ("v", (ROWS, D), BF)],
        name="queries", **extra)


def split_heads(t):
    zero = jnp.zeros((HEAD_DIM, t.shape[1]), t.dtype)
    first = jnp.concatenate([t[:HEAD_DIM], zero], axis=0)
    second = jnp.concatenate([zero, t[HEAD_DIM:]], axis=0)
    return jnp.concatenate([first, second], axis=1)


def join_heads(t):
    n = t.shape[1] // 2
    return jnp.concatenate([t[:HEAD_DIM, :n], t[HEAD_DIM:, n:]], axis=0)


def stack_heads(t):
    lane = lax.broadcasted_iota(jnp.int32, (1, PAIR), 1)
    first = (lane < HEAD_DIM).astype(F32).astype(BF)
    second = (lane >= HEAD_DIM).astype(F32).astype(BF)
    return jnp.concatenate([t * first, t * second], axis=0)


def rows_of(near, far, cols):
    return jnp.concatenate([near[:, cols], far[:, cols]], axis=0)


def attend_body(layer, ids, lengths, x_ref, qt_ref, wo, gain_ref, keys, values, far_keys, far_values,
                y_ref, h_ref, e_ref, factor_ref, ctx_t_ref, ctx, sems):
    row = lax.broadcasted_iota(jnp.int32, (BLOCK, 2 * ROWS), 0)
    counts = lengths[ids[MINE]]
    live = counts[:, :1] + counts[:, 1:] + 4
    limits = [live - BLOCK * ids[BLOCKS + b] for b in range(4)]
    for pair in range(PAIRS):
        cols = slice(pair * PAIR, (pair + 1) * PAIR)
        raw = dot(rows_of(keys, far_keys, cols), split_heads(qt_ref[cols, :]))
        scores = jnp.concatenate(
            [jnp.where(row < limits[b], raw[b * BLOCK:(b + 1) * BLOCK], -1000000000.0) for b in range(4)],
            axis=0,
        )
        grown = jnp.exp(scores - jnp.max(scores, axis=0, keepdims=True))
        factor = 1.0 / jnp.sum(grown, axis=0, keepdims=True)
        factor_ref[pair:pair + 1, :] = factor
        e_ref[pair] = grown.astype(BF)
        ctx_t = join_heads(dot(rows_of(values, far_values, cols).T, e_ref[pair]) * factor)
        ctx_t_ref[cols, :] = ctx_t
        ctx[:, cols] = ctx_t.astype(BF).T
    h = x_ref[...].astype(F32) + dot(ctx[...], wo[...])
    h_ref[...] = h
    y_ref[...] = normed(h)[0] * gain_ref[layer, 0:1, :]


def attend_call(seq, layer, lengths, x, qt, kv, wo, gain, **extra):
    return seq(
        functools.partial(attend_body, layer),
        [None] + [("v", t) for t in (lengths, x, qt, wo, gain, *kv)],
        [("v", (ROWS, D), F32), ("v", (ROWS, D), F32), ("v", (PAIRS, LEN, 2 * ROWS), BF), ("v", (PAIRS, 2 * ROWS), F32),
         ("v", (D, ROWS), F32)],
        [((ROWS, D), BF)], name="attention", **extra)


def move(pairs):
    for source, target in pairs:
        target[...] = source[...].reshape(target.shape)


def ffn_hidden(yb, w_in, a_ref, g_ref, slots):
    for slot in slots:
        z = dot(yb, w_in[slot].reshape(D, CB))
        cdf = 0.5 * (1.0 + lax.erf(z * (0.5 ** 0.5)))
        g_ref[slot] = (cdf + z * (jnp.exp(-0.5 * z * z) * 0.3989422804014327)).astype(BF)
        a_ref[slot] = (z * cdf).astype(BF)


def ffn_result(ids, total, a_ref, w_out, y=None):
    size = CB if y is None else CB // 2
    for slot in range(NCB):
        if y is None:
            hidden, rows = a_ref[slot], w_out[ids[SLOTS + slot]]
        else:
            hidden = a_ref[slot, :, pl.ds(pl.multiple_of(y * size, size), size)]
            rows = w_out[ids[SLOTS + slot], y]
        total = total + dot(hidden, rows.reshape(size, D))
    return total


def ffn_backward(layer, ids, c, h2, g_ref, h1, gain_ref, w_in, w_out, dh_ref):
    dh2 = norm_back(h2, gain_ref[layer, 1:2, :], c)
    dfb = dh2.astype(BF)
    total = dh2
    for slot in range(NCB):
        da = dot_nt(dfb, w_out[ids[SLOTS + slot]].reshape(CB, D))
        dz = (g_ref[slot].astype(F32) * da).astype(BF)
        total = total + dot_nt(dz, w_in[slot].reshape(D, CB))
    dh1 = norm_back(h1, gain_ref[layer, 0:1, :], total)
    dh_ref[...] = dh1


FFN_SHAPE = (NCB, ROWS, CB)


def ffn_first_body(ids, y_ref, in_ref, cut_ref, in_z, in_y, in_far, own_y, first, out0_z,
                   w_in, w_out, a_ref, g_ref, sems):
    copy = Copies(sems)
    w_in = [w_in.at[layer] for layer in range(LAYERS)]
    w_out = [w_out.at[layer] for layer in range(LAYERS)]
    owns = [[copy(source, target) for source, target in own_in(layer, ids, in_ref, w_in[layer])] for layer in range(LAYERS)]
    own_out = [copy(cut_ref.at[layer], w_out[layer].at[ids[Z], ids[Y]]) for layer in range(LAYERS)]
    lines = [(in_z, 0), (first, 0), (in_y, 0), (first, 6), (own_y, 0), (first, 3), (in_far, 0), (first, 9)]
    move(pieces_in(0, ids, lines, w_in[0]))
    for wait in owns[0]:
        wait.wait()
    ffn_hidden(y_ref[...].astype(BF), w_in[0], a_ref, g_ref, range(NCB // 2))
    move(pieces_in(1, ids, lines, w_in[1]))
    for side, line in enumerate([(out0_z, 0), (first, 13)]):
        move(line_moves(ids, line, side, slice(None), out_target(w_out[0], ids[Y])))
    for side, (ref, start) in enumerate([(own_y, 0), (first, 3)]):
        core = ids[CORE] if side == 0 else ids[OTHER_CORE]
        for layer in range(LAYERS):
            move([(ref.at[start + 1 + layer], w_out[layer].at[ids[Z], ids[OTHER_Y], core])])
    for wait in owns[1] + own_out:
        wait.wait()


def ffn_second_body(layer, slots, moves, n_refs, ids, y_ref, gain_ref, *rest):
    refs, rest = rest[:n_refs], rest[n_refs:]
    w_in, w_out, a_ref, g_ref, x_ref, h_ref, _ = rest
    move(moves[0](ids, refs, w_in, w_out))
    ffn_hidden(y_ref[...].astype(BF), w_in.at[layer], a_ref, g_ref, slots)
    move(moves[1](ids, refs, w_in, w_out))
    h_ref[...] = ffn_result(ids, y_ref[...], a_ref, w_out.at[layer])
    x_ref[...] = normed(h_ref[...])[0] * gain_ref[layer, 1:2, :]


def ffn_second_call(seq, layer, slots, moves, refs, y, gain, w_in, w_out, a, g, **extra):
    return seq(
        functools.partial(ffn_second_body, layer, slots, moves, len(refs)),
        [None, ("v", y), ("v", gain)] + [("v", t) for t in refs],
        [("v", (ROWS, D), F32), ("v", (ROWS, D), F32)], name="ffn", fill=[w_in, w_out, a, g], **extra)


FFN_SHAPE = (NCB, ROWS, CB)


def ffn_hidden_body(layer, slots, moves, n_refs, ids, y_ref, *rest):
    refs, (w_in, a_ref, g_ref, _) = rest[:n_refs], rest[n_refs:]
    move(moves(ids, refs, w_in.at[layer]))
    ffn_hidden(y_ref[...].astype(BF), w_in.at[layer], a_ref, g_ref, slots)


def ffn_hidden_call(seq, layer, slots, w_in, moves, refs, y, **extra):
    return seq(
        functools.partial(ffn_hidden_body, layer, slots, moves, len(refs)),
        [None, ("v", y)] + [("v", t) for t in refs], [("v", FFN_SHAPE, BF)] * 2, name="ffn_hidden", fill=[w_in], **extra)


def ffn_near_body(layer, slots, moves, n_refs, ids, y_ref, w_in, *rest):
    refs, (w_out, a_ref, g_ref, near_ref, _) = rest[:n_refs], rest[n_refs:]
    ffn_hidden(y_ref[...].astype(BF), w_in.at[layer], a_ref, g_ref, slots)
    w_out = w_out.at[layer]
    move(moves(ids, refs, w_out))
    near_ref[...] = ffn_result(ids, y_ref[...], a_ref, w_out, ids[Y])


def ffn_near_call(seq, layer, slots, w_in, w_out, a, g, moves, refs, y, **extra):
    return seq(
        functools.partial(ffn_near_body, layer, slots, moves, len(refs)),
        [None, ("v", y), ("v", w_in)] + [("v", t) for t in refs],
        [("v", (ROWS, D), F32)], name="ffn_near", fill=[w_out, a, g], **extra)


def ffn_both_body(layer, moves, n_refs, near, ids, y_ref, h1, gain_ref, got_ref, w_in, a_ref, g_ref, c_ref, *rest):
    refs, rest = rest[:n_refs], rest[n_refs:]
    w_out, x_ref, send_ref, dh_ref, c, sems = rest
    own = Copies(sems)(c_ref.at[ids[MINE]], c.at[pl.ds(0, BLOCK)])
    w_in, w_out = w_in.at[layer], w_out.at[layer]
    move(moves(ids, refs, w_out))
    h2 = ffn_result(ids, y_ref[...], a_ref, w_out, ids[OTHER_Y] if near else None)
    dh_ref[...] = h2
    x = normed(h2)[0] * gain_ref[layer, 1:2, :]
    x_ref[...] = x[:BLOCK].astype(BF)
    send_ref[...] = x[BLOCK:].astype(BF)
    own.wait()
    c[BLOCK:] = got_ref[1].astype(F32)
    ffn_backward(layer, ids, c[...], dh_ref[...], g_ref, h1[...], gain_ref, w_in, w_out, dh_ref)


def ffn_both_call(seq, layer, w_in, w_out, a, g, moves, refs, near, y, h1, gain, got, c, **extra):
    return seq(
        functools.partial(ffn_both_body, layer, moves, len(refs), near),
        [None] + [("v", t) for t in (y, h1, gain, got, w_in, a, g)] + [("h", c)] + [("v", t) for t in refs],
        [("v", (BLOCK, D), BF), ("v", (BLOCK, D), BF), ("v", (ROWS, D), F32)],
        [((ROWS, D), F32)], 1, "ffn_both", fill=[w_out], **extra)


def ffn_back_body(layer, ids, c_ref, h2, g, h1, gain_ref, w_in, w_out, dh_ref, sems):
    ffn_backward(layer, ids, c_ref[...], h2[...], g, h1[...], gain_ref, w_in.at[layer], w_out.at[layer], dh_ref)


def ffn_back_call(seq, layer, c, h2, g, h1, gain, w_in, w_out, **extra):
    return seq(
        functools.partial(ffn_back_body, layer),
        [None] + [("v", t) for t in (c, h2, g, h1, gain, w_in, w_out)],
        [("v", (ROWS, D), F32)], name="ffn_back", **extra)


def attend_back_body(dh_ref, wo, q, factor_ref, ctx_t_ref, keys, values, far_keys, far_values,
                     e_ref, own_ref, send_ref, dctx_ref, sems):
    dctx_ref[...] = dot_nt(dh_ref[...].astype(BF), wo[...]).astype(BF)
    for pair in range(PAIRS):
        cols = slice(pair * PAIR, (pair + 1) * PAIR)
        vcols = slice(D + pair * PAIR, D + (pair + 1) * PAIR)
        factor = factor_ref[pair:pair + 1, :]
        scaled = (split_heads(dctx_ref[:, cols].T).astype(F32) * factor).astype(BF)
        inner = jnp.sum(scaled.astype(F32) * split_heads(ctx_t_ref[cols, :]), axis=0, keepdims=True)
        e = e_ref[pair]
        ds = (e.astype(F32) * (dot(rows_of(values, far_values, cols), scaled) - inner)).astype(BF)
        dv = dot(e, scaled.T)
        dk = dot(ds[ROWS:], stack_heads(q[:, cols])) * SCALE
        own_ref[:, cols] = dv[:ROWS]
        send_ref[:, cols] = dk.astype(BF)
        send_ref[:, vcols] = dv[ROWS:].astype(BF)
        e_ref[pair] = ds


def attend_back_call(seq, dh, wo, q, kv, weights, **extra):
    e, *rest = weights
    return seq(
        attend_back_body,
        [("v", t) for t in (dh, wo, q, *rest, *kv)],
        [("v", (ROWS, D), F32), ("v", (ROWS, 2 * D), BF)],
        [((ROWS, D), BF)], name="attention_back", fill=[e], **extra)


def dq_body(layer, dh_ref, ds_ref, q, keys, far_keys, lift, inner, wq, up, sd_ref, sb_ref,
            dx_ref, dub_ref, dk_ref, gd_ref, gb_ref, dq_ref, sems):
    for pair in range(PAIRS):
        cols = slice(pair * PAIR, (pair + 1) * PAIR)
        dq_t = join_heads(dot(rows_of(keys, far_keys, cols).T, ds_ref[pair])) * SCALE
        dq_ref[:, cols] = dq_t.T.astype(BF)
        dk_ref[:, cols] = dot(ds_ref[pair, :ROWS], stack_heads(q[:, cols])) * SCALE
    dq = dq_ref[...]
    dqf = dq.astype(F32)
    gb_ref[...] = jnp.sum(dqf * lift[...].astype(F32), axis=0, keepdims=True)
    dpq = dot_nt((sb_ref[layer, 0:1, :] * dqf).astype(BF), up[...])
    gd_ref[...] = jnp.sum(dpq * inner[...].astype(F32), axis=0, keepdims=True)
    dub_ref[...] = sd_ref[layer, 0:1, :] * dpq
    dx_ref[...] = dh_ref[...] + dot_nt(dq, wq[...])


def dq_call(seq, layer, dh, ds, q, kv, lift, inner, wq, up, sd, sb, **extra):
    return seq(
        functools.partial(dq_body, layer),
        [("v", t) for t in (dh, ds, q, kv[0], kv[2], lift, inner, wq, up, sd, sb)],
        [("v", (ROWS, D), F32), ("v", (ROWS, RANK), F32), ("v", (ROWS, D), F32), ("v", (1, RANK), F32), ("v", (1, D), F32)],
        [((ROWS, D), BF)], name="queries_back", **extra)


def dv_body(layer, dub_ref, own_ref, got_ref, lift, inner, up, sd_ref, sb_ref, gdq_ref, gbq_ref, before_ref,
            dub_out, dv_ref, sums_ref, sems):
    sums_ref[...] = before_ref[...]
    sums_ref[4 * layer:4 * layer + 1, :] = gdq_ref[...]
    sums_ref[4 * layer + 2:4 * layer + 3, :D] = gbq_ref[...]
    dv = (own_ref[...] + got_ref[:, D:].astype(F32)).astype(BF)
    dv_ref[...] = dv
    dvf = dv.astype(F32)
    sums_ref[4 * layer + 3:4 * layer + 4, :D] = jnp.sum(dvf * lift[...].astype(F32), axis=0, keepdims=True)
    dpv = dot_nt((sb_ref[layer, 1:2, :] * dvf).astype(BF), up[...])
    sums_ref[4 * layer + 1:4 * layer + 2, :] = jnp.sum(dpv * inner[...].astype(F32), axis=0, keepdims=True)
    dub_out[...] = (dub_ref[...] + sd_ref[layer, 1:2, :] * dpv).astype(BF)


def dv_call(seq, layer, dub, own, got, lift, inner, up, sd, sb, gd, gb, before, **extra):
    return seq(
        functools.partial(dv_body, layer),
        [("v", t) for t in (dub, own, got, lift, inner, up, sd, sb, gd, gb, before)],
        [("v", (ROWS, RANK), BF), ("v", (ROWS, D), BF), ("v", (4 * LAYERS, RANK), F32)],
        name="values_back", **extra)


def dx_body(layer, dx_ref, dub_ref, dk_ref, got_ref, dv_ref, wk, wv, down, *rest):
    total = dx_ref[...] + dot_nt(dub_ref[...], down[...])
    total = total + dot_nt(dv_ref[...], wv[...])
    dk = (dk_ref[...] + got_ref[:, :D].astype(F32)).astype(BF)
    total = total + dot_nt(dk, wk[...])
    if layer == 0:
        own_ref, send_ref, _ = rest
        own_ref[...] = total[:BLOCK]
        send_ref[...] = total[BLOCK:].astype(BF)
    else:
        rest[0][...] = total


def dx_call(seq, layer, dx, dub, dk, got, dv, wk, wv, down, **extra):
    return seq(
        functools.partial(dx_body, layer),
        [("v", t) for t in (dx, dub, dk, got, dv, wk, wv, down)],
        [("v", (BLOCK, D), F32), ("v", (BLOCK, D), BF)] if layer == 0 else [("v", (ROWS, D), F32)],
        name="input_back", **extra)


def dx_kv_call(seq, dx, dk, got, dv, wk, wv):
    def body(dx_ref, dk_ref, got_ref, dv_ref, wk, wv, total_ref, sems):
        dk = (dk_ref[...] + got_ref[:, :D].astype(F32)).astype(BF)
        total_ref[...] = dx_ref[...] + dot_nt(dv_ref[...], wv[...]) + dot_nt(dk, wk[...])

    [total] = seq(body, [("v", t) for t in (dx, dk, got, dv, wk, wv)], [("v", (ROWS, D), F32)], name="keys_values_back")
    return total


def dx_rest_call(seq, dx, dub, down):
    def body(dx_ref, dub_ref, down, own_ref, send_ref, sems):
        total = dx_ref[...] + dot_nt(dub_ref[...], down[...])
        own_ref[...] = total[:BLOCK]
        send_ref[...] = total[BLOCK:].astype(BF)

    return seq(body, [("v", t) for t in (dx, dub, down)], [("v", (BLOCK, D), F32), ("v", (BLOCK, D), BF)], name="input_back")


def add_call(seq, *terms, **extra):
    def body(*refs):
        total = refs[0][...]
        for ref in refs[1:len(terms)]:
            total = total + ref[...]
        refs[len(terms)][...] = total

    return seq(body, [("v", t) for t in terms], [("v", terms[0].shape, F32)], name="add", **extra)


def store_call(seq, output, other_output, rows):
    def body(ids_ref, output_ref, other_ref, rows_ref, block_ref, grad_ref, sems):
        copy = Copies(sems)
        mine = ids_ref[MINE]
        stores = [copy(rows_ref, grad_ref.at[mine]), copy(output_ref, block_ref.at[mine]), copy(other_ref, block_ref.at[1 - mine])]
        for store in stores:
            store.wait()

    return seq(body, [None] + [("v", t) for t in (output, other_output, rows)],
               [("h", (2,) + t.shape, t.dtype) for t in (output, rows)], [], 3, "store")


def finish_call(seq, terms, got, input_grad):
    def body(ids_ref, got_ref, *refs):
        *terms_refs, grad_ref, gd_out, gb_out, wide, gd_ref, gb_ref, sems = refs
        copy = Copies(sems)
        wide[...] = got_ref[...].astype(F32)
        stores = [copy(wide, grad_ref.at[1 - ids_ref[MINE]])]
        total = terms_refs[0][...]
        for ref in terms_refs[1:]:
            total = total + ref[...]
        for layer in range(LAYERS):
            gd_ref[layer] = total[4 * layer:4 * layer + 2]
            gb_ref[layer] = total[4 * layer + 2:4 * layer + 4, :D]
        stores += [copy(gd_ref, gd_out), copy(gb_ref, gb_out)]
        for store in stores:
            store.wait()

    shapes = [((LAYERS, 2, RANK), F32), ((LAYERS, 2, D), F32)]
    return seq(body, [None, ("v", got)] + [("v", t) for t in terms], [("h", *t) for t in shapes],
               [(got.shape, F32)] + shapes, 3, "finish", fill_hbm=[input_grad])


def columns(block):
    return pl.ds(pl.multiple_of(block * CB, CB), CB)


def prepare_line_body(ids, in_ref, a_in, sems):
    copy, rows, waits = Copies(sems), in_ref.shape[1], []
    for layer in range(LAYERS):
        for q in range(2):
            waits.append(copy(in_ref.at[layer, :, columns(2 * ids[MINE] + q)], a_in.at[q, pl.ds(layer * rows, rows)]))
    for wait in waits:
        wait.wait()


def prepare_body(ids, x_ref, c_ref, in_ref, out_ref, own, sent, b_in, own_a, own_b, c_send, sems):
    copy = Copies(sems)
    here, core, mine = ids[HERE], ids[CORE], ids[MINE]
    rows = in_ref.shape[1]
    waits = [copy(c_ref.at[1 - mine], c_send)]
    for layer in range(LAYERS):
        part = pl.ds(layer * rows, rows)
        waits.append(copy(in_ref.at[layer, :, columns(here)], b_in.at[part]))
        waits.append(copy(in_ref.at[layer, :, columns(here)], own_a.at[part]))
    piece = own_a.shape[0] - rows
    half = pl.ds(0, rows), pl.ds(rows, rows)
    waits.append(copy(out_ref.at[0, core, half[0]], own_a.at[pl.ds(piece, rows)]))
    waits.append(copy(out_ref.at[0, core, half[1]], own_b.at[half[0]]))
    waits.append(copy(out_ref.at[1, core], own_b.at[pl.ds(rows, piece)]))
    waits += [copy(x_ref.at[1 - mine], sent.at[0]), copy(x_ref.at[mine], own)]
    waits[0].wait()
    sent[1] = c_send[...].astype(BF)
    for wait in waits[1:]:
        wait.wait()


def prepare_call(seq, x, c, ffn_in, halves):
    rows = (BLOCK, D)
    piece = halves.shape[2:]
    [a_in] = seq(prepare_line_body, [None, ("h", ffn_in)], [("v", (2,) + piece, BF)], [], 2 * LAYERS, "prepare")
    own, sent, *rest = seq(
        prepare_body,
        [None, ("h", x), ("h", c), ("h", ffn_in), ("h", halves)],
        [("v", rows, BF), ("v", (2,) + rows, BF), ("v", piece, BF)]
        + [("v", (piece[0] * 3 // 2,) + piece[1:], BF)] * 2,
        [(rows, F32)], 6 + 2 * LAYERS, "prepare")
    return own, sent, a_in, *rest


def everywhere(target):
    pairs = []
    for z in range(4):
        for y in range(2):
            for head in range(4):
                z_to, y_to, head_to = target(z, y, head)
                pairs.append(((2 * z + y) * 4 + head, (2 * (z_to % 4) + y_to) * 4 + head_to))
    return pairs


Z_ONE = everywhere(lambda z, y, head: (z + 1 - 2 * (head % 2), y, head))
TWO = everywhere(lambda z, y, head: (z + 2, y, head))
Y_SWAP = [(i, i ^ 1) for i in range(8)]
BOTH_SWAP = everywhere(lambda z, y, head: (z, 1 - y, head ^ 2))
Z_ALL = [everywhere(lambda z, y, head, other=other: (z ^ other, y, head)) for other in (2, 3, 1)]
ACROSS = [(i, i ^ 2) for i in range(4)]
BESIDE = [(i, i ^ 1) for i in range(4)]


def swap(t, pairs):
    return lax.ppermute(t, "head", pairs)


def both_axes(t, pairs):
    return lax.ppermute(t, ("dp", "head"), pairs)


def across_y(t):
    return lax.ppermute(t, "dp", Y_SWAP)


def lay_call(seq, arrays, outs, **extra):
    piece = arrays[0].shape[-2:]

    def length(part):
        return 1 if part is None else part.stop - part.start

    def body(*refs):
        for out, result in zip(outs, refs[len(arrays):], strict=False):
            start = 0
            for index, part in out:
                stop = start + length(part)
                result[start:stop] = refs[index][...][None] if part is None else refs[index][part]
                start = stop

    shapes = [(sum(length(part) for _, part in out),) + piece for out in outs]
    return seq(body, [("v", t) for t in arrays], [("v", shape, BF) for shape in shapes], name="lay", **extra)


def cut_call(seq, cuts):
    cut = cuts.shape[3:]

    def body(ids_ref, cuts_ref, a_ref, b_ref, sems):
        copy = Copies(sems)
        waits = []
        for core, target in ((0, a_ref.at[0]), (1, a_ref.at[1]), (ids_ref[CORE], b_ref)):
            waits.append(copy(cuts_ref.at[1, core, ids_ref[MINE]], target.at[0]))
            waits.append(copy(cuts_ref.at[1, core, pl.ds(2, 2)], target.at[pl.ds(1, 2)]))
        for wait in waits:
            wait.wait()

    return seq(body, [None, ("h", cuts)], [("v", (2, 3) + cut, BF), ("v", (3,) + cut, BF)], [], 6, "cut")


def cut_lay_call(seq, out_a, out_b, in_y_far, out0_y):
    cut = out_b.shape[1:]

    def body_z(a_ref, b_ref, line_ref, sems):
        line_ref[:2] = a_ref[...]
        line_ref[2] = b_ref[...]

    [line] = seq(body_z, [("v", out_a), ("v", out_b)], [("v", (3, 3) + cut, BF)], name="lay")
    return cut_lay_rest_call(seq, line, in_y_far, out0_y)


def cut_lay_rest_call(seq, line, in_y_far, out0_y):
    cut = line.shape[2:]
    piece = out0_y.shape[1:]

    def body(z_ref, far_ref, y_ref, line_ref, own_ref, common_ref, second_ref, sems):
        rows = piece[0] // LAYERS
        line_ref[:, :3] = z_ref[...]
        line_ref[:, 3:] = far_ref[:, rows:].reshape((3, 2) + cut)
        own_ref[...] = z_ref[:, 0]
        common_ref[...] = z_ref[:, 1:]
        second_ref[:, :rows] = far_ref[:, :rows]
        second_ref[:, rows:] = y_ref[...]

    return seq(body, [("v", t) for t in (line, in_y_far, out0_y)],
               [("v", (3, 5) + cut, BF), ("v", (3,) + cut, BF), ("v", (3, 2) + cut, BF),
                ("v", (3, piece[0] // LAYERS + piece[0]) + piece[1:], BF)], name="lay")


def window_lay_call(seq, in_a, in_b, own_a, own_b):
    piece = in_b.shape

    def body(a_ref, b_ref, own_a_ref, own_b_ref, z_ref, x_ref, own_ref, sems):
        full, half = piece[0], piece[0] // 2
        own_ref[0] = own_a_ref[:full]
        own_ref[1, :half] = own_a_ref[full:]
        own_ref[1, half:] = own_b_ref[:half]
        own_ref[2] = own_b_ref[half:]
        for ref in (z_ref, x_ref):
            ref[:2] = a_ref[...]
            ref[2] = b_ref[...]
        x_ref[3] = own_a_ref[:full]

    return seq(body, [("v", t) for t in (in_a, in_b, own_a, own_b)],
               [("v", (count,) + piece, BF) for count in (3, 4, 3)], name="lay")


def first_lay_call(seq, arrays):
    piece = arrays[0].shape[-2:]
    extra = -(-2 * ROWS // piece[0])

    def body(out0_z, in_z, own_y, in_y, in_far, keys, values, first_ref, sems):
        for start, ref in ((0, in_z), (3, own_y), (6, in_y), (9, in_far), (13, out0_z)):
            first_ref[start:start + ref.shape[0]] = ref[...]
        both = jnp.concatenate([keys[...], values[...]], axis=0)
        for i in range(extra):
            rows = min(piece[0], 2 * ROWS - i * piece[0])
            first_ref[16 + i, :rows] = both[i * piece[0]:i * piece[0] + rows]

    return seq(body, [("v", t) for t in arrays], [("v", (16 + extra,) + piece, BF)], name="lay")


def far_body(first_ref, keys, values, sems):
    rows, count = first_ref.shape[1], first_ref.shape[0] - 16
    both = first_ref[16:].reshape(count * rows, D)
    keys[...] = both[:ROWS]
    values[...] = both[ROWS:2 * ROWS]


def last_body(own_y, common_y, own_yx, out_ref, sems):
    out_ref[:, 0] = own_y[...]
    out_ref[:, 1:3] = common_y[...]
    out_ref[:, 3] = own_yx[...]


def line_moves(ids, line, side, part, target):
    core, z_near = (ids[CORE], ids[Z_NEAR]) if side == 0 else (ids[OTHER_CORE], ids[Z_BESIDE])
    ref, start = line
    return [(ref.at[pl.ds(start, 2), part], target(z_near, pl.ds(0, 2))),
            (ref.at[start + 2, part], target(ids[Z_TWO], core))]


def in_target(dst, slot, y):
    def target(z, piece):
        return dst.at[pl.ds(slot, 2) if not isinstance(piece, jax.Array) else slot + piece, z, y]

    return target


def own_in(layer, ids, ref, dst):
    columns = [pl.ds(pl.multiple_of(ids[SLOTS + slot] * CB, CB), CB) for slot in range(NCB)]
    return [(ref.at[layer, :, columns[slot]], dst.at[slot, ids[Z], ids[Y]]) for slot in range(NCB)]


def pieces_in(layer, ids, lines, dst):
    part = pl.ds(layer * dst.shape[3], dst.shape[3])
    z, y = ids[Z], (ids[Y], ids[OTHER_Y])
    moves = []
    for side in range(2):
        core = ids[CORE] if side == 0 else ids[OTHER_CORE]
        along, across, own, far = lines[side::2]
        moves += line_moves(ids, along, side, part, in_target(dst, 0, y[0]))
        moves += line_moves(ids, across, side, part, in_target(dst, 0, y[1]))
        moves.append((own[0].at[own[1], part], dst.at[core, z, y[1]]))
        moves += line_moves(ids, far, side, part, in_target(dst, 2, y[0]))
        moves.append((far[0].at[far[1] + 3, part], dst.at[2 + core, z, y[1]]))
    return moves


def out_target(dst, y, cut=None):
    def target(z, piece):
        if not isinstance(piece, jax.Array):
            return dst.at[z, y] if cut is None else dst.at[z, y, :, cut]
        return dst.at[z, y, piece] if cut is None else dst.at[z, y, piece, cut]

    return target


def last_pieces(ids, refs, w_in, w_out):
    rows = pl.ds(0, w_in.shape[4])
    return [pair for side in range(2)
            for pair in line_moves(ids, (refs[side], 0), side, rows, in_target(w_in.at[0], 2, ids[OTHER_Y]))]


def last_pieces_more(ids, refs, w_in, w_out):
    in_y_far, second, out0_y, out1_z = refs
    rows = w_in.shape[4]
    moves = line_moves(ids, (out0_y, 0), 0, slice(None), out_target(w_out.at[0], ids[OTHER_Y]))
    moves += line_moves(ids, (second, 0), 1, pl.ds(rows, second.shape[1] - rows), out_target(w_out.at[0], ids[OTHER_Y]))
    moves += line_moves(ids, (in_y_far, 0), 0, pl.ds(rows, rows), in_target(w_in.at[1], 2, ids[OTHER_Y]))
    return moves + cut_line(ids, out1_z, 0, w_out.at[1])


def cut_line(ids, ref, side, dst):
    x, y = ids[MINE], ids[Y]
    return (line_moves(ids, (ref, 0), side, 0, out_target(dst, y, x))
            + line_moves(ids, (ref, 0), side, pl.ds(1, 2), out_target(dst, y, pl.ds(2, 2))))


def line_pieces(ids, refs, w_in):
    return line_moves(ids, (refs[0], 0), 1, pl.ds(3, 2), in_target(w_in, 2, ids[OTHER_Y]))


def near_pieces(ids, refs, w_out):
    core_line, *refs, last = refs
    moves = cut_line(ids, core_line, 1, w_out)
    for side in range(2):
        moves += line_moves(ids, (refs[side], 0), side, slice(None), out_target(w_out, ids[Y], 1 - ids[MINE]))
    return moves + cut_pieces(ids, [last], w_out, 0)


def cut_pieces(ids, refs, w_out, side=1):
    x, moves = ids[MINE], []
    for part, cut in ((0, x), (pl.ds(1, 2), pl.ds(2, 2)), (3, 1 - x)):
        moves += line_moves(ids, (refs[0], 0), side, part, out_target(w_out, ids[OTHER_Y], cut))
    return moves


def nothing(*_):
    return []


def plain_gather(ffn_in, ffn_out):
    whole_in = lax.all_gather(ffn_in, "dp", axis=1, tiled=True)
    whole_out = lax.all_gather(ffn_out, "dp", axis=1, tiled=True)
    return jnp.stack([whole_in[:, :, cb * CB:(cb + 1) * CB] for cb in range(NCB)], axis=1), whole_out.reshape(LAYERS, NCB, CB, D)


def local(block_input, part_lengths, query_weight, key_weight, value_weight, out_weight, down_shared, up_shared,
          scale_d, scale_b, ln_gain, ffn_in, ffn_out, out_grad):
    mine = lax.axis_index("head") // 2
    dp = lax.axis_size("dp")
    seq = Sequence(dp)
    halves = ffn_out.reshape(LAYERS, 2, ffn_out.shape[1] // 2, D)
    scales = (scale_d, scale_b)
    if dp == 8:
        rows_in, piece = ffn_in.shape[1], halves.shape[2:]
        cuts = halves.reshape(LAYERS, 2, 4, piece[0] // 4, D)
        cut = cuts.shape[3:]
        line = [(0, slice(0, 2)), (1, None)]

        own, sent, a_in, b_in, own_a, own_b = prepare_call(seq, block_input, out_grad, ffn_in, halves)
        in_a, in_b = both_axes(a_in, Z_ONE), both_axes(b_in, TWO)
        got, own_a, own_b = swap(sent, ACROSS), across_y(own_a), across_y(own_b)
        wk0, wv0, down, up, a_out, b_out = seq(
            None, [None], [], name="fetch",
            fetch=[(key_weight, 0), (value_weight, 0), (down_shared, None), (up_shared, None),
                   (halves, 0), (halves, ((lambda ids_ref: (0, ids_ref[CORE])), piece))])
        keys, values, inner0, lift_v0, xb, wq0 = kv_call(
            seq, 0, own, got, wk0, wv0, down, up, *scales, fetch=[(query_weight, 0)])
        q0, qt, lift_q0, wo0 = q_call(seq, 0, xb, inner0, wq0, up, *scales, fetch=[(out_weight, 0)])
        in_z, in_x, own_y = window_lay_call(seq, in_a, in_b, own_a, own_b)
        out_a, out_b = both_axes(a_out, Z_ONE), both_axes(b_out, TWO)
        in_y, in_far = across_y(in_z), swap(in_x, ACROSS)
        a_out, b_out = cut_call(seq, cuts)
        [out0_z] = lay_call(seq, [out_a, out_b], [line])
        [first] = first_lay_call(seq, [out0_z, in_z, own_y, in_y, in_far, keys, values])
        out_a, out_b = both_axes(a_out, Z_ONE), both_axes(b_out, TWO)
        out0_y, in_y_far, first = across_y(out0_z), swap(in_y, ACROSS), swap(first, BESIDE)
        kv = (keys, values, *seq(far_body, [("v", first)], [("v", (ROWS, D), BF)] * 2, name="far"))
        y, h10, *p0 = attend_call(seq, 0, part_lengths, xb, qt, kv, wo0, ln_gain)
        stored0 = (kv, q0, inner0, lift_q0, lift_v0, h10, p0, wk0, wv0, wq0, wo0)
        w_in, w_out, a, g0, wk, wv, wq, wo = seq(
            ffn_first_body,
            [None, ("v", y), ("h", ffn_in), ("h", cuts)]
            + [("v", t) for t in (in_z, in_y, in_far, own_y, first, out0_z)],
            [("v", (LAYERS, NCB, 4, 2, rows_in, CB), BF), ("v", (LAYERS, NCB, 2, 2, 4) + cut, BF)]
            + [("v", FFN_SHAPE, BF)] * 2, [], 2 * NCB + 2, "ffn_first",
            fetch=[(t, 1) for t in (key_weight, value_weight, query_weight, out_weight)])
        out1_z, out1_own, out1_common, second = cut_lay_call(seq, out_a, out_b, in_y_far, out0_y)
        out1_own_y, out1_own_x, out1_common_y = across_y(out1_own), swap(out1_own, ACROSS), across_y(out1_common)
        second, out1_z_core = swap(second, BESIDE), swap(out1_z, BESIDE)
        x, h20, w_in, w_out, a, g0 = ffn_second_call(
            seq, 0, range(NCB // 2, NCB), (last_pieces, last_pieces_more), [in_y_far, second, out0_y, out1_z],
            y, ln_gain, w_in, w_out, a, g0)
        keys, values, inner, lift_v, xb, out1_z_core = kv_call(
            seq, 1, x, got, wk, wv, down, up, *scales, through=[out1_z_core])
        [out1_own_x] = seq(None, [], [], through=[out1_own_x])
        out1_own_yx, third_core = swap(out1_own_y, ACROSS), swap(out1_own_x, BESIDE)
        kv = (keys, values, swap(keys, BESIDE), swap(values, BESIDE))
        q, qt, lift_q = q_call(seq, 1, xb, inner, wq, up, *scales)
        y, h1, *p = attend_call(seq, 1, part_lengths, x, qt, kv, wo, ln_gain)
        a, g, w_in = ffn_hidden_call(seq, 1, range(NCB - 1), w_in, line_pieces, [out1_z_core], y)
        last, third_core = seq(last_body, [("v", t) for t in (out1_own_y, out1_common_y, out1_own_yx)],
                               [("v", (3, 4) + cut, BF)], name="lay", through=[third_core])
        last_core = swap(last, BESIDE)
        y, w_out, a, g = ffn_near_call(
            seq, 1, range(NCB - 1, NCB), w_in, w_out, a, g, near_pieces, [out1_z_core, out1_own_x, third_core, last], y)
        moves, refs = cut_pieces, [last_core]
    else:
        def pick(t, index):
            return lax.dynamic_index_in_dim(t, index, 0, keepdims=False)

        x = pick(block_input, mine)
        got = swap(jnp.stack([pick(block_input, 1 - mine), pick(out_grad, 1 - mine).astype(BF)]), ACROSS)
        blocks_in, blocks_out = plain_gather(ffn_in, ffn_out)
        for layer in range(LAYERS):
            wk, wv, down, up, wq, wo = seq(
                None, [], [], name="fetch",
                fetch=[(key_weight, layer), (value_weight, layer), (down_shared, None), (up_shared, None),
                       (query_weight, layer), (out_weight, layer)])
            keys, values, inner, lift_v, xb = kv_call(seq, layer, x, got, wk, wv, down, up, *scales)
            kv = (keys, values, swap(keys, BESIDE), swap(values, BESIDE))
            q, qt, lift_q = q_call(seq, layer, xb, inner, wq, up, *scales)
            y, h1, *p = attend_call(
                seq, layer, part_lengths, xb if layer == 0 else x, qt, kv, wo, ln_gain)
            if layer == 0:
                a, g0 = seq(None, [], [("v", FFN_SHAPE, BF)] * 2)
                w_in, w_out = seq(None, [], [], name="fetch", fetch=[(blocks_in, None), (blocks_out, None)])
                x, h20, w_in, w_out, a, g0 = ffn_second_call(
                    seq, 0, range(NCB), (nothing, nothing), [], y, ln_gain, w_in, w_out, a, g0)
                stored0 = (kv, q, inner, lift_q, lift_v, h1, p, wk, wv, wq, wo)
        a, g, w_in = ffn_hidden_call(seq, 1, range(NCB), w_in, nothing, [], y)
        moves, refs = nothing, []
    output, other_output, dh, w_out = ffn_both_call(
        seq, 1, w_in, w_out, a, g, moves, refs, dp == 8, y, h1, ln_gain, got, out_grad)
    own, send, ds = attend_back_call(seq, dh, wo, q, kv, p)
    got = swap(send, BESIDE)
    dx, dub, dk, gd_q, gb_q = dq_call(seq, 1, dh, ds, q, kv, lift_q, inner, wq, up, *scales)
    dub, dv, sums = dv_call(
        seq, 1, dub, own, got, lift_v, inner, up, *scales, gd_q, gb_q, jnp.zeros((4 * LAYERS, RANK), F32))
    [cotangent] = dx_call(seq, 1, dx, dub, dk, got, dv, wk, wv, down)
    kv, q, inner, lift_q, lift_v, h1, p, wk, wv, wq, wo = stored0
    [dh] = ffn_back_call(seq, 0, cotangent, h20, g0, h1, ln_gain, w_in, w_out)
    own, send, ds, other_output = attend_back_call(seq, dh, wo, q, kv, p, through=[other_output])
    got, other_output = swap(send, BESIDE), swap(other_output, ACROSS)
    dx, dub, dk, gd_q, gb_q = dq_call(seq, 0, dh, ds, q, kv, lift_q, inner, wq, up, *scales)
    dub, dv, sums = dv_call(seq, 0, dub, own, got, lift_v, inner, up, *scales, gd_q, gb_q, sums)
    if dp == 8:
        other_sums = swap(sums, BESIDE)
        dx = dx_kv_call(seq, dx, dk, got, dv, wk, wv)
        [sums] = add_call(seq, sums, other_sums)
        parts = [both_axes(sums, BOTH_SWAP), swap(sums, ACROSS), across_y(sums)]
        rows, last_rows = dx_rest_call(seq, dx, dub, down)
        got = swap(last_rows, ACROSS)
        [sums] = add_call(seq, sums, *parts, cost=10)
        parts = [both_axes(sums, along) for along in Z_ALL]
    else:
        rows, last_rows = dx_call(seq, 0, dx, dub, dk, got, dv, wk, wv, down)
        got = swap(last_rows, ACROSS)
        sums, parts = lax.psum(sums, ("dp", "head")), []
    block_output, input_grad = store_call(seq, output, other_output, rows)
    grad_d, grad_b, input_grad = finish_call(seq, [sums, *parts], got, input_grad)
    return block_output, input_grad, grad_d, grad_b


def solution(mesh):
    both = P(None, ("dp", "head"), None)
    in_specs = (both, P(None, "dp", None), P(), P(), P(), P(), P(), P(), P(), P(), P(),
                P(None, "dp", None), P(None, "dp", None), both)
    out_specs = (both, both, P(), P())
    return jax.shard_map(local, mesh=mesh, in_specs=in_specs, out_specs=out_specs, check_vma=False)
```
